128 devices in a mesh: seq: 16 (over x, y_hi, core), grp: 8 (over y_lo, z).
Axes of the slice: x: 4, y: 4 (y_hi: 2, y_lo: 2; y = y_hi * 2 + y_lo), z: 4, core: 2. Of those that a mesh axis runs over, the one named last changes fastest.
Arguments:
- inputs: bfloat16 [32768, 1024], P('seq'), may hold values from -13 to 13
- latents: bfloat16 [8192, 1024], P('seq'), may hold values from -27 to 27
- w_query: bfloat16 [1024, 1024], P(None, 'grp')
- w_key: bfloat16 [1024, 1024], P(None, 'grp')
- w_value: bfloat16 [1024, 1024], P(None, 'grp'), may hold values from -0.1875 to 0.1875
- w_out: bfloat16 [1024, 1024], P('grp'), may hold values from -6 to 6
- positions: int32 [8192], replicated, may hold values from 8192 to 32767, as said below
- block_mask: int32 [64, 256], replicated, may hold values 0 or 1
Outputs:
- latent_update: bfloat16 [8192, 1024], P(('seq', 'grp'))
The draws below stay inside these ranges and needn't reach their ends.
Inputs may be any that keep to these rules, and one draw needn't show every extreme that they name: `positions`: each latent's position in the input sequence.
All inputs are finite; a program needn't handle non-finite values.
Results may differ from the reference program's by a relative error of at most 0.035.
Values may be sent and summed in bfloat16 or wider, within the bound.
No kernel may reach another device: no remote copies, remote signals or barrier semaphores. Data moves between devices by JAX's collectives and lax.ppermute only.
A program may use at most 128 MiB of HBM per device.

```python
import jax
import jax.numpy as jnp
from jax import lax

D = 1024
H = 16
HS = 64
BLOCK = 128
LAT_DEV = 512
LAT = 8192
N_IN = 32768


def shared_positions(key):
    inner = jax.random.fold_in(key, 101)
    spots = jax.random.randint(inner, (LAT,), N_IN // 4, N_IN, dtype=jnp.int32)
    first_end = jax.random.randint(jax.random.fold_in(key, 102), (), 0, LAT, dtype=jnp.int32)
    offset = jax.random.randint(jax.random.fold_in(key, 106), (), 1, LAT, dtype=jnp.int32)
    spots = spots.at[first_end].set(N_IN - 1)
    spots = spots.at[(first_end + offset) % LAT].set(N_IN // 4)
    return spots


def shared_query(key):
    raw = jnp.clip(jax.random.normal(jax.random.fold_in(key, 105), (D, H * HS), jnp.float32), -6.0, 6.0)
    return raw * D ** (-0.5)


def draw_positions(key, part):
    return shared_positions(key)


def draw_latents(key, part):
    key = jax.random.fold_in(key, 1)
    drawn = jnp.clip(jax.random.normal(key, (LAT, D), jnp.float32), -4.0, 4.0)
    return drawn.astype(jnp.bfloat16)


def draw_inputs(key, part):
    key = jax.random.fold_in(key, 2)
    drawn = jnp.clip(jax.random.normal(key, (N_IN, D), jnp.float32), -4.0, 4.0)
    return drawn.astype(jnp.bfloat16)


def draw_w_query(key, part):
    base = shared_query(key)
    return base.astype(jnp.bfloat16)


def draw_w_key(key, part):
    key = jax.random.fold_in(key, 5)
    own = jnp.clip(jax.random.normal(key, (D, H * HS), jnp.float32), -6.0, 6.0) * D ** (-0.5)
    result = own
    return result.astype(jnp.bfloat16)


def plant(drawn, own_key, low, high):
    extent = drawn.shape
    spot = [jax.random.randint(jax.random.fold_in(own_key, axis), (), 0, extent[axis]) for axis in range(len(extent))]
    drawn = drawn.at[tuple(spot)].set(low)
    longest = extent.index(max(extent))
    spot[longest] = (spot[longest] + 1) % extent[longest]
    return drawn.at[tuple(spot)].set(high)


def steps_of(own_key, dims, pieces, low, top_value):
    factor_of = 1.0
    for axis_at, shards_of in pieces:
        draws = jax.random.uniform(jax.random.fold_in(jax.random.fold_in(own_key, 6), axis_at), (shards_of,), jnp.float32, low / len(pieces), top_value / len(pieces))
        factor_of = factor_of * jnp.repeat(jnp.exp(draws), dims[axis_at] // shards_of).reshape((-1,) + (1,) * (len(dims) - 1 - axis_at))
    return factor_of


def normal_values(key, extent, spread, bound, cuts=(), held_as=jnp.bfloat16):
    factor_of = steps_of(key, extent, cuts, -0.22, 0.18) if cuts else 1.0
    values = jax.random.normal(key, extent, jnp.float32) * spread * factor_of
    return jnp.minimum(jnp.maximum(values, -bound), bound).astype(held_as)


def setup_inputs(seed: int = 0) -> dict:
    key_of = jax.random.split(jax.random.key(seed), 9)
    return {
        "inputs": draw_inputs(jax.random.fold_in(key_of[8], 71), 0),
        "latents": draw_latents(jax.random.fold_in(key_of[8], 71), 0),
        "w_query": draw_w_query(jax.random.fold_in(key_of[8], 71), 0),
        "w_key": draw_w_key(jax.random.fold_in(key_of[8], 71), 0),
        "w_value": normal_values(key_of[4], (D, H * HS), D ** -0.5, 0.1875, ((1, 8),)),
        "w_out": normal_values(key_of[5], (H * HS, D), 1 ** -0.5, 6.0, ((0, 8),)),
        "positions": draw_positions(jax.random.fold_in(key_of[8], 71), 0),
        "block_mask": plant((jax.random.randint(key_of[7], (LAT // BLOCK, N_IN // BLOCK), 0, 2) < 1).astype(jnp.int32), jax.random.fold_in(key_of[7], 1), 0, 1),
    }


masked_score = -1.0e30


def allowed_pairs(row_spots, mask_rows, key_first, key_total):
    key_index = key_first + jnp.arange(key_total, dtype=jnp.int32)
    causal = key_index[None, :] <= row_spots[:, None]
    own_block = (key_index // BLOCK)[None, :] == (row_spots // BLOCK)[:, None]
    listed = jnp.repeat(jnp.repeat(mask_rows, BLOCK, axis=0), BLOCK, axis=1) == 1
    return causal & (listed | own_block)


def reference(inputs, latents, w_query, w_key, w_value, w_out, positions, block_mask):
    key_proj = jnp.dot(inputs, w_key, preferred_element_type=jnp.float32).astype(jnp.bfloat16)
    key_proj = key_proj.reshape(N_IN, H, HS).transpose(1, 0, 2)
    value_proj = jnp.dot(inputs, w_value, preferred_element_type=jnp.float32).astype(jnp.bfloat16)
    value_proj = value_proj.reshape(N_IN, H, HS).transpose(1, 0, 2)
    query_proj = jnp.dot(latents, w_query, preferred_element_type=jnp.float32).astype(jnp.bfloat16)
    query_proj = query_proj.reshape(LAT, H, HS).transpose(1, 0, 2)
    row_count = LAT_DEV

    def one_block(block_index):
        row_spots = lax.dynamic_slice_in_dim(positions, block_index * row_count, row_count, 0)
        mask_rows = lax.dynamic_slice_in_dim(block_mask, block_index * (row_count // BLOCK), row_count // BLOCK, 0)
        allowed = allowed_pairs(row_spots, mask_rows, 0, N_IN)

        def one_head(head_index):
            query_rows = lax.dynamic_slice_in_dim(query_proj[head_index], block_index * row_count, row_count, 0)
            scores = jnp.dot(query_rows, key_proj[head_index].T, preferred_element_type=jnp.float32) * HS ** -0.5
            masked = jnp.where(allowed, scores, masked_score)
            row_max = jnp.max(masked, axis=1, keepdims=True)
            weights = jnp.where(allowed, jnp.exp(masked - row_max), 0.0)
            denominator = jnp.sum(weights, axis=1, keepdims=True)
            summed = jnp.dot(weights.astype(jnp.bfloat16), value_proj[head_index], preferred_element_type=jnp.float32)
            return (summed / denominator).astype(jnp.bfloat16)

        return lax.map(one_head, jnp.arange(H, dtype=jnp.int32))

    attention = lax.map(one_block, jnp.arange(LAT // row_count, dtype=jnp.int32))
    attention = attention.transpose(0, 2, 1, 3).reshape(LAT, H * HS)
    return jnp.dot(attention, w_out, preferred_element_type=jnp.float32).astype(jnp.bfloat16)
```

```python
import functools

import jax
import jax.numpy as jnp
from jax import lax
from jax.experimental import pallas as pl
from jax.experimental.pallas import tpu as pltpu
from jax.sharding import PartitionSpec as P

HS = 64
BLOCK = 128
CHUNK = 8
KEY_BLOCKS = 32
ACC_ROWS = 72
LOG2E = 1.4426950408889634
masked_score = -1e30
lowest_max = -1e29


def attention_kernel(n_ref, code_ref, base_ref, q_ref, pos_ref, kv_ref, o_ref, s_a, s_b, acc, vt):
    row_blocks = n_ref.shape[0]
    per_shard = q_ref.shape[2] // BLOCK
    own_base = base_ref[0]
    partner_base = base_ref[1]
    key_iota = lax.broadcasted_iota(jnp.int32, (BLOCK, BLOCK), 0)

    for t in range(KEY_BLOCKS):
        tile = kv_ref[t * BLOCK : (t + 1) * BLOCK, :].T
        vt[:HS, t * BLOCK : (t + 1) * BLOCK] = tile[HS:, :]
    vt[HS:, :] = jnp.ones((ACC_ROWS - HS, KEY_BLOCKS * BLOCK), jnp.bfloat16)

    def clamp(r):
        return jnp.minimum(r, row_blocks - 1)

    def advance(r, c):
        last = c + 1 >= n_ref[clamp(r)]
        return jnp.where(last, jnp.minimum(r + 1, row_blocks), r), jnp.where(last, 0, c + 1)

    def key_offset(r, c, t):
        return pl.multiple_of(jnp.bitwise_and(code_ref[r, c * CHUNK + t], 31) * BLOCK, BLOCK)

    def scores(s_ref, r, c, max_before):
        r = clamp(r)
        cols = pl.ds(pl.multiple_of(lax.rem(r, per_shard) * BLOCK, BLOCK), BLOCK)
        q = q_ref[lax.div(r, per_shard), :, cols]
        q = jnp.concatenate([q, jnp.zeros_like(q)], 0)
        pos = pos_ref[pl.ds(r, 1), :]
        keys = jnp.concatenate([kv_ref[pl.ds(key_offset(r, c, t), BLOCK), :] for t in range(CHUNK)], 0)
        s_all = jnp.dot(keys, q, preferred_element_type=jnp.float32)
        best = None
        for t in range(CHUNK):
            code = code_ref[r, c * CHUNK + t]
            k = jnp.bitwise_and(code, 31)
            base = jnp.where(k < 16, own_base, partner_base - 16 * BLOCK) + k * BLOCK
            reach = jnp.where(jnp.bitwise_and(code, 32) > 0, 1 << 30, BLOCK)
            reach = jnp.where(code >= 64, reach, -(1 << 30))
            ahead = pos - base
            last_key = jnp.where(ahead < reach, ahead, -1)
            s = jnp.where(key_iota <= last_key, s_all[t * BLOCK : (t + 1) * BLOCK], masked_score)
            s_ref[t * BLOCK : (t + 1) * BLOCK, :] = s
            part = jnp.max(s.reshape(16, 8, BLOCK), 0)
            best = part if best is None else jnp.maximum(best, part)
        before = jnp.where(c == 0, lowest_max, max_before)
        now = jnp.maximum(before, jnp.max(best, 0, keepdims=True))
        return now.astype(jnp.bfloat16).astype(jnp.float32)

    def weigh(s_ref, r, c, max_before, max_now):
        p = jnp.exp2((s_ref[...] - max_now) * LOG2E).astype(jnp.bfloat16)
        shrink = jnp.where(c == 0, 0.0, jnp.exp2((max_before - max_now) * LOG2E))
        rr = clamp(r)
        values = jnp.concatenate([vt[:, pl.ds(key_offset(rr, c, t), BLOCK)] for t in range(CHUNK)], 1)
        a = acc[...] * shrink + jnp.dot(values, p, preferred_element_type=jnp.float32)
        acc[...] = a
        total = a[HS : HS + 1]
        low = total - total.astype(jnp.bfloat16).astype(jnp.float32)
        out = jnp.concatenate([a[: HS + 1], max_now, low, a[HS + 3 :]], 0).astype(jnp.bfloat16)
        cols = pl.ds(pl.multiple_of(lax.rem(r, per_shard) * BLOCK, BLOCK), BLOCK)
        o_ref[lax.div(r, per_shard), :, cols] = out

    acc[...] = jnp.zeros_like(acc)
    items = lax.fori_loop(0, row_blocks, lambda r, total: total + n_ref[r], jnp.int32(0))
    start = jnp.full((1, BLOCK), lowest_max, jnp.float32)
    first = scores(s_a, jnp.int32(0), jnp.int32(0), start)

    def two_items(_, state):
        r, c, max_before, max_now = state
        r1, c1 = advance(r, c)
        max_1 = scores(s_b, r1, c1, max_now)
        weigh(s_a, r, c, max_before, max_now)
        r2, c2 = advance(r1, c1)
        max_2 = scores(s_a, r2, c2, max_1)
        weigh(s_b, r1, c1, max_now, max_1)
        return r2, c2, max_1, max_2

    lax.fori_loop(0, lax.div(items + 1, 2), two_items, (jnp.int32(0), jnp.int32(0), start, first))


def attend(chunks, codes, bases, queries, spots, kv):
    shards, _, rows = queries.shape
    smem = pl.BlockSpec(memory_space=pltpu.SMEM)
    vmem = pl.BlockSpec(memory_space=pltpu.VMEM)
    return pl.pallas_call(
        attention_kernel,
        in_specs=[smem] * 3 + [vmem] * 3,
        out_specs=vmem,
        out_shape=jax.ShapeDtypeStruct((shards + 1, ACC_ROWS, rows), jnp.bfloat16),
        scratch_shapes=[
            pltpu.VMEM((CHUNK * BLOCK, BLOCK), jnp.float32),
            pltpu.VMEM((CHUNK * BLOCK, BLOCK), jnp.float32),
            pltpu.VMEM((ACC_ROWS, BLOCK), jnp.float32),
            pltpu.VMEM((ACC_ROWS, KEY_BLOCKS * BLOCK), jnp.bfloat16),
        ],
        compiler_params=pltpu.CompilerParams(vmem_limit_bytes=40 * 2**20),
        cost_estimate=pl.CostEstimate(flops=10**10, bytes_accessed=4 * 2**20, transcendentals=2**24),
    )(chunks, codes, bases, queries, spots, kv)


def work_list(spots, block_mask, key_blocks):
    listed = jnp.concatenate(
        [lax.dynamic_slice_in_dim(block_mask, first, 16, 1) for first in (key_blocks[0], key_blocks[16])], 1
    ) == 1
    own = jnp.any((spots // BLOCK)[:, :, None] == key_blocks[None, None, :], axis=1)
    reached = (key_blocks * BLOCK)[None, :] <= jnp.max(spots, axis=1)[:, None]
    active = (listed & reached) | own
    index = jnp.arange(KEY_BLOCKS, dtype=jnp.int32)
    earlier = index[None, :] < index[:, None]
    place = jnp.sum(active[:, None, :] & earlier[None], axis=2, dtype=jnp.int32)
    value = index[None, :] + 32 * listed.astype(jnp.int32) + 64
    chosen = active[:, None, :] & (place[:, None, :] == index[None, :, None])
    codes = jnp.sum(jnp.where(chosen, value[:, None, :], 0), axis=2, dtype=jnp.int32)
    count = jnp.sum(active, axis=1, dtype=jnp.int32)
    return jnp.maximum((count + CHUNK - 1) // CHUNK, 1), codes


def gather_groups(block):
    me = lax.axis_index("grp")
    other = lax.ppermute(block, "grp", [(g, g ^ 4) for g in range(8)])
    low = me < 4
    pair = jnp.stack([jnp.where(low, block, other), jnp.where(low, other, block)])
    turns = [pair] + [
        lax.ppermute(pair, "grp", [(g, (g & 4) | ((g + k) & 3)) for g in range(8)]) for k in (1, 2, 3)
    ]
    z = me % 4
    stacked = jnp.stack(turns)
    ordered = jnp.stack([lax.dynamic_index_in_dim(stacked, (z - i) % 4, 0, False) for i in range(4)], 1)
    return ordered.reshape(8 * block.shape[0], block.shape[1])


def body(inputs, latents, w_query, w_key, w_value, w_out, positions, block_mask):
    s = lax.axis_index("seq")
    core = s % 2
    spots = positions.reshape(-1, BLOCK)
    index = jnp.arange(16, dtype=jnp.int32)
    key_blocks = jnp.concatenate([s * 16 + index, (s ^ 1) * 16 + index])

    queries = lax.dot_general(
        w_query, latents, (((0,), (1,)), ((), ())), preferred_element_type=jnp.float32
    ).astype(jnp.bfloat16) * jnp.bfloat16(HS ** -0.5)
    halves = queries.reshape(2, HS, queries.shape[1])
    queries = lax.all_to_all(jnp.tile(halves, (8, 1, 1)), "seq", 0, 0)

    def head_weights(head):
        return jnp.concatenate(
            [lax.dynamic_slice_in_dim(w, head * HS, HS, 1) for w in (w_key, w_value)], 1
        )

    kv_own = jnp.dot(inputs, head_weights(core), preferred_element_type=jnp.float32).astype(jnp.bfloat16)
    kv_other = jnp.dot(inputs, head_weights(1 - core), preferred_element_type=jnp.float32).astype(jnp.bfloat16)
    kv_partner = lax.ppermute(kv_other, "seq", [(i, i ^ 1) for i in range(16)])
    kv = jnp.concatenate([kv_own, kv_partner], 0)

    chunks, codes = work_list(spots, block_mask, key_blocks)
    bases = jnp.stack([key_blocks[0] * BLOCK, key_blocks[16] * BLOCK])
    parts = attend(chunks, codes, bases, queries, spots, kv)[:16]
    parts = lax.all_to_all(parts, "seq", 0, 0).astype(jnp.float32)

    parts = parts.reshape(8, 2, ACC_ROWS, parts.shape[2])
    maxima = parts[:, :, HS + 1]
    scale = jnp.exp(maxima - jnp.max(maxima, axis=0, keepdims=True))
    total = jnp.sum((parts[:, :, HS] + parts[:, :, HS + 2]) * scale, axis=0)
    summed = jnp.sum(parts[:, :, :HS] * scale[:, :, None], axis=0)
    attention = (summed / total[:, None]).astype(jnp.bfloat16)
    attention = attention.reshape(2 * HS, -1).T.reshape(8, -1, 2 * HS)
    attention = lax.all_to_all(attention, "grp", 0, 0).transpose(1, 0, 2)
    attention = attention.reshape(attention.shape[0], -1)
    w_all = gather_groups(w_out)
    return jnp.dot(attention, w_all, preferred_element_type=jnp.float32).astype(jnp.bfloat16)


def solution(mesh):
    return jax.shard_map(
        body,
        mesh=mesh,
        in_specs=(
            P("seq", None),
            P("seq", None),
            P(None, "grp"),
            P(None, "grp"),
            P(None, "grp"),
            P("grp", None),
            P(),
            P(),
        ),
        out_specs=P(("seq", "grp"), None),
        check_vma=False,
    )
```

```python
import functools

import jax
import jax.numpy as jnp
from jax import lax
from jax.experimental import pallas as pl
from jax.experimental.pallas import tpu as pltpu
from jax.sharding import PartitionSpec as P

HS = 64
BLOCK = 128
TILES = 4
SLOTS = 4
KEY_BLOCKS = 32
ACC_ROWS = 72
LOG2E = 1.4426950408889634
SAFE_SCORE = 60.0
masked_score = -1e30
lowest_max = -1e29
SMEM = pl.BlockSpec(memory_space=pltpu.SMEM)
VMEM = pl.BlockSpec(memory_space=pltpu.VMEM)


def project_kernel(core_ref, x_ref, wk_ref, wv_ref, own_ref, other_ref, w_own, w_other):
    @pl.when(pl.program_id(0) == 0)
    def _():
        first = core_ref[0] == 0
        wk, wv = wk_ref[...], wv_ref[...]
        head_0 = jnp.concatenate([wk[:, :HS], wv[:, :HS]], 1)
        head_1 = jnp.concatenate([wk[:, HS:], wv[:, HS:]], 1)
        w_own[...] = jnp.where(first, head_0, head_1)
        w_other[...] = jnp.where(first, head_1, head_0)

    x = x_ref[...]
    own_ref[...] = jnp.dot(x, w_own[...], preferred_element_type=jnp.float32).astype(jnp.bfloat16)
    other_ref[...] = jnp.dot(x, w_other[...], preferred_element_type=jnp.float32).astype(jnp.bfloat16)


def project(core, inputs, w_key, w_value):
    keys, width = inputs.shape
    rows = 256
    out = jax.ShapeDtypeStruct((keys, 2 * HS), jnp.bfloat16)
    tile = pl.BlockSpec((rows, 2 * HS), lambda i: (i, 0))
    whole = pl.BlockSpec((width, 2 * HS), lambda i: (0, 0))
    return pl.pallas_call(
        project_kernel,
        grid=(keys // rows,),
        in_specs=[SMEM, pl.BlockSpec((rows, width), lambda i: (i, 0)), whole, whole],
        out_specs=[tile, tile],
        out_shape=[out, out],
        scratch_shapes=[pltpu.VMEM((width, 2 * HS), jnp.bfloat16)] * 2,
        compiler_params=pltpu.CompilerParams(vmem_limit_bytes=32 * 2**20),
        cost_estimate=pl.CostEstimate(flops=2 * keys * width * 4 * HS, bytes_accessed=5 * 2**20, transcendentals=0),
    )(core, inputs, w_key, w_value)


def prepare_kernel(own_ref, partner_ref, kv_ref, vt_ref, norm_ref):
    most = None
    for t in range(KEY_BLOCKS):
        source, at = (own_ref, t) if t < KEY_BLOCKS // 2 else (partner_ref, t - KEY_BLOCKS // 2)
        tile = source[at * BLOCK : (at + 1) * BLOCK, :]
        kv_ref[t * BLOCK : (t + 1) * BLOCK, :] = tile
        turned = tile.T
        vt_ref[:HS, t * BLOCK : (t + 1) * BLOCK] = turned[HS:, :]
        k = turned[:HS, :].astype(jnp.float32)
        squares = jnp.sum(k * k, axis=0, keepdims=True)
        most = squares if most is None else jnp.maximum(most, squares)
    vt_ref[HS:, :] = jnp.ones((ACC_ROWS - HS, KEY_BLOCKS * BLOCK), jnp.bfloat16)
    norm_ref[0] = jnp.max(most)


def prepare(own, partner):
    keys = 2 * own.shape[0]
    return pl.pallas_call(
        prepare_kernel,
        in_specs=[VMEM, VMEM],
        out_specs=[VMEM, VMEM, SMEM],
        out_shape=[
            jax.ShapeDtypeStruct((keys, 2 * HS), jnp.bfloat16),
            jax.ShapeDtypeStruct((ACC_ROWS, keys), jnp.bfloat16),
            jax.ShapeDtypeStruct((1,), jnp.float32),
        ],
        compiler_params=pltpu.CompilerParams(vmem_limit_bytes=32 * 2**20),
    )(own, partner)


def attention_kernel(chips, count_ref, code_ref, base_ref, shard_ref, norm_ref, pos_ref, kv_ref, vt_ref, *rest):
    q_refs, o_refs = rest[:chips], rest[chips : 2 * chips]
    q_all, p_a, p_b, s_all, acc = rest[2 * chips :]
    blocks = 8 * chips
    own_base = base_ref[0]
    partner_base = base_ref[1]
    iota = lax.broadcasted_iota(jnp.int32, (BLOCK, BLOCK), 0)
    iota_half = iota.astype(jnp.float32).astype(jnp.bfloat16)

    most = None
    for i in range(chips):
        for j in range(2):
            q = q_refs[i][j]
            q_all[2 * i + j] = q
            q = q.astype(jnp.float32)
            squares = jnp.sum(q * q, axis=0, keepdims=True)
            most = squares if most is None else jnp.maximum(most, squares)
    safe = jnp.max(most) * norm_ref[0] <= SAFE_SCORE * SAFE_SCORE

    def clamp(r):
        return jnp.minimum(r, blocks - 1)

    def whole_block(r):
        return shard_ref[lax.div(r, 4)] * 4 + lax.rem(r, 4)

    def offset(i):
        return pl.multiple_of(i * BLOCK, BLOCK)

    def query(r):
        q = q_all[lax.div(r, 4), :, pl.ds(offset(lax.rem(r, 4)), BLOCK)]
        return jnp.concatenate([q, jnp.zeros_like(q)], 0)

    def key_blocks(row, c):
        return [jnp.bitwise_and(code_ref[row, c * TILES + t], KEY_BLOCKS - 1) for t in range(TILES)]

    def products(row, r, c):
        keys = jnp.concatenate([kv_ref[pl.ds(offset(k), BLOCK), :] for k in key_blocks(row, c)], 0)
        return jnp.dot(keys, query(r), preferred_element_type=jnp.float32)

    def values(row, c):
        return jnp.concatenate([vt_ref[:, pl.ds(offset(k), BLOCK)] for k in key_blocks(row, c)], 1)

    def last_key(row, c, t, pos, real):
        code = code_ref[row, c * TILES + t]
        k = jnp.bitwise_and(code, KEY_BLOCKS - 1)
        half = KEY_BLOCKS // 2
        base = jnp.where(k < half, own_base, partner_base - half * BLOCK) + k * BLOCK
        reach = jnp.where(jnp.bitwise_and(code, KEY_BLOCKS) > 0, 1 << 30, BLOCK)
        reach = jnp.where(jnp.logical_and(real, code >= 2 * KEY_BLOCKS), reach, -(1 << 30))
        ahead = pos - base
        return jnp.where(ahead < reach, jnp.minimum(ahead, BLOCK - 1), -1)

    def store(r, a, top):
        total = a[HS : HS + 1]
        low = total - total.astype(jnp.bfloat16).astype(jnp.float32)
        out = jnp.concatenate([a[: HS + 1], top, low, a[HS + 3 :]], 0).astype(jnp.bfloat16)
        return out

    def put(i, rr, out):
        o_refs[i][lax.div(rr, 4), :, pl.ds(offset(lax.rem(rr, 4)), BLOCK)] = out

    def advance(r, c):
        last = c + 1 >= count_ref[whole_block(clamp(r))]
        return jnp.where(last, jnp.minimum(r + 1, blocks), r), jnp.where(last, 0, c + 1)

    def step_slots(r, c):
        slots = []
        for _ in range(SLOTS):
            slots.append((r, c))
            r, c = advance(r, c)
        return slots, r, c

    @pl.when(safe)
    def _():
        acc[...] = jnp.zeros_like(acc)

        def weigh(p_ref, slots):
            for g, (r, c) in enumerate(slots):
                rr = clamp(r)
                row = whole_block(rr)
                s = products(row, rr, c)
                pos = pos_ref[pl.ds(row, 1), :]
                for t in range(TILES):
                    p = jnp.exp2(s[t * BLOCK : (t + 1) * BLOCK] * LOG2E).astype(jnp.bfloat16)
                    last = last_key(row, c, t, pos, r < blocks).astype(jnp.float32).astype(jnp.bfloat16)
                    at = (g * TILES + t) * BLOCK
                    p_ref[at : at + BLOCK, :] = jnp.where(iota_half <= last, p, jnp.zeros_like(p))

        def add(p_ref, slots):
            for g, (r, c) in enumerate(slots):
                v = values(whole_block(clamp(r)), c)
                at = g * TILES * BLOCK
                acc[r] += jnp.dot(v, p_ref[at : at + TILES * BLOCK, :], preferred_element_type=jnp.float32)

        slots_0, r0, c0 = step_slots(jnp.int32(0), jnp.int32(0))
        weigh(p_a, slots_0)

        def two_steps(_, state):
            r, c, r1, c1 = state
            slots, _, _ = step_slots(r, c)
            slots_1, r2, c2 = step_slots(r1, c1)
            weigh(p_b, slots_1)
            add(p_a, slots)
            slots_2, r3, c3 = step_slots(r2, c2)
            weigh(p_a, slots_2)
            add(p_b, slots_1)
            return r2, c2, r3, c3

        items = lax.fori_loop(0, blocks, lambda r, n: n + count_ref[whole_block(r)], jnp.int32(0))
        steps = lax.div(items + (2 * SLOTS - 1), 2 * SLOTS)
        lax.fori_loop(0, steps, two_steps, (jnp.int32(0), jnp.int32(0), r0, c0))

        for i in range(chips):
            def finish(rr, _, i=i):
                a = acc[i * 8 + rr]
                put(i, rr, store(rr, a, jnp.where(a[HS : HS + 1] > 0, 0.0, lowest_max)))
                return 0

            lax.fori_loop(0, 8, finish, 0)

    @pl.when(jnp.logical_not(safe))
    def _():
        for i in range(chips):
            def one_block(rr, _, i=i):
                r = i * 8 + rr
                row = whole_block(r)
                pos = pos_ref[pl.ds(row, 1), :]
                acc[0] = jnp.zeros((ACC_ROWS, BLOCK), jnp.float32)

                def one_slot(c, top):
                    s = products(row, r, c)
                    best = top
                    for t in range(TILES):
                        tile = s[t * BLOCK : (t + 1) * BLOCK]
                        tile = jnp.where(iota <= last_key(row, c, t, pos, True), tile, masked_score)
                        s_all[t * BLOCK : (t + 1) * BLOCK, :] = tile
                        best = jnp.maximum(best, jnp.max(tile, 0, keepdims=True))
                    best = best.astype(jnp.bfloat16).astype(jnp.float32)
                    p = jnp.exp2((s_all[...] - best) * LOG2E).astype(jnp.bfloat16)
                    shrink = jnp.exp2((top - best) * LOG2E)
                    acc[0] = acc[0] * shrink + jnp.dot(values(row, c), p, preferred_element_type=jnp.float32)
                    return best

                start = jnp.full((1, BLOCK), lowest_max, jnp.bfloat16).astype(jnp.float32)
                top = lax.fori_loop(0, count_ref[row], one_slot, start)
                put(i, rr, store(rr, acc[0], top))
                return 0

            lax.fori_loop(0, 8, one_block, 0)


def attend(counts, codes, bases, shards, norm, spots, kv, vt, queries):
    chips = len(queries)
    out = jax.ShapeDtypeStruct((2, ACC_ROWS, queries[0].shape[2]), jnp.bfloat16)
    return pl.pallas_call(
        functools.partial(attention_kernel, chips),
        in_specs=[SMEM] * 5 + [VMEM] * (3 + chips),
        out_specs=[VMEM] * chips,
        out_shape=[out] * chips,
        scratch_shapes=[
            pltpu.VMEM((2 * chips, HS, queries[0].shape[2]), jnp.bfloat16),
            pltpu.VMEM((SLOTS * TILES * BLOCK, BLOCK), jnp.bfloat16),
            pltpu.VMEM((SLOTS * TILES * BLOCK, BLOCK), jnp.bfloat16),
            pltpu.VMEM((TILES * BLOCK, BLOCK), jnp.float32),
            pltpu.VMEM((8 * chips + 1, ACC_ROWS, BLOCK), jnp.float32),
        ],
        compiler_params=pltpu.CompilerParams(vmem_limit_bytes=32 * 2**20),
        cost_estimate=pl.CostEstimate(
            flops=chips * 6 * 10**9, bytes_accessed=4 * 2**20, transcendentals=chips * 2**20
        ),
    )(counts, codes, bases, shards, norm, spots, kv, vt, *queries)


def combine_kernel(*refs):
    parts, out_ref = refs[:-1], refs[-1]
    for j in range(2):
        tops = [p[j, HS + 1 : HS + 2, :].astype(jnp.float32) for p in parts]
        top = functools.reduce(jnp.maximum, tops)
        scales = [jnp.exp(t - top) for t in tops]
        total = sum(
            (p[j, HS : HS + 1, :].astype(jnp.float32) + p[j, HS + 2 : HS + 3, :].astype(jnp.float32)) * scale
            for p, scale in zip(parts, scales)
        )
        summed = sum(p[j, :HS, :].astype(jnp.float32) * scale for p, scale in zip(parts, scales))
        out_ref[j] = (summed / total).astype(jnp.bfloat16)


def combine(parts):
    return pl.pallas_call(
        combine_kernel,
        in_specs=[VMEM] * len(parts),
        out_specs=VMEM,
        out_shape=jax.ShapeDtypeStruct((2, HS, parts[0].shape[2]), jnp.bfloat16),
        compiler_params=pltpu.CompilerParams(vmem_limit_bytes=32 * 2**20),
    )(*parts)


def work_list(spots, block_mask, first_own, first_partner):
    half = KEY_BLOCKS // 2
    index = jnp.arange(KEY_BLOCKS, dtype=jnp.int32)
    key_blocks = jnp.where(index < half, first_own, first_partner - half) + index
    listed = jnp.concatenate(
        [lax.dynamic_slice_in_dim(block_mask, first, half, 1) for first in (first_own, first_partner)], 1
    ) == 1
    own = jnp.any((spots // BLOCK)[:, :, None] == key_blocks[None, None, :], axis=1)
    reached = (key_blocks * BLOCK)[None, :] <= jnp.max(spots, axis=1)[:, None]
    active = (listed & reached) | own
    earlier = index[None, :] < index[:, None]
    place = jnp.sum(active[:, None, :] & earlier[None], axis=2, dtype=jnp.int32)
    value = index[None, :] + KEY_BLOCKS * listed.astype(jnp.int32) + 2 * KEY_BLOCKS
    chosen = active[:, None, :] & (place[:, None, :] == index[None, :, None])
    codes = jnp.sum(jnp.where(chosen, value[:, None, :], 0), axis=2, dtype=jnp.int32)
    count = jnp.sum(active, axis=1, dtype=jnp.int32)
    return jnp.maximum((count + TILES - 1) // TILES, 1), codes


def shifted(x_by, y_by):
    return [(s, ((s // 4 + x_by) % 4) * 4 + (s % 4 ^ 2 * y_by)) for s in range(16)]


def back(route):
    return [(b, a) for a, b in route]


CALLS = (((0, 1), (1, 0)), ((3, 0), (1, 1)), ((3, 1), (2, 0)), ((2, 1),), ((0, 0),))
SWAP = [(i, i ^ 1) for i in range(16)]


def body(inputs, latents, w_query, w_key, w_value, w_out, positions, block_mask):
    s = lax.axis_index("seq")
    core = s % 2
    me = lax.axis_index("grp")

    queries = lax.dot_general(
        w_query, latents, (((0,), (1,)), ((), ())), preferred_element_type=jnp.float32
    ).astype(jnp.bfloat16) * jnp.bfloat16(HS ** -0.5)
    first, second = queries[:HS], queries[HS:]
    mine = jnp.where(core == 0, first, second)
    theirs = jnp.where(core == 0, second, first)
    q_chip = jnp.stack([mine, lax.ppermute(theirs, "seq", SWAP)])
    arrived = {
        step: q_chip if step == (0, 0) else lax.ppermute(q_chip, "seq", shifted(*step))
        for call in CALLS
        for step in call
    }

    w_other = lax.ppermute(w_out, "grp", [(g, g ^ 4) for g in range(8)])
    w_pair = jnp.concatenate([w_out, w_other], 0)
    w_turns = [w_pair] + [
        lax.ppermute(w_pair, "grp", [(g, (g & 4) | ((g + k) & 3)) for g in range(8)]) for k in (1, 2, 3)
    ]

    kv_own, kv_other = project(core[None], inputs, w_key, w_value)
    kv, vt, norm = prepare(kv_own, lax.ppermute(kv_other, "seq", SWAP))

    per_device = inputs.shape[0] // BLOCK
    spots = positions.reshape(-1, BLOCK)
    counts, codes = work_list(spots, block_mask, s * per_device, (s ^ 1) * per_device)
    bases = jnp.stack([s, s ^ 1]) * inputs.shape[0]

    parts = []
    for n, call in enumerate(CALLS):
        came_from = [(((s // 4 + 4 - x_by) % 4) * 4 + (s % 4 ^ 2 * y_by)) for x_by, y_by in call]
        shards = jnp.stack([shard for c in came_from for shard in (c, c ^ 1)])
        blocks = [arrived[step] for step in call]
        if 1 <= n <= 3:
            blocks[0], w_turns[n] = lax.optimization_barrier((blocks[0], w_turns[n]))
        done = attend(counts, codes, bases, shards, norm, spots, kv, vt, blocks)
        for step, part in zip(call, done):
            parts.append(part if step == (0, 0) else lax.ppermute(part, "seq", back(shifted(*step))))

    attention = combine(parts)
    rows = attention.shape[2]
    swapped = lax.ppermute(attention[1], "seq", SWAP)
    attention = jnp.where(
        core == 0, jnp.concatenate([attention[0], swapped], 0), jnp.concatenate([swapped, attention[0]], 0)
    )
    attention = attention.T.reshape(8, rows // 8, 2 * HS)
    attention = lax.all_to_all(attention, "grp", 0, 0)
    result = 0.0
    for k, w in enumerate(w_turns):
        group = (me & 4) | ((me - k) & 3)
        heads = jnp.concatenate([attention[group], attention[group ^ 4]], 1)
        result += jnp.dot(heads, w, preferred_element_type=jnp.float32)
    return result.astype(jnp.bfloat16)


def solution(mesh):
    return jax.shard_map(
        body,
        mesh=mesh,
        in_specs=(
            P("seq", None),
            P("seq", None),
            P(None, "grp"),
            P(None, "grp"),
            P(None, "grp"),
            P("grp", None),
            P(),
            P(),
        ),
        out_specs=P(("seq", "grp"), None),
        check_vma=False,
    )
```

```python
import functools

import jax
import jax.numpy as jnp
from jax import lax
from jax.experimental import pallas as pl
from jax.experimental.pallas import tpu as pltpu
from jax.sharding import PartitionSpec as P

HS = 64
BLOCK = 128
TILES = 4
SLOTS = 2
ROWS = 2 * BLOCK
KEY_BLOCKS = 32
ACC_ROWS = 72
LOG2E = 1.4426950408889634
SAFE_SCORE = 60.0
masked_score = -1e30
lowest_max = -1e29
SMEM = pl.BlockSpec(memory_space=pltpu.SMEM)
VMEM = pl.BlockSpec(memory_space=pltpu.VMEM)


def project_kernel(core_ref, x_ref, wk_ref, wv_ref, own_ref, other_ref, w_all):
    @pl.when(pl.program_id(0) == 0)
    def _():
        first = core_ref[0] == 0
        wk, wv = wk_ref[...], wv_ref[...]
        head_0 = jnp.concatenate([wk[:, :HS], wv[:, :HS]], 1)
        head_1 = jnp.concatenate([wk[:, HS:], wv[:, HS:]], 1)
        w_all[:, : 2 * HS] = jnp.where(first, head_0, head_1)
        w_all[:, 2 * HS :] = jnp.where(first, head_1, head_0)

    both = jnp.dot(x_ref[...], w_all[...], preferred_element_type=jnp.float32).astype(jnp.bfloat16)
    own_ref[...] = both[:, : 2 * HS]
    other_ref[...] = both[:, 2 * HS :]


def project(core, inputs, w_key, w_value):
    keys, width = inputs.shape
    rows = 256
    out = jax.ShapeDtypeStruct((keys, 2 * HS), jnp.bfloat16)
    tile = pl.BlockSpec((rows, 2 * HS), lambda i: (i, 0))
    whole = pl.BlockSpec((width, 2 * HS), lambda i: (0, 0))
    return pl.pallas_call(
        project_kernel,
        grid=(keys // rows,),
        in_specs=[SMEM, pl.BlockSpec((rows, width), lambda i: (i, 0)), whole, whole],
        out_specs=[tile, tile],
        out_shape=[out, out],
        scratch_shapes=[pltpu.VMEM((width, 4 * HS), jnp.bfloat16)],
        compiler_params=pltpu.CompilerParams(vmem_limit_bytes=60 * 2**20),
        cost_estimate=pl.CostEstimate(flops=2 * keys * width * 4 * HS, bytes_accessed=5 * 2**20, transcendentals=0),
    )(core, inputs, w_key, w_value)


def prepare_kernel(own_ref, partner_ref, kv_ref, vt_ref, norm_ref):
    most = None
    for t in range(KEY_BLOCKS):
        source, at = (own_ref, t) if t < KEY_BLOCKS // 2 else (partner_ref, t - KEY_BLOCKS // 2)
        tile = source[at * BLOCK : (at + 1) * BLOCK, :]
        kv_ref[t * BLOCK : (t + 1) * BLOCK, :] = tile
        turned = tile.T
        vt_ref[:HS, t * BLOCK : (t + 1) * BLOCK] = turned[HS:, :]
        k = turned[:HS, :].astype(jnp.float32)
        squares = jnp.sum(k * k, axis=0, keepdims=True)
        most = squares if most is None else jnp.maximum(most, squares)
    vt_ref[HS:, :] = jnp.ones((ACC_ROWS - HS, KEY_BLOCKS * BLOCK), jnp.bfloat16)
    norm_ref[0] = jnp.max(most)


def prepare(own, partner):
    keys = 2 * own.shape[0]
    return pl.pallas_call(
        prepare_kernel,
        in_specs=[VMEM, VMEM],
        out_specs=[VMEM, VMEM, SMEM],
        out_shape=[
            jax.ShapeDtypeStruct((keys, 2 * HS), jnp.bfloat16),
            jax.ShapeDtypeStruct((ACC_ROWS, keys), jnp.bfloat16),
            jax.ShapeDtypeStruct((1,), jnp.float32),
        ],
        compiler_params=pltpu.CompilerParams(vmem_limit_bytes=32 * 2**20),
    )(own, partner)


def attention_kernel(chips, count_ref, code_ref, base_ref, shard_ref, norm_ref, pos_ref, kv_ref, vt_ref, *rest):
    q_refs, o_refs = rest[:chips], rest[chips : 2 * chips]
    q_all, p_a, p_b, s_all, acc = rest[2 * chips :]
    blocks = 4 * chips
    own_base = base_ref[0]
    partner_base = base_ref[1]
    iota = lax.broadcasted_iota(jnp.int32, (BLOCK, ROWS), 0)
    in_first = lax.broadcasted_iota(jnp.int32, (1, ROWS), 1) < BLOCK
    iota_half = iota.astype(jnp.float32).astype(jnp.bfloat16)

    most = None
    for i in range(chips):
        for j in range(2):
            q = q_refs[i][j]
            q_all[2 * i + j] = q
            q = q.astype(jnp.float32)
            squares = jnp.sum(q * q, axis=0, keepdims=True)
            most = squares if most is None else jnp.maximum(most, squares)
    safe = jnp.max(most) * norm_ref[0] <= SAFE_SCORE * SAFE_SCORE

    def clamp(r):
        return jnp.minimum(r, blocks - 1)

    def whole_block(r):
        return shard_ref[lax.div(r, 2)] * 2 + lax.rem(r, 2)

    def offset(i):
        return pl.multiple_of(i * BLOCK, BLOCK)

    def row_offset(i):
        return pl.multiple_of(i * ROWS, ROWS)

    def query(r):
        q = q_all[lax.div(r, 2), :, pl.ds(row_offset(lax.rem(r, 2)), ROWS)]
        return jnp.concatenate([q, jnp.zeros_like(q)], 0)

    def key_blocks(row, c):
        return [jnp.bitwise_and(code_ref[row, c * TILES + t], KEY_BLOCKS - 1) for t in range(TILES)]

    def products(row, r, c):
        keys = jnp.concatenate([kv_ref[pl.ds(offset(k), BLOCK), :] for k in key_blocks(row, c)], 0)
        return jnp.dot(keys, query(r), preferred_element_type=jnp.float32)

    def values(row, c):
        return jnp.concatenate([vt_ref[:, pl.ds(offset(k), BLOCK)] for k in key_blocks(row, c)], 1)

    def last_key(row, c, t, pos, real):
        code = code_ref[row, c * TILES + t]
        k = jnp.bitwise_and(code, KEY_BLOCKS - 1)
        half = KEY_BLOCKS // 2
        base = jnp.where(k < half, own_base, partner_base - half * BLOCK) + k * BLOCK
        real = jnp.logical_and(real, code >= 4 * KEY_BLOCKS)
        reach = [jnp.where(jnp.bitwise_and(code, n * KEY_BLOCKS) > 0, 1 << 30, BLOCK) for n in (1, 2)]
        reach = jnp.where(in_first, *[jnp.where(real, n, -(1 << 30)) for n in reach])
        ahead = pos - base
        return jnp.where(ahead < reach, jnp.minimum(ahead, BLOCK - 1), -1)

    def store(r, a, top):
        total = a[HS : HS + 1]
        low = total - total.astype(jnp.bfloat16).astype(jnp.float32)
        out = jnp.concatenate([a[: HS + 1], top, low, a[HS + 3 :]], 0).astype(jnp.bfloat16)
        return out

    def put(i, rr, out):
        o_refs[i][lax.div(rr, 2), :, pl.ds(row_offset(lax.rem(rr, 2)), ROWS)] = out

    def advance(r, c):
        last = c + 1 >= count_ref[whole_block(clamp(r))]
        return jnp.where(last, jnp.minimum(r + 1, blocks), r), jnp.where(last, 0, c + 1)

    def step_slots(r, c):
        slots = []
        for _ in range(SLOTS):
            slots.append((r, c))
            r, c = advance(r, c)
        return slots, r, c

    @pl.when(safe)
    def _():
        acc[...] = jnp.zeros_like(acc)

        def weigh(p_ref, slots):
            for g, (r, c) in enumerate(slots):
                rr = clamp(r)
                row = whole_block(rr)
                s = products(row, rr, c)
                pos = pos_ref[pl.ds(row, 1), :]
                for t in range(TILES):
                    p = jnp.exp2(s[t * BLOCK : (t + 1) * BLOCK] * LOG2E).astype(jnp.bfloat16)
                    last = last_key(row, c, t, pos, r < blocks).astype(jnp.float32).astype(jnp.bfloat16)
                    at = (g * TILES + t) * BLOCK
                    p_ref[at : at + BLOCK, :] = jnp.where(iota_half <= last, p, jnp.zeros_like(p))

        def add(p_ref, slots):
            for g, (r, c) in enumerate(slots):
                v = values(whole_block(clamp(r)), c)
                at = g * TILES * BLOCK
                acc[r] += jnp.dot(v, p_ref[at : at + TILES * BLOCK, :], preferred_element_type=jnp.float32)

        slots_0, r0, c0 = step_slots(jnp.int32(0), jnp.int32(0))
        weigh(p_a, slots_0)

        def two_steps(_, state):
            r, c, r1, c1 = state
            slots, _, _ = step_slots(r, c)
            slots_1, r2, c2 = step_slots(r1, c1)
            weigh(p_b, slots_1)
            add(p_a, slots)
            slots_2, r3, c3 = step_slots(r2, c2)
            weigh(p_a, slots_2)
            add(p_b, slots_1)
            return r2, c2, r3, c3

        items = lax.fori_loop(0, blocks, lambda r, n: n + count_ref[whole_block(r)], jnp.int32(0))
        steps = lax.div(items + (2 * SLOTS - 1), 2 * SLOTS)
        lax.fori_loop(0, steps, two_steps, (jnp.int32(0), jnp.int32(0), r0, c0))

        for i in range(chips):
            def finish(rr, _, i=i):
                a = acc[i * 4 + rr]
                put(i, rr, store(rr, a, jnp.where(a[HS : HS + 1] > 0, 0.0, lowest_max)))
                return 0

            lax.fori_loop(0, 4, finish, 0)

    @pl.when(jnp.logical_not(safe))
    def _():
        for i in range(chips):
            def one_block(rr, _, i=i):
                r = i * 4 + rr
                row = whole_block(r)
                pos = pos_ref[pl.ds(row, 1), :]
                acc[0] = jnp.zeros((ACC_ROWS, ROWS), jnp.float32)

                def one_slot(c, top):
                    s = products(row, r, c)
                    best = top
                    for t in range(TILES):
                        tile = s[t * BLOCK : (t + 1) * BLOCK]
                        tile = jnp.where(iota <= last_key(row, c, t, pos, True), tile, masked_score)
                        s_all[t * BLOCK : (t + 1) * BLOCK, :] = tile
                        best = jnp.maximum(best, jnp.max(tile, 0, keepdims=True))
                    best = best.astype(jnp.bfloat16).astype(jnp.float32)
                    p = jnp.exp2((s_all[...] - best) * LOG2E).astype(jnp.bfloat16)
                    shrink = jnp.exp2((top - best) * LOG2E)
                    acc[0] = acc[0] * shrink + jnp.dot(values(row, c), p, preferred_element_type=jnp.float32)
                    return best

                start = jnp.full((1, ROWS), lowest_max, jnp.bfloat16).astype(jnp.float32)
                top = lax.fori_loop(0, count_ref[row], one_slot, start)
                put(i, rr, store(rr, acc[0], top))
                return 0

            lax.fori_loop(0, 4, one_block, 0)


def attend(counts, codes, bases, shards, norm, spots, kv, vt, queries):
    chips = len(queries)
    out = jax.ShapeDtypeStruct((2, ACC_ROWS, queries[0].shape[2]), jnp.bfloat16)
    return pl.pallas_call(
        functools.partial(attention_kernel, chips),
        in_specs=[SMEM] * 5 + [VMEM] * (3 + chips),
        out_specs=[VMEM] * chips,
        out_shape=[out] * chips,
        scratch_shapes=[
            pltpu.VMEM((2 * chips, HS, queries[0].shape[2]), jnp.bfloat16),
            pltpu.VMEM((SLOTS * TILES * BLOCK, ROWS), jnp.bfloat16),
            pltpu.VMEM((SLOTS * TILES * BLOCK, ROWS), jnp.bfloat16),
            pltpu.VMEM((TILES * BLOCK, ROWS), jnp.float32),
            pltpu.VMEM((4 * chips + 1, ACC_ROWS, ROWS), jnp.float32),
        ],
        compiler_params=pltpu.CompilerParams(vmem_limit_bytes=32 * 2**20),
        cost_estimate=pl.CostEstimate(
            flops=chips * 6 * 10**9, bytes_accessed=4 * 2**20, transcendentals=chips * 2**20
        ),
    )(counts, codes, bases, shards, norm, spots, kv, vt, *queries)


def combine_kernel(core_ref, *refs):
    parts, out_ref = refs[:-1], refs[-1]
    groups = out_ref.shape[0] // 2
    half = out_ref.shape[1]
    for j in range(2):
        tops = [p[j, HS + 1 : HS + 2, :].astype(jnp.float32) for p in parts]
        top = functools.reduce(jnp.maximum, tops)
        scales = [jnp.exp(t - top) for t in tops]
        total = sum(
            (p[j, HS : HS + 1, :].astype(jnp.float32) + p[j, HS + 2 : HS + 3, :].astype(jnp.float32)) * scale
            for p, scale in zip(parts, scales)
        )
        summed = sum(p[j, :HS, :].astype(jnp.float32) * scale for p, scale in zip(parts, scales))
        rows = (summed / total).T.astype(jnp.bfloat16)
        first = jnp.bitwise_xor(core_ref[0], j) * groups
        for g in range(groups):
            upper = rows[2 * g * half : (2 * g + 1) * half]
            lower = rows[(2 * g + 1) * half : (2 * g + 2) * half]
            out_ref[first + g] = jnp.concatenate([upper, lower], 1)


def combine(core, parts):
    half = parts[0].shape[2] // 16
    return pl.pallas_call(
        combine_kernel,
        in_specs=[SMEM] + [VMEM] * len(parts),
        out_specs=VMEM,
        out_shape=jax.ShapeDtypeStruct((16, half, 2 * HS), jnp.bfloat16),
        compiler_params=pltpu.CompilerParams(vmem_limit_bytes=32 * 2**20),
    )(core, *parts)


def finish_kernel(pieces_ref, w_ref, out_ref):
    groups = pieces_ref.shape[0] // 2
    order = [c * groups + g for g in range(groups) for c in range(2)]
    upper = jnp.concatenate([pieces_ref[i][:, :HS] for i in order], 1)
    lower = jnp.concatenate([pieces_ref[i][:, HS:] for i in order], 1)
    attention = jnp.concatenate([upper, lower], 0)
    out_ref[...] = jnp.dot(attention, w_ref[...], preferred_element_type=jnp.float32).astype(jnp.bfloat16)


def finish(pieces, w_all):
    return pl.pallas_call(
        finish_kernel,
        in_specs=[VMEM, VMEM],
        out_specs=VMEM,
        out_shape=jax.ShapeDtypeStruct((2 * pieces.shape[1], w_all.shape[1]), jnp.bfloat16),
        compiler_params=pltpu.CompilerParams(vmem_limit_bytes=32 * 2**20),
    )(pieces, w_all)


def work_list(positions, block_mask, first_own, first_partner):
    half = KEY_BLOCKS // 2
    spots = positions.reshape(-1, BLOCK)
    index = jnp.arange(KEY_BLOCKS, dtype=jnp.int32)
    key_blocks = jnp.where(index < half, first_own, first_partner - half) + index
    listed = jnp.concatenate(
        [lax.dynamic_slice_in_dim(block_mask, first, half, 1) for first in (first_own, first_partner)], 1
    ) == 1
    own = jnp.any((spots // BLOCK)[:, :, None] == key_blocks[None, None, :], axis=1)
    reached = (key_blocks * BLOCK)[None, :] <= jnp.max(spots, axis=1)[:, None]
    active = ((listed & reached) | own).reshape(-1, 2, KEY_BLOCKS)
    active = active[:, 0] | active[:, 1]
    listed = listed.reshape(-1, 2, KEY_BLOCKS).astype(jnp.int32)
    earlier = index[None, :] < index[:, None]
    place = jnp.sum(active[:, None, :] & earlier[None], axis=2, dtype=jnp.int32)
    value = index[None, :] + KEY_BLOCKS * (listed[:, 0] + 2 * listed[:, 1] + 4)
    chosen = active[:, None, :] & (place[:, None, :] == index[None, :, None])
    codes = jnp.sum(jnp.where(chosen, value[:, None, :], 0), axis=2, dtype=jnp.int32)
    count = jnp.sum(active, axis=1, dtype=jnp.int32)
    return jnp.maximum((count + TILES - 1) // TILES, 1), codes


def shifted(x_by, y_by):
    return [(s, ((s // 4 + x_by) % 4) * 4 + (s % 4 ^ 2 * y_by)) for s in range(16)]


def back(route):
    return [(b, a) for a, b in route]


CALLS = (((0, 1), (1, 0)), ((3, 0), (1, 1)), ((3, 1), (2, 0)), ((2, 1),), ((0, 0),))
SWAP = [(i, i ^ 1) for i in range(16)]


def body(inputs, latents, w_query, w_key, w_value, w_out, positions, block_mask):
    s = lax.axis_index("seq")
    core = s % 2
    w_all = lax.all_gather(w_out, "grp", axis=0, tiled=True)

    queries = lax.dot_general(
        w_query, latents, (((0,), (1,)), ((), ())), preferred_element_type=jnp.float32
    ).astype(jnp.bfloat16) * jnp.bfloat16(HS ** -0.5)
    first, second = queries[:HS], queries[HS:]
    mine = jnp.where(core == 0, first, second)
    theirs = jnp.where(core == 0, second, first)
    q_chip = jnp.stack([mine, lax.ppermute(theirs, "seq", SWAP)])
    q_chip, inputs = lax.optimization_barrier((q_chip, inputs))
    arrived = {
        step: q_chip if step == (0, 0) else lax.ppermute(q_chip, "seq", shifted(*step))
        for call in CALLS
        for step in call
    }

    kv_own, kv_other = project(core[None], inputs, w_key, w_value)
    kv, vt, norm = prepare(kv_own, lax.ppermute(kv_other, "seq", SWAP))

    per_device = inputs.shape[0] // BLOCK
    counts, codes = work_list(positions, block_mask, s * per_device, (s ^ 1) * per_device)
    bases = jnp.stack([s, s ^ 1]) * inputs.shape[0]
    spots = positions.reshape(-1, ROWS)

    parts = []
    for call in CALLS:
        came_from = [(((s // 4 + 4 - x_by) % 4) * 4 + (s % 4 ^ 2 * y_by)) for x_by, y_by in call]
        shards = jnp.stack([shard for c in came_from for shard in (c, c ^ 1)])
        blocks = [arrived[step] for step in call]
        done = attend(counts, codes, bases, shards, norm, spots, kv, vt, blocks)
        for step, part in zip(call, done):
            parts.append(part if step == (0, 0) else lax.ppermute(part, "seq", back(shifted(*step))))

    pieces = combine(core[None], parts)
    owners = [[(4 * x + 2 * y + c) * 8 + g for c in range(2) for g in range(8)] for x in range(4) for y in range(2)]
    pieces = lax.all_to_all(pieces, ("seq", "grp"), 0, 0, axis_index_groups=owners)
    return finish(pieces, w_all)


def solution(mesh):
    return jax.shard_map(
        body,
        mesh=mesh,
        in_specs=(
            P("seq", None),
            P("seq", None),
            P(None, "grp"),
            P(None, "grp"),
            P(None, "grp"),
            P("grp", None),
            P(),
            P(),
        ),
        out_specs=P(("seq", "grp"), None),
        check_vma=False,
    )
```

```python
import functools

import jax
import jax.numpy as jnp
from jax import lax
from jax.experimental import pallas as pl
from jax.experimental.pallas import tpu as pltpu
from jax.sharding import PartitionSpec as P

HS = 64
BLOCK = 128
TILES = 4
SLOTS = 2
ROWS = 2 * BLOCK
KEY_BLOCKS = 32
ACC_ROWS = 72
LOG2E = 1.4426950408889634
SAFE_SCORE = 60.0
masked_score = -1e30
lowest_max = -1e29
SMEM = pl.BlockSpec(memory_space=pltpu.SMEM)
VMEM = pl.BlockSpec(memory_space=pltpu.VMEM)


def list_work(me, pos_ref, mask_ref, code_ref, listed_all):
    half = KEY_BLOCKS // 2
    pairs = code_ref.shape[0]

    def held(t):
        return jnp.where(t < half, me * half, jnp.bitwise_xor(me, 1) * half - half) + t

    columns = mask_ref.shape[1]
    at = lax.broadcasted_iota(jnp.int32, (columns, BLOCK), 0)
    lane = lax.broadcasted_iota(jnp.int32, (columns, BLOCK), 1)
    pick = ((at == held(lane)) & (lane < KEY_BLOCKS)).astype(jnp.float32).astype(jnp.bfloat16)
    listed = (mask_ref[...] == 1).astype(jnp.float32).astype(jnp.bfloat16)
    listed_all[...] = jnp.dot(listed, pick, preferred_element_type=jnp.float32)

    lane = lax.broadcasted_iota(jnp.int32, (pairs, BLOCK), 1)
    value = jnp.full((pairs, BLOCK), 4 * KEY_BLOCKS, jnp.int32) + lane
    active = jnp.zeros((pairs, BLOCK), jnp.bool_)
    for n in range(2):
        spots = pos_ref[pl.ds(n, pairs, stride=2), :]
        listed = listed_all[pl.ds(n, pairs, stride=2), :] > 0.5
        blocks = lax.shift_right_logical(spots, 7)
        own = jnp.zeros((pairs, BLOCK), jnp.int32)
        for t in range(KEY_BLOCKS):
            any_own = jnp.max((blocks == held(t)).astype(jnp.int32), axis=1, keepdims=True)
            own = jnp.where(lane == t, any_own, own)
        reached = held(lane) * BLOCK <= jnp.max(spots, axis=1, keepdims=True)
        active = active | (own > 0) | (listed & reached)
        value = value + jnp.where(listed, (n + 1) * KEY_BLOCKS, 0)
    active = active & (lane < KEY_BLOCKS)
    ones = active.astype(jnp.float32)
    row = lax.broadcasted_iota(jnp.int32, (BLOCK, BLOCK), 0)
    col = lax.broadcasted_iota(jnp.int32, (BLOCK, BLOCK), 1)
    earlier = (row < col).astype(jnp.float32).astype(jnp.bfloat16)
    place = jnp.dot(ones.astype(jnp.bfloat16), earlier, preferred_element_type=jnp.float32).astype(jnp.int32)
    packed = jnp.where(active, place * 512 + value, -1)
    codes = jnp.zeros((pairs, BLOCK), jnp.int32)
    for t in range(KEY_BLOCKS):
        one = packed[:, t : t + 1]
        codes = jnp.where(lax.shift_right_arithmetic(one, 9) == lane, jnp.bitwise_and(one, 511), codes)
    count = jnp.sum(ones, axis=1, keepdims=True).astype(jnp.int32)
    slots = jnp.maximum(lax.shift_right_logical(count + (TILES - 1), 2), 1)
    code_ref[...] = jnp.where(lane == KEY_BLOCKS, slots, codes)


def front_kernel(seq_ref, lat_hbm, x_hbm, wq_hbm, wk_hbm, wv_hbm, pos_hbm, mask_hbm, *rest):
    mine_ref, theirs_ref, own_ref, other_ref, code_ref = rest[:5]
    lat, x, wq, wk, wv, pos, mask, w_all, listed_all, sems, x_sems = rest[5:]
    small = [
        pltpu.make_async_copy(source, target, sems.at[i])
        for i, (source, target) in enumerate(
            [(pos_hbm, pos), (mask_hbm, mask), (wq_hbm, wq), (lat_hbm, lat), (wk_hbm, wk), (wv_hbm, wv)]
        )
    ]
    rows = x.shape[0] // x_sems.shape[0]
    parts = [pl.ds(i * rows, rows) for i in range(x_sems.shape[0])]
    large = [pltpu.make_async_copy(x_hbm.at[p], x.at[p], x_sems.at[i]) for i, p in enumerate(parts)]
    for copy in small + large:
        copy.start()
    got_pos, got_mask, got_wq, got_lat, got_wk, got_wv = small
    first = jnp.bitwise_and(seq_ref[0], 1) == 0

    got_pos.wait()
    got_mask.wait()
    list_work(seq_ref[0], pos, mask, code_ref, listed_all)

    got_wq.wait()
    got_lat.wait()
    q = jnp.dot(lat[...], wq[...], preferred_element_type=jnp.float32).T
    q = q.astype(jnp.bfloat16) * jnp.bfloat16(HS ** -0.5)
    mine_ref[...] = jnp.where(first, q[:HS], q[HS:])
    theirs_ref[...] = jnp.where(first, q[HS:], q[:HS])

    got_wk.wait()
    got_wv.wait()
    k, v = wk[...], wv[...]
    head_0 = jnp.concatenate([k[:, :HS], v[:, :HS]], 1)
    head_1 = jnp.concatenate([k[:, HS:], v[:, HS:]], 1)
    w_all[:, : 2 * HS] = jnp.where(first, head_0, head_1)
    w_all[:, 2 * HS :] = jnp.where(first, head_1, head_0)
    for copy, part in zip(large, parts):
        copy.wait()
        both = jnp.dot(x[part, :], w_all[...], preferred_element_type=jnp.float32).astype(jnp.bfloat16)
        own_ref[part, :] = both[:, : 2 * HS]
        other_ref[part, :] = both[:, 2 * HS :]


def front(seq, latents, inputs, w_query, w_key, w_value, positions, block_mask):
    rows, width = latents.shape
    keys = inputs.shape[0]
    spots = positions.reshape(-1, BLOCK)
    operands = (latents, inputs, w_query, w_key, w_value, spots, block_mask)
    q = jax.ShapeDtypeStruct((HS, rows), jnp.bfloat16)
    kv = jax.ShapeDtypeStruct((keys, 2 * HS), jnp.bfloat16)
    return pl.pallas_call(
        front_kernel,
        in_specs=[SMEM] + [pl.BlockSpec(memory_space=pl.ANY)] * len(operands),
        out_specs=[VMEM] * 5,
        out_shape=[q, q, kv, kv, jax.ShapeDtypeStruct((spots.shape[0] // 2, BLOCK), jnp.int32)],
        scratch_shapes=[pltpu.VMEM(a.shape, a.dtype) for a in operands]
        + [
            pltpu.VMEM((width, 4 * HS), jnp.bfloat16),
            pltpu.VMEM(spots.shape, jnp.float32),
            pltpu.SemaphoreType.DMA((6,)),
            pltpu.SemaphoreType.DMA((4,)),
        ],
        compiler_params=pltpu.CompilerParams(vmem_limit_bytes=61 * 2**20),
        cost_estimate=pl.CostEstimate(
            flops=2 * (keys * 4 + rows * 2) * width * HS, bytes_accessed=6 * 2**20, transcendentals=0
        ),
    )(seq, *operands)


def prepare_kernel(own_ref, partner_ref, kv_ref, vt_ref, norm_ref):
    most = None
    for t in range(KEY_BLOCKS):
        source, at = (own_ref, t) if t < KEY_BLOCKS // 2 else (partner_ref, t - KEY_BLOCKS // 2)
        tile = source[at * BLOCK : (at + 1) * BLOCK, :]
        kv_ref[t * BLOCK : (t + 1) * BLOCK, :] = tile
        turned = tile.T
        vt_ref[:HS, t * BLOCK : (t + 1) * BLOCK] = turned[HS:, :]
        k = turned[:HS, :].astype(jnp.float32)
        squares = jnp.sum(k * k, axis=0, keepdims=True)
        most = squares if most is None else jnp.maximum(most, squares)
    vt_ref[HS:, :] = jnp.ones((ACC_ROWS - HS, KEY_BLOCKS * BLOCK), jnp.bfloat16)
    norm_ref[0] = jnp.max(most)


def prepare(own, partner):
    keys = 2 * own.shape[0]
    return pl.pallas_call(
        prepare_kernel,
        in_specs=[VMEM, VMEM],
        out_specs=[VMEM, VMEM, SMEM],
        out_shape=[
            jax.ShapeDtypeStruct((keys, 2 * HS), jnp.bfloat16),
            jax.ShapeDtypeStruct((ACC_ROWS, keys), jnp.bfloat16),
            jax.ShapeDtypeStruct((1,), jnp.float32),
        ],
        compiler_params=pltpu.CompilerParams(vmem_limit_bytes=32 * 2**20),
    )(own, partner)


def attention_kernel(steps, takes, seq_ref, code_ref, norm_ref, pos_ref, kv_ref, vt_ref, *rest):
    chips = len(steps)
    q_refs, o_refs = rest[:takes], rest[takes : takes + chips]
    q_all, p_a, p_b, s_all, acc = rest[takes + chips :]
    blocks = 4 * chips
    me = seq_ref[0]
    own_base = me * (KEY_BLOCKS // 2 * BLOCK)
    partner_base = jnp.bitwise_xor(me, 1) * (KEY_BLOCKS // 2 * BLOCK)
    sources = [came_from(me, *step) for step in steps]
    iota = lax.broadcasted_iota(jnp.int32, (BLOCK, ROWS), 0)
    in_first = lax.broadcasted_iota(jnp.int32, (1, ROWS), 1) < BLOCK
    iota_half = iota.astype(jnp.float32).astype(jnp.bfloat16)

    most = None
    for i, ref in enumerate(q_refs):
        for j in range(ref.shape[0]):
            q = ref[j]
            q_all[i * ref.shape[0] + j] = q
            q = q.astype(jnp.float32)
            squares = jnp.sum(q * q, axis=0, keepdims=True)
            most = squares if most is None else jnp.maximum(most, squares)
    safe = jnp.max(most) * norm_ref[0] <= SAFE_SCORE * SAFE_SCORE

    def clamp(r):
        return jnp.minimum(r, blocks - 1)

    def whole_block(r):
        shard = sources[-1]
        for i in range(chips - 1):
            shard = jnp.where(lax.div(r, 4) == i, sources[i], shard)
        return jnp.bitwise_xor(shard, jnp.bitwise_and(lax.div(r, 2), 1)) * 2 + lax.rem(r, 2)

    def offset(i):
        return pl.multiple_of(i * BLOCK, BLOCK)

    def row_offset(i):
        return pl.multiple_of(i * ROWS, ROWS)

    def query(r):
        q = q_all[lax.div(r, 2), :, pl.ds(row_offset(lax.rem(r, 2)), ROWS)]
        return jnp.concatenate([q, jnp.zeros_like(q)], 0)

    def key_blocks(row, c):
        return [jnp.bitwise_and(code_ref[row, c * TILES + t], KEY_BLOCKS - 1) for t in range(TILES)]

    def products(row, r, c):
        keys = jnp.concatenate([kv_ref[pl.ds(offset(k), BLOCK), :] for k in key_blocks(row, c)], 0)
        return jnp.dot(keys, query(r), preferred_element_type=jnp.float32)

    def values(row, c):
        return jnp.concatenate([vt_ref[:, pl.ds(offset(k), BLOCK)] for k in key_blocks(row, c)], 1)

    def last_key(row, c, t, pos, real):
        code = code_ref[row, c * TILES + t]
        k = jnp.bitwise_and(code, KEY_BLOCKS - 1)
        half = KEY_BLOCKS // 2
        base = jnp.where(k < half, own_base, partner_base - half * BLOCK) + k * BLOCK
        real = jnp.logical_and(real, code >= 4 * KEY_BLOCKS)
        reach = [jnp.where(jnp.bitwise_and(code, n * KEY_BLOCKS) > 0, 1 << 30, BLOCK) for n in (1, 2)]
        reach = jnp.where(in_first, *[jnp.where(real, n, -(1 << 30)) for n in reach])
        ahead = pos - base
        return jnp.where(ahead < reach, jnp.minimum(ahead, BLOCK - 1), -1)

    def store(r, a, top):
        total = a[HS : HS + 1]
        low = total - total.astype(jnp.bfloat16).astype(jnp.float32)
        out = jnp.concatenate([a[: HS + 1], top, low, a[HS + 3 :]], 0).astype(jnp.bfloat16)
        return out

    def put(i, rr, out):
        o_refs[i][lax.div(rr, 2), :, pl.ds(row_offset(lax.rem(rr, 2)), ROWS)] = out

    def advance(r, c):
        last = c + 1 >= code_ref[whole_block(clamp(r)), KEY_BLOCKS]
        return jnp.where(last, jnp.minimum(r + 1, blocks), r), jnp.where(last, 0, c + 1)

    def step_slots(r, c):
        slots = []
        for _ in range(SLOTS):
            slots.append((r, c))
            r, c = advance(r, c)
        return slots, r, c

    @pl.when(safe)
    def _():
        acc[...] = jnp.zeros_like(acc)

        def weigh(p_ref, slots):
            for g, (r, c) in enumerate(slots):
                rr = clamp(r)
                row = whole_block(rr)
                s = products(row, rr, c)
                pos = pos_ref[pl.ds(row, 1), :]
                for t in range(TILES):
                    p = jnp.exp2(s[t * BLOCK : (t + 1) * BLOCK] * LOG2E).astype(jnp.bfloat16)
                    last = last_key(row, c, t, pos, r < blocks).astype(jnp.float32).astype(jnp.bfloat16)
                    at = (g * TILES + t) * BLOCK
                    p_ref[at : at + BLOCK, :] = jnp.where(iota_half <= last, p, jnp.zeros_like(p))

        def add(p_ref, slots):
            for g, (r, c) in enumerate(slots):
                v = values(whole_block(clamp(r)), c)
                at = g * TILES * BLOCK
                acc[r] += jnp.dot(v, p_ref[at : at + TILES * BLOCK, :], preferred_element_type=jnp.float32)

        slots_0, r0, c0 = step_slots(jnp.int32(0), jnp.int32(0))
        weigh(p_a, slots_0)

        def two_steps(_, state):
            r, c, r1, c1 = state
            slots, _, _ = step_slots(r, c)
            slots_1, r2, c2 = step_slots(r1, c1)
            weigh(p_b, slots_1)
            add(p_a, slots)
            slots_2, r3, c3 = step_slots(r2, c2)
            weigh(p_a, slots_2)
            add(p_b, slots_1)
            return r2, c2, r3, c3

        items = lax.fori_loop(0, blocks, lambda r, n: n + code_ref[whole_block(r), KEY_BLOCKS], jnp.int32(0))
        turns = lax.div(items + (2 * SLOTS - 1), 2 * SLOTS)
        lax.fori_loop(0, turns, two_steps, (jnp.int32(0), jnp.int32(0), r0, c0))

        for i in range(chips):
            def finish(rr, _, i=i):
                a = acc[i * 4 + rr]
                put(i, rr, store(rr, a, jnp.where(a[HS : HS + 1] > 0, 0.0, lowest_max)))
                return 0

            lax.fori_loop(0, 4, finish, 0)

    @pl.when(jnp.logical_not(safe))
    def _():
        for i in range(chips):
            def one_block(rr, _, i=i):
                r = i * 4 + rr
                row = whole_block(r)
                pos = pos_ref[pl.ds(row, 1), :]
                acc[0] = jnp.zeros((ACC_ROWS, ROWS), jnp.float32)

                def one_slot(c, top):
                    s = products(row, r, c)
                    best = top
                    for t in range(TILES):
                        tile = s[t * BLOCK : (t + 1) * BLOCK]
                        tile = jnp.where(iota <= last_key(row, c, t, pos, True), tile, masked_score)
                        s_all[t * BLOCK : (t + 1) * BLOCK, :] = tile
                        best = jnp.maximum(best, jnp.max(tile, 0, keepdims=True))
                    best = best.astype(jnp.bfloat16).astype(jnp.float32)
                    p = jnp.exp2((s_all[...] - best) * LOG2E).astype(jnp.bfloat16)
                    shrink = jnp.exp2((top - best) * LOG2E)
                    acc[0] = acc[0] * shrink + jnp.dot(values(row, c), p, preferred_element_type=jnp.float32)
                    return best

                start = jnp.full((1, ROWS), lowest_max, jnp.bfloat16).astype(jnp.float32)
                top = lax.fori_loop(0, code_ref[row, KEY_BLOCKS], one_slot, start)
                put(i, rr, store(rr, acc[0], top))
                return 0

            lax.fori_loop(0, 4, one_block, 0)


def attend(steps, seq, codes, norm, spots, kv, vt, queries):
    chips = len(steps)
    out = jax.ShapeDtypeStruct((2, ACC_ROWS, queries[0].shape[2]), jnp.bfloat16)
    return pl.pallas_call(
        functools.partial(attention_kernel, steps, len(queries)),
        in_specs=[SMEM] * 3 + [VMEM] * (3 + len(queries)),
        out_specs=[VMEM] * chips,
        out_shape=[out] * chips,
        scratch_shapes=[
            pltpu.VMEM((2 * chips, HS, queries[0].shape[2]), jnp.bfloat16),
            pltpu.VMEM((SLOTS * TILES * BLOCK, ROWS), jnp.bfloat16),
            pltpu.VMEM((SLOTS * TILES * BLOCK, ROWS), jnp.bfloat16),
            pltpu.VMEM((TILES * BLOCK, ROWS), jnp.float32),
            pltpu.VMEM((4 * chips + 1, ACC_ROWS, ROWS), jnp.float32),
        ],
        compiler_params=pltpu.CompilerParams(vmem_limit_bytes=32 * 2**20),
        cost_estimate=pl.CostEstimate(
            flops=chips * 6 * 10**9, bytes_accessed=4 * 2**20, transcendentals=chips * 2**20
        ),
    )(seq, codes, norm, spots, kv, vt, *queries)


def combine_kernel(core_ref, *refs):
    parts, out_ref = refs[:-1], refs[-1]
    groups = out_ref.shape[0] // 2
    half = out_ref.shape[1]
    for j in range(2):
        tops = [p[j, HS + 1 : HS + 2, :].astype(jnp.float32) for p in parts]
        top = functools.reduce(jnp.maximum, tops)
        scales = [jnp.exp(t - top) for t in tops]
        total = sum(
            (p[j, HS : HS + 1, :].astype(jnp.float32) + p[j, HS + 2 : HS + 3, :].astype(jnp.float32)) * scale
            for p, scale in zip(parts, scales)
        )
        summed = sum(p[j, :HS, :].astype(jnp.float32) * scale for p, scale in zip(parts, scales))
        rows = (summed / total).T.astype(jnp.bfloat16)
        first = jnp.bitwise_xor(core_ref[0], j) * groups
        for g in range(groups):
            upper = rows[2 * g * half : (2 * g + 1) * half]
            lower = rows[(2 * g + 1) * half : (2 * g + 2) * half]
            out_ref[first + g] = jnp.concatenate([upper, lower], 1)


def combine(core, parts):
    half = parts[0].shape[2] // 16
    return pl.pallas_call(
        combine_kernel,
        in_specs=[SMEM] + [VMEM] * len(parts),
        out_specs=VMEM,
        out_shape=jax.ShapeDtypeStruct((16, half, 2 * HS), jnp.bfloat16),
        compiler_params=pltpu.CompilerParams(vmem_limit_bytes=32 * 2**20),
    )(core, *parts)


def finish_kernel(grp_ref, pieces_ref, *refs):
    w_refs, out_ref = refs[:-1], refs[-1]
    groups = pieces_ref.shape[0] // 2
    me = grp_ref[0]
    result = None
    for k, w_ref in enumerate(w_refs):
        near = jnp.bitwise_or(jnp.bitwise_and(me, 4), jnp.bitwise_and(me - k, 3))
        order = [c * groups + g for g in (near, jnp.bitwise_xor(near, 4)) for c in range(2)]
        blocks = [pieces_ref[i] for i in order]
        upper = jnp.concatenate([p[:, :HS] for p in blocks], 1)
        lower = jnp.concatenate([p[:, HS:] for p in blocks], 1)
        attention = jnp.concatenate([upper, lower], 0)
        term = jnp.dot(attention, w_ref[...], preferred_element_type=jnp.float32)
        result = term if result is None else result + term
    out_ref[...] = result.astype(jnp.bfloat16)


def finish(grp, pieces, w_turns):
    return pl.pallas_call(
        finish_kernel,
        in_specs=[SMEM] + [VMEM] * (1 + len(w_turns)),
        out_specs=VMEM,
        out_shape=jax.ShapeDtypeStruct((2 * pieces.shape[1], w_turns[0].shape[1]), jnp.bfloat16),
        compiler_params=pltpu.CompilerParams(vmem_limit_bytes=24 * 2**20),
    )(grp, pieces, *w_turns)


def shifted(x_by, y_by):
    return [(s, ((s // 4 + x_by) % 4) * 4 + (s % 4 ^ 2 * y_by)) for s in range(16)]


def back(route):
    return [(b, a) for a, b in route]


def came_from(s, x_by, y_by):
    moved = jnp.bitwise_and(s - 4 * x_by, 12)
    return moved + jnp.bitwise_xor(jnp.bitwise_and(s, 3), 2 * y_by)


CALLS = (((0, 1),), ((1, 0), (1, 1), (3, 0), (3, 1)), ((2, 0), (2, 1)), ((0, 0),))
SWAP = [(i, i ^ 1) for i in range(16)]


def body(inputs, latents, w_query, w_key, w_value, w_out, positions, block_mask):
    seq = lax.axis_index("seq")[None]
    grp = lax.axis_index("grp")[None]
    core = jnp.bitwise_and(seq, 1)

    w_other = lax.ppermute(w_out, "grp", [(g, g ^ 4) for g in range(8)])
    mine, theirs, kv_own, kv_other, codes = front(
        seq, latents, inputs, w_query, w_key, w_value, positions, block_mask
    )
    q_chip = jnp.stack([mine, lax.ppermute(theirs, "seq", SWAP)])
    arrived = {
        step: q_chip if step == (0, 0) else lax.ppermute(q_chip, "seq", shifted(*step))
        for call in CALLS
        for step in call
    }
    kv, vt, norm = prepare(kv_own, lax.ppermute(kv_other, "seq", SWAP))

    w_pair = jnp.concatenate([w_out, w_other], 0)
    w_turns = [w_pair] + [
        lax.ppermute(w_pair, "grp", [(g, (g & 4) | ((g + k) & 3)) for g in range(8)]) for k in (1, 2, 3)
    ]
    arrived[2, 0], w_turns = lax.optimization_barrier((arrived[2, 0], w_turns))

    spots = positions.reshape(-1, ROWS)
    parts = []
    for call in CALLS:
        if parts:
            arrived[call[0]], parts[-1] = lax.optimization_barrier((arrived[call[0]], parts[-1]))
        done = attend(call, seq, codes, norm, spots, kv, vt, [arrived[step] for step in call])
        parts += done

    order = [step for call in CALLS for step in call]
    parts = [
        part if step == (0, 0) else lax.ppermute(part, "seq", back(shifted(*step)))
        for step, part in zip(order, parts)
    ]
    pieces = combine(core, parts)
    owners = [[(4 * x + 2 * y + c) * 8 + g for c in range(2) for g in range(8)] for x in range(4) for y in range(2)]
    pieces = lax.all_to_all(pieces, ("seq", "grp"), 0, 0, axis_index_groups=owners)
    return finish(grp, pieces, w_turns)


def solution(mesh):
    return jax.shard_map(
        body,
        mesh=mesh,
        in_specs=(
            P("seq", None),
            P("seq", None),
            P(None, "grp"),
            P(None, "grp"),
            P(None, "grp"),
            P("grp", None),
            P(),
            P(),
        ),
        out_specs=P(("seq", "grp"), None),
        check_vma=False,
    )
```

```python
import functools

import jax
import jax.numpy as jnp
from jax import lax
from jax.experimental import pallas as pl
from jax.experimental.pallas import tpu as pltpu
from jax.sharding import PartitionSpec as P

HS = 64
BLOCK = 128
TILES = 4
SLOTS = 2
ROWS = 2 * BLOCK
FAR = 64
KEY_BLOCKS = 32
ACC_ROWS = 72
LOG2E = 1.4426950408889634
SAFE_SCORE = 60.0
masked_score = -1e30
lowest_max = -1e29
SMEM = pl.BlockSpec(memory_space=pltpu.SMEM)
VMEM = pl.BlockSpec(memory_space=pltpu.VMEM)


def list_work(me, pos_ref, mask_ref, code_ref):
    half = KEY_BLOCKS // 2
    both = 2 * KEY_BLOCKS
    blocks = pos_ref.shape[0]

    def held(t):
        source = jnp.bitwise_xor(me, lax.shift_right_logical(t, 4))
        return source * half + jnp.bitwise_and(t, half - 1)

    spots = pos_ref[...].T
    own_block = lax.shift_right_logical(spots, 7)
    furthest = jnp.max(own_block, axis=0, keepdims=True)
    t_rows = lax.broadcasted_iota(jnp.int32, (both, blocks), 0)
    own = jnp.zeros((both, blocks), jnp.int32)
    for t in range(both):
        found = jnp.max((own_block == held(jnp.int32(t))).astype(jnp.int32), axis=0, keepdims=True)
        own = jnp.where(t_rows == t, found, own)

    def exact(condition):
        return condition.astype(jnp.float32).astype(jnp.bfloat16)

    columns = mask_ref.shape[1]
    pick = exact(
        lax.broadcasted_iota(jnp.int32, (both, columns), 1)
        == held(lax.broadcasted_iota(jnp.int32, (both, columns), 0))
    )
    listed = lax.dot_general(
        pick, exact(mask_ref[...] == 1), (((1,), (1,)), ((), ())), preferred_element_type=jnp.float32
    )
    active = exact((own > 0) | ((listed > 0.5) & (held(t_rows) <= furthest)))
    listed = exact(listed > 0.5)

    row = lax.broadcasted_iota(jnp.int32, (blocks, BLOCK), 0)
    col = lax.broadcasted_iota(jnp.int32, (blocks, BLOCK), 1)
    first, second = exact(row == 2 * col), exact(row == 2 * col + 1)
    active = jnp.dot(active, first + second, preferred_element_type=jnp.float32) > 0.5
    listed = [jnp.dot(listed, pairs, preferred_element_type=jnp.float32).astype(jnp.int32) for pairs in (first, second)]
    row = lax.broadcasted_iota(jnp.int32, (both, both), 0)
    col = lax.broadcasted_iota(jnp.int32, (both, both), 1)
    earlier = exact((col < row) & (lax.shift_right_logical(row, 5) == lax.shift_right_logical(col, 5)))
    place = jnp.dot(earlier, exact(active), preferred_element_type=jnp.float32).astype(jnp.int32)
    t_rows = lax.broadcasted_iota(jnp.int32, (both, BLOCK), 0)
    value = jnp.bitwise_and(t_rows, KEY_BLOCKS - 1) + KEY_BLOCKS * (listed[0] + 2 * listed[1] + 4)
    packed = jnp.where(active, place * 512 + value, -1)
    ones = active.astype(jnp.int32)
    slot_rows = lax.broadcasted_iota(jnp.int32, (KEY_BLOCKS, BLOCK), 0)
    tables = []
    for n in range(2):
        codes = jnp.zeros((KEY_BLOCKS, BLOCK), jnp.int32)
        for t in range(n * KEY_BLOCKS, (n + 1) * KEY_BLOCKS):
            one = packed[t : t + 1, :]
            codes = jnp.where(lax.shift_right_arithmetic(one, 9) == slot_rows, jnp.bitwise_and(one, 511), codes)
        count = jnp.sum(ones[n * KEY_BLOCKS : (n + 1) * KEY_BLOCKS], axis=0, keepdims=True)
        slots = jnp.maximum(lax.shift_right_logical(count + (TILES - 1), 2), 1)
        tables += [codes, jnp.broadcast_to(slots, (FAR - KEY_BLOCKS, BLOCK))]
    code_ref[...] = jnp.concatenate(tables, 0).T[: code_ref.shape[0]]


def front_kernel(seq_ref, lat_hbm, x_hbm, wq_hbm, wk_hbm, wv_hbm, pos_hbm, mask_hbm, *rest):
    mine_ref, theirs_ref, own_ref, other_ref, code_ref = rest[:5]
    lat, x, wq, wk, wv, pos, mask, w_all, sems, x_sems = rest[5:]
    small = [
        pltpu.make_async_copy(source, target, sems.at[i])
        for i, (source, target) in enumerate(
            [(pos_hbm, pos), (mask_hbm, mask), (wq_hbm, wq), (lat_hbm, lat), (wk_hbm, wk), (wv_hbm, wv)]
        )
    ]
    rows = x.shape[0] // x_sems.shape[0]
    parts = [pl.ds(i * rows, rows) for i in range(x_sems.shape[0])]
    large = [pltpu.make_async_copy(x_hbm.at[p], x.at[p], x_sems.at[i]) for i, p in enumerate(parts)]
    for copy in small + large:
        copy.start()
    got_pos, got_mask, got_wq, got_lat, got_wk, got_wv = small
    first = jnp.bitwise_and(seq_ref[0], 1) == 0

    got_pos.wait()
    got_mask.wait()
    list_work(seq_ref[0], pos, mask, code_ref)

    got_wq.wait()
    got_lat.wait()
    q = jnp.dot(lat[...], wq[...], preferred_element_type=jnp.float32).T
    q = q.astype(jnp.bfloat16) * jnp.bfloat16(HS ** -0.5)
    mine_ref[...] = jnp.where(first, q[:HS], q[HS:])
    theirs_ref[...] = jnp.where(first, q[HS:], q[:HS])

    got_wk.wait()
    got_wv.wait()
    k, v = wk[...], wv[...]
    head_0 = jnp.concatenate([k[:, :HS], v[:, :HS]], 1)
    head_1 = jnp.concatenate([k[:, HS:], v[:, HS:]], 1)
    w_all[:, : 2 * HS] = jnp.where(first, head_0, head_1)
    w_all[:, 2 * HS :] = jnp.where(first, head_1, head_0)
    for copy, part in zip(large, parts):
        copy.wait()
        both = jnp.dot(x[part, :], w_all[...], preferred_element_type=jnp.float32).astype(jnp.bfloat16)
        own_ref[part, :] = both[:, : 2 * HS]
        other_ref[part, :] = both[:, 2 * HS :]


def front(seq, latents, inputs, w_query, w_key, w_value, positions, block_mask):
    rows, width = latents.shape
    keys = inputs.shape[0]
    spots = positions.reshape(-1, BLOCK)
    operands = (latents, inputs, w_query, w_key, w_value, spots, block_mask)
    q = jax.ShapeDtypeStruct((HS, rows), jnp.bfloat16)
    kv = jax.ShapeDtypeStruct((keys, 2 * HS), jnp.bfloat16)
    return pl.pallas_call(
        front_kernel,
        in_specs=[SMEM] + [pl.BlockSpec(memory_space=pl.ANY)] * len(operands),
        out_specs=[VMEM] * 5,
        out_shape=[q, q, kv, kv, jax.ShapeDtypeStruct((spots.shape[0] // 2, BLOCK), jnp.int32)],
        scratch_shapes=[pltpu.VMEM(a.shape, a.dtype) for a in operands]
        + [
            pltpu.VMEM((width, 4 * HS), jnp.bfloat16),
            pltpu.SemaphoreType.DMA((6,)),
            pltpu.SemaphoreType.DMA((4,)),
        ],
        compiler_params=pltpu.CompilerParams(vmem_limit_bytes=61 * 2**20),
        cost_estimate=pl.CostEstimate(
            flops=2 * (keys * 4 + rows * 2) * width * HS, bytes_accessed=6 * 2**20, transcendentals=0
        ),
    )(seq, *operands)


def prepare_kernel(*refs):
    sources, (kv_ref, vt_ref, norm_ref) = refs[:-3], refs[-3:]
    each = KEY_BLOCKS // len(sources)
    most = None
    for t in range(KEY_BLOCKS):
        at = t % each
        tile = sources[t // each][at * BLOCK : (at + 1) * BLOCK, :]
        kv_ref[t * BLOCK : (t + 1) * BLOCK, :] = tile
        turned = tile.T
        vt_ref[:HS, t * BLOCK : (t + 1) * BLOCK] = turned[HS:, :]
        k = turned[:HS, :].astype(jnp.float32)
        squares = jnp.sum(k * k, axis=0, keepdims=True)
        most = squares if most is None else jnp.maximum(most, squares)
    vt_ref[HS:, :] = jnp.ones((ACC_ROWS - HS, KEY_BLOCKS * BLOCK), jnp.bfloat16)
    norm_ref[0] = jnp.max(most)


def prepare(*sources):
    keys = sum(source.shape[0] for source in sources)
    return pl.pallas_call(
        prepare_kernel,
        in_specs=[VMEM] * len(sources),
        out_specs=[VMEM, VMEM, SMEM],
        out_shape=[
            jax.ShapeDtypeStruct((keys, 2 * HS), jnp.bfloat16),
            jax.ShapeDtypeStruct((ACC_ROWS, keys), jnp.bfloat16),
            jax.ShapeDtypeStruct((1,), jnp.float32),
        ],
        compiler_params=pltpu.CompilerParams(vmem_limit_bytes=24 * 2**20),
    )(*sources)


def attention_kernel(steps, far, seq_ref, code_ref, norm_ref, pos_ref, kv_ref, vt_ref, *rest):
    chips = len(steps)
    q_refs, rest = rest[:chips], rest[chips:]
    before_refs, rest = (rest[:chips], rest[chips:]) if far else (None, rest)
    o_refs, (q_all, p_a, p_b, s_all, acc) = rest[:chips], rest[chips:]
    table = FAR if far else 0
    blocks = 4 * chips
    me = seq_ref[0]
    keys_of = jnp.bitwise_xor(me, 2) if far else me
    own_base = keys_of * (KEY_BLOCKS // 2 * BLOCK)
    partner_base = jnp.bitwise_xor(keys_of, 1) * (KEY_BLOCKS // 2 * BLOCK)
    sources = [came_from(me, step) for step in steps]
    iota = lax.broadcasted_iota(jnp.int32, (BLOCK, ROWS), 0)
    in_first = lax.broadcasted_iota(jnp.int32, (1, ROWS), 1) < BLOCK
    iota_half = iota.astype(jnp.float32).astype(jnp.bfloat16)

    most = None
    for i, ref in enumerate(q_refs):
        for j in range(ref.shape[0]):
            q = ref[j]
            q_all[i * ref.shape[0] + j] = q
            q = q.astype(jnp.float32)
            squares = jnp.sum(q * q, axis=0, keepdims=True)
            most = squares if most is None else jnp.maximum(most, squares)
    safe = jnp.max(most) * norm_ref[0] <= SAFE_SCORE * SAFE_SCORE

    def clamp(r):
        return jnp.minimum(r, blocks - 1)

    def whole_block(r):
        shard = sources[-1]
        for i in range(chips - 1):
            shard = jnp.where(lax.div(r, 4) == i, sources[i], shard)
        return jnp.bitwise_xor(shard, jnp.bitwise_and(lax.div(r, 2), 1)) * 2 + lax.rem(r, 2)

    def offset(i):
        return pl.multiple_of(i * BLOCK, BLOCK)

    def row_offset(i):
        return pl.multiple_of(i * ROWS, ROWS)

    def query(r):
        q = q_all[lax.div(r, 2), :, pl.ds(row_offset(lax.rem(r, 2)), ROWS)]
        return jnp.concatenate([q, jnp.zeros_like(q)], 0)

    def key_blocks(row, c):
        return [jnp.bitwise_and(code_ref[row, table + c * TILES + t], KEY_BLOCKS - 1) for t in range(TILES)]

    def products(row, r, c):
        keys = jnp.concatenate([kv_ref[pl.ds(offset(k), BLOCK), :] for k in key_blocks(row, c)], 0)
        return jnp.dot(keys, query(r), preferred_element_type=jnp.float32)

    def values(row, c):
        return jnp.concatenate([vt_ref[:, pl.ds(offset(k), BLOCK)] for k in key_blocks(row, c)], 1)

    def last_key(row, c, t, pos, real):
        code = code_ref[row, table + c * TILES + t]
        k = jnp.bitwise_and(code, KEY_BLOCKS - 1)
        half = KEY_BLOCKS // 2
        base = jnp.where(k < half, own_base, partner_base - half * BLOCK) + k * BLOCK
        real = jnp.logical_and(real, code >= 4 * KEY_BLOCKS)
        reach = [jnp.where(jnp.bitwise_and(code, n * KEY_BLOCKS) > 0, 1 << 30, BLOCK) for n in (1, 2)]
        reach = jnp.where(in_first, *[jnp.where(real, n, -(1 << 30)) for n in reach])
        ahead = pos - base
        return jnp.where(ahead < reach, jnp.minimum(ahead, BLOCK - 1), -1)

    def put(i, rr, a, top):
        at = (lax.div(rr, 2), slice(None), pl.ds(row_offset(lax.rem(rr, 2)), ROWS))
        if far:
            before = before_refs[i][at].astype(jnp.float32)
            top_before, top_now = before[HS + 1 : HS + 2], top
            top = jnp.maximum(top_before, top_now)
            shrink, shrink_before = jnp.exp(top_now - top), jnp.exp(top_before - top)
            total = a[HS : HS + 1] * shrink + (before[HS : HS + 1] + before[HS + 2 : HS + 3]) * shrink_before
            a = a * shrink + before * shrink_before
        else:
            total = a[HS : HS + 1]
        low = total - total.astype(jnp.bfloat16).astype(jnp.float32)
        out = jnp.concatenate([a[:HS], total, top, low, a[HS + 3 :]], 0)
        o_refs[i][at] = out.astype(jnp.bfloat16)

    def advance(r, c):
        last = c + 1 >= code_ref[whole_block(clamp(r)), table + KEY_BLOCKS]
        return jnp.where(last, jnp.minimum(r + 1, blocks), r), jnp.where(last, 0, c + 1)

    def step_slots(r, c):
        slots = []
        for _ in range(SLOTS):
            slots.append((r, c))
            r, c = advance(r, c)
        return slots, r, c

    @pl.when(safe)
    def _():
        acc[...] = jnp.zeros_like(acc)

        def weigh(p_ref, slots):
            for g, (r, c) in enumerate(slots):
                rr = clamp(r)
                row = whole_block(rr)
                s = products(row, rr, c)
                pos = pos_ref[pl.ds(row, 1), :]
                for t in range(TILES):
                    p = jnp.exp2(s[t * BLOCK : (t + 1) * BLOCK] * LOG2E).astype(jnp.bfloat16)
                    last = last_key(row, c, t, pos, r < blocks).astype(jnp.float32).astype(jnp.bfloat16)
                    at = (g * TILES + t) * BLOCK
                    p_ref[at : at + BLOCK, :] = jnp.where(iota_half <= last, p, jnp.zeros_like(p))

        def add(p_ref, slots):
            for g, (r, c) in enumerate(slots):
                v = values(whole_block(clamp(r)), c)
                at = g * TILES * BLOCK
                acc[r] += jnp.dot(v, p_ref[at : at + TILES * BLOCK, :], preferred_element_type=jnp.float32)

        slots_0, r0, c0 = step_slots(jnp.int32(0), jnp.int32(0))
        weigh(p_a, slots_0)

        def two_steps(_, state):
            r, c, r1, c1 = state
            slots, _, _ = step_slots(r, c)
            slots_1, r2, c2 = step_slots(r1, c1)
            weigh(p_b, slots_1)
            add(p_a, slots)
            slots_2, r3, c3 = step_slots(r2, c2)
            weigh(p_a, slots_2)
            add(p_b, slots_1)
            return r2, c2, r3, c3

        items = lax.fori_loop(0, blocks, lambda r, n: n + code_ref[whole_block(r), table + KEY_BLOCKS], jnp.int32(0))
        turns = lax.div(items + (2 * SLOTS - 1), 2 * SLOTS)
        lax.fori_loop(0, turns, two_steps, (jnp.int32(0), jnp.int32(0), r0, c0))

        for i in range(chips):
            def finish(rr, _, i=i):
                a = acc[i * 4 + rr]
                put(i, rr, a, jnp.where(a[HS : HS + 1] > 0, 0.0, lowest_max))
                return 0

            lax.fori_loop(0, 4, finish, 0)

    @pl.when(jnp.logical_not(safe))
    def _():
        for i in range(chips):
            def one_block(rr, _, i=i):
                r = i * 4 + rr
                row = whole_block(r)
                pos = pos_ref[pl.ds(row, 1), :]
                acc[0] = jnp.zeros((ACC_ROWS, ROWS), jnp.float32)

                def one_slot(c, top):
                    s = products(row, r, c)
                    best = top
                    for t in range(TILES):
                        tile = s[t * BLOCK : (t + 1) * BLOCK]
                        tile = jnp.where(iota <= last_key(row, c, t, pos, True), tile, masked_score)
                        s_all[t * BLOCK : (t + 1) * BLOCK, :] = tile
                        best = jnp.maximum(best, jnp.max(tile, 0, keepdims=True))
                    best = best.astype(jnp.bfloat16).astype(jnp.float32)
                    p = jnp.exp2((s_all[...] - best) * LOG2E).astype(jnp.bfloat16)
                    shrink = jnp.exp2((top - best) * LOG2E)
                    acc[0] = acc[0] * shrink + jnp.dot(values(row, c), p, preferred_element_type=jnp.float32)
                    return best

                start = jnp.full((1, ROWS), lowest_max, jnp.bfloat16).astype(jnp.float32)
                top = lax.fori_loop(0, code_ref[row, table + KEY_BLOCKS], one_slot, start)
                put(i, rr, acc[0], top)
                return 0

            lax.fori_loop(0, 4, one_block, 0)


def attend(steps, seq, codes, spots, held, queries, before=()):
    kv, vt, norm = held
    chips = len(steps)
    out = jax.ShapeDtypeStruct((2, ACC_ROWS, queries[0].shape[2]), jnp.bfloat16)
    return pl.pallas_call(
        functools.partial(attention_kernel, steps, bool(before)),
        in_specs=[SMEM] * 3 + [VMEM] * (3 + len(queries) + len(before)),
        out_specs=[VMEM] * chips,
        out_shape=[out] * chips,
        scratch_shapes=[
            pltpu.VMEM((2 * chips, HS, queries[0].shape[2]), jnp.bfloat16),
            pltpu.VMEM((SLOTS * TILES * BLOCK, ROWS), jnp.bfloat16),
            pltpu.VMEM((SLOTS * TILES * BLOCK, ROWS), jnp.bfloat16),
            pltpu.VMEM((TILES * BLOCK, ROWS), jnp.float32),
            pltpu.VMEM((4 * chips + 1, ACC_ROWS, ROWS), jnp.float32),
        ],
        compiler_params=pltpu.CompilerParams(vmem_limit_bytes=32 * 2**20),
        cost_estimate=pl.CostEstimate(
            flops=chips * 6 * 10**9, bytes_accessed=4 * 2**20, transcendentals=chips * 2**20
        ),
    )(seq, codes, norm, spots, kv, vt, *queries, *before)


def combine_kernel(core_ref, *refs):
    parts, out_ref = refs[:-1], refs[-1]
    groups = out_ref.shape[0] // 2
    half = out_ref.shape[1]
    for j in range(2):
        tops = [p[j, HS + 1 : HS + 2, :].astype(jnp.float32) for p in parts]
        top = functools.reduce(jnp.maximum, tops)
        scales = [jnp.exp(t - top) for t in tops]
        total = sum(
            (p[j, HS : HS + 1, :].astype(jnp.float32) + p[j, HS + 2 : HS + 3, :].astype(jnp.float32)) * scale
            for p, scale in zip(parts, scales)
        )
        summed = sum(p[j, :HS, :].astype(jnp.float32) * scale for p, scale in zip(parts, scales))
        rows = (summed / total).T.astype(jnp.bfloat16)
        first = jnp.bitwise_xor(core_ref[0], j) * groups
        for g in range(groups):
            upper = rows[2 * g * half : (2 * g + 1) * half]
            lower = rows[(2 * g + 1) * half : (2 * g + 2) * half]
            out_ref[first + g] = jnp.concatenate([upper, lower], 1)


def combine(core, parts):
    half = parts[0].shape[2] // 16
    return pl.pallas_call(
        combine_kernel,
        in_specs=[SMEM] + [VMEM] * len(parts),
        out_specs=VMEM,
        out_shape=jax.ShapeDtypeStruct((16, half, 2 * HS), jnp.bfloat16),
        compiler_params=pltpu.CompilerParams(vmem_limit_bytes=32 * 2**20),
    )(core, *parts)


def finish_kernel(grp_ref, pieces_ref, *refs):
    w_refs, out_ref = refs[:-1], refs[-1]
    groups = pieces_ref.shape[0] // 2
    me = grp_ref[0]
    result = None
    for k, w_ref in enumerate(w_refs):
        near = jnp.bitwise_or(jnp.bitwise_and(me, 4), jnp.bitwise_and(me - k, 3))
        order = [c * groups + g for g in (near, jnp.bitwise_xor(near, 4)) for c in range(2)]
        blocks = [pieces_ref[i] for i in order]
        upper = jnp.concatenate([p[:, :HS] for p in blocks], 1)
        lower = jnp.concatenate([p[:, HS:] for p in blocks], 1)
        attention = jnp.concatenate([upper, lower], 0)
        term = jnp.dot(attention, w_ref[...], preferred_element_type=jnp.float32)
        result = term if result is None else result + term
    out_ref[...] = result.astype(jnp.bfloat16)


def finish(grp, pieces, w_turns):
    return pl.pallas_call(
        finish_kernel,
        in_specs=[SMEM] + [VMEM] * (1 + len(w_turns)),
        out_specs=VMEM,
        out_shape=jax.ShapeDtypeStruct((2 * pieces.shape[1], w_turns[0].shape[1]), jnp.bfloat16),
        compiler_params=pltpu.CompilerParams(vmem_limit_bytes=24 * 2**20),
    )(grp, pieces, *w_turns)


def along_x(by):
    return [(s, (s + 4 * by) % 16) for s in range(16)]


def came_from(s, by):
    return jnp.bitwise_and(s - 4 * by, 15)


NEAR_CALLS = ((0,), (1, 3, 2))
FAR_CALLS = ((2, 1, 3), (0,))
CORE_SWAP = [(s, s ^ 1) for s in range(16)]
Y_SWAP = [(s, s ^ 2) for s in range(16)]


def body(inputs, latents, w_query, w_key, w_value, w_out, positions, block_mask):
    seq = lax.axis_index("seq")[None]
    grp = lax.axis_index("grp")[None]
    core = jnp.bitwise_and(seq, 1)

    mine, theirs, kv_own, kv_other, codes = front(
        seq, latents, inputs, w_query, w_key, w_value, positions, block_mask
    )
    q_chip = jnp.stack([mine, lax.ppermute(theirs, "seq", CORE_SWAP)])
    queries = {by: q_chip if by == 0 else lax.ppermute(q_chip, "seq", along_x(by)) for by in (0, 1, 3, 2)}
    kv_partner = lax.ppermute(kv_other, "seq", CORE_SWAP)
    near = prepare(kv_own, kv_partner)
    kv_far = [lax.ppermute(kv, "seq", Y_SWAP) for kv in (kv_own, kv_partner)]

    w_other = lax.ppermute(w_out, "grp", [(g, g ^ 4) for g in range(8)])
    spots = positions.reshape(-1, ROWS)
    near_parts = dict(zip(NEAR_CALLS[0], attend(NEAR_CALLS[0], seq, codes, spots, near, [q_chip])))
    w_pair, near_parts[0] = lax.optimization_barrier((jnp.concatenate([w_out, w_other], 0), near_parts[0]))
    w_turns = [w_pair] + [
        lax.ppermute(w_pair, "grp", [(g, (g & 4) | ((g + k) & 3)) for g in range(8)]) for k in (1, 2, 3)
    ]

    parts = {}
    last = 0
    for call in NEAR_CALLS[1:]:
        queries[call[0]], near_parts[last], kv_far[0] = lax.optimization_barrier(
            (queries[call[0]], near_parts[last], kv_far[0])
        )
        near_parts.update(zip(call, attend(call, seq, codes, spots, near, [queries[by] for by in call])))
        last = call[-1]
    kv_far, w_turns, near_parts[last] = lax.optimization_barrier((kv_far, w_turns, near_parts[last]))
    far = prepare(*kv_far)
    last = None
    for call in FAR_CALLS:
        if last is not None:
            queries[call[0]], parts[last] = lax.optimization_barrier((queries[call[0]], parts[last]))
        done = attend(
            call, seq, codes, spots, far, [queries[by] for by in call], [near_parts[by] for by in call]
        )
        parts.update(zip(call, done))
        last = call[-1]

    parts = [part if by == 0 else lax.ppermute(part, "seq", along_x(-by)) for by, part in parts.items()]
    pieces = combine(core, parts)
    owners = [[(4 * x + 2 * y + c) * 8 + g for c in range(2) for g in range(8)] for x in range(4) for y in range(2)]
    pieces = lax.all_to_all(pieces, ("seq", "grp"), 0, 0, axis_index_groups=owners)
    return finish(grp, pieces, w_turns)


def solution(mesh):
    return jax.shard_map(
        body,
        mesh=mesh,
        in_specs=(
            P("seq", None),
            P("seq", None),
            P(None, "grp"),
            P(None, "grp"),
            P(None, "grp"),
            P("grp", None),
            P(),
            P(),
        ),
        out_specs=P(("seq", "grp"), None),
        check_vma=False,
    )
```

```python
import functools

import jax
import jax.numpy as jnp
from jax import lax
from jax.experimental import pallas as pl
from jax.experimental.pallas import tpu as pltpu
from jax.sharding import PartitionSpec as P

HS = 64
BLOCK = 128
TILES = 4
SLOTS = 2
ROWS = 2 * BLOCK
FAR = 64
KEY_BLOCKS = 32
ACC_ROWS = 72
LOG2E = 1.4426950408889634
SAFE_SCORE = 60.0
masked_score = -1e30
lowest_max = -1e29
SMEM = pl.BlockSpec(memory_space=pltpu.SMEM)
VMEM = pl.BlockSpec(memory_space=pltpu.VMEM)


def list_work(me, pos_ref, mask_ref, code_ref):
    half = KEY_BLOCKS // 2
    both = 2 * KEY_BLOCKS
    blocks = pos_ref.shape[0]

    def held(t):
        source = jnp.bitwise_xor(me, lax.shift_right_logical(t, 4))
        return source * half + jnp.bitwise_and(t, half - 1)

    spots = pos_ref[...].T
    own_block = lax.shift_right_logical(spots, 7)
    furthest = jnp.max(own_block, axis=0, keepdims=True)
    t_rows = lax.broadcasted_iota(jnp.int32, (both, blocks), 0)
    own = jnp.zeros((both, blocks), jnp.int32)
    for t in range(both):
        found = jnp.max((own_block == held(jnp.int32(t))).astype(jnp.int32), axis=0, keepdims=True)
        own = jnp.where(t_rows == t, found, own)

    def exact(condition):
        return condition.astype(jnp.float32).astype(jnp.bfloat16)

    columns = mask_ref.shape[1]
    pick = exact(
        lax.broadcasted_iota(jnp.int32, (both, columns), 1)
        == held(lax.broadcasted_iota(jnp.int32, (both, columns), 0))
    )
    listed = lax.dot_general(
        pick, exact(mask_ref[...] == 1), (((1,), (1,)), ((), ())), preferred_element_type=jnp.float32
    )
    active = exact((own > 0) | ((listed > 0.5) & (held(t_rows) <= furthest)))
    listed = exact(listed > 0.5)

    row = lax.broadcasted_iota(jnp.int32, (blocks, BLOCK), 0)
    col = lax.broadcasted_iota(jnp.int32, (blocks, BLOCK), 1)
    first, second = exact(row == 2 * col), exact(row == 2 * col + 1)
    active = jnp.dot(active, first + second, preferred_element_type=jnp.float32) > 0.5
    listed = [jnp.dot(listed, pairs, preferred_element_type=jnp.float32).astype(jnp.int32) for pairs in (first, second)]
    row = lax.broadcasted_iota(jnp.int32, (both, both), 0)
    col = lax.broadcasted_iota(jnp.int32, (both, both), 1)
    earlier = exact((col < row) & (lax.shift_right_logical(row, 5) == lax.shift_right_logical(col, 5)))
    place = jnp.dot(earlier, exact(active), preferred_element_type=jnp.float32).astype(jnp.int32)
    t_rows = lax.broadcasted_iota(jnp.int32, (both, BLOCK), 0)
    value = jnp.bitwise_and(t_rows, KEY_BLOCKS - 1) + KEY_BLOCKS * (listed[0] + 2 * listed[1] + 4)
    packed = jnp.where(active, place * 512 + value, -1)
    ones = active.astype(jnp.int32)
    slot_rows = lax.broadcasted_iota(jnp.int32, (KEY_BLOCKS, BLOCK), 0)
    tables = []
    for n in range(2):
        codes = jnp.zeros((KEY_BLOCKS, BLOCK), jnp.int32)
        for t in range(n * KEY_BLOCKS, (n + 1) * KEY_BLOCKS):
            one = packed[t : t + 1, :]
            codes = jnp.where(lax.shift_right_arithmetic(one, 9) == slot_rows, jnp.bitwise_and(one, 511), codes)
        count = jnp.sum(ones[n * KEY_BLOCKS : (n + 1) * KEY_BLOCKS], axis=0, keepdims=True)
        slots = jnp.maximum(lax.shift_right_logical(count + (TILES - 1), 2), 1)
        tables += [codes, jnp.broadcast_to(slots, (FAR - KEY_BLOCKS, BLOCK))]
    code_ref[...] = jnp.concatenate(tables, 0).T[: code_ref.shape[0]]


def front_kernel(seq_ref, lat_hbm, x_hbm, wq_hbm, wk_hbm, wv_hbm, pos_hbm, mask_hbm, *rest):
    mine_ref, theirs_ref, own_ref, other_ref, code_ref = rest[:5]
    lat, x, wq, wk, wv, pos, mask, w_all, sems, x_sems = rest[5:]
    small = [
        pltpu.make_async_copy(source, target, sems.at[i])
        for i, (source, target) in enumerate(
            [(pos_hbm, pos), (mask_hbm, mask), (wq_hbm, wq), (lat_hbm, lat), (wk_hbm, wk), (wv_hbm, wv)]
        )
    ]
    rows = x.shape[0] // x_sems.shape[0]
    parts = [pl.ds(i * rows, rows) for i in range(x_sems.shape[0])]
    large = [pltpu.make_async_copy(x_hbm.at[p], x.at[p], x_sems.at[i]) for i, p in enumerate(parts)]
    for copy in small + large:
        copy.start()
    got_pos, got_mask, got_wq, got_lat, got_wk, got_wv = small
    first = jnp.bitwise_and(seq_ref[0], 1) == 0

    got_pos.wait()
    got_mask.wait()
    list_work(seq_ref[0], pos, mask, code_ref)

    got_wq.wait()
    got_lat.wait()
    q = jnp.dot(lat[...], wq[...], preferred_element_type=jnp.float32).T
    q = q.astype(jnp.bfloat16) * jnp.bfloat16(HS ** -0.5)
    mine_ref[...] = jnp.where(first, q[:HS], q[HS:])
    theirs_ref[...] = jnp.where(first, q[HS:], q[:HS])

    got_wk.wait()
    got_wv.wait()
    k, v = wk[...], wv[...]
    head_0 = jnp.concatenate([k[:, :HS], v[:, :HS]], 1)
    head_1 = jnp.concatenate([k[:, HS:], v[:, HS:]], 1)
    w_all[:, : 2 * HS] = jnp.where(first, head_0, head_1)
    w_all[:, 2 * HS :] = jnp.where(first, head_1, head_0)
    for copy, part in zip(large, parts):
        copy.wait()
        both = jnp.dot(x[part, :], w_all[...], preferred_element_type=jnp.float32).astype(jnp.bfloat16)
        own_ref[part, :] = both[:, : 2 * HS]
        other_ref[part, :] = both[:, 2 * HS :]


def front(seq, latents, inputs, w_query, w_key, w_value, positions, block_mask):
    rows, width = latents.shape
    keys = inputs.shape[0]
    spots = positions.reshape(-1, BLOCK)
    operands = (latents, inputs, w_query, w_key, w_value, spots, block_mask)
    q = jax.ShapeDtypeStruct((HS, rows), jnp.bfloat16)
    kv = jax.ShapeDtypeStruct((keys, 2 * HS), jnp.bfloat16)
    return pl.pallas_call(
        front_kernel,
        in_specs=[SMEM] + [pl.BlockSpec(memory_space=pl.ANY)] * len(operands),
        out_specs=[VMEM] * 5,
        out_shape=[q, q, kv, kv, jax.ShapeDtypeStruct((spots.shape[0] // 2, BLOCK), jnp.int32)],
        scratch_shapes=[pltpu.VMEM(a.shape, a.dtype) for a in operands]
        + [
            pltpu.VMEM((width, 4 * HS), jnp.bfloat16),
            pltpu.SemaphoreType.DMA((6,)),
            pltpu.SemaphoreType.DMA((4,)),
        ],
        compiler_params=pltpu.CompilerParams(vmem_limit_bytes=61 * 2**20),
        cost_estimate=pl.CostEstimate(
            flops=2 * (keys * 4 + rows * 2) * width * HS, bytes_accessed=6 * 2**20, transcendentals=0
        ),
    )(seq, *operands)


def prepare_kernel(*refs):
    sources, (kv_ref, vt_ref, norm_ref) = refs[:-3], refs[-3:]
    each = KEY_BLOCKS // len(sources)
    most = None
    for t in range(KEY_BLOCKS):
        at = t % each
        tile = sources[t // each][at * BLOCK : (at + 1) * BLOCK, :]
        kv_ref[t * BLOCK : (t + 1) * BLOCK, :] = tile
        turned = tile.T
        vt_ref[:HS, t * BLOCK : (t + 1) * BLOCK] = turned[HS:, :]
        k = turned[:HS, :].astype(jnp.float32)
        squares = jnp.sum(k * k, axis=0, keepdims=True)
        most = squares if most is None else jnp.maximum(most, squares)
    vt_ref[HS:, :] = jnp.ones((ACC_ROWS - HS, KEY_BLOCKS * BLOCK), jnp.bfloat16)
    norm_ref[0] = jnp.max(most)


def prepare(*sources):
    keys = sum(source.shape[0] for source in sources)
    return pl.pallas_call(
        prepare_kernel,
        in_specs=[VMEM] * len(sources),
        out_specs=[VMEM, VMEM, SMEM],
        out_shape=[
            jax.ShapeDtypeStruct((keys, 2 * HS), jnp.bfloat16),
            jax.ShapeDtypeStruct((ACC_ROWS, keys), jnp.bfloat16),
            jax.ShapeDtypeStruct((1,), jnp.float32),
        ],
        compiler_params=pltpu.CompilerParams(vmem_limit_bytes=24 * 2**20),
    )(*sources)


def attention_kernel(steps, far, seq_ref, code_ref, norm_ref, pos_ref, kv_ref, vt_ref, *rest):
    chips = len(steps)
    q_refs, rest = rest[:chips], rest[chips:]
    before_refs, rest = (rest[:chips], rest[chips:]) if far else (None, rest)
    o_refs, (q_all, p_a, p_b, s_all, acc) = rest[:chips], rest[chips:]
    table = FAR if far else 0
    blocks = 4 * chips
    me = seq_ref[0]
    keys_of = jnp.bitwise_xor(me, 2) if far else me
    own_base = keys_of * (KEY_BLOCKS // 2 * BLOCK)
    partner_base = jnp.bitwise_xor(keys_of, 1) * (KEY_BLOCKS // 2 * BLOCK)
    sources = [came_from(me, step) for step in steps]
    iota = lax.broadcasted_iota(jnp.int32, (BLOCK, ROWS), 0)
    in_first = lax.broadcasted_iota(jnp.int32, (1, ROWS), 1) < BLOCK
    iota_half = iota.astype(jnp.float32).astype(jnp.bfloat16)

    most = None
    for i, ref in enumerate(q_refs):
        for j in range(ref.shape[0]):
            q = ref[j]
            q_all[i * ref.shape[0] + j] = q
            q = q.astype(jnp.float32)
            squares = jnp.sum(q * q, axis=0, keepdims=True)
            most = squares if most is None else jnp.maximum(most, squares)
    safe = jnp.max(most) * norm_ref[0] <= SAFE_SCORE * SAFE_SCORE

    def clamp(r):
        return jnp.minimum(r, blocks - 1)

    def whole_block(r):
        shard = sources[-1]
        for i in range(chips - 1):
            shard = jnp.where(lax.div(r, 4) == i, sources[i], shard)
        return jnp.bitwise_xor(shard, jnp.bitwise_and(lax.div(r, 2), 1)) * 2 + lax.rem(r, 2)

    def offset(i):
        return pl.multiple_of(i * BLOCK, BLOCK)

    def row_offset(i):
        return pl.multiple_of(i * ROWS, ROWS)

    def query(r):
        q = q_all[lax.div(r, 2), :, pl.ds(row_offset(lax.rem(r, 2)), ROWS)]
        return jnp.concatenate([q, jnp.zeros_like(q)], 0)

    def key_blocks(row, c):
        return [jnp.bitwise_and(code_ref[row, table + c * TILES + t], KEY_BLOCKS - 1) for t in range(TILES)]

    def products(row, r, c):
        keys = jnp.concatenate([kv_ref[pl.ds(offset(k), BLOCK), :] for k in key_blocks(row, c)], 0)
        return jnp.dot(keys, query(r), preferred_element_type=jnp.float32)

    def values(row, c):
        return jnp.concatenate([vt_ref[:, pl.ds(offset(k), BLOCK)] for k in key_blocks(row, c)], 1)

    def last_key(row, c, t, pos, real):
        code = code_ref[row, table + c * TILES + t]
        k = jnp.bitwise_and(code, KEY_BLOCKS - 1)
        half = KEY_BLOCKS // 2
        base = jnp.where(k < half, own_base, partner_base - half * BLOCK) + k * BLOCK
        real = jnp.logical_and(real, code >= 4 * KEY_BLOCKS)
        reach = [jnp.where(jnp.bitwise_and(code, n * KEY_BLOCKS) > 0, 1 << 30, BLOCK) for n in (1, 2)]
        reach = jnp.where(in_first, *[jnp.where(real, n, -(1 << 30)) for n in reach])
        ahead = pos - base
        return jnp.where(ahead < reach, jnp.minimum(ahead, BLOCK - 1), -1)

    def put(i, rr, a, top):
        at = (lax.div(rr, 2), slice(None), pl.ds(row_offset(lax.rem(rr, 2)), ROWS))
        if far:
            before = before_refs[i][at].astype(jnp.float32)
            top_before, top_now = before[HS + 1 : HS + 2], top
            top = jnp.maximum(top_before, top_now)
            shrink, shrink_before = jnp.exp(top_now - top), jnp.exp(top_before - top)
            total = a[HS : HS + 1] * shrink + (before[HS : HS + 1] + before[HS + 2 : HS + 3]) * shrink_before
            a = a * shrink + before * shrink_before
        else:
            total = a[HS : HS + 1]
        low = total - total.astype(jnp.bfloat16).astype(jnp.float32)
        out = jnp.concatenate([a[:HS], total, top, low, a[HS + 3 :]], 0)
        o_refs[i][at] = out.astype(jnp.bfloat16)

    def advance(r, c):
        last = c + 1 >= code_ref[whole_block(clamp(r)), table + KEY_BLOCKS]
        return jnp.where(last, jnp.minimum(r + 1, blocks), r), jnp.where(last, 0, c + 1)

    def step_slots(r, c):
        slots = []
        for _ in range(SLOTS):
            slots.append((r, c))
            r, c = advance(r, c)
        return slots, r, c

    @pl.when(safe)
    def _():
        acc[...] = jnp.zeros_like(acc)

        def weigh(p_ref, slots):
            for g, (r, c) in enumerate(slots):
                rr = clamp(r)
                row = whole_block(rr)
                s = products(row, rr, c)
                pos = pos_ref[pl.ds(row, 1), :]
                for t in range(TILES):
                    p = jnp.exp2(s[t * BLOCK : (t + 1) * BLOCK] * LOG2E).astype(jnp.bfloat16)
                    last = last_key(row, c, t, pos, r < blocks).astype(jnp.float32).astype(jnp.bfloat16)
                    at = (g * TILES + t) * BLOCK
                    p_ref[at : at + BLOCK, :] = jnp.where(iota_half <= last, p, jnp.zeros_like(p))

        def add(p_ref, slots):
            for g, (r, c) in enumerate(slots):
                v = values(whole_block(clamp(r)), c)
                at = g * TILES * BLOCK
                acc[r] += jnp.dot(v, p_ref[at : at + TILES * BLOCK, :], preferred_element_type=jnp.float32)

        slots_0, r0, c0 = step_slots(jnp.int32(0), jnp.int32(0))
        weigh(p_a, slots_0)

        def two_steps(_, state):
            r, c, r1, c1 = state
            slots, _, _ = step_slots(r, c)
            slots_1, r2, c2 = step_slots(r1, c1)
            weigh(p_b, slots_1)
            add(p_a, slots)
            slots_2, r3, c3 = step_slots(r2, c2)
            weigh(p_a, slots_2)
            add(p_b, slots_1)
            return r2, c2, r3, c3

        items = lax.fori_loop(0, blocks, lambda r, n: n + code_ref[whole_block(r), table + KEY_BLOCKS], jnp.int32(0))
        turns = lax.div(items + (2 * SLOTS - 1), 2 * SLOTS)
        lax.fori_loop(0, turns, two_steps, (jnp.int32(0), jnp.int32(0), r0, c0))

        for i in range(chips):
            def finish(rr, _, i=i):
                a = acc[i * 4 + rr]
                put(i, rr, a, jnp.where(a[HS : HS + 1] > 0, 0.0, lowest_max))
                return 0

            lax.fori_loop(0, 4, finish, 0)

    @pl.when(jnp.logical_not(safe))
    def _():
        for i in range(chips):
            def one_block(rr, _, i=i):
                r = i * 4 + rr
                row = whole_block(r)
                pos = pos_ref[pl.ds(row, 1), :]
                acc[0] = jnp.zeros((ACC_ROWS, ROWS), jnp.float32)

                def one_slot(c, top):
                    s = products(row, r, c)
                    best = top
                    for t in range(TILES):
                        tile = s[t * BLOCK : (t + 1) * BLOCK]
                        tile = jnp.where(iota <= last_key(row, c, t, pos, True), tile, masked_score)
                        s_all[t * BLOCK : (t + 1) * BLOCK, :] = tile
                        best = jnp.maximum(best, jnp.max(tile, 0, keepdims=True))
                    best = best.astype(jnp.bfloat16).astype(jnp.float32)
                    p = jnp.exp2((s_all[...] - best) * LOG2E).astype(jnp.bfloat16)
                    shrink = jnp.exp2((top - best) * LOG2E)
                    acc[0] = acc[0] * shrink + jnp.dot(values(row, c), p, preferred_element_type=jnp.float32)
                    return best

                start = jnp.full((1, ROWS), lowest_max, jnp.bfloat16).astype(jnp.float32)
                top = lax.fori_loop(0, code_ref[row, table + KEY_BLOCKS], one_slot, start)
                put(i, rr, acc[0], top)
                return 0

            lax.fori_loop(0, 4, one_block, 0)


def attend(steps, seq, codes, spots, held, queries, before=()):
    kv, vt, norm = held
    chips = len(steps)
    out = jax.ShapeDtypeStruct((2, ACC_ROWS, queries[0].shape[2]), jnp.bfloat16)
    return pl.pallas_call(
        functools.partial(attention_kernel, steps, bool(before)),
        in_specs=[SMEM] * 3 + [VMEM] * (3 + len(queries) + len(before)),
        out_specs=[VMEM] * chips,
        out_shape=[out] * chips,
        scratch_shapes=[
            pltpu.VMEM((2 * chips, HS, queries[0].shape[2]), jnp.bfloat16),
            pltpu.VMEM((SLOTS * TILES * BLOCK, ROWS), jnp.bfloat16),
            pltpu.VMEM((SLOTS * TILES * BLOCK, ROWS), jnp.bfloat16),
            pltpu.VMEM((TILES * BLOCK, ROWS), jnp.float32),
            pltpu.VMEM((4 * chips + 1, ACC_ROWS, ROWS), jnp.float32),
        ],
        compiler_params=pltpu.CompilerParams(vmem_limit_bytes=32 * 2**20),
        cost_estimate=pl.CostEstimate(
            flops=chips * 6 * 10**9, bytes_accessed=4 * 2**20, transcendentals=chips * 2**20
        ),
    )(seq, codes, norm, spots, kv, vt, *queries, *before)


def combine_kernel(core_ref, *refs):
    parts, out_ref = refs[:-1], refs[-1]
    groups = out_ref.shape[0] // 2
    half = out_ref.shape[1]
    for j in range(2):
        tops = [p[j, HS + 1 : HS + 2, :].astype(jnp.float32) for p in parts]
        top = functools.reduce(jnp.maximum, tops)
        scales = [jnp.exp(t - top) for t in tops]
        total = sum(
            (p[j, HS : HS + 1, :].astype(jnp.float32) + p[j, HS + 2 : HS + 3, :].astype(jnp.float32)) * scale
            for p, scale in zip(parts, scales)
        )
        summed = sum(p[j, :HS, :].astype(jnp.float32) * scale for p, scale in zip(parts, scales))
        rows = (summed / total).T.astype(jnp.bfloat16)
        first = jnp.bitwise_xor(core_ref[0], j) * groups
        for g in range(groups):
            upper = rows[2 * g * half : (2 * g + 1) * half]
            lower = rows[(2 * g + 1) * half : (2 * g + 2) * half]
            out_ref[first + g] = jnp.concatenate([upper, lower], 1)


def combine(core, parts):
    half = parts[0].shape[2] // 16
    return pl.pallas_call(
        combine_kernel,
        in_specs=[SMEM] + [VMEM] * len(parts),
        out_specs=VMEM,
        out_shape=jax.ShapeDtypeStruct((16, half, 2 * HS), jnp.bfloat16),
        compiler_params=pltpu.CompilerParams(vmem_limit_bytes=32 * 2**20),
    )(core, *parts)


def finish_kernel(grp_ref, pieces_ref, *refs):
    w_refs, out_ref = refs[:-1], refs[-1]
    groups = pieces_ref.shape[0] // 2
    me = grp_ref[0]
    result = None
    for k, w_ref in enumerate(w_refs):
        near = jnp.bitwise_or(jnp.bitwise_and(me, 4), jnp.bitwise_and(me - k, 3))
        order = [c * groups + g for g in (near, jnp.bitwise_xor(near, 4)) for c in range(2)]
        blocks = [pieces_ref[i] for i in order]
        upper = jnp.concatenate([p[:, :HS] for p in blocks], 1)
        lower = jnp.concatenate([p[:, HS:] for p in blocks], 1)
        attention = jnp.concatenate([upper, lower], 0)
        term = jnp.dot(attention, w_ref[...], preferred_element_type=jnp.float32)
        result = term if result is None else result + term
    out_ref[...] = result.astype(jnp.bfloat16)


def finish(grp, pieces, w_turns):
    return pl.pallas_call(
        finish_kernel,
        in_specs=[SMEM] + [VMEM] * (1 + len(w_turns)),
        out_specs=VMEM,
        out_shape=jax.ShapeDtypeStruct((2 * pieces.shape[1], w_turns[0].shape[1]), jnp.bfloat16),
        compiler_params=pltpu.CompilerParams(vmem_limit_bytes=24 * 2**20),
    )(grp, pieces, *w_turns)


def along_x(by):
    return [(s, (s + 4 * by) % 16) for s in range(16)]


def came_from(s, by):
    return jnp.bitwise_and(s - 4 * by, 15)


NEAR_CALLS = ((0,), (1, 3, 2))
FAR_CALLS = ((2, 1, 3), (0,))
CORE_SWAP = [(s, s ^ 1) for s in range(16)]
Y_SWAP = [(s, s ^ 2) for s in range(16)]


def body(inputs, latents, w_query, w_key, w_value, w_out, positions, block_mask):
    seq = lax.axis_index("seq")[None]
    grp = lax.axis_index("grp")[None]
    core = jnp.bitwise_and(seq, 1)

    mine, theirs, kv_own, kv_other, codes = front(
        seq, latents, inputs, w_query, w_key, w_value, positions, block_mask
    )
    q_chip = jnp.stack([mine, lax.ppermute(theirs, "seq", CORE_SWAP)])
    queries = {by: q_chip if by == 0 else lax.ppermute(q_chip, "seq", along_x(by)) for by in (0, 1, 3, 2)}
    kv_partner = lax.ppermute(kv_other, "seq", CORE_SWAP)
    near = prepare(kv_own, kv_partner)
    kv_far = [lax.ppermute(kv, "seq", Y_SWAP) for kv in (kv_own, kv_partner)]

    w_other = lax.ppermute(w_out, "grp", [(g, g ^ 4) for g in range(8)])
    spots = positions.reshape(-1, ROWS)
    near_parts = dict(zip(NEAR_CALLS[0], attend(NEAR_CALLS[0], seq, codes, spots, near, [q_chip])))
    w_other, near_parts[0] = lax.optimization_barrier((w_other, near_parts[0]))
    w_pair = jnp.concatenate([w_out, w_other], 0)
    w_turns = [w_pair] + [
        lax.ppermute(w_pair, "grp", [(g, (g & 4) | ((g + k) & 3)) for g in range(8)]) for k in (1, 2, 3)
    ]

    parts = {}
    last = 0
    for call in NEAR_CALLS[1:]:
        queries[call[0]], near_parts[last], kv_far[0] = lax.optimization_barrier(
            (queries[call[0]], near_parts[last], kv_far[0])
        )
        near_parts.update(zip(call, attend(call, seq, codes, spots, near, [queries[by] for by in call])))
        last = call[-1]
    w_early = w_turns[1], w_turns[3]
    kv_far, w_early, near_parts[last] = lax.optimization_barrier((kv_far, w_early, near_parts[last]))
    w_turns[1], w_turns[3] = w_early
    far = prepare(*kv_far)
    last = None
    for call in FAR_CALLS:
        if last is not None:
            queries[call[0]], parts[last] = lax.optimization_barrier((queries[call[0]], parts[last]))
        done = attend(
            call, seq, codes, spots, far, [queries[by] for by in call], [near_parts[by] for by in call]
        )
        parts.update(zip(call, done))
        last = call[-1]

    parts = [part if by == 0 else lax.ppermute(part, "seq", along_x(-by)) for by, part in parts.items()]
    parts, w_turns[2] = lax.optimization_barrier((parts, w_turns[2]))
    pieces = combine(core, parts)
    owners = [[(4 * x + 2 * y + c) * 8 + g for c in range(2) for g in range(8)] for x in range(4) for y in range(2)]
    pieces = lax.all_to_all(pieces, ("seq", "grp"), 0, 0, axis_index_groups=owners)
    return finish(grp, pieces, w_turns)


def solution(mesh):
    return jax.shard_map(
        body,
        mesh=mesh,
        in_specs=(
            P("seq", None),
            P("seq", None),
            P(None, "grp"),
            P(None, "grp"),
            P(None, "grp"),
            P("grp", None),
            P(),
            P(),
        ),
        out_specs=P(("seq", "grp"), None),
        check_vma=False,
    )
```

```python
import functools

import jax
import jax.numpy as jnp
from jax import lax
from jax.experimental import pallas as pl
from jax.experimental.pallas import tpu as pltpu
from jax.sharding import PartitionSpec as P

HS = 64
BLOCK = 128
TILES = 4
SLOTS = 2
ROWS = 2 * BLOCK
FAR = 64
KEY_BLOCKS = 32
ACC_ROWS = 72
LOG2E = 1.4426950408889634
SAFE_SCORE = 60.0
masked_score = -1e30
lowest_max = -1e29
SMEM = pl.BlockSpec(memory_space=pltpu.SMEM)
VMEM = pl.BlockSpec(memory_space=pltpu.VMEM)


def in_hbm(*arrays):
    return [pltpu.with_memory_space_constraint(a, pltpu.HBM) for a in arrays]


def list_work(me, pos_ref, mask_ref, code_ref):
    half = KEY_BLOCKS // 2
    both = 2 * KEY_BLOCKS
    blocks = pos_ref.shape[0]

    def held(t):
        source = jnp.bitwise_xor(me, lax.shift_right_logical(t, 4))
        return source * half + jnp.bitwise_and(t, half - 1)

    spots = pos_ref[...].T
    own_block = lax.shift_right_logical(spots, 7)
    furthest = jnp.max(own_block, axis=0, keepdims=True)
    t_rows = lax.broadcasted_iota(jnp.int32, (both, blocks), 0)
    own = jnp.zeros((both, blocks), jnp.int32)
    for t in range(both):
        found = jnp.max((own_block == held(jnp.int32(t))).astype(jnp.int32), axis=0, keepdims=True)
        own = jnp.where(t_rows == t, found, own)

    def exact(condition):
        return condition.astype(jnp.float32).astype(jnp.bfloat16)

    columns = mask_ref.shape[1]
    pick = exact(
        lax.broadcasted_iota(jnp.int32, (both, columns), 1)
        == held(lax.broadcasted_iota(jnp.int32, (both, columns), 0))
    )
    listed = lax.dot_general(
        pick, exact(mask_ref[...] == 1), (((1,), (1,)), ((), ())), preferred_element_type=jnp.float32
    )
    active = exact((own > 0) | ((listed > 0.5) & (held(t_rows) <= furthest)))
    listed = exact(listed > 0.5)

    row = lax.broadcasted_iota(jnp.int32, (blocks, BLOCK), 0)
    col = lax.broadcasted_iota(jnp.int32, (blocks, BLOCK), 1)
    first, second = exact(row == 2 * col), exact(row == 2 * col + 1)
    active = jnp.dot(active, first + second, preferred_element_type=jnp.float32) > 0.5
    listed = [jnp.dot(listed, pairs, preferred_element_type=jnp.float32).astype(jnp.int32) for pairs in (first, second)]
    row = lax.broadcasted_iota(jnp.int32, (both, both), 0)
    col = lax.broadcasted_iota(jnp.int32, (both, both), 1)
    earlier = exact((col < row) & (lax.shift_right_logical(row, 5) == lax.shift_right_logical(col, 5)))
    place = jnp.dot(earlier, exact(active), preferred_element_type=jnp.float32).astype(jnp.int32)
    t_rows = lax.broadcasted_iota(jnp.int32, (both, BLOCK), 0)
    value = jnp.bitwise_and(t_rows, KEY_BLOCKS - 1) + KEY_BLOCKS * (listed[0] + 2 * listed[1] + 4)
    packed = jnp.where(active, place * 512 + value, -1)
    ones = active.astype(jnp.int32)
    slot_rows = lax.broadcasted_iota(jnp.int32, (KEY_BLOCKS, BLOCK), 0)
    tables = []
    for n in range(2):
        codes = jnp.zeros((KEY_BLOCKS, BLOCK), jnp.int32)
        for t in range(n * KEY_BLOCKS, (n + 1) * KEY_BLOCKS):
            one = packed[t : t + 1, :]
            codes = jnp.where(lax.shift_right_arithmetic(one, 9) == slot_rows, jnp.bitwise_and(one, 511), codes)
        count = jnp.sum(ones[n * KEY_BLOCKS : (n + 1) * KEY_BLOCKS], axis=0, keepdims=True)
        slots = jnp.maximum(lax.shift_right_logical(count + (TILES - 1), 2), 1)
        tables += [codes, jnp.broadcast_to(slots, (FAR - KEY_BLOCKS, BLOCK))]
    code_ref[...] = jnp.concatenate(tables, 0).T[: code_ref.shape[0]]


def front_kernel(seq_ref, lat_hbm, x_hbm, wq_hbm, wk_hbm, wv_hbm, pos_hbm, mask_hbm, *rest):
    mine_ref, theirs_ref, own_ref, other_ref, code_ref = rest[:5]
    lat, x, wq, wk, wv, pos, mask, w_all, sems, x_sems = rest[5:]
    small = [
        pltpu.make_async_copy(source, target, sems.at[i])
        for i, (source, target) in enumerate(
            [(pos_hbm, pos), (mask_hbm, mask), (wq_hbm, wq), (lat_hbm, lat), (wk_hbm, wk), (wv_hbm, wv)]
        )
    ]
    rows = x.shape[0] // x_sems.shape[0]
    parts = [pl.ds(i * rows, rows) for i in range(x_sems.shape[0])]
    large = [pltpu.make_async_copy(x_hbm.at[p], x.at[p], x_sems.at[i]) for i, p in enumerate(parts)]
    for copy in small + large:
        copy.start()
    got_pos, got_mask, got_wq, got_lat, got_wk, got_wv = small
    first = jnp.bitwise_and(seq_ref[0], 1) == 0

    got_pos.wait()
    got_mask.wait()
    list_work(seq_ref[0], pos, mask, code_ref)

    got_wq.wait()
    got_lat.wait()
    q = jnp.dot(lat[...], wq[...], preferred_element_type=jnp.float32).T
    q = q.astype(jnp.bfloat16) * jnp.bfloat16(HS ** -0.5)
    mine_ref[...] = jnp.where(first, q[:HS], q[HS:])
    theirs_ref[...] = jnp.where(first, q[HS:], q[:HS])

    got_wk.wait()
    got_wv.wait()
    k, v = wk[...], wv[...]
    head_0 = jnp.concatenate([k[:, :HS], v[:, :HS]], 1)
    head_1 = jnp.concatenate([k[:, HS:], v[:, HS:]], 1)
    w_all[:, : 2 * HS] = jnp.where(first, head_0, head_1)
    w_all[:, 2 * HS :] = jnp.where(first, head_1, head_0)
    for copy, part in zip(large, parts):
        copy.wait()
        both = jnp.dot(x[part, :], w_all[...], preferred_element_type=jnp.float32).astype(jnp.bfloat16)
        own_ref[part, :] = both[:, : 2 * HS]
        other_ref[part, :] = both[:, 2 * HS :]


def front(seq, latents, inputs, w_query, w_key, w_value, positions, block_mask):
    rows, width = latents.shape
    keys = inputs.shape[0]
    spots = positions.reshape(-1, BLOCK)
    operands = (latents, inputs, w_query, w_key, w_value, spots, block_mask)
    q = jax.ShapeDtypeStruct((HS, rows), jnp.bfloat16)
    kv = jax.ShapeDtypeStruct((keys, 2 * HS), jnp.bfloat16)
    return pl.pallas_call(
        front_kernel,
        in_specs=[SMEM] + [pl.BlockSpec(memory_space=pl.ANY)] * len(operands),
        out_specs=[VMEM] * 5,
        out_shape=[q, q, kv, kv, jax.ShapeDtypeStruct((spots.shape[0] // 2, BLOCK), jnp.int32)],
        scratch_shapes=[pltpu.VMEM(a.shape, a.dtype) for a in operands]
        + [
            pltpu.VMEM((width, 4 * HS), jnp.bfloat16),
            pltpu.SemaphoreType.DMA((6,)),
            pltpu.SemaphoreType.DMA((4,)),
        ],
        compiler_params=pltpu.CompilerParams(vmem_limit_bytes=61 * 2**20),
        cost_estimate=pl.CostEstimate(
            flops=2 * (keys * 4 + rows * 2) * width * HS, bytes_accessed=6 * 2**20, transcendentals=0
        ),
    )(seq, *operands)


def prepare_kernel(*refs):
    sources, (kv_ref, vt_ref, norm_ref) = refs[:-3], refs[-3:]
    each = KEY_BLOCKS // len(sources)
    most = None
    for t in range(KEY_BLOCKS):
        at = t % each
        tile = sources[t // each][at * BLOCK : (at + 1) * BLOCK, :]
        kv_ref[t * BLOCK : (t + 1) * BLOCK, :] = tile
        turned = tile.T
        vt_ref[:HS, t * BLOCK : (t + 1) * BLOCK] = turned[HS:, :]
        k = turned[:HS, :].astype(jnp.float32)
        squares = jnp.sum(k * k, axis=0, keepdims=True)
        most = squares if most is None else jnp.maximum(most, squares)
    vt_ref[HS:, :] = jnp.ones((ACC_ROWS - HS, KEY_BLOCKS * BLOCK), jnp.bfloat16)
    norm_ref[0] = jnp.max(most)


def prepare(*sources):
    keys = sum(source.shape[0] for source in sources)
    return pl.pallas_call(
        prepare_kernel,
        in_specs=[VMEM] * len(sources),
        out_specs=[VMEM, VMEM, SMEM],
        out_shape=[
            pltpu.HBM((keys, 2 * HS), jnp.bfloat16),
            pltpu.HBM((ACC_ROWS, keys), jnp.bfloat16),
            jax.ShapeDtypeStruct((1,), jnp.float32),
        ],
        compiler_params=pltpu.CompilerParams(vmem_limit_bytes=24 * 2**20),
    )(*sources)


def attention_kernel(steps, far, seq_ref, code_ref, norm_ref, pos_ref, kv_ref, vt_ref, *rest):
    chips = len(steps)
    q_refs, rest = rest[:chips], rest[chips:]
    before_refs, rest = (rest[:chips], rest[chips:]) if far else (None, rest)
    o_refs, (q_all, p_a, p_b, s_all, acc) = rest[:chips], rest[chips:]
    table = FAR if far else 0
    blocks = 4 * chips
    me = seq_ref[0]
    keys_of = jnp.bitwise_xor(me, 2) if far else me
    own_base = keys_of * (KEY_BLOCKS // 2 * BLOCK)
    partner_base = jnp.bitwise_xor(keys_of, 1) * (KEY_BLOCKS // 2 * BLOCK)
    sources = [came_from(me, step) for step in steps]
    iota = lax.broadcasted_iota(jnp.int32, (BLOCK, ROWS), 0)
    in_first = lax.broadcasted_iota(jnp.int32, (1, ROWS), 1) < BLOCK
    iota_half = iota.astype(jnp.float32).astype(jnp.bfloat16)

    most = None
    for i, ref in enumerate(q_refs):
        for j in range(ref.shape[0]):
            q = ref[j]
            q_all[i * ref.shape[0] + j] = q
            q = q.astype(jnp.float32)
            squares = jnp.sum(q * q, axis=0, keepdims=True)
            most = squares if most is None else jnp.maximum(most, squares)
    safe = jnp.max(most) * norm_ref[0] <= SAFE_SCORE * SAFE_SCORE

    def clamp(r):
        return jnp.minimum(r, blocks - 1)

    def whole_block(r):
        shard = sources[-1]
        for i in range(chips - 1):
            shard = jnp.where(lax.div(r, 4) == i, sources[i], shard)
        return jnp.bitwise_xor(shard, jnp.bitwise_and(lax.div(r, 2), 1)) * 2 + lax.rem(r, 2)

    def offset(i):
        return pl.multiple_of(i * BLOCK, BLOCK)

    def row_offset(i):
        return pl.multiple_of(i * ROWS, ROWS)

    def query(r):
        q = q_all[lax.div(r, 2), :, pl.ds(row_offset(lax.rem(r, 2)), ROWS)]
        return jnp.concatenate([q, jnp.zeros_like(q)], 0)

    def key_blocks(row, c):
        return [jnp.bitwise_and(code_ref[row, table + c * TILES + t], KEY_BLOCKS - 1) for t in range(TILES)]

    def products(row, r, c):
        keys = jnp.concatenate([kv_ref[pl.ds(offset(k), BLOCK), :] for k in key_blocks(row, c)], 0)
        return jnp.dot(keys, query(r), preferred_element_type=jnp.float32)

    def values(row, c):
        return jnp.concatenate([vt_ref[:, pl.ds(offset(k), BLOCK)] for k in key_blocks(row, c)], 1)

    def last_key(row, c, t, pos, real):
        code = code_ref[row, table + c * TILES + t]
        k = jnp.bitwise_and(code, KEY_BLOCKS - 1)
        half = KEY_BLOCKS // 2
        base = jnp.where(k < half, own_base, partner_base - half * BLOCK) + k * BLOCK
        real = jnp.logical_and(real, code >= 4 * KEY_BLOCKS)
        reach = [jnp.where(jnp.bitwise_and(code, n * KEY_BLOCKS) > 0, 1 << 30, BLOCK) for n in (1, 2)]
        reach = jnp.where(in_first, *[jnp.where(real, n, -(1 << 30)) for n in reach])
        ahead = pos - base
        return jnp.where(ahead < reach, jnp.minimum(ahead, BLOCK - 1), -1)

    def put(i, rr, a, top):
        at = (lax.div(rr, 2), slice(None), pl.ds(row_offset(lax.rem(rr, 2)), ROWS))
        if far:
            before = before_refs[i][at].astype(jnp.float32)
            top_before, top_now = before[HS + 1 : HS + 2], top
            top = jnp.maximum(top_before, top_now)
            shrink, shrink_before = jnp.exp(top_now - top), jnp.exp(top_before - top)
            total = a[HS : HS + 1] * shrink + (before[HS : HS + 1] + before[HS + 2 : HS + 3]) * shrink_before
            a = a * shrink + before * shrink_before
        else:
            total = a[HS : HS + 1]
        low = total - total.astype(jnp.bfloat16).astype(jnp.float32)
        out = jnp.concatenate([a[:HS], total, top, low, a[HS + 3 :]], 0)
        o_refs[i][at] = out.astype(jnp.bfloat16)

    def advance(r, c):
        last = c + 1 >= code_ref[whole_block(clamp(r)), table + KEY_BLOCKS]
        return jnp.where(last, jnp.minimum(r + 1, blocks), r), jnp.where(last, 0, c + 1)

    def step_slots(r, c):
        slots = []
        for _ in range(SLOTS):
            slots.append((r, c))
            r, c = advance(r, c)
        return slots, r, c

    @pl.when(safe)
    def _():
        acc[...] = jnp.zeros_like(acc)

        def weigh(p_ref, slots):
            for g, (r, c) in enumerate(slots):
                rr = clamp(r)
                row = whole_block(rr)
                s = products(row, rr, c)
                pos = pos_ref[pl.ds(row, 1), :]
                for t in range(TILES):
                    p = jnp.exp2(s[t * BLOCK : (t + 1) * BLOCK] * LOG2E).astype(jnp.bfloat16)
                    last = last_key(row, c, t, pos, r < blocks).astype(jnp.float32).astype(jnp.bfloat16)
                    at = (g * TILES + t) * BLOCK
                    p_ref[at : at + BLOCK, :] = jnp.where(iota_half <= last, p, jnp.zeros_like(p))

        def add(p_ref, slots):
            for g, (r, c) in enumerate(slots):
                v = values(whole_block(clamp(r)), c)
                at = g * TILES * BLOCK
                acc[r] += jnp.dot(v, p_ref[at : at + TILES * BLOCK, :], preferred_element_type=jnp.float32)

        slots_0, r0, c0 = step_slots(jnp.int32(0), jnp.int32(0))
        weigh(p_a, slots_0)

        def two_steps(_, state):
            r, c, r1, c1 = state
            slots, _, _ = step_slots(r, c)
            slots_1, r2, c2 = step_slots(r1, c1)
            weigh(p_b, slots_1)
            add(p_a, slots)
            slots_2, r3, c3 = step_slots(r2, c2)
            weigh(p_a, slots_2)
            add(p_b, slots_1)
            return r2, c2, r3, c3

        items = lax.fori_loop(0, blocks, lambda r, n: n + code_ref[whole_block(r), table + KEY_BLOCKS], jnp.int32(0))
        turns = lax.div(items + (2 * SLOTS - 1), 2 * SLOTS)
        lax.fori_loop(0, turns, two_steps, (jnp.int32(0), jnp.int32(0), r0, c0))

        for i in range(chips):
            def finish(rr, _, i=i):
                a = acc[i * 4 + rr]
                put(i, rr, a, jnp.where(a[HS : HS + 1] > 0, 0.0, lowest_max))
                return 0

            lax.fori_loop(0, 4, finish, 0)

    @pl.when(jnp.logical_not(safe))
    def _():
        for i in range(chips):
            def one_block(rr, _, i=i):
                r = i * 4 + rr
                row = whole_block(r)
                pos = pos_ref[pl.ds(row, 1), :]
                acc[0] = jnp.zeros((ACC_ROWS, ROWS), jnp.float32)

                def one_slot(c, top):
                    s = products(row, r, c)
                    best = top
                    for t in range(TILES):
                        tile = s[t * BLOCK : (t + 1) * BLOCK]
                        tile = jnp.where(iota <= last_key(row, c, t, pos, True), tile, masked_score)
                        s_all[t * BLOCK : (t + 1) * BLOCK, :] = tile
                        best = jnp.maximum(best, jnp.max(tile, 0, keepdims=True))
                    best = best.astype(jnp.bfloat16).astype(jnp.float32)
                    p = jnp.exp2((s_all[...] - best) * LOG2E).astype(jnp.bfloat16)
                    shrink = jnp.exp2((top - best) * LOG2E)
                    acc[0] = acc[0] * shrink + jnp.dot(values(row, c), p, preferred_element_type=jnp.float32)
                    return best

                start = jnp.full((1, ROWS), lowest_max, jnp.bfloat16).astype(jnp.float32)
                top = lax.fori_loop(0, code_ref[row, table + KEY_BLOCKS], one_slot, start)
                put(i, rr, acc[0], top)
                return 0

            lax.fori_loop(0, 4, one_block, 0)


def attend(steps, seq, codes, spots, held, queries, before=()):
    kv, vt, norm = held
    kv, vt, codes = in_hbm(kv, vt, codes)
    chips = len(steps)
    out = jax.ShapeDtypeStruct((2, ACC_ROWS, queries[0].shape[2]), jnp.bfloat16)
    return pl.pallas_call(
        functools.partial(attention_kernel, steps, bool(before)),
        in_specs=[SMEM] * 3 + [VMEM] * (3 + len(queries) + len(before)),
        out_specs=[VMEM] * chips,
        out_shape=[out] * chips,
        scratch_shapes=[
            pltpu.VMEM((2 * chips, HS, queries[0].shape[2]), jnp.bfloat16),
            pltpu.VMEM((SLOTS * TILES * BLOCK, ROWS), jnp.bfloat16),
            pltpu.VMEM((SLOTS * TILES * BLOCK, ROWS), jnp.bfloat16),
            pltpu.VMEM((TILES * BLOCK, ROWS), jnp.float32),
            pltpu.VMEM((4 * chips + 1, ACC_ROWS, ROWS), jnp.float32),
        ],
        compiler_params=pltpu.CompilerParams(vmem_limit_bytes=32 * 2**20),
        cost_estimate=pl.CostEstimate(
            flops=chips * 6 * 10**9, bytes_accessed=4 * 2**20, transcendentals=chips * 2**20
        ),
    )(seq, codes, norm, spots, kv, vt, *queries, *before)


def combine_kernel(core_ref, *refs):
    parts, out_ref = refs[:-1], refs[-1]
    groups = out_ref.shape[0] // 2
    half = out_ref.shape[1]
    for j in range(2):
        tops = [p[j, HS + 1 : HS + 2, :].astype(jnp.float32) for p in parts]
        top = functools.reduce(jnp.maximum, tops)
        scales = [jnp.exp(t - top) for t in tops]
        total = sum(
            (p[j, HS : HS + 1, :].astype(jnp.float32) + p[j, HS + 2 : HS + 3, :].astype(jnp.float32)) * scale
            for p, scale in zip(parts, scales)
        )
        summed = sum(p[j, :HS, :].astype(jnp.float32) * scale for p, scale in zip(parts, scales))
        rows = (summed / total).T.astype(jnp.bfloat16)
        first = jnp.bitwise_xor(core_ref[0], j) * groups
        for g in range(groups):
            upper = rows[2 * g * half : (2 * g + 1) * half]
            lower = rows[(2 * g + 1) * half : (2 * g + 2) * half]
            out_ref[first + g] = jnp.concatenate([upper, lower], 1)


def combine(core, parts):
    half = parts[0].shape[2] // 16
    return pl.pallas_call(
        combine_kernel,
        in_specs=[SMEM] + [VMEM] * len(parts),
        out_specs=VMEM,
        out_shape=jax.ShapeDtypeStruct((16, half, 2 * HS), jnp.bfloat16),
        compiler_params=pltpu.CompilerParams(vmem_limit_bytes=32 * 2**20),
    )(core, *parts)


def finish_kernel(grp_ref, pieces_ref, *refs):
    w_refs, out_ref = refs[:-1], refs[-1]
    groups = pieces_ref.shape[0] // 2
    me = grp_ref[0]
    result = None
    for k, w_ref in enumerate(w_refs):
        near = jnp.bitwise_or(jnp.bitwise_and(me, 4), jnp.bitwise_and(me - k, 3))
        order = [c * groups + g for g in (near, jnp.bitwise_xor(near, 4)) for c in range(2)]
        blocks = [pieces_ref[i] for i in order]
        upper = jnp.concatenate([p[:, :HS] for p in blocks], 1)
        lower = jnp.concatenate([p[:, HS:] for p in blocks], 1)
        attention = jnp.concatenate([upper, lower], 0)
        term = jnp.dot(attention, w_ref[...], preferred_element_type=jnp.float32)
        result = term if result is None else result + term
    out_ref[...] = result.astype(jnp.bfloat16)


def finish(grp, pieces, w_turns):
    return pl.pallas_call(
        finish_kernel,
        in_specs=[SMEM] + [VMEM] * (1 + len(w_turns)),
        out_specs=VMEM,
        out_shape=jax.ShapeDtypeStruct((2 * pieces.shape[1], w_turns[0].shape[1]), jnp.bfloat16),
        compiler_params=pltpu.CompilerParams(vmem_limit_bytes=24 * 2**20),
    )(grp, pieces, *w_turns)


def along_x(by):
    return [(s, (s + 4 * by) % 16) for s in range(16)]


def came_from(s, by):
    return jnp.bitwise_and(s - 4 * by, 15)


NEAR_CALLS = ((0,), (1, 3, 2))
FAR_CALLS = ((2, 1, 3), (0,))
CORE_SWAP = [(s, s ^ 1) for s in range(16)]
Y_SWAP = [(s, s ^ 2) for s in range(16)]


def body(inputs, latents, w_query, w_key, w_value, w_out, positions, block_mask):
    seq = lax.axis_index("seq")[None]
    grp = lax.axis_index("grp")[None]
    core = jnp.bitwise_and(seq, 1)

    mine, theirs, kv_own, kv_other, codes = front(
        seq, latents, inputs, w_query, w_key, w_value, positions, block_mask
    )
    q_chip = jnp.stack([mine, lax.ppermute(theirs, "seq", CORE_SWAP)])
    queries = {by: q_chip if by == 0 else lax.ppermute(q_chip, "seq", along_x(by)) for by in (0, 1, 3, 2)}
    kv_partner = lax.ppermute(kv_other, "seq", CORE_SWAP)
    near = prepare(*in_hbm(kv_own), kv_partner)
    kv_far = [lax.ppermute(kv, "seq", Y_SWAP) for kv in (kv_own, kv_partner)]

    w_other = lax.ppermute(w_out, "grp", [(g, g ^ 4) for g in range(8)])
    spots = positions.reshape(-1, ROWS)
    near_parts = dict(zip(NEAR_CALLS[0], attend(NEAR_CALLS[0], seq, codes, spots, near, [q_chip])))
    w_other, near_parts[0] = lax.optimization_barrier((w_other, near_parts[0]))
    w_pair = jnp.concatenate([w_out, w_other], 0)
    w_turns = [w_pair] + [
        lax.ppermute(w_pair, "grp", [(g, (g & 4) | ((g + k) & 3)) for g in range(8)]) for k in (1, 2, 3)
    ]

    parts = {}
    last = 0
    for call in NEAR_CALLS[1:]:
        queries[call[0]], near_parts[last], kv_far[0] = lax.optimization_barrier(
            (queries[call[0]], near_parts[last], kv_far[0])
        )
        near_parts.update(zip(call, attend(call, seq, codes, spots, near, [queries[by] for by in call])))
        last = call[-1]
    kv_far, near_parts[last] = lax.optimization_barrier((kv_far, near_parts[last]))
    far = prepare(*kv_far)
    last = None
    for call in FAR_CALLS:
        if last is not None:
            queries[call[0]], parts[last] = lax.optimization_barrier((queries[call[0]], parts[last]))
        done = attend(
            call, seq, codes, spots, far, [queries[by] for by in call], [near_parts[by] for by in call]
        )
        parts.update(zip(call, done))
        last = call[-1]

    parts = [part if by == 0 else lax.ppermute(part, "seq", along_x(-by)) for by, part in parts.items()]
    parts, w_turns = lax.optimization_barrier((parts, w_turns))
    pieces = combine(core, parts)
    owners = [[(4 * x + 2 * y + c) * 8 + g for c in range(2) for g in range(8)] for x in range(4) for y in range(2)]
    pieces = lax.all_to_all(pieces, ("seq", "grp"), 0, 0, axis_index_groups=owners)
    return finish(grp, pieces, w_turns)


def solution(mesh):
    return jax.shard_map(
        body,
        mesh=mesh,
        in_specs=(
            P("seq", None),
            P("seq", None),
            P(None, "grp"),
            P(None, "grp"),
            P(None, "grp"),
            P("grp", None),
            P(),
            P(),
        ),
        out_specs=P(("seq", "grp"), None),
        check_vma=False,
    )
```

```python
import functools

import jax
import jax.numpy as jnp
from jax import lax
from jax.experimental import pallas as pl
from jax.experimental.pallas import tpu as pltpu
from jax.sharding import PartitionSpec as P

HS = 64
BLOCK = 128
TILES = 4
SLOTS = 2
ROWS = 2 * BLOCK
FAR = 64
KEY_BLOCKS = 32
ACC_ROWS = 72
LOG2E = 1.4426950408889634
SAFE_SCORE = 60.0
masked_score = -1e30
lowest_max = -1e29
SMEM = pl.BlockSpec(memory_space=pltpu.SMEM)
VMEM = pl.BlockSpec(memory_space=pltpu.VMEM)


def in_hbm(*arrays):
    return [pltpu.with_memory_space_constraint(a, pltpu.HBM) for a in arrays]


def list_work(me, pos_ref, mask_ref, code_ref):
    half = KEY_BLOCKS // 2
    both = 2 * KEY_BLOCKS
    blocks = pos_ref.shape[0]

    def held(t):
        source = jnp.bitwise_xor(me, lax.shift_right_logical(t, 4))
        return source * half + jnp.bitwise_and(t, half - 1)

    spots = pos_ref[...].T
    own_block = lax.shift_right_logical(spots, 7)
    furthest = jnp.max(own_block, axis=0, keepdims=True)
    t_rows = lax.broadcasted_iota(jnp.int32, (both, blocks), 0)
    own = jnp.zeros((both, blocks), jnp.int32)
    for t in range(both):
        found = jnp.max((own_block == held(jnp.int32(t))).astype(jnp.int32), axis=0, keepdims=True)
        own = jnp.where(t_rows == t, found, own)

    def exact(condition):
        return condition.astype(jnp.float32).astype(jnp.bfloat16)

    columns = mask_ref.shape[1]
    pick = exact(
        lax.broadcasted_iota(jnp.int32, (both, columns), 1)
        == held(lax.broadcasted_iota(jnp.int32, (both, columns), 0))
    )
    listed = lax.dot_general(
        pick, exact(mask_ref[...] == 1), (((1,), (1,)), ((), ())), preferred_element_type=jnp.float32
    )
    active = exact((own > 0) | ((listed > 0.5) & (held(t_rows) <= furthest)))
    listed = exact(listed > 0.5)

    row = lax.broadcasted_iota(jnp.int32, (blocks, BLOCK), 0)
    col = lax.broadcasted_iota(jnp.int32, (blocks, BLOCK), 1)
    first, second = exact(row == 2 * col), exact(row == 2 * col + 1)
    active = jnp.dot(active, first + second, preferred_element_type=jnp.float32) > 0.5
    listed = [jnp.dot(listed, pairs, preferred_element_type=jnp.float32).astype(jnp.int32) for pairs in (first, second)]
    row = lax.broadcasted_iota(jnp.int32, (both, both), 0)
    col = lax.broadcasted_iota(jnp.int32, (both, both), 1)
    earlier = exact((col < row) & (lax.shift_right_logical(row, 5) == lax.shift_right_logical(col, 5)))
    place = jnp.dot(earlier, exact(active), preferred_element_type=jnp.float32).astype(jnp.int32)
    t_rows = lax.broadcasted_iota(jnp.int32, (both, BLOCK), 0)
    value = jnp.bitwise_and(t_rows, KEY_BLOCKS - 1) + KEY_BLOCKS * (listed[0] + 2 * listed[1] + 4)
    packed = jnp.where(active, place * 512 + value, -1)
    ones = active.astype(jnp.int32)
    slot_rows = lax.broadcasted_iota(jnp.int32, (KEY_BLOCKS, BLOCK), 0)
    tables = []
    for n in range(2):
        codes = jnp.zeros((KEY_BLOCKS, BLOCK), jnp.int32)
        for t in range(n * KEY_BLOCKS, (n + 1) * KEY_BLOCKS):
            one = packed[t : t + 1, :]
            codes = jnp.where(lax.shift_right_arithmetic(one, 9) == slot_rows, jnp.bitwise_and(one, 511), codes)
        count = jnp.sum(ones[n * KEY_BLOCKS : (n + 1) * KEY_BLOCKS], axis=0, keepdims=True)
        slots = jnp.maximum(lax.shift_right_logical(count + (TILES - 1), 2), 1)
        tables += [codes, jnp.broadcast_to(slots, (FAR - KEY_BLOCKS, BLOCK))]
    code_ref[...] = jnp.concatenate(tables, 0).T[: code_ref.shape[0]]


def front_kernel(seq_ref, lat_hbm, x_hbm, wq_hbm, wk_hbm, wv_hbm, pos_hbm, mask_hbm, *rest):
    mine_hbm, theirs_hbm, own_hbm, other_hbm, code_hbm = rest[:5]
    lat, x, wq, wk, wv, pos, mask, mine_ref, theirs_ref, own_ref, other_ref, code_ref = rest[5:17]
    w_all, sems, x_sems, out_sems = rest[17:]
    sent = []

    def send(source, target):
        sent.append(pltpu.make_async_copy(source, target, out_sems.at[len(sent)]))
        sent[-1].start()

    small = [
        pltpu.make_async_copy(source, target, sems.at[i])
        for i, (source, target) in enumerate(
            [(pos_hbm, pos), (mask_hbm, mask), (wq_hbm, wq), (lat_hbm, lat), (wk_hbm, wk), (wv_hbm, wv)]
        )
    ]
    rows = x.shape[0] // x_sems.shape[0]
    parts = [pl.ds(i * rows, rows) for i in range(x_sems.shape[0])]
    large = [pltpu.make_async_copy(x_hbm.at[p], x.at[p], x_sems.at[i]) for i, p in enumerate(parts)]
    for copy in small + large:
        copy.start()
    got_pos, got_mask, got_wq, got_lat, got_wk, got_wv = small
    first = jnp.bitwise_and(seq_ref[0], 1) == 0

    got_pos.wait()
    got_mask.wait()
    list_work(seq_ref[0], pos, mask, code_ref)
    send(code_ref, code_hbm)

    got_wq.wait()
    got_lat.wait()
    q = jnp.dot(lat[...], wq[...], preferred_element_type=jnp.float32).T
    q = q.astype(jnp.bfloat16) * jnp.bfloat16(HS ** -0.5)
    mine_ref[...] = jnp.where(first, q[:HS], q[HS:])
    theirs_ref[...] = jnp.where(first, q[HS:], q[:HS])
    send(mine_ref, mine_hbm)
    send(theirs_ref, theirs_hbm)

    got_wk.wait()
    got_wv.wait()
    k, v = wk[...], wv[...]
    head_0 = jnp.concatenate([k[:, :HS], v[:, :HS]], 1)
    head_1 = jnp.concatenate([k[:, HS:], v[:, HS:]], 1)
    w_all[:, : 2 * HS] = jnp.where(first, head_0, head_1)
    w_all[:, 2 * HS :] = jnp.where(first, head_1, head_0)
    for copy, part in zip(large, parts):
        copy.wait()
        both = jnp.dot(x[part, :], w_all[...], preferred_element_type=jnp.float32).astype(jnp.bfloat16)
        own_ref[part, :] = both[:, : 2 * HS]
        other_ref[part, :] = both[:, 2 * HS :]
        send(own_ref.at[part], own_hbm.at[part])
        send(other_ref.at[part], other_hbm.at[part])
    for copy in sent:
        copy.wait()


def front(seq, latents, inputs, w_query, w_key, w_value, positions, block_mask):
    rows, width = latents.shape
    keys = inputs.shape[0]
    spots = positions.reshape(-1, BLOCK)
    operands = (latents, inputs, w_query, w_key, w_value, spots, block_mask)
    q = jax.ShapeDtypeStruct((HS, rows), jnp.bfloat16)
    kv = jax.ShapeDtypeStruct((keys, 2 * HS), jnp.bfloat16)
    results = [q, q, kv, kv, jax.ShapeDtypeStruct((spots.shape[0] // 2, BLOCK), jnp.int32)]
    return pl.pallas_call(
        front_kernel,
        in_specs=[SMEM] + [pl.BlockSpec(memory_space=pl.ANY)] * len(operands),
        out_specs=[pl.BlockSpec(memory_space=pl.ANY)] * 5,
        out_shape=results,
        scratch_shapes=[pltpu.VMEM(a.shape, a.dtype) for a in (*operands, *results)]
        + [
            pltpu.VMEM((width, 4 * HS), jnp.bfloat16),
            pltpu.SemaphoreType.DMA((6,)),
            pltpu.SemaphoreType.DMA((4,)),
            pltpu.SemaphoreType.DMA((11,)),
        ],
        compiler_params=pltpu.CompilerParams(vmem_limit_bytes=61 * 2**20),
        cost_estimate=pl.CostEstimate(
            flops=2 * (keys * 4 + rows * 2) * width * HS, bytes_accessed=6 * 2**20, transcendentals=0
        ),
    )(seq, *operands)


def prepare_kernel(*refs):
    sources, (kv_ref, vt_ref, norm_ref) = refs[:-3], refs[-3:]
    each = KEY_BLOCKS // len(sources)
    most = None
    for t in range(KEY_BLOCKS):
        at = t % each
        tile = sources[t // each][at * BLOCK : (at + 1) * BLOCK, :]
        kv_ref[t * BLOCK : (t + 1) * BLOCK, :] = tile
        turned = tile.T
        vt_ref[:HS, t * BLOCK : (t + 1) * BLOCK] = turned[HS:, :]
        k = turned[:HS, :].astype(jnp.float32)
        squares = jnp.sum(k * k, axis=0, keepdims=True)
        most = squares if most is None else jnp.maximum(most, squares)
    vt_ref[HS:, :] = jnp.ones((ACC_ROWS - HS, KEY_BLOCKS * BLOCK), jnp.bfloat16)
    norm_ref[0] = jnp.max(most)


def prepare(*sources):
    keys = sum(source.shape[0] for source in sources)
    return pl.pallas_call(
        prepare_kernel,
        in_specs=[VMEM] * len(sources),
        out_specs=[VMEM, VMEM, SMEM],
        out_shape=[
            jax.ShapeDtypeStruct((keys, 2 * HS), jnp.bfloat16),
            jax.ShapeDtypeStruct((ACC_ROWS, keys), jnp.bfloat16),
            jax.ShapeDtypeStruct((1,), jnp.float32),
        ],
        compiler_params=pltpu.CompilerParams(vmem_limit_bytes=24 * 2**20),
    )(*sources)


def attention_kernel(steps, far, seq_ref, code_ref, norm_ref, pos_ref, kv_ref, vt_ref, *rest):
    chips = len(steps)
    q_refs, rest = rest[:chips], rest[chips:]
    before_refs, rest = (rest[:chips], rest[chips:]) if far else (None, rest)
    o_refs, (q_all, p_a, p_b, s_all, acc) = rest[:chips], rest[chips:]
    table = FAR if far else 0
    blocks = 4 * chips
    me = seq_ref[0]
    keys_of = jnp.bitwise_xor(me, 2) if far else me
    own_base = keys_of * (KEY_BLOCKS // 2 * BLOCK)
    partner_base = jnp.bitwise_xor(keys_of, 1) * (KEY_BLOCKS // 2 * BLOCK)
    sources = [came_from(me, step) for step in steps]
    iota = lax.broadcasted_iota(jnp.int32, (BLOCK, ROWS), 0)
    in_first = lax.broadcasted_iota(jnp.int32, (1, ROWS), 1) < BLOCK
    iota_half = iota.astype(jnp.float32).astype(jnp.bfloat16)

    most = None
    for i, ref in enumerate(q_refs):
        for j in range(ref.shape[0]):
            q = ref[j]
            q_all[i * ref.shape[0] + j] = q
            q = q.astype(jnp.float32)
            squares = jnp.sum(q * q, axis=0, keepdims=True)
            most = squares if most is None else jnp.maximum(most, squares)
    safe = jnp.max(most) * norm_ref[0] <= SAFE_SCORE * SAFE_SCORE

    def clamp(r):
        return jnp.minimum(r, blocks - 1)

    def whole_block(r):
        shard = sources[-1]
        for i in range(chips - 1):
            shard = jnp.where(lax.div(r, 4) == i, sources[i], shard)
        return jnp.bitwise_xor(shard, jnp.bitwise_and(lax.div(r, 2), 1)) * 2 + lax.rem(r, 2)

    def offset(i):
        return pl.multiple_of(i * BLOCK, BLOCK)

    def row_offset(i):
        return pl.multiple_of(i * ROWS, ROWS)

    def query(r):
        q = q_all[lax.div(r, 2), :, pl.ds(row_offset(lax.rem(r, 2)), ROWS)]
        return jnp.concatenate([q, jnp.zeros_like(q)], 0)

    def key_blocks(row, c):
        return [jnp.bitwise_and(code_ref[row, table + c * TILES + t], KEY_BLOCKS - 1) for t in range(TILES)]

    def products(row, r, c):
        keys = jnp.concatenate([kv_ref[pl.ds(offset(k), BLOCK), :] for k in key_blocks(row, c)], 0)
        return jnp.dot(keys, query(r), preferred_element_type=jnp.float32)

    def values(row, c):
        return jnp.concatenate([vt_ref[:, pl.ds(offset(k), BLOCK)] for k in key_blocks(row, c)], 1)

    def last_key(row, c, t, pos, real):
        code = code_ref[row, table + c * TILES + t]
        k = jnp.bitwise_and(code, KEY_BLOCKS - 1)
        half = KEY_BLOCKS // 2
        base = jnp.where(k < half, own_base, partner_base - half * BLOCK) + k * BLOCK
        real = jnp.logical_and(real, code >= 4 * KEY_BLOCKS)
        reach = [jnp.where(jnp.bitwise_and(code, n * KEY_BLOCKS) > 0, 1 << 30, BLOCK) for n in (1, 2)]
        reach = jnp.where(in_first, *[jnp.where(real, n, -(1 << 30)) for n in reach])
        ahead = pos - base
        return jnp.where(ahead < reach, jnp.minimum(ahead, BLOCK - 1), -1)

    def put(i, rr, a, top):
        at = (lax.div(rr, 2), slice(None), pl.ds(row_offset(lax.rem(rr, 2)), ROWS))
        if far:
            before = before_refs[i][at].astype(jnp.float32)
            top_before, top_now = before[HS + 1 : HS + 2], top
            top = jnp.maximum(top_before, top_now)
            shrink, shrink_before = jnp.exp(top_now - top), jnp.exp(top_before - top)
            total = a[HS : HS + 1] * shrink + (before[HS : HS + 1] + before[HS + 2 : HS + 3]) * shrink_before
            a = a * shrink + before * shrink_before
        else:
            total = a[HS : HS + 1]
        low = total - total.astype(jnp.bfloat16).astype(jnp.float32)
        out = jnp.concatenate([a[:HS], total, top, low, a[HS + 3 :]], 0)
        o_refs[i][at] = out.astype(jnp.bfloat16)

    def advance(r, c):
        last = c + 1 >= code_ref[whole_block(clamp(r)), table + KEY_BLOCKS]
        return jnp.where(last, jnp.minimum(r + 1, blocks), r), jnp.where(last, 0, c + 1)

    def step_slots(r, c):
        slots = []
        for _ in range(SLOTS):
            slots.append((r, c))
            r, c = advance(r, c)
        return slots, r, c

    @pl.when(safe)
    def _():
        acc[...] = jnp.zeros_like(acc)

        def weigh(p_ref, slots):
            for g, (r, c) in enumerate(slots):
                rr = clamp(r)
                row = whole_block(rr)
                s = products(row, rr, c)
                pos = pos_ref[pl.ds(row, 1), :]
                for t in range(TILES):
                    p = jnp.exp2(s[t * BLOCK : (t + 1) * BLOCK] * LOG2E).astype(jnp.bfloat16)
                    last = last_key(row, c, t, pos, r < blocks).astype(jnp.float32).astype(jnp.bfloat16)
                    at = (g * TILES + t) * BLOCK
                    p_ref[at : at + BLOCK, :] = jnp.where(iota_half <= last, p, jnp.zeros_like(p))

        def add(p_ref, slots):
            for g, (r, c) in enumerate(slots):
                v = values(whole_block(clamp(r)), c)
                at = g * TILES * BLOCK
                acc[r] += jnp.dot(v, p_ref[at : at + TILES * BLOCK, :], preferred_element_type=jnp.float32)

        slots_0, r0, c0 = step_slots(jnp.int32(0), jnp.int32(0))
        weigh(p_a, slots_0)

        def two_steps(_, state):
            r, c, r1, c1 = state
            slots, _, _ = step_slots(r, c)
            slots_1, r2, c2 = step_slots(r1, c1)
            weigh(p_b, slots_1)
            add(p_a, slots)
            slots_2, r3, c3 = step_slots(r2, c2)
            weigh(p_a, slots_2)
            add(p_b, slots_1)
            return r2, c2, r3, c3

        items = lax.fori_loop(0, blocks, lambda r, n: n + code_ref[whole_block(r), table + KEY_BLOCKS], jnp.int32(0))
        turns = lax.div(items + (2 * SLOTS - 1), 2 * SLOTS)
        lax.fori_loop(0, turns, two_steps, (jnp.int32(0), jnp.int32(0), r0, c0))

        for i in range(chips):
            def finish(rr, _, i=i):
                a = acc[i * 4 + rr]
                put(i, rr, a, jnp.where(a[HS : HS + 1] > 0, 0.0, lowest_max))
                return 0

            lax.fori_loop(0, 4, finish, 0)

    @pl.when(jnp.logical_not(safe))
    def _():
        for i in range(chips):
            def one_block(rr, _, i=i):
                r = i * 4 + rr
                row = whole_block(r)
                pos = pos_ref[pl.ds(row, 1), :]
                acc[0] = jnp.zeros((ACC_ROWS, ROWS), jnp.float32)

                def one_slot(c, top):
                    s = products(row, r, c)
                    best = top
                    for t in range(TILES):
                        tile = s[t * BLOCK : (t + 1) * BLOCK]
                        tile = jnp.where(iota <= last_key(row, c, t, pos, True), tile, masked_score)
                        s_all[t * BLOCK : (t + 1) * BLOCK, :] = tile
                        best = jnp.maximum(best, jnp.max(tile, 0, keepdims=True))
                    best = best.astype(jnp.bfloat16).astype(jnp.float32)
                    p = jnp.exp2((s_all[...] - best) * LOG2E).astype(jnp.bfloat16)
                    shrink = jnp.exp2((top - best) * LOG2E)
                    acc[0] = acc[0] * shrink + jnp.dot(values(row, c), p, preferred_element_type=jnp.float32)
                    return best

                start = jnp.full((1, ROWS), lowest_max, jnp.bfloat16).astype(jnp.float32)
                top = lax.fori_loop(0, code_ref[row, table + KEY_BLOCKS], one_slot, start)
                put(i, rr, acc[0], top)
                return 0

            lax.fori_loop(0, 4, one_block, 0)


def attend(steps, seq, codes, spots, held, queries, before=()):
    kv, vt, norm = held
    codes, = in_hbm(codes)
    chips = len(steps)
    out = jax.ShapeDtypeStruct((2, ACC_ROWS, queries[0].shape[2]), jnp.bfloat16)
    return pl.pallas_call(
        functools.partial(attention_kernel, steps, bool(before)),
        in_specs=[SMEM] * 3 + [VMEM] * (3 + len(queries) + len(before)),
        out_specs=[VMEM] * chips,
        out_shape=[out] * chips,
        scratch_shapes=[
            pltpu.VMEM((2 * chips, HS, queries[0].shape[2]), jnp.bfloat16),
            pltpu.VMEM((SLOTS * TILES * BLOCK, ROWS), jnp.bfloat16),
            pltpu.VMEM((SLOTS * TILES * BLOCK, ROWS), jnp.bfloat16),
            pltpu.VMEM((TILES * BLOCK, ROWS), jnp.float32),
            pltpu.VMEM((4 * chips + 1, ACC_ROWS, ROWS), jnp.float32),
        ],
        compiler_params=pltpu.CompilerParams(vmem_limit_bytes=32 * 2**20),
        cost_estimate=pl.CostEstimate(
            flops=chips * 6 * 10**9, bytes_accessed=4 * 2**20, transcendentals=chips * 2**20
        ),
    )(seq, codes, norm, spots, kv, vt, *queries, *before)


def combine_kernel(core_ref, *refs):
    parts, out_ref = refs[:-1], refs[-1]
    groups = out_ref.shape[0] // 2
    half = out_ref.shape[1]
    for j in range(2):
        tops = [p[j, HS + 1 : HS + 2, :].astype(jnp.float32) for p in parts]
        top = functools.reduce(jnp.maximum, tops)
        scales = [jnp.exp(t - top) for t in tops]
        total = sum(
            (p[j, HS : HS + 1, :].astype(jnp.float32) + p[j, HS + 2 : HS + 3, :].astype(jnp.float32)) * scale
            for p, scale in zip(parts, scales)
        )
        summed = sum(p[j, :HS, :].astype(jnp.float32) * scale for p, scale in zip(parts, scales))
        rows = (summed / total).T.astype(jnp.bfloat16)
        first = jnp.bitwise_xor(core_ref[0], j) * groups
        for g in range(groups):
            upper = rows[2 * g * half : (2 * g + 1) * half]
            lower = rows[(2 * g + 1) * half : (2 * g + 2) * half]
            out_ref[first + g] = jnp.concatenate([upper, lower], 1)


def combine(core, parts):
    half = parts[0].shape[2] // 16
    return pl.pallas_call(
        combine_kernel,
        in_specs=[SMEM] + [VMEM] * len(parts),
        out_specs=VMEM,
        out_shape=jax.ShapeDtypeStruct((16, half, 2 * HS), jnp.bfloat16),
        compiler_params=pltpu.CompilerParams(vmem_limit_bytes=32 * 2**20),
    )(core, *parts)


def finish_kernel(grp_ref, pieces_ref, *refs):
    w_refs, out_ref = refs[:-1], refs[-1]
    groups = pieces_ref.shape[0] // 2
    me = grp_ref[0]
    result = None
    for k, w_ref in enumerate(w_refs):
        near = jnp.bitwise_or(jnp.bitwise_and(me, 4), jnp.bitwise_and(me - k, 3))
        order = [c * groups + g for g in (near, jnp.bitwise_xor(near, 4)) for c in range(2)]
        blocks = [pieces_ref[i] for i in order]
        upper = jnp.concatenate([p[:, :HS] for p in blocks], 1)
        lower = jnp.concatenate([p[:, HS:] for p in blocks], 1)
        attention = jnp.concatenate([upper, lower], 0)
        term = jnp.dot(attention, w_ref[...], preferred_element_type=jnp.float32)
        result = term if result is None else result + term
    out_ref[...] = result.astype(jnp.bfloat16)


def finish(grp, pieces, w_turns):
    return pl.pallas_call(
        finish_kernel,
        in_specs=[SMEM] + [VMEM] * (1 + len(w_turns)),
        out_specs=VMEM,
        out_shape=jax.ShapeDtypeStruct((2 * pieces.shape[1], w_turns[0].shape[1]), jnp.bfloat16),
        compiler_params=pltpu.CompilerParams(vmem_limit_bytes=24 * 2**20),
    )(grp, pieces, *w_turns)


def along_x(by):
    return [(s, (s + 4 * by) % 16) for s in range(16)]


def came_from(s, by):
    return jnp.bitwise_and(s - 4 * by, 15)


NEAR_CALLS = ((0,), (1, 3, 2))
FAR_CALLS = ((2, 1, 3), (0,))
CORE_SWAP = [(s, s ^ 1) for s in range(16)]
Y_SWAP = [(s, s ^ 2) for s in range(16)]


def body(inputs, latents, w_query, w_key, w_value, w_out, positions, block_mask):
    seq = lax.axis_index("seq")[None]
    grp = lax.axis_index("grp")[None]
    core = jnp.bitwise_and(seq, 1)

    mine, theirs, kv_own, kv_other, codes = front(
        seq, latents, inputs, w_query, w_key, w_value, positions, block_mask
    )
    q_chip = jnp.stack([mine, lax.ppermute(theirs, "seq", CORE_SWAP)])
    queries = {by: q_chip if by == 0 else lax.ppermute(q_chip, "seq", along_x(by)) for by in (0, 1, 3, 2)}
    kv_partner = lax.ppermute(kv_other, "seq", CORE_SWAP)
    near = prepare(*in_hbm(kv_own), kv_partner)
    kv_far = [lax.ppermute(kv, "seq", Y_SWAP) for kv in (kv_own, kv_partner)]

    w_other = lax.ppermute(w_out, "grp", [(g, g ^ 4) for g in range(8)])
    spots = positions.reshape(-1, ROWS)
    near_parts = dict(zip(NEAR_CALLS[0], attend(NEAR_CALLS[0], seq, codes, spots, near, [q_chip])))
    w_other, near_parts[0] = lax.optimization_barrier((w_other, near_parts[0]))
    w_pair = jnp.concatenate([w_out, w_other], 0)
    w_turns = [w_pair] + [
        lax.ppermute(w_pair, "grp", [(g, (g & 4) | ((g + k) & 3)) for g in range(8)]) for k in (1, 2, 3)
    ]

    parts = {}
    last = 0
    for call in NEAR_CALLS[1:]:
        queries[call[0]], near_parts[last], kv_far[0] = lax.optimization_barrier(
            (queries[call[0]], near_parts[last], kv_far[0])
        )
        near_parts.update(zip(call, attend(call, seq, codes, spots, near, [queries[by] for by in call])))
        last = call[-1]
    kv_far, near_parts[last] = lax.optimization_barrier((kv_far, near_parts[last]))
    far = prepare(*kv_far)
    last = None
    for call in FAR_CALLS:
        if last is not None:
            queries[call[0]], parts[last] = lax.optimization_barrier((queries[call[0]], parts[last]))
        done = attend(
            call, seq, codes, spots, far, [queries[by] for by in call], [near_parts[by] for by in call]
        )
        parts.update(zip(call, done))
        last = call[-1]

    parts = [part if by == 0 else lax.ppermute(part, "seq", along_x(-by)) for by, part in parts.items()]
    parts, w_turns = lax.optimization_barrier((parts, w_turns))
    pieces = combine(core, parts)
    owners = [[(4 * x + 2 * y + c) * 8 + g for c in range(2) for g in range(8)] for x in range(4) for y in range(2)]
    pieces = lax.all_to_all(pieces, ("seq", "grp"), 0, 0, axis_index_groups=owners)
    return finish(grp, pieces, w_turns)


def solution(mesh):
    return jax.shard_map(
        body,
        mesh=mesh,
        in_specs=(
            P("seq", None),
            P("seq", None),
            P(None, "grp"),
            P(None, "grp"),
            P(None, "grp"),
            P("grp", None),
            P(),
            P(),
        ),
        out_specs=P(("seq", "grp"), None),
        check_vma=False,
    )
```

```python
import functools

import jax
import jax.numpy as jnp
from jax import lax
from jax.experimental import pallas as pl
from jax.experimental.pallas import tpu as pltpu
from jax.sharding import PartitionSpec as P

HS = 64
BLOCK = 128
TILES = 4
SLOTS = 2
ROWS = 2 * BLOCK
FAR = 64
KEY_BLOCKS = 32
ACC_ROWS = 72
LOG2E = 1.4426950408889634
SAFE_SCORE = 60.0
masked_score = -1e30
lowest_max = -1e29
SMEM = pl.BlockSpec(memory_space=pltpu.SMEM)
VMEM = pl.BlockSpec(memory_space=pltpu.VMEM)


def in_hbm(*arrays):
    return [pltpu.with_memory_space_constraint(a, pltpu.HBM) for a in arrays]


def list_work(me, pos_ref, mask_ref, code_ref):
    half = KEY_BLOCKS // 2
    both = 2 * KEY_BLOCKS
    blocks = pos_ref.shape[0]

    def held(t):
        source = jnp.bitwise_xor(me, lax.shift_right_logical(t, 4))
        return source * half + jnp.bitwise_and(t, half - 1)

    spots = pos_ref[...].T
    own_block = lax.shift_right_logical(spots, 7)
    furthest = jnp.max(own_block, axis=0, keepdims=True)
    t_rows = lax.broadcasted_iota(jnp.int32, (both, blocks), 0)
    own = jnp.zeros((both, blocks), jnp.int32)
    for t in range(both):
        found = jnp.max((own_block == held(jnp.int32(t))).astype(jnp.int32), axis=0, keepdims=True)
        own = jnp.where(t_rows == t, found, own)

    def exact(condition):
        return condition.astype(jnp.float32).astype(jnp.bfloat16)

    columns = mask_ref.shape[1]
    pick = exact(
        lax.broadcasted_iota(jnp.int32, (both, columns), 1)
        == held(lax.broadcasted_iota(jnp.int32, (both, columns), 0))
    )
    listed = lax.dot_general(
        pick, exact(mask_ref[...] == 1), (((1,), (1,)), ((), ())), preferred_element_type=jnp.float32
    )
    active = exact((own > 0) | ((listed > 0.5) & (held(t_rows) <= furthest)))
    listed = exact(listed > 0.5)

    row = lax.broadcasted_iota(jnp.int32, (blocks, BLOCK), 0)
    col = lax.broadcasted_iota(jnp.int32, (blocks, BLOCK), 1)
    first, second = exact(row == 2 * col), exact(row == 2 * col + 1)
    active = jnp.dot(active, first + second, preferred_element_type=jnp.float32) > 0.5
    listed = [jnp.dot(listed, pairs, preferred_element_type=jnp.float32).astype(jnp.int32) for pairs in (first, second)]
    row = lax.broadcasted_iota(jnp.int32, (both, both), 0)
    col = lax.broadcasted_iota(jnp.int32, (both, both), 1)
    earlier = exact((col < row) & (lax.shift_right_logical(row, 5) == lax.shift_right_logical(col, 5)))
    place = jnp.dot(earlier, exact(active), preferred_element_type=jnp.float32).astype(jnp.int32)
    t_rows = lax.broadcasted_iota(jnp.int32, (both, BLOCK), 0)
    value = jnp.bitwise_and(t_rows, KEY_BLOCKS - 1) + KEY_BLOCKS * (listed[0] + 2 * listed[1] + 4)
    packed = jnp.where(active, place * 512 + value, -1)
    ones = active.astype(jnp.int32)
    slot_rows = lax.broadcasted_iota(jnp.int32, (KEY_BLOCKS, BLOCK), 0)
    tables = []
    for n in range(2):
        codes = jnp.zeros((KEY_BLOCKS, BLOCK), jnp.int32)
        for t in range(n * KEY_BLOCKS, (n + 1) * KEY_BLOCKS):
            one = packed[t : t + 1, :]
            codes = jnp.where(lax.shift_right_arithmetic(one, 9) == slot_rows, jnp.bitwise_and(one, 511), codes)
        count = jnp.sum(ones[n * KEY_BLOCKS : (n + 1) * KEY_BLOCKS], axis=0, keepdims=True)
        slots = jnp.maximum(lax.shift_right_logical(count + (TILES - 1), 2), 1)
        tables += [codes, jnp.broadcast_to(slots, (FAR - KEY_BLOCKS, BLOCK))]
    code_ref[...] = jnp.concatenate(tables, 0).T[: code_ref.shape[0]]


def front_kernel(seq_ref, lat_hbm, x_hbm, wq_hbm, wk_hbm, wv_hbm, pos_hbm, mask_hbm, *rest):
    pair_hbm, theirs_hbm, own_hbm, other_hbm, code_hbm = rest[:5]
    lat, x, wq, wk, wv, pos, mask, pair_ref, theirs_ref, own_ref, other_ref, code_ref = rest[5:17]
    w_all, sems, x_sems, out_sems = rest[17:]
    sent = []

    def send(source, target):
        sent.append(pltpu.make_async_copy(source, target, out_sems.at[len(sent)]))
        sent[-1].start()

    small = [
        pltpu.make_async_copy(source, target, sems.at[i])
        for i, (source, target) in enumerate(
            [(pos_hbm, pos), (mask_hbm, mask), (wq_hbm, wq), (lat_hbm, lat), (wk_hbm, wk), (wv_hbm, wv)]
        )
    ]
    rows = x.shape[0] // x_sems.shape[0]
    parts = [pl.ds(i * rows, rows) for i in range(x_sems.shape[0])]
    large = [pltpu.make_async_copy(x_hbm.at[p], x.at[p], x_sems.at[i]) for i, p in enumerate(parts)]
    for copy in small + large:
        copy.start()
    got_pos, got_mask, got_wq, got_lat, got_wk, got_wv = small
    first = jnp.bitwise_and(seq_ref[0], 1) == 0

    got_pos.wait()
    got_mask.wait()
    list_work(seq_ref[0], pos, mask, code_ref)
    send(code_ref, code_hbm)

    got_wq.wait()
    got_lat.wait()
    q = jnp.dot(lat[...], wq[...], preferred_element_type=jnp.float32).T
    q = q.astype(jnp.bfloat16) * jnp.bfloat16(HS ** -0.5)
    mine = jnp.where(first, q[:HS], q[HS:])
    pair_ref[0] = mine
    pair_ref[1] = mine
    theirs_ref[...] = jnp.where(first, q[HS:], q[:HS])
    send(pair_ref, pair_hbm)
    send(theirs_ref, theirs_hbm)

    got_wk.wait()
    got_wv.wait()
    k, v = wk[...], wv[...]
    head_0 = jnp.concatenate([k[:, :HS], v[:, :HS]], 1)
    head_1 = jnp.concatenate([k[:, HS:], v[:, HS:]], 1)
    w_all[:, : 2 * HS] = jnp.where(first, head_0, head_1)
    w_all[:, 2 * HS :] = jnp.where(first, head_1, head_0)
    for copy, part in zip(large, parts):
        copy.wait()
        both = jnp.dot(x[part, :], w_all[...], preferred_element_type=jnp.float32).astype(jnp.bfloat16)
        own_ref[part, :] = both[:, : 2 * HS]
        other_ref[part, :] = both[:, 2 * HS :]
        send(own_ref.at[part], own_hbm.at[part])
        send(other_ref.at[part], other_hbm.at[part])
    for copy in sent:
        copy.wait()


def front(seq, latents, inputs, w_query, w_key, w_value, positions, block_mask):
    rows, width = latents.shape
    keys = inputs.shape[0]
    spots = positions.reshape(-1, BLOCK)
    operands = (latents, inputs, w_query, w_key, w_value, spots, block_mask)
    q = jax.ShapeDtypeStruct((HS, rows), jnp.bfloat16)
    kv = jax.ShapeDtypeStruct((keys, 2 * HS), jnp.bfloat16)
    results = [jax.ShapeDtypeStruct((2, HS, rows), jnp.bfloat16), q, kv, kv, jax.ShapeDtypeStruct((spots.shape[0] // 2, BLOCK), jnp.int32)]
    return pl.pallas_call(
        front_kernel,
        in_specs=[SMEM] + [pl.BlockSpec(memory_space=pl.ANY)] * len(operands),
        out_specs=[pl.BlockSpec(memory_space=pl.ANY)] * 5,
        out_shape=results,
        scratch_shapes=[pltpu.VMEM(a.shape, a.dtype) for a in (*operands, *results)]
        + [
            pltpu.VMEM((width, 4 * HS), jnp.bfloat16),
            pltpu.SemaphoreType.DMA((6,)),
            pltpu.SemaphoreType.DMA((4,)),
            pltpu.SemaphoreType.DMA((11,)),
        ],
        compiler_params=pltpu.CompilerParams(vmem_limit_bytes=61 * 2**20),
        cost_estimate=pl.CostEstimate(
            flops=2 * (keys * 4 + rows * 2) * width * HS, bytes_accessed=6 * 2**20, transcendentals=0
        ),
    )(seq, *operands)


def prepare_kernel(*refs):
    sources, (kv_ref, vt_ref, norm_ref) = refs[:-3], refs[-3:]
    each = KEY_BLOCKS // len(sources)
    most = None
    for t in range(KEY_BLOCKS):
        at = t % each
        tile = sources[t // each][at * BLOCK : (at + 1) * BLOCK, :]
        kv_ref[t * BLOCK : (t + 1) * BLOCK, :] = tile
        turned = tile.T
        vt_ref[:HS, t * BLOCK : (t + 1) * BLOCK] = turned[HS:, :]
        k = turned[:HS, :].astype(jnp.float32)
        squares = jnp.sum(k * k, axis=0, keepdims=True)
        most = squares if most is None else jnp.maximum(most, squares)
    vt_ref[HS:, :] = jnp.ones((ACC_ROWS - HS, KEY_BLOCKS * BLOCK), jnp.bfloat16)
    norm_ref[0] = jnp.max(most)


def prepare(*sources):
    keys = sum(source.shape[0] for source in sources)
    return pl.pallas_call(
        prepare_kernel,
        in_specs=[VMEM] * len(sources),
        out_specs=[VMEM, VMEM, SMEM],
        out_shape=[
            jax.ShapeDtypeStruct((keys, 2 * HS), jnp.bfloat16),
            jax.ShapeDtypeStruct((ACC_ROWS, keys), jnp.bfloat16),
            jax.ShapeDtypeStruct((1,), jnp.float32),
        ],
        compiler_params=pltpu.CompilerParams(vmem_limit_bytes=24 * 2**20),
    )(*sources)


def attention_kernel(steps, far, seq_ref, code_ref, norm_ref, pos_ref, kv_ref, vt_ref, *rest):
    chips = len(steps)
    q_refs, rest = rest[:chips], rest[chips:]
    before_refs, rest = (rest[:chips], rest[chips:]) if far else (None, rest)
    o_refs, (q_all, p_a, p_b, s_all, acc) = rest[:chips], rest[chips:]
    table = FAR if far else 0
    blocks = 4 * chips
    me = seq_ref[0]
    keys_of = jnp.bitwise_xor(me, 2) if far else me
    own_base = keys_of * (KEY_BLOCKS // 2 * BLOCK)
    partner_base = jnp.bitwise_xor(keys_of, 1) * (KEY_BLOCKS // 2 * BLOCK)
    sources = [came_from(me, step) for step in steps]
    iota = lax.broadcasted_iota(jnp.int32, (BLOCK, ROWS), 0)
    in_first = lax.broadcasted_iota(jnp.int32, (1, ROWS), 1) < BLOCK
    iota_half = iota.astype(jnp.float32).astype(jnp.bfloat16)

    most = None
    for i, ref in enumerate(q_refs):
        for j in range(ref.shape[0]):
            q = ref[j]
            q_all[i * ref.shape[0] + j] = q
            q = q.astype(jnp.float32)
            squares = jnp.sum(q * q, axis=0, keepdims=True)
            most = squares if most is None else jnp.maximum(most, squares)
    safe = jnp.max(most) * norm_ref[0] <= SAFE_SCORE * SAFE_SCORE

    def clamp(r):
        return jnp.minimum(r, blocks - 1)

    def whole_block(r):
        shard = sources[-1]
        for i in range(chips - 1):
            shard = jnp.where(lax.div(r, 4) == i, sources[i], shard)
        return jnp.bitwise_xor(shard, jnp.bitwise_and(lax.div(r, 2), 1)) * 2 + lax.rem(r, 2)

    def offset(i):
        return pl.multiple_of(i * BLOCK, BLOCK)

    def row_offset(i):
        return pl.multiple_of(i * ROWS, ROWS)

    def query(r):
        q = q_all[lax.div(r, 2), :, pl.ds(row_offset(lax.rem(r, 2)), ROWS)]
        return jnp.concatenate([q, jnp.zeros_like(q)], 0)

    def key_blocks(row, c):
        return [jnp.bitwise_and(code_ref[row, table + c * TILES + t], KEY_BLOCKS - 1) for t in range(TILES)]

    def products(row, r, c):
        keys = jnp.concatenate([kv_ref[pl.ds(offset(k), BLOCK), :] for k in key_blocks(row, c)], 0)
        return jnp.dot(keys, query(r), preferred_element_type=jnp.float32)

    def values(row, c):
        return jnp.concatenate([vt_ref[:, pl.ds(offset(k), BLOCK)] for k in key_blocks(row, c)], 1)

    def last_key(row, c, t, pos, real):
        code = code_ref[row, table + c * TILES + t]
        k = jnp.bitwise_and(code, KEY_BLOCKS - 1)
        half = KEY_BLOCKS // 2
        base = jnp.where(k < half, own_base, partner_base - half * BLOCK) + k * BLOCK
        real = jnp.logical_and(real, code >= 4 * KEY_BLOCKS)
        reach = [jnp.where(jnp.bitwise_and(code, n * KEY_BLOCKS) > 0, 1 << 30, BLOCK) for n in (1, 2)]
        reach = jnp.where(in_first, *[jnp.where(real, n, -(1 << 30)) for n in reach])
        ahead = pos - base
        return jnp.where(ahead < reach, jnp.minimum(ahead, BLOCK - 1), -1)

    def put(i, rr, a, top):
        at = (lax.div(rr, 2), slice(None), pl.ds(row_offset(lax.rem(rr, 2)), ROWS))
        if far:
            before = before_refs[i][at].astype(jnp.float32)
            top_before, top_now = before[HS + 1 : HS + 2], top
            top = jnp.maximum(top_before, top_now)
            shrink, shrink_before = jnp.exp(top_now - top), jnp.exp(top_before - top)
            total = a[HS : HS + 1] * shrink + (before[HS : HS + 1] + before[HS + 2 : HS + 3]) * shrink_before
            a = a * shrink + before * shrink_before
        else:
            total = a[HS : HS + 1]
        low = total - total.astype(jnp.bfloat16).astype(jnp.float32)
        out = jnp.concatenate([a[:HS], total, top, low, a[HS + 3 :]], 0)
        o_refs[i][at] = out.astype(jnp.bfloat16)

    def advance(r, c):
        last = c + 1 >= code_ref[whole_block(clamp(r)), table + KEY_BLOCKS]
        return jnp.where(last, jnp.minimum(r + 1, blocks), r), jnp.where(last, 0, c + 1)

    def step_slots(r, c):
        slots = []
        for _ in range(SLOTS):
            slots.append((r, c))
            r, c = advance(r, c)
        return slots, r, c

    @pl.when(safe)
    def _():
        acc[...] = jnp.zeros_like(acc)

        def weigh(p_ref, slots):
            for g, (r, c) in enumerate(slots):
                rr = clamp(r)
                row = whole_block(rr)
                s = products(row, rr, c)
                pos = pos_ref[pl.ds(row, 1), :]
                for t in range(TILES):
                    p = jnp.exp2(s[t * BLOCK : (t + 1) * BLOCK] * LOG2E).astype(jnp.bfloat16)
                    last = last_key(row, c, t, pos, r < blocks).astype(jnp.float32).astype(jnp.bfloat16)
                    at = (g * TILES + t) * BLOCK
                    p_ref[at : at + BLOCK, :] = jnp.where(iota_half <= last, p, jnp.zeros_like(p))

        def add(p_ref, slots):
            for g, (r, c) in enumerate(slots):
                v = values(whole_block(clamp(r)), c)
                at = g * TILES * BLOCK
                acc[r] += jnp.dot(v, p_ref[at : at + TILES * BLOCK, :], preferred_element_type=jnp.float32)

        slots_0, r0, c0 = step_slots(jnp.int32(0), jnp.int32(0))
        weigh(p_a, slots_0)

        def two_steps(_, state):
            r, c, r1, c1 = state
            slots, _, _ = step_slots(r, c)
            slots_1, r2, c2 = step_slots(r1, c1)
            weigh(p_b, slots_1)
            add(p_a, slots)
            slots_2, r3, c3 = step_slots(r2, c2)
            weigh(p_a, slots_2)
            add(p_b, slots_1)
            return r2, c2, r3, c3

        items = lax.fori_loop(0, blocks, lambda r, n: n + code_ref[whole_block(r), table + KEY_BLOCKS], jnp.int32(0))
        turns = lax.div(items + (2 * SLOTS - 1), 2 * SLOTS)
        lax.fori_loop(0, turns, two_steps, (jnp.int32(0), jnp.int32(0), r0, c0))

        for i in range(chips):
            def finish(rr, _, i=i):
                a = acc[i * 4 + rr]
                put(i, rr, a, jnp.where(a[HS : HS + 1] > 0, 0.0, lowest_max))
                return 0

            lax.fori_loop(0, 4, finish, 0)

    @pl.when(jnp.logical_not(safe))
    def _():
        for i in range(chips):
            def one_block(rr, _, i=i):
                r = i * 4 + rr
                row = whole_block(r)
                pos = pos_ref[pl.ds(row, 1), :]
                acc[0] = jnp.zeros((ACC_ROWS, ROWS), jnp.float32)

                def one_slot(c, top):
                    s = products(row, r, c)
                    best = top
                    for t in range(TILES):
                        tile = s[t * BLOCK : (t + 1) * BLOCK]
                        tile = jnp.where(iota <= last_key(row, c, t, pos, True), tile, masked_score)
                        s_all[t * BLOCK : (t + 1) * BLOCK, :] = tile
                        best = jnp.maximum(best, jnp.max(tile, 0, keepdims=True))
                    best = best.astype(jnp.bfloat16).astype(jnp.float32)
                    p = jnp.exp2((s_all[...] - best) * LOG2E).astype(jnp.bfloat16)
                    shrink = jnp.exp2((top - best) * LOG2E)
                    acc[0] = acc[0] * shrink + jnp.dot(values(row, c), p, preferred_element_type=jnp.float32)
                    return best

                start = jnp.full((1, ROWS), lowest_max, jnp.bfloat16).astype(jnp.float32)
                top = lax.fori_loop(0, code_ref[row, table + KEY_BLOCKS], one_slot, start)
                put(i, rr, acc[0], top)
                return 0

            lax.fori_loop(0, 4, one_block, 0)


def attend(steps, seq, codes, spots, held, queries, before=()):
    kv, vt, norm = held
    codes, = in_hbm(codes)
    chips = len(steps)
    out = jax.ShapeDtypeStruct((2, ACC_ROWS, queries[0].shape[2]), jnp.bfloat16)
    return pl.pallas_call(
        functools.partial(attention_kernel, steps, bool(before)),
        in_specs=[SMEM] * 3 + [VMEM] * (3 + len(queries) + len(before)),
        out_specs=[VMEM] * chips,
        out_shape=[out] * chips,
        scratch_shapes=[
            pltpu.VMEM((2 * chips, HS, queries[0].shape[2]), jnp.bfloat16),
            pltpu.VMEM((SLOTS * TILES * BLOCK, ROWS), jnp.bfloat16),
            pltpu.VMEM((SLOTS * TILES * BLOCK, ROWS), jnp.bfloat16),
            pltpu.VMEM((TILES * BLOCK, ROWS), jnp.float32),
            pltpu.VMEM((4 * chips + 1, ACC_ROWS, ROWS), jnp.float32),
        ],
        compiler_params=pltpu.CompilerParams(vmem_limit_bytes=32 * 2**20),
        cost_estimate=pl.CostEstimate(
            flops=chips * 6 * 10**9, bytes_accessed=4 * 2**20, transcendentals=chips * 2**20
        ),
    )(seq, codes, norm, spots, kv, vt, *queries, *before)


def combine_kernel(core_ref, *refs):
    parts, out_ref = refs[:-1], refs[-1]
    groups = out_ref.shape[0] // 2
    half = out_ref.shape[1]
    for j in range(2):
        tops = [p[j, HS + 1 : HS + 2, :].astype(jnp.float32) for p in parts]
        top = functools.reduce(jnp.maximum, tops)
        scales = [jnp.exp(t - top) for t in tops]
        total = sum(
            (p[j, HS : HS + 1, :].astype(jnp.float32) + p[j, HS + 2 : HS + 3, :].astype(jnp.float32)) * scale
            for p, scale in zip(parts, scales)
        )
        summed = sum(p[j, :HS, :].astype(jnp.float32) * scale for p, scale in zip(parts, scales))
        rows = (summed / total).T.astype(jnp.bfloat16)
        first = jnp.bitwise_xor(core_ref[0], j) * groups
        for g in range(groups):
            upper = rows[2 * g * half : (2 * g + 1) * half]
            lower = rows[(2 * g + 1) * half : (2 * g + 2) * half]
            out_ref[first + g] = jnp.concatenate([upper, lower], 1)


def combine(core, parts):
    half = parts[0].shape[2] // 16
    return pl.pallas_call(
        combine_kernel,
        in_specs=[SMEM] + [VMEM] * len(parts),
        out_specs=VMEM,
        out_shape=jax.ShapeDtypeStruct((16, half, 2 * HS), jnp.bfloat16),
        compiler_params=pltpu.CompilerParams(vmem_limit_bytes=32 * 2**20),
    )(core, *parts)


def finish_kernel(grp_ref, pieces_ref, *refs):
    w_refs, out_ref = refs[:-1], refs[-1]
    groups = pieces_ref.shape[0] // 2
    me = grp_ref[0]
    result = None
    for k, w_ref in enumerate(w_refs):
        near = jnp.bitwise_xor(me, k)
        order = [c * groups + g for g in (near, jnp.bitwise_xor(near, 4)) for c in range(2)]
        blocks = [pieces_ref[i] for i in order]
        upper = jnp.concatenate([p[:, :HS] for p in blocks], 1)
        lower = jnp.concatenate([p[:, HS:] for p in blocks], 1)
        attention = jnp.concatenate([upper, lower], 0)
        term = jnp.dot(attention, w_ref[...], preferred_element_type=jnp.float32)
        result = term if result is None else result + term
    out_ref[...] = result.astype(jnp.bfloat16)


def finish(grp, pieces, w_turns):
    return pl.pallas_call(
        finish_kernel,
        in_specs=[SMEM] + [VMEM] * (1 + len(w_turns)),
        out_specs=VMEM,
        out_shape=jax.ShapeDtypeStruct((2 * pieces.shape[1], w_turns[0].shape[1]), jnp.bfloat16),
        compiler_params=pltpu.CompilerParams(vmem_limit_bytes=24 * 2**20),
    )(grp, pieces, *w_turns)


def along_x(by):
    return [(s, s ^ (4 * by)) for s in range(16)]


def came_from(s, by):
    return jnp.bitwise_xor(s, 4 * by)


NEAR_CALLS = ((0,), (1, 3, 2))
FAR_CALLS = ((2, 1, 3), (0,))
CORE_SWAP = [(s, s ^ 1) for s in range(16)]
Y_SWAP = [(s, s ^ 2) for s in range(16)]


def body(inputs, latents, w_query, w_key, w_value, w_out, positions, block_mask):
    seq = lax.axis_index("seq")[None]
    grp = lax.axis_index("grp")[None]
    core = jnp.bitwise_and(seq, 1)

    q_chip, theirs, kv_own, kv_other, codes = front(
        seq, latents, inputs, w_query, w_key, w_value, positions, block_mask
    )
    q_chip = q_chip.at[1].set(lax.ppermute(theirs, "seq", CORE_SWAP))
    queries = {by: q_chip if by == 0 else lax.ppermute(q_chip, "seq", along_x(by)) for by in (0, 1, 3, 2)}
    kv_partner = lax.ppermute(kv_other, "seq", CORE_SWAP)
    near = prepare(*in_hbm(kv_own), kv_partner)
    kv_far = [lax.ppermute(kv, "seq", Y_SWAP) for kv in (kv_own, kv_partner)]

    w_other = lax.ppermute(w_out, "grp", [(g, g ^ 4) for g in range(8)])
    spots = positions.reshape(-1, ROWS)
    queries[0], = in_hbm(q_chip)
    near_parts = dict(zip(NEAR_CALLS[0], attend(NEAR_CALLS[0], seq, codes, spots, near, [queries[0]])))
    w_other, near_parts[0] = lax.optimization_barrier((w_other, near_parts[0]))
    w_pair = jnp.concatenate([w_out, w_other], 0)
    w_turns = [w_pair] + [
        lax.ppermute(w_pair, "grp", [(g, g ^ k) for g in range(8)]) for k in (1, 2, 3)
    ]

    parts = {}
    last = 0
    for call in NEAR_CALLS[1:]:
        queries[call[0]], near_parts[last], kv_far[0] = lax.optimization_barrier(
            (queries[call[0]], near_parts[last], kv_far[0])
        )
        near_parts.update(zip(call, attend(call, seq, codes, spots, near, [queries[by] for by in call])))
        last = call[-1]
    kv_far, near_parts[last] = lax.optimization_barrier((kv_far, near_parts[last]))
    far = prepare(*kv_far)
    last = None
    for call in FAR_CALLS:
        if last is not None:
            queries[call[0]], parts[last] = lax.optimization_barrier((queries[call[0]], parts[last]))
        done = attend(
            call, seq, codes, spots, far, [queries[by] for by in call], [near_parts[by] for by in call]
        )
        parts.update(zip(call, done))
        last = call[-1]

    parts = [part if by == 0 else lax.ppermute(part, "seq", along_x(by)) for by, part in parts.items()]
    parts, w_turns = lax.optimization_barrier((parts, w_turns))
    pieces = combine(core, parts)
    owners = [[(4 * x + 2 * y + c) * 8 + g for c in range(2) for g in range(8)] for x in range(4) for y in range(2)]
    pieces = lax.all_to_all(pieces, ("seq", "grp"), 0, 0, axis_index_groups=owners)
    return finish(grp, pieces, w_turns)


def solution(mesh):
    return jax.shard_map(
        body,
        mesh=mesh,
        in_specs=(
            P("seq", None),
            P("seq", None),
            P(None, "grp"),
            P(None, "grp"),
            P(None, "grp"),
            P("grp", None),
            P(),
            P(),
        ),
        out_specs=P(("seq", "grp"), None),
        check_vma=False,
    )
```

```python
import functools

import jax
import jax.numpy as jnp
from jax import lax
from jax.experimental import pallas as pl
from jax.experimental.pallas import tpu as pltpu
from jax.sharding import PartitionSpec as P

HS = 64
BLOCK = 128
TILES = 4
SLOTS = 2
ROWS = 2 * BLOCK
FAR = 64
KEY_BLOCKS = 32
ACC_ROWS = 72
LOG2E = 1.4426950408889634
SAFE_SCORE = 60.0
masked_score = -1e30
lowest_max = -1e29
SMEM = pl.BlockSpec(memory_space=pltpu.SMEM)
VMEM = pl.BlockSpec(memory_space=pltpu.VMEM)


def in_hbm(*arrays):
    return [pltpu.with_memory_space_constraint(a, pltpu.HBM) for a in arrays]


def list_work(me, pos_ref, mask_ref, code_ref):
    half = KEY_BLOCKS // 2
    both = 2 * KEY_BLOCKS
    blocks = pos_ref.shape[0]

    def held(t):
        source = jnp.bitwise_xor(me, lax.shift_right_logical(t, 4))
        return source * half + jnp.bitwise_and(t, half - 1)

    spots = pos_ref[...].T
    own_block = lax.shift_right_logical(spots, 7)
    furthest = jnp.max(own_block, axis=0, keepdims=True)
    t_rows = lax.broadcasted_iota(jnp.int32, (both, blocks), 0)
    own = jnp.zeros((both, blocks), jnp.int32)
    for t in range(both):
        found = jnp.max((own_block == held(jnp.int32(t))).astype(jnp.int32), axis=0, keepdims=True)
        own = jnp.where(t_rows == t, found, own)

    def exact(condition):
        return condition.astype(jnp.float32).astype(jnp.bfloat16)

    columns = mask_ref.shape[1]
    pick = exact(
        lax.broadcasted_iota(jnp.int32, (both, columns), 1)
        == held(lax.broadcasted_iota(jnp.int32, (both, columns), 0))
    )
    listed = lax.dot_general(
        pick, exact(mask_ref[...] == 1), (((1,), (1,)), ((), ())), preferred_element_type=jnp.float32
    )
    active = exact((own > 0) | ((listed > 0.5) & (held(t_rows) <= furthest)))
    listed = exact(listed > 0.5)

    row = lax.broadcasted_iota(jnp.int32, (blocks, BLOCK), 0)
    col = lax.broadcasted_iota(jnp.int32, (blocks, BLOCK), 1)
    first, second = exact(row == 2 * col), exact(row == 2 * col + 1)
    active = jnp.dot(active, first + second, preferred_element_type=jnp.float32) > 0.5
    listed = [jnp.dot(listed, pairs, preferred_element_type=jnp.float32).astype(jnp.int32) for pairs in (first, second)]
    row = lax.broadcasted_iota(jnp.int32, (both, both), 0)
    col = lax.broadcasted_iota(jnp.int32, (both, both), 1)
    earlier = exact((col < row) & (lax.shift_right_logical(row, 5) == lax.shift_right_logical(col, 5)))
    place = jnp.dot(earlier, exact(active), preferred_element_type=jnp.float32).astype(jnp.int32)
    t_rows = lax.broadcasted_iota(jnp.int32, (both, BLOCK), 0)
    value = jnp.bitwise_and(t_rows, KEY_BLOCKS - 1) + KEY_BLOCKS * (listed[0] + 2 * listed[1] + 4)
    packed = jnp.where(active, place * 512 + value, -1)
    ones = active.astype(jnp.int32)
    slot_rows = lax.broadcasted_iota(jnp.int32, (KEY_BLOCKS, BLOCK), 0)
    tables = []
    for n in range(2):
        codes = jnp.zeros((KEY_BLOCKS, BLOCK), jnp.int32)
        for t in range(n * KEY_BLOCKS, (n + 1) * KEY_BLOCKS):
            one = packed[t : t + 1, :]
            codes = jnp.where(lax.shift_right_arithmetic(one, 9) == slot_rows, jnp.bitwise_and(one, 511), codes)
        count = jnp.sum(ones[n * KEY_BLOCKS : (n + 1) * KEY_BLOCKS], axis=0, keepdims=True)
        slots = jnp.maximum(lax.shift_right_logical(count + (TILES - 1), 2), 1)
        tables += [codes, jnp.broadcast_to(slots, (FAR - KEY_BLOCKS, BLOCK))]
    code_ref[...] = jnp.concatenate(tables, 0).T[: code_ref.shape[0]]


def front_kernel(seq_ref, lat_hbm, x_hbm, wq_hbm, wk_hbm, wv_hbm, pos_hbm, mask_hbm, *rest):
    pair_hbm, theirs_hbm, own_hbm, other_hbm, code_hbm = rest[:5]
    lat, x, wq, wk, wv, pos, mask, pair_ref, theirs_ref, own_ref, other_ref, code_ref = rest[5:17]
    w_all, sems, x_sems, out_sems = rest[17:]
    sent = []

    def send(source, target):
        sent.append(pltpu.make_async_copy(source, target, out_sems.at[len(sent)]))
        sent[-1].start()

    small = [
        pltpu.make_async_copy(source, target, sems.at[i])
        for i, (source, target) in enumerate(
            [(pos_hbm, pos), (mask_hbm, mask), (wq_hbm, wq), (lat_hbm, lat), (wk_hbm, wk), (wv_hbm, wv)]
        )
    ]
    rows = x.shape[0] // x_sems.shape[0]
    parts = [pl.ds(i * rows, rows) for i in range(x_sems.shape[0])]
    large = [pltpu.make_async_copy(x_hbm.at[p], x.at[p], x_sems.at[i]) for i, p in enumerate(parts)]
    for copy in small + large:
        copy.start()
    got_pos, got_mask, got_wq, got_lat, got_wk, got_wv = small
    first = jnp.bitwise_and(seq_ref[0], 1) == 0

    got_pos.wait()
    got_mask.wait()
    list_work(seq_ref[0], pos, mask, code_ref)
    send(code_ref, code_hbm)

    got_wq.wait()
    got_lat.wait()
    q = jnp.dot(lat[...], wq[...], preferred_element_type=jnp.float32).T
    q = q.astype(jnp.bfloat16) * jnp.bfloat16(HS ** -0.5)
    mine = jnp.where(first, q[:HS], q[HS:])
    pair_ref[0] = mine
    pair_ref[1] = mine
    theirs_ref[...] = jnp.where(first, q[HS:], q[:HS])
    send(pair_ref, pair_hbm)
    send(theirs_ref, theirs_hbm)

    got_wk.wait()
    got_wv.wait()
    k, v = wk[...], wv[...]
    head_0 = jnp.concatenate([k[:, :HS], v[:, :HS]], 1)
    head_1 = jnp.concatenate([k[:, HS:], v[:, HS:]], 1)
    w_all[:, : 2 * HS] = jnp.where(first, head_0, head_1)
    w_all[:, 2 * HS :] = jnp.where(first, head_1, head_0)
    for copy, part in zip(large, parts):
        copy.wait()
        both = jnp.dot(x[part, :], w_all[...], preferred_element_type=jnp.float32).astype(jnp.bfloat16)
        own_ref[part, :] = both[:, : 2 * HS]
        other_ref[part, :] = both[:, 2 * HS :]
        send(own_ref.at[part], own_hbm.at[part])
        send(other_ref.at[part], other_hbm.at[part])
    for copy in sent:
        copy.wait()


def front(seq, latents, inputs, w_query, w_key, w_value, positions, block_mask):
    rows, width = latents.shape
    keys = inputs.shape[0]
    spots = positions.reshape(-1, BLOCK)
    operands = (latents, inputs, w_query, w_key, w_value, spots, block_mask)
    q = jax.ShapeDtypeStruct((HS, rows), jnp.bfloat16)
    kv = jax.ShapeDtypeStruct((keys, 2 * HS), jnp.bfloat16)
    results = [jax.ShapeDtypeStruct((2, HS, rows), jnp.bfloat16), q, kv, kv, jax.ShapeDtypeStruct((spots.shape[0] // 2, BLOCK), jnp.int32)]
    return pl.pallas_call(
        front_kernel,
        in_specs=[SMEM] + [pl.BlockSpec(memory_space=pl.ANY)] * len(operands),
        out_specs=[pl.BlockSpec(memory_space=pl.ANY)] * 5,
        out_shape=results,
        scratch_shapes=[pltpu.VMEM(a.shape, a.dtype) for a in (*operands, *results)]
        + [
            pltpu.VMEM((width, 4 * HS), jnp.bfloat16),
            pltpu.SemaphoreType.DMA((6,)),
            pltpu.SemaphoreType.DMA((4,)),
            pltpu.SemaphoreType.DMA((11,)),
        ],
        compiler_params=pltpu.CompilerParams(vmem_limit_bytes=61 * 2**20),
        cost_estimate=pl.CostEstimate(
            flops=2 * (keys * 4 + rows * 2) * width * HS, bytes_accessed=6 * 2**20, transcendentals=0
        ),
    )(seq, *operands)


def prepare_kernel(*refs):
    sources, (kv_ref, vt_ref, norm_ref) = refs[:-3], refs[-3:]
    each = KEY_BLOCKS // len(sources)
    most = None
    for t in range(KEY_BLOCKS):
        at = t % each
        tile = sources[t // each][at * BLOCK : (at + 1) * BLOCK, :]
        kv_ref[t * BLOCK : (t + 1) * BLOCK, :] = tile
        turned = tile.T
        vt_ref[:HS, t * BLOCK : (t + 1) * BLOCK] = turned[HS:, :]
        k = turned[:HS, :].astype(jnp.float32)
        squares = jnp.sum(k * k, axis=0, keepdims=True)
        most = squares if most is None else jnp.maximum(most, squares)
    vt_ref[HS:, :] = jnp.ones((ACC_ROWS - HS, KEY_BLOCKS * BLOCK), jnp.bfloat16)
    norm_ref[0] = jnp.max(most)


def prepare(*sources):
    keys = sum(source.shape[0] for source in sources)
    return pl.pallas_call(
        prepare_kernel,
        in_specs=[VMEM] * len(sources),
        out_specs=[VMEM, VMEM, SMEM],
        out_shape=[
            jax.ShapeDtypeStruct((keys, 2 * HS), jnp.bfloat16),
            jax.ShapeDtypeStruct((ACC_ROWS, keys), jnp.bfloat16),
            jax.ShapeDtypeStruct((1,), jnp.float32),
        ],
        compiler_params=pltpu.CompilerParams(vmem_limit_bytes=24 * 2**20),
    )(*sources)


def attention_kernel(steps, far, seq_ref, code_ref, norm_ref, pos_ref, kv_ref, vt_ref, *rest):
    chips = len(steps)
    q_refs, rest = rest[:chips], rest[chips:]
    before_refs, rest = (rest[:chips], rest[chips:]) if far else (None, rest)
    o_refs, (q_all, p_a, p_b, s_all, acc) = rest[:chips], rest[chips:]
    table = FAR if far else 0
    blocks = 4 * chips
    me = seq_ref[0]
    keys_of = jnp.bitwise_xor(me, 2) if far else me
    own_base = keys_of * (KEY_BLOCKS // 2 * BLOCK)
    partner_base = jnp.bitwise_xor(keys_of, 1) * (KEY_BLOCKS // 2 * BLOCK)
    sources = [came_from(me, step) for step in steps]
    iota = lax.broadcasted_iota(jnp.int32, (BLOCK, ROWS), 0)
    in_first = lax.broadcasted_iota(jnp.int32, (1, ROWS), 1) < BLOCK
    iota_half = iota.astype(jnp.float32).astype(jnp.bfloat16)

    most = None
    for i, ref in enumerate(q_refs):
        for j in range(ref.shape[0]):
            q = ref[j]
            q_all[i * ref.shape[0] + j] = q
            q = q.astype(jnp.float32)
            squares = jnp.sum(q * q, axis=0, keepdims=True)
            most = squares if most is None else jnp.maximum(most, squares)
    safe = jnp.max(most) * norm_ref[0] <= SAFE_SCORE * SAFE_SCORE

    def clamp(r):
        return jnp.minimum(r, blocks - 1)

    def whole_block(r):
        shard = sources[-1]
        for i in range(chips - 1):
            shard = jnp.where(lax.div(r, 4) == i, sources[i], shard)
        return jnp.bitwise_xor(shard, jnp.bitwise_and(lax.div(r, 2), 1)) * 2 + lax.rem(r, 2)

    def offset(i):
        return pl.multiple_of(i * BLOCK, BLOCK)

    def row_offset(i):
        return pl.multiple_of(i * ROWS, ROWS)

    def query(r):
        q = q_all[lax.div(r, 2), :, pl.ds(row_offset(lax.rem(r, 2)), ROWS)]
        return jnp.concatenate([q, jnp.zeros_like(q)], 0)

    def key_blocks(row, c):
        return [jnp.bitwise_and(code_ref[row, table + c * TILES + t], KEY_BLOCKS - 1) for t in range(TILES)]

    def products(row, r, c):
        keys = jnp.concatenate([kv_ref[pl.ds(offset(k), BLOCK), :] for k in key_blocks(row, c)], 0)
        return jnp.dot(keys, query(r), preferred_element_type=jnp.float32)

    def values(row, c):
        return jnp.concatenate([vt_ref[:, pl.ds(offset(k), BLOCK)] for k in key_blocks(row, c)], 1)

    def last_key(row, c, t, pos, real):
        code = code_ref[row, table + c * TILES + t]
        k = jnp.bitwise_and(code, KEY_BLOCKS - 1)
        half = KEY_BLOCKS // 2
        base = jnp.where(k < half, own_base, partner_base - half * BLOCK) + k * BLOCK
        real = jnp.logical_and(real, code >= 4 * KEY_BLOCKS)
        reach = [jnp.where(jnp.bitwise_and(code, n * KEY_BLOCKS) > 0, 1 << 30, BLOCK) for n in (1, 2)]
        reach = jnp.where(in_first, *[jnp.where(real, n, -(1 << 30)) for n in reach])
        ahead = pos - base
        return jnp.where(ahead < reach, jnp.minimum(ahead, BLOCK - 1), -1)

    def put(i, rr, a, top):
        at = (lax.div(rr, 2), slice(None), pl.ds(row_offset(lax.rem(rr, 2)), ROWS))
        if far:
            before = before_refs[i][at].astype(jnp.float32)
            top_before, top_now = before[HS + 1 : HS + 2], top
            top = jnp.maximum(top_before, top_now)
            shrink, shrink_before = jnp.exp(top_now - top), jnp.exp(top_before - top)
            total = a[HS : HS + 1] * shrink + (before[HS : HS + 1] + before[HS + 2 : HS + 3]) * shrink_before
            a = a * shrink + before * shrink_before
        else:
            total = a[HS : HS + 1]
        low = total - total.astype(jnp.bfloat16).astype(jnp.float32)
        out = jnp.concatenate([a[:HS], total, top, low, a[HS + 3 :]], 0)
        o_refs[i][at] = out.astype(jnp.bfloat16)

    def advance(r, c):
        last = c + 1 >= code_ref[whole_block(clamp(r)), table + KEY_BLOCKS]
        return jnp.where(last, jnp.minimum(r + 1, blocks), r), jnp.where(last, 0, c + 1)

    def step_slots(r, c):
        slots = []
        for _ in range(SLOTS):
            slots.append((r, c))
            r, c = advance(r, c)
        return slots, r, c

    @pl.when(safe)
    def _():
        acc[...] = jnp.zeros_like(acc)

        def weigh(p_ref, slots):
            for g, (r, c) in enumerate(slots):
                rr = clamp(r)
                row = whole_block(rr)
                s = products(row, rr, c)
                pos = pos_ref[pl.ds(row, 1), :]
                for t in range(TILES):
                    p = jnp.exp2(s[t * BLOCK : (t + 1) * BLOCK] * LOG2E).astype(jnp.bfloat16)
                    last = last_key(row, c, t, pos, r < blocks).astype(jnp.float32).astype(jnp.bfloat16)
                    at = (g * TILES + t) * BLOCK
                    p_ref[at : at + BLOCK, :] = jnp.where(iota_half <= last, p, jnp.zeros_like(p))

        def add(p_ref, slots):
            for g, (r, c) in enumerate(slots):
                v = values(whole_block(clamp(r)), c)
                at = g * TILES * BLOCK
                acc[r] += jnp.dot(v, p_ref[at : at + TILES * BLOCK, :], preferred_element_type=jnp.float32)

        slots_0, r0, c0 = step_slots(jnp.int32(0), jnp.int32(0))
        weigh(p_a, slots_0)

        def two_steps(_, state):
            r, c, r1, c1 = state
            slots, _, _ = step_slots(r, c)
            slots_1, r2, c2 = step_slots(r1, c1)
            weigh(p_b, slots_1)
            add(p_a, slots)
            slots_2, r3, c3 = step_slots(r2, c2)
            weigh(p_a, slots_2)
            add(p_b, slots_1)
            return r2, c2, r3, c3

        items = lax.fori_loop(0, blocks, lambda r, n: n + code_ref[whole_block(r), table + KEY_BLOCKS], jnp.int32(0))
        turns = lax.div(items + (2 * SLOTS - 1), 2 * SLOTS)
        lax.fori_loop(0, turns, two_steps, (jnp.int32(0), jnp.int32(0), r0, c0))

        for i in range(chips):
            def finish(rr, _, i=i):
                a = acc[i * 4 + rr]
                put(i, rr, a, jnp.where(a[HS : HS + 1] > 0, 0.0, lowest_max))
                return 0

            lax.fori_loop(0, 4, finish, 0)

    @pl.when(jnp.logical_not(safe))
    def _():
        for i in range(chips):
            def one_block(rr, _, i=i):
                r = i * 4 + rr
                row = whole_block(r)
                pos = pos_ref[pl.ds(row, 1), :]
                acc[0] = jnp.zeros((ACC_ROWS, ROWS), jnp.float32)

                def one_slot(c, top):
                    s = products(row, r, c)
                    best = top
                    for t in range(TILES):
                        tile = s[t * BLOCK : (t + 1) * BLOCK]
                        tile = jnp.where(iota <= last_key(row, c, t, pos, True), tile, masked_score)
                        s_all[t * BLOCK : (t + 1) * BLOCK, :] = tile
                        best = jnp.maximum(best, jnp.max(tile, 0, keepdims=True))
                    best = best.astype(jnp.bfloat16).astype(jnp.float32)
                    p = jnp.exp2((s_all[...] - best) * LOG2E).astype(jnp.bfloat16)
                    shrink = jnp.exp2((top - best) * LOG2E)
                    acc[0] = acc[0] * shrink + jnp.dot(values(row, c), p, preferred_element_type=jnp.float32)
                    return best

                start = jnp.full((1, ROWS), lowest_max, jnp.bfloat16).astype(jnp.float32)
                top = lax.fori_loop(0, code_ref[row, table + KEY_BLOCKS], one_slot, start)
                put(i, rr, acc[0], top)
                return 0

            lax.fori_loop(0, 4, one_block, 0)


def attend(steps, seq, codes, spots, held, queries, before=()):
    kv, vt, norm = held
    codes, = in_hbm(codes)
    chips = len(steps)
    out = jax.ShapeDtypeStruct((2, ACC_ROWS, queries[0].shape[2]), jnp.bfloat16)
    return pl.pallas_call(
        functools.partial(attention_kernel, steps, bool(before)),
        in_specs=[SMEM] * 3 + [VMEM] * (3 + len(queries) + len(before)),
        out_specs=[VMEM] * chips,
        out_shape=[out] * chips,
        scratch_shapes=[
            pltpu.VMEM((2 * chips, HS, queries[0].shape[2]), jnp.bfloat16),
            pltpu.VMEM((SLOTS * TILES * BLOCK, ROWS), jnp.bfloat16),
            pltpu.VMEM((SLOTS * TILES * BLOCK, ROWS), jnp.bfloat16),
            pltpu.VMEM((TILES * BLOCK, ROWS), jnp.float32),
            pltpu.VMEM((4 * chips + 1, ACC_ROWS, ROWS), jnp.float32),
        ],
        compiler_params=pltpu.CompilerParams(vmem_limit_bytes=32 * 2**20),
        cost_estimate=pl.CostEstimate(
            flops=chips * 6 * 10**9, bytes_accessed=4 * 2**20, transcendentals=chips * 2**20
        ),
    )(seq, codes, norm, spots, kv, vt, *queries, *before)


def combine_kernel(core_ref, *refs):
    parts, out_ref = refs[:-1], refs[-1]
    groups = out_ref.shape[0] // 2
    half = out_ref.shape[1]
    for j in range(2):
        tops = [p[j, HS + 1 : HS + 2, :].astype(jnp.float32) for p in parts]
        top = functools.reduce(jnp.maximum, tops)
        scales = [jnp.exp(t - top) for t in tops]
        total = sum(
            (p[j, HS : HS + 1, :].astype(jnp.float32) + p[j, HS + 2 : HS + 3, :].astype(jnp.float32)) * scale
            for p, scale in zip(parts, scales)
        )
        summed = sum(p[j, :HS, :].astype(jnp.float32) * scale for p, scale in zip(parts, scales))
        rows = (summed / total).T.astype(jnp.bfloat16)
        first = jnp.bitwise_xor(core_ref[0], j) * groups
        for g in range(groups):
            upper = rows[2 * g * half : (2 * g + 1) * half]
            lower = rows[(2 * g + 1) * half : (2 * g + 2) * half]
            out_ref[first + g] = jnp.concatenate([upper, lower], 1)


def combine(core, parts):
    half = parts[0].shape[2] // 16
    return pl.pallas_call(
        combine_kernel,
        in_specs=[SMEM] + [VMEM] * len(parts),
        out_specs=VMEM,
        out_shape=jax.ShapeDtypeStruct((16, half, 2 * HS), jnp.bfloat16),
        compiler_params=pltpu.CompilerParams(vmem_limit_bytes=32 * 2**20),
    )(core, *parts)


def finish_kernel(pieces_ref, w_ref, out_ref):
    groups = pieces_ref.shape[0] // 2
    order = [c * groups + g for g in range(groups) for c in range(2)]
    upper = jnp.concatenate([pieces_ref[i][:, :HS] for i in order], 1)
    lower = jnp.concatenate([pieces_ref[i][:, HS:] for i in order], 1)
    attention = jnp.concatenate([upper, lower], 0)
    out_ref[...] = jnp.dot(attention, w_ref[...], preferred_element_type=jnp.float32).astype(jnp.bfloat16)


def finish(pieces, w_all):
    return pl.pallas_call(
        finish_kernel,
        in_specs=[VMEM, VMEM],
        out_specs=VMEM,
        out_shape=jax.ShapeDtypeStruct((2 * pieces.shape[1], w_all.shape[1]), jnp.bfloat16),
        compiler_params=pltpu.CompilerParams(vmem_limit_bytes=24 * 2**20),
    )(pieces, w_all)


def along_x(by):
    return [(s, s ^ (4 * by)) for s in range(16)]


def came_from(s, by):
    return jnp.bitwise_xor(s, 4 * by)


NEAR_CALLS = ((0,), (1, 3, 2))
FAR_CALLS = ((2, 1, 3), (0,))
CORE_SWAP = [(s, s ^ 1) for s in range(16)]
Y_SWAP = [(s, s ^ 2) for s in range(16)]


def body(inputs, latents, w_query, w_key, w_value, w_out, positions, block_mask):
    seq = lax.axis_index("seq")[None]
    core = jnp.bitwise_and(seq, 1)

    q_chip, theirs, kv_own, kv_other, codes = front(
        seq, latents, inputs, w_query, w_key, w_value, positions, block_mask
    )
    q_chip = q_chip.at[1].set(lax.ppermute(theirs, "seq", CORE_SWAP))
    queries = {by: q_chip if by == 0 else lax.ppermute(q_chip, "seq", along_x(by)) for by in (0, 1, 3, 2)}
    kv_partner = lax.ppermute(kv_other, "seq", CORE_SWAP)
    near = prepare(*in_hbm(kv_own), kv_partner)
    kv_far = [lax.ppermute(kv, "seq", Y_SWAP) for kv in (kv_own, kv_partner)]

    spots = positions.reshape(-1, ROWS)
    queries[0], = in_hbm(q_chip)
    near_parts = dict(zip(NEAR_CALLS[0], attend(NEAR_CALLS[0], seq, codes, spots, near, [queries[0]])))
    w_mine, near_parts[0] = lax.optimization_barrier((w_out, near_parts[0]))
    w_all = lax.all_to_all(jnp.broadcast_to(w_mine, (8, *w_out.shape)), "grp", 0, 0)

    parts = {}
    last = 0
    for call in NEAR_CALLS[1:]:
        queries[call[0]], near_parts[last], kv_far[0] = lax.optimization_barrier(
            (queries[call[0]], near_parts[last], kv_far[0])
        )
        near_parts.update(zip(call, attend(call, seq, codes, spots, near, [queries[by] for by in call])))
        last = call[-1]
    kv_far, near_parts[last] = lax.optimization_barrier((kv_far, near_parts[last]))
    far = prepare(*kv_far)
    last = None
    for call in FAR_CALLS:
        if last is not None:
            queries[call[0]], parts[last] = lax.optimization_barrier((queries[call[0]], parts[last]))
        done = attend(
            call, seq, codes, spots, far, [queries[by] for by in call], [near_parts[by] for by in call]
        )
        parts.update(zip(call, done))
        last = call[-1]

    parts = [part if by == 0 else lax.ppermute(part, "seq", along_x(by)) for by, part in parts.items()]
    parts, w_all = lax.optimization_barrier((parts, w_all))
    pieces = combine(core, parts)
    owners = [[(4 * x + 2 * y + c) * 8 + g for c in range(2) for g in range(8)] for x in range(4) for y in range(2)]
    pieces = lax.all_to_all(pieces, ("seq", "grp"), 0, 0, axis_index_groups=owners)
    return finish(pieces, w_all.reshape(-1, w_out.shape[1]))


def solution(mesh):
    return jax.shard_map(
        body,
        mesh=mesh,
        in_specs=(
            P("seq", None),
            P("seq", None),
            P(None, "grp"),
            P(None, "grp"),
            P(None, "grp"),
            P("grp", None),
            P(),
            P(),
        ),
        out_specs=P(("seq", "grp"), None),
        check_vma=False,
    )
```

```python
import functools

import jax
import jax.numpy as jnp
from jax import lax
from jax.experimental import pallas as pl
from jax.experimental.pallas import tpu as pltpu
from jax.sharding import PartitionSpec as P

HS = 64
BLOCK = 128
TILES = 4
SLOTS = 2
ROWS = 2 * BLOCK
FAR = 64
KEY_BLOCKS = 32
ACC_ROWS = 72
LOG2E = 1.4426950408889634
SAFE_SCORE = 60.0
masked_score = -1e30
lowest_max = -1e29
SMEM = pl.BlockSpec(memory_space=pltpu.SMEM)
VMEM = pl.BlockSpec(memory_space=pltpu.VMEM)


def in_hbm(*arrays):
    return [pltpu.with_memory_space_constraint(a, pltpu.HBM) for a in arrays]


def list_work(me, pos_ref, mask_ref, code_ref):
    half = KEY_BLOCKS // 2
    both = 2 * KEY_BLOCKS
    blocks = pos_ref.shape[0]

    def held(t):
        source = jnp.bitwise_xor(me, lax.shift_right_logical(t, 4))
        return source * half + jnp.bitwise_and(t, half - 1)

    spots = pos_ref[...].T
    own_block = lax.shift_right_logical(spots, 7)
    furthest = jnp.max(own_block, axis=0, keepdims=True)
    t_rows = lax.broadcasted_iota(jnp.int32, (both, blocks), 0)
    own = jnp.zeros((both, blocks), jnp.int32)
    for t in range(both):
        found = jnp.max((own_block == held(jnp.int32(t))).astype(jnp.int32), axis=0, keepdims=True)
        own = jnp.where(t_rows == t, found, own)

    def exact(condition):
        return condition.astype(jnp.float32).astype(jnp.bfloat16)

    columns = mask_ref.shape[1]
    pick = exact(
        lax.broadcasted_iota(jnp.int32, (both, columns), 1)
        == held(lax.broadcasted_iota(jnp.int32, (both, columns), 0))
    )
    listed = lax.dot_general(
        pick, exact(mask_ref[...] == 1), (((1,), (1,)), ((), ())), preferred_element_type=jnp.float32
    )
    active = exact((own > 0) | ((listed > 0.5) & (held(t_rows) <= furthest)))
    listed = exact(listed > 0.5)

    row = lax.broadcasted_iota(jnp.int32, (blocks, BLOCK), 0)
    col = lax.broadcasted_iota(jnp.int32, (blocks, BLOCK), 1)
    first, second = exact(row == 2 * col), exact(row == 2 * col + 1)
    active = jnp.dot(active, first + second, preferred_element_type=jnp.float32) > 0.5
    listed = [jnp.dot(listed, pairs, preferred_element_type=jnp.float32).astype(jnp.int32) for pairs in (first, second)]
    row = lax.broadcasted_iota(jnp.int32, (both, both), 0)
    col = lax.broadcasted_iota(jnp.int32, (both, both), 1)
    earlier = exact((col < row) & (lax.shift_right_logical(row, 5) == lax.shift_right_logical(col, 5)))
    place = jnp.dot(earlier, exact(active), preferred_element_type=jnp.float32).astype(jnp.int32)
    t_rows = lax.broadcasted_iota(jnp.int32, (both, BLOCK), 0)
    value = jnp.bitwise_and(t_rows, KEY_BLOCKS - 1) + KEY_BLOCKS * (listed[0] + 2 * listed[1] + 4)
    packed = jnp.where(active, place * 512 + value, -1)
    ones = active.astype(jnp.int32)
    slot_rows = lax.broadcasted_iota(jnp.int32, (KEY_BLOCKS, BLOCK), 0)
    tables = []
    for n in range(2):
        codes = jnp.zeros((KEY_BLOCKS, BLOCK), jnp.int32)
        for t in range(n * KEY_BLOCKS, (n + 1) * KEY_BLOCKS):
            one = packed[t : t + 1, :]
            codes = jnp.where(lax.shift_right_arithmetic(one, 9) == slot_rows, jnp.bitwise_and(one, 511), codes)
        count = jnp.sum(ones[n * KEY_BLOCKS : (n + 1) * KEY_BLOCKS], axis=0, keepdims=True)
        slots = jnp.maximum(lax.shift_right_logical(count + (TILES - 1), 2), 1)
        tables += [codes, jnp.broadcast_to(slots, (FAR - KEY_BLOCKS, BLOCK))]
    code_ref[...] = jnp.concatenate(tables, 0).T[: code_ref.shape[0]]


def front_kernel(seq_ref, lat_hbm, x_hbm, wq_hbm, wk_hbm, wv_hbm, pos_hbm, mask_hbm, *rest):
    pair_hbm, theirs_hbm, own_hbm, other_hbm, code_hbm = rest[:5]
    lat, x, wq, wk, wv, pos, mask, pair_ref, theirs_ref, own_ref, other_ref, code_ref = rest[5:17]
    w_all, sems, x_sems, out_sems = rest[17:]
    sent = []

    def send(source, target):
        sent.append(pltpu.make_async_copy(source, target, out_sems.at[len(sent)]))
        sent[-1].start()

    small = [
        pltpu.make_async_copy(source, target, sems.at[i])
        for i, (source, target) in enumerate(
            [(pos_hbm, pos), (mask_hbm, mask), (wq_hbm, wq), (lat_hbm, lat), (wk_hbm, wk), (wv_hbm, wv)]
        )
    ]
    rows = x.shape[0] // x_sems.shape[0]
    parts = [pl.ds(i * rows, rows) for i in range(x_sems.shape[0])]
    large = [pltpu.make_async_copy(x_hbm.at[p], x.at[p], x_sems.at[i]) for i, p in enumerate(parts)]
    for copy in small + large:
        copy.start()
    got_pos, got_mask, got_wq, got_lat, got_wk, got_wv = small
    first = jnp.bitwise_and(seq_ref[0], 1) == 0

    got_pos.wait()
    got_mask.wait()
    list_work(seq_ref[0], pos, mask, code_ref)
    send(code_ref, code_hbm)

    got_wq.wait()
    got_lat.wait()
    q = jnp.dot(lat[...], wq[...], preferred_element_type=jnp.float32).T
    q = q.astype(jnp.bfloat16) * jnp.bfloat16(HS ** -0.5)
    mine = jnp.where(first, q[:HS], q[HS:])
    pair_ref[0] = mine
    pair_ref[1] = mine
    theirs_ref[...] = jnp.where(first, q[HS:], q[:HS])
    send(pair_ref, pair_hbm)
    send(theirs_ref, theirs_hbm)

    got_wk.wait()
    got_wv.wait()
    k, v = wk[...], wv[...]
    head_0 = jnp.concatenate([k[:, :HS], v[:, :HS]], 1)
    head_1 = jnp.concatenate([k[:, HS:], v[:, HS:]], 1)
    w_all[:, : 2 * HS] = jnp.where(first, head_0, head_1)
    w_all[:, 2 * HS :] = jnp.where(first, head_1, head_0)
    for copy, part in zip(large, parts):
        copy.wait()
        both = jnp.dot(x[part, :], w_all[...], preferred_element_type=jnp.float32).astype(jnp.bfloat16)
        own_ref[part, :] = both[:, : 2 * HS]
        other_ref[part, :] = both[:, 2 * HS :]
        send(own_ref.at[part], own_hbm.at[part])
        send(other_ref.at[part], other_hbm.at[part])
    for copy in sent:
        copy.wait()


def front(seq, latents, inputs, w_query, w_key, w_value, positions, block_mask):
    rows, width = latents.shape
    keys = inputs.shape[0]
    spots = positions.reshape(-1, BLOCK)
    operands = (latents, inputs, w_query, w_key, w_value, spots, block_mask)
    q = jax.ShapeDtypeStruct((HS, rows), jnp.bfloat16)
    kv = jax.ShapeDtypeStruct((keys, 2 * HS), jnp.bfloat16)
    results = [jax.ShapeDtypeStruct((2, HS, rows), jnp.bfloat16), q, kv, kv, jax.ShapeDtypeStruct((spots.shape[0] // 2, BLOCK), jnp.int32)]
    return pl.pallas_call(
        front_kernel,
        in_specs=[SMEM] + [pl.BlockSpec(memory_space=pl.ANY)] * len(operands),
        out_specs=[pl.BlockSpec(memory_space=pl.ANY)] * 5,
        out_shape=results,
        scratch_shapes=[pltpu.VMEM(a.shape, a.dtype) for a in (*operands, *results)]
        + [
            pltpu.VMEM((width, 4 * HS), jnp.bfloat16),
            pltpu.SemaphoreType.DMA((6,)),
            pltpu.SemaphoreType.DMA((4,)),
            pltpu.SemaphoreType.DMA((11,)),
        ],
        compiler_params=pltpu.CompilerParams(vmem_limit_bytes=24 * 2**20),
        cost_estimate=pl.CostEstimate(
            flops=2 * (keys * 4 + rows * 2) * width * HS, bytes_accessed=6 * 2**20, transcendentals=0
        ),
    )(seq, *in_hbm(*operands))


def prepare_kernel(*refs):
    sources, (kv_ref, vt_ref, norm_ref) = refs[:-3], refs[-3:]
    each = KEY_BLOCKS // len(sources)
    most = None
    for t in range(KEY_BLOCKS):
        at = t % each
        tile = sources[t // each][at * BLOCK : (at + 1) * BLOCK, :]
        kv_ref[t * BLOCK : (t + 1) * BLOCK, :] = tile
        turned = tile.T
        vt_ref[:HS, t * BLOCK : (t + 1) * BLOCK] = turned[HS:, :]
        k = turned[:HS, :].astype(jnp.float32)
        squares = jnp.sum(k * k, axis=0, keepdims=True)
        most = squares if most is None else jnp.maximum(most, squares)
    vt_ref[HS:, :] = jnp.ones((ACC_ROWS - HS, KEY_BLOCKS * BLOCK), jnp.bfloat16)
    norm_ref[0] = jnp.max(most)


def prepare(*sources):
    keys = sum(source.shape[0] for source in sources)
    return pl.pallas_call(
        prepare_kernel,
        in_specs=[VMEM] * len(sources),
        out_specs=[VMEM, VMEM, SMEM],
        out_shape=[
            jax.ShapeDtypeStruct((keys, 2 * HS), jnp.bfloat16),
            jax.ShapeDtypeStruct((ACC_ROWS, keys), jnp.bfloat16),
            jax.ShapeDtypeStruct((1,), jnp.float32),
        ],
        compiler_params=pltpu.CompilerParams(vmem_limit_bytes=24 * 2**20),
    )(*sources)


def attention_kernel(steps, far, seq_ref, code_ref, norm_ref, pos_ref, kv_ref, vt_ref, *rest):
    chips = len(steps)
    q_refs, rest = rest[:chips], rest[chips:]
    before_refs, rest = (rest[:chips], rest[chips:]) if far else (None, rest)
    o_refs, (q_all, p_a, p_b, s_all, acc) = rest[:chips], rest[chips:]
    table = FAR if far else 0
    blocks = 4 * chips
    me = seq_ref[0]
    keys_of = jnp.bitwise_xor(me, 2) if far else me
    own_base = keys_of * (KEY_BLOCKS // 2 * BLOCK)
    partner_base = jnp.bitwise_xor(keys_of, 1) * (KEY_BLOCKS // 2 * BLOCK)
    sources = [came_from(me, step) for step in steps]
    iota = lax.broadcasted_iota(jnp.int32, (BLOCK, ROWS), 0)
    in_first = lax.broadcasted_iota(jnp.int32, (1, ROWS), 1) < BLOCK
    iota_half = iota.astype(jnp.float32).astype(jnp.bfloat16)

    most = None
    for i, ref in enumerate(q_refs):
        for j in range(ref.shape[0]):
            q = ref[j]
            q_all[i * ref.shape[0] + j] = q
            q = q.astype(jnp.float32)
            squares = jnp.sum(q * q, axis=0, keepdims=True)
            most = squares if most is None else jnp.maximum(most, squares)
    safe = jnp.max(most) * norm_ref[0] <= SAFE_SCORE * SAFE_SCORE

    def clamp(r):
        return jnp.minimum(r, blocks - 1)

    def whole_block(r):
        shard = sources[-1]
        for i in range(chips - 1):
            shard = jnp.where(lax.div(r, 4) == i, sources[i], shard)
        return jnp.bitwise_xor(shard, jnp.bitwise_and(lax.div(r, 2), 1)) * 2 + lax.rem(r, 2)

    def offset(i):
        return pl.multiple_of(i * BLOCK, BLOCK)

    def row_offset(i):
        return pl.multiple_of(i * ROWS, ROWS)

    def query(r):
        q = q_all[lax.div(r, 2), :, pl.ds(row_offset(lax.rem(r, 2)), ROWS)]
        return jnp.concatenate([q, jnp.zeros_like(q)], 0)

    def key_blocks(row, c):
        return [jnp.bitwise_and(code_ref[row, table + c * TILES + t], KEY_BLOCKS - 1) for t in range(TILES)]

    def products(row, r, c):
        keys = jnp.concatenate([kv_ref[pl.ds(offset(k), BLOCK), :] for k in key_blocks(row, c)], 0)
        return jnp.dot(keys, query(r), preferred_element_type=jnp.float32)

    def values(row, c):
        return jnp.concatenate([vt_ref[:, pl.ds(offset(k), BLOCK)] for k in key_blocks(row, c)], 1)

    def last_key(row, c, t, pos, real):
        code = code_ref[row, table + c * TILES + t]
        k = jnp.bitwise_and(code, KEY_BLOCKS - 1)
        half = KEY_BLOCKS // 2
        base = jnp.where(k < half, own_base, partner_base - half * BLOCK) + k * BLOCK
        real = jnp.logical_and(real, code >= 4 * KEY_BLOCKS)
        reach = [jnp.where(jnp.bitwise_and(code, n * KEY_BLOCKS) > 0, 1 << 30, BLOCK) for n in (1, 2)]
        reach = jnp.where(in_first, *[jnp.where(real, n, -(1 << 30)) for n in reach])
        ahead = pos - base
        return jnp.where(ahead < reach, jnp.minimum(ahead, BLOCK - 1), -1)

    def put(i, rr, a, top):
        at = (lax.div(rr, 2), slice(None), pl.ds(row_offset(lax.rem(rr, 2)), ROWS))
        if far:
            before = before_refs[i][at].astype(jnp.float32)
            top_before, top_now = before[HS + 1 : HS + 2], top
            top = jnp.maximum(top_before, top_now)
            shrink, shrink_before = jnp.exp(top_now - top), jnp.exp(top_before - top)
            total = a[HS : HS + 1] * shrink + (before[HS : HS + 1] + before[HS + 2 : HS + 3]) * shrink_before
            a = a * shrink + before * shrink_before
        else:
            total = a[HS : HS + 1]
        low = total - total.astype(jnp.bfloat16).astype(jnp.float32)
        out = jnp.concatenate([a[:HS], total, top, low, a[HS + 3 :]], 0)
        o_refs[i][at] = out.astype(jnp.bfloat16)

    def advance(r, c):
        last = c + 1 >= code_ref[whole_block(clamp(r)), table + KEY_BLOCKS]
        return jnp.where(last, jnp.minimum(r + 1, blocks), r), jnp.where(last, 0, c + 1)

    def step_slots(r, c):
        slots = []
        for _ in range(SLOTS):
            slots.append((r, c))
            r, c = advance(r, c)
        return slots, r, c

    @pl.when(safe)
    def _():
        acc[...] = jnp.zeros_like(acc)

        def weigh(p_ref, slots):
            for g, (r, c) in enumerate(slots):
                rr = clamp(r)
                row = whole_block(rr)
                s = products(row, rr, c)
                pos = pos_ref[pl.ds(row, 1), :]
                for t in range(TILES):
                    p = jnp.exp2(s[t * BLOCK : (t + 1) * BLOCK] * LOG2E).astype(jnp.bfloat16)
                    last = last_key(row, c, t, pos, r < blocks).astype(jnp.float32).astype(jnp.bfloat16)
                    at = (g * TILES + t) * BLOCK
                    p_ref[at : at + BLOCK, :] = jnp.where(iota_half <= last, p, jnp.zeros_like(p))

        def add(p_ref, slots):
            for g, (r, c) in enumerate(slots):
                v = values(whole_block(clamp(r)), c)
                at = g * TILES * BLOCK
                acc[r] += jnp.dot(v, p_ref[at : at + TILES * BLOCK, :], preferred_element_type=jnp.float32)

        slots_0, r0, c0 = step_slots(jnp.int32(0), jnp.int32(0))
        weigh(p_a, slots_0)

        def two_steps(_, state):
            r, c, r1, c1 = state
            slots, _, _ = step_slots(r, c)
            slots_1, r2, c2 = step_slots(r1, c1)
            weigh(p_b, slots_1)
            add(p_a, slots)
            slots_2, r3, c3 = step_slots(r2, c2)
            weigh(p_a, slots_2)
            add(p_b, slots_1)
            return r2, c2, r3, c3

        items = lax.fori_loop(0, blocks, lambda r, n: n + code_ref[whole_block(r), table + KEY_BLOCKS], jnp.int32(0))
        turns = lax.div(items + (2 * SLOTS - 1), 2 * SLOTS)
        lax.fori_loop(0, turns, two_steps, (jnp.int32(0), jnp.int32(0), r0, c0))

        for i in range(chips):
            def finish(rr, _, i=i):
                a = acc[i * 4 + rr]
                put(i, rr, a, jnp.where(a[HS : HS + 1] > 0, 0.0, lowest_max))
                return 0

            lax.fori_loop(0, 4, finish, 0)

    @pl.when(jnp.logical_not(safe))
    def _():
        for i in range(chips):
            def one_block(rr, _, i=i):
                r = i * 4 + rr
                row = whole_block(r)
                pos = pos_ref[pl.ds(row, 1), :]
                acc[0] = jnp.zeros((ACC_ROWS, ROWS), jnp.float32)

                def one_slot(c, top):
                    s = products(row, r, c)
                    best = top
                    for t in range(TILES):
                        tile = s[t * BLOCK : (t + 1) * BLOCK]
                        tile = jnp.where(iota <= last_key(row, c, t, pos, True), tile, masked_score)
                        s_all[t * BLOCK : (t + 1) * BLOCK, :] = tile
                        best = jnp.maximum(best, jnp.max(tile, 0, keepdims=True))
                    best = best.astype(jnp.bfloat16).astype(jnp.float32)
                    p = jnp.exp2((s_all[...] - best) * LOG2E).astype(jnp.bfloat16)
                    shrink = jnp.exp2((top - best) * LOG2E)
                    acc[0] = acc[0] * shrink + jnp.dot(values(row, c), p, preferred_element_type=jnp.float32)
                    return best

                start = jnp.full((1, ROWS), lowest_max, jnp.bfloat16).astype(jnp.float32)
                top = lax.fori_loop(0, code_ref[row, table + KEY_BLOCKS], one_slot, start)
                put(i, rr, acc[0], top)
                return 0

            lax.fori_loop(0, 4, one_block, 0)


def attend(steps, seq, codes, spots, held, queries, before=()):
    kv, vt, norm = held
    chips = len(steps)
    out = jax.ShapeDtypeStruct((2, ACC_ROWS, queries[0].shape[2]), jnp.bfloat16)
    return pl.pallas_call(
        functools.partial(attention_kernel, steps, bool(before)),
        in_specs=[SMEM] * 3 + [VMEM] * (3 + len(queries) + len(before)),
        out_specs=[VMEM] * chips,
        out_shape=[out] * chips,
        scratch_shapes=[
            pltpu.VMEM((2 * chips, HS, queries[0].shape[2]), jnp.bfloat16),
            pltpu.VMEM((SLOTS * TILES * BLOCK, ROWS), jnp.bfloat16),
            pltpu.VMEM((SLOTS * TILES * BLOCK, ROWS), jnp.bfloat16),
            pltpu.VMEM((TILES * BLOCK, ROWS), jnp.float32),
            pltpu.VMEM((4 * chips + 1, ACC_ROWS, ROWS), jnp.float32),
        ],
        compiler_params=pltpu.CompilerParams(vmem_limit_bytes=32 * 2**20),
        cost_estimate=pl.CostEstimate(
            flops=chips * 6 * 10**9, bytes_accessed=4 * 2**20, transcendentals=chips * 2**20
        ),
    )(seq, codes, norm, spots, kv, vt, *queries, *before)


def combine_kernel(core_ref, *refs):
    parts, out_ref = refs[:-1], refs[-1]
    groups = out_ref.shape[0] // 2
    half = out_ref.shape[1]
    for j in range(2):
        tops = [p[j, HS + 1 : HS + 2, :].astype(jnp.float32) for p in parts]
        top = functools.reduce(jnp.maximum, tops)
        scales = [jnp.exp(t - top) for t in tops]
        total = sum(
            (p[j, HS : HS + 1, :].astype(jnp.float32) + p[j, HS + 2 : HS + 3, :].astype(jnp.float32)) * scale
            for p, scale in zip(parts, scales)
        )
        summed = sum(p[j, :HS, :].astype(jnp.float32) * scale for p, scale in zip(parts, scales))
        rows = (summed / total).T.astype(jnp.bfloat16)
        first = jnp.bitwise_xor(core_ref[0], j) * groups
        for g in range(groups):
            upper = rows[2 * g * half : (2 * g + 1) * half]
            lower = rows[(2 * g + 1) * half : (2 * g + 2) * half]
            out_ref[first + g] = jnp.concatenate([upper, lower], 1)


def combine(core, parts):
    half = parts[0].shape[2] // 16
    return pl.pallas_call(
        combine_kernel,
        in_specs=[SMEM] + [VMEM] * len(parts),
        out_specs=VMEM,
        out_shape=jax.ShapeDtypeStruct((16, half, 2 * HS), jnp.bfloat16),
        compiler_params=pltpu.CompilerParams(vmem_limit_bytes=32 * 2**20),
    )(core, *parts)


def finish_kernel(grp_ref, pieces_ref, *refs):
    w_refs, out_ref = refs[:-1], refs[-1]
    groups = pieces_ref.shape[0] // 2
    me = grp_ref[0]
    result = None
    for k, w_ref in enumerate(w_refs):
        near = jnp.bitwise_xor(me, k)
        order = [c * groups + g for g in (near, jnp.bitwise_xor(near, 4)) for c in range(2)]
        blocks = [pieces_ref[i] for i in order]
        upper = jnp.concatenate([p[:, :HS] for p in blocks], 1)
        lower = jnp.concatenate([p[:, HS:] for p in blocks], 1)
        attention = jnp.concatenate([upper, lower], 0)
        term = jnp.dot(attention, w_ref[...], preferred_element_type=jnp.float32)
        result = term if result is None else result + term
    out_ref[...] = result.astype(jnp.bfloat16)


def finish(grp, pieces, w_turns):
    return pl.pallas_call(
        finish_kernel,
        in_specs=[SMEM] + [VMEM] * (1 + len(w_turns)),
        out_specs=VMEM,
        out_shape=jax.ShapeDtypeStruct((2 * pieces.shape[1], w_turns[0].shape[1]), jnp.bfloat16),
        compiler_params=pltpu.CompilerParams(vmem_limit_bytes=24 * 2**20),
    )(grp, pieces, *w_turns)


def along_x(by):
    return [(s, s ^ (4 * by)) for s in range(16)]


def came_from(s, by):
    return jnp.bitwise_xor(s, 4 * by)


NEAR_CALLS = ((0,), (1, 3, 2))
FAR_CALLS = ((2, 1, 3), (0,))
CORE_SWAP = [(s, s ^ 1) for s in range(16)]
Y_SWAP = [(s, s ^ 2) for s in range(16)]


def body(inputs, latents, w_query, w_key, w_value, w_out, positions, block_mask):
    seq = lax.axis_index("seq")[None]
    grp = lax.axis_index("grp")[None]
    core = jnp.bitwise_and(seq, 1)

    q_chip, theirs, kv_own, kv_other, codes = front(
        seq, latents, inputs, w_query, w_key, w_value, positions, block_mask
    )
    q_chip = q_chip.at[1].set(lax.ppermute(theirs, "seq", CORE_SWAP))
    queries = {by: q_chip if by == 0 else lax.ppermute(q_chip, "seq", along_x(by)) for by in (0, 1, 3, 2)}
    kv_partner = lax.ppermute(kv_other, "seq", CORE_SWAP)
    near = prepare(kv_own, kv_partner)
    kv_far = [lax.ppermute(kv, "seq", Y_SWAP) for kv in (kv_own, kv_partner)]

    w_other = lax.ppermute(w_out, "grp", [(g, g ^ 4) for g in range(8)])
    spots = positions.reshape(-1, ROWS)
    near_parts = dict(zip(NEAR_CALLS[0], attend(NEAR_CALLS[0], seq, codes, spots, near, [q_chip])))
    w_other, near_parts[0] = lax.optimization_barrier((w_other, near_parts[0]))
    w_pair = jnp.concatenate([w_out, w_other], 0)
    w_turns = [w_pair] + [
        lax.ppermute(w_pair, "grp", [(g, g ^ k) for g in range(8)]) for k in (1, 2, 3)
    ]

    parts = {}
    last = 0
    for call in NEAR_CALLS[1:]:
        queries[call[0]], near_parts[last], kv_far[0] = lax.optimization_barrier(
            (queries[call[0]], near_parts[last], kv_far[0])
        )
        near_parts.update(zip(call, attend(call, seq, codes, spots, near, [queries[by] for by in call])))
        last = call[-1]
    kv_far, near_parts[last] = lax.optimization_barrier((kv_far, near_parts[last]))
    far = prepare(*kv_far)
    last = None
    for call in FAR_CALLS:
        if last is not None:
            queries[call[0]], parts[last] = lax.optimization_barrier((queries[call[0]], parts[last]))
        done = attend(
            call, seq, codes, spots, far, [queries[by] for by in call], [near_parts[by] for by in call]
        )
        parts.update(zip(call, done))
        last = call[-1]

    parts = [part if by == 0 else lax.ppermute(part, "seq", along_x(by)) for by, part in parts.items()]
    parts, w_turns = lax.optimization_barrier((parts, w_turns))
    pieces = combine(core, parts)
    owners = [[(4 * x + 2 * y + c) * 8 + g for c in range(2) for g in range(8)] for x in range(4) for y in range(2)]
    pieces = lax.all_to_all(pieces, ("seq", "grp"), 0, 0, axis_index_groups=owners)
    return finish(grp, pieces, w_turns)


def solution(mesh):
    return jax.shard_map(
        body,
        mesh=mesh,
        in_specs=(
            P("seq", None),
            P("seq", None),
            P(None, "grp"),
            P(None, "grp"),
            P(None, "grp"),
            P("grp", None),
            P(),
            P(),
        ),
        out_specs=P(("seq", "grp"), None),
        check_vma=False,
    )
```

```python
import functools

import jax
import jax.numpy as jnp
from jax import lax
from jax.experimental import pallas as pl
from jax.experimental.pallas import tpu as pltpu
from jax.sharding import PartitionSpec as P

HS = 64
BLOCK = 128
TILES = 4
SLOTS = 2
ROWS = 2 * BLOCK
FAR = 64
KEY_BLOCKS = 32
ACC_ROWS = 72
LOG2E = 1.4426950408889634
SAFE_SCORE = 60.0
masked_score = -1e30
lowest_max = -1e29
SMEM = pl.BlockSpec(memory_space=pltpu.SMEM)
VMEM = pl.BlockSpec(memory_space=pltpu.VMEM)


def in_hbm(*arrays):
    return [pltpu.with_memory_space_constraint(a, pltpu.HBM) for a in arrays]


def list_work(me, pos_ref, mask_ref, code_ref):
    half = KEY_BLOCKS // 2
    both = 2 * KEY_BLOCKS
    blocks = pos_ref.shape[0]

    def held(t):
        source = jnp.bitwise_xor(me, lax.shift_right_logical(t, 4))
        return source * half + jnp.bitwise_and(t, half - 1)

    spots = pos_ref[...].T
    own_block = lax.shift_right_logical(spots, 7)
    furthest = jnp.max(own_block, axis=0, keepdims=True)
    t_rows = lax.broadcasted_iota(jnp.int32, (both, blocks), 0)
    own = jnp.zeros((both, blocks), jnp.int32)
    for t in range(both):
        found = jnp.max((own_block == held(jnp.int32(t))).astype(jnp.int32), axis=0, keepdims=True)
        own = jnp.where(t_rows == t, found, own)

    def exact(condition):
        return condition.astype(jnp.float32).astype(jnp.bfloat16)

    columns = mask_ref.shape[1]
    pick = exact(
        lax.broadcasted_iota(jnp.int32, (both, columns), 1)
        == held(lax.broadcasted_iota(jnp.int32, (both, columns), 0))
    )
    listed = lax.dot_general(
        pick, exact(mask_ref[...] == 1), (((1,), (1,)), ((), ())), preferred_element_type=jnp.float32
    )
    active = exact((own > 0) | ((listed > 0.5) & (held(t_rows) <= furthest)))
    listed = exact(listed > 0.5)

    row = lax.broadcasted_iota(jnp.int32, (blocks, BLOCK), 0)
    col = lax.broadcasted_iota(jnp.int32, (blocks, BLOCK), 1)
    first, second = exact(row == 2 * col), exact(row == 2 * col + 1)
    active = jnp.dot(active, first + second, preferred_element_type=jnp.float32) > 0.5
    listed = [jnp.dot(listed, pairs, preferred_element_type=jnp.float32).astype(jnp.int32) for pairs in (first, second)]
    row = lax.broadcasted_iota(jnp.int32, (both, both), 0)
    col = lax.broadcasted_iota(jnp.int32, (both, both), 1)
    earlier = exact((col < row) & (lax.shift_right_logical(row, 5) == lax.shift_right_logical(col, 5)))
    place = jnp.dot(earlier, exact(active), preferred_element_type=jnp.float32).astype(jnp.int32)
    t_rows = lax.broadcasted_iota(jnp.int32, (both, BLOCK), 0)
    value = jnp.bitwise_and(t_rows, KEY_BLOCKS - 1) + KEY_BLOCKS * (listed[0] + 2 * listed[1] + 4)
    packed = jnp.where(active, place * 512 + value, -1)
    ones = active.astype(jnp.int32)
    slot_rows = lax.broadcasted_iota(jnp.int32, (KEY_BLOCKS, BLOCK), 0)
    tables = []
    for n in range(2):
        codes = jnp.zeros((KEY_BLOCKS, BLOCK), jnp.int32)
        for t in range(n * KEY_BLOCKS, (n + 1) * KEY_BLOCKS):
            one = packed[t : t + 1, :]
            codes = jnp.where(lax.shift_right_arithmetic(one, 9) == slot_rows, jnp.bitwise_and(one, 511), codes)
        count = jnp.sum(ones[n * KEY_BLOCKS : (n + 1) * KEY_BLOCKS], axis=0, keepdims=True)
        slots = jnp.maximum(lax.shift_right_logical(count + (TILES - 1), 2), 1)
        tables += [codes, jnp.broadcast_to(slots, (FAR - KEY_BLOCKS, BLOCK))]
    code_ref[...] = jnp.concatenate(tables, 0).T[: code_ref.shape[0]]


def front_kernel(seq_ref, lat_hbm, x_hbm, wq_hbm, wk_hbm, wv_hbm, pos_hbm, mask_hbm, *rest):
    pair_hbm, theirs_hbm, own_hbm, other_hbm, code_hbm = rest[:5]
    lat, x, wq, wk, wv, pos, mask, pair_ref, theirs_ref, own_ref, other_ref, code_ref = rest[5:17]
    w_all, sems, x_sems, out_sems = rest[17:]
    sent = []

    def send(source, target):
        sent.append(pltpu.make_async_copy(source, target, out_sems.at[len(sent)]))
        sent[-1].start()

    small = [
        pltpu.make_async_copy(source, target, sems.at[i])
        for i, (source, target) in enumerate(
            [(pos_hbm, pos), (mask_hbm, mask), (wq_hbm, wq), (lat_hbm, lat), (wk_hbm, wk), (wv_hbm, wv)]
        )
    ]
    rows = x.shape[0] // x_sems.shape[0]
    parts = [pl.ds(i * rows, rows) for i in range(x_sems.shape[0])]
    large = [pltpu.make_async_copy(x_hbm.at[p], x.at[p], x_sems.at[i]) for i, p in enumerate(parts)]
    for copy in small + large:
        copy.start()
    got_pos, got_mask, got_wq, got_lat, got_wk, got_wv = small
    first = jnp.bitwise_and(seq_ref[0], 1) == 0

    got_pos.wait()
    got_mask.wait()
    list_work(seq_ref[0], pos, mask, code_ref)
    send(code_ref, code_hbm)

    got_wq.wait()
    got_lat.wait()
    q = jnp.dot(lat[...], wq[...], preferred_element_type=jnp.float32).T
    q = q.astype(jnp.bfloat16) * jnp.bfloat16(HS ** -0.5)
    mine = jnp.where(first, q[:HS], q[HS:])
    pair_ref[0] = mine
    pair_ref[1] = mine
    theirs_ref[...] = jnp.where(first, q[HS:], q[:HS])
    send(pair_ref, pair_hbm)
    send(theirs_ref, theirs_hbm)

    got_wk.wait()
    got_wv.wait()
    k, v = wk[...], wv[...]
    head_0 = jnp.concatenate([k[:, :HS], v[:, :HS]], 1)
    head_1 = jnp.concatenate([k[:, HS:], v[:, HS:]], 1)
    w_all[:, : 2 * HS] = jnp.where(first, head_0, head_1)
    w_all[:, 2 * HS :] = jnp.where(first, head_1, head_0)
    for copy, part in zip(large, parts):
        copy.wait()
        both = jnp.dot(x[part, :], w_all[...], preferred_element_type=jnp.float32).astype(jnp.bfloat16)
        own_ref[part, :] = both[:, : 2 * HS]
        other_ref[part, :] = both[:, 2 * HS :]
        send(own_ref.at[part], own_hbm.at[part])
        send(other_ref.at[part], other_hbm.at[part])
    for copy in sent:
        copy.wait()


def front(seq, latents, inputs, w_query, w_key, w_value, positions, block_mask):
    rows, width = latents.shape
    keys = inputs.shape[0]
    spots = positions.reshape(-1, BLOCK)
    operands = (latents, inputs, w_query, w_key, w_value, spots, block_mask)
    q = jax.ShapeDtypeStruct((HS, rows), jnp.bfloat16)
    kv = jax.ShapeDtypeStruct((keys, 2 * HS), jnp.bfloat16)
    results = [jax.ShapeDtypeStruct((2, HS, rows), jnp.bfloat16), q, kv, kv, jax.ShapeDtypeStruct((spots.shape[0] // 2, BLOCK), jnp.int32)]
    return pl.pallas_call(
        front_kernel,
        in_specs=[SMEM] + [pl.BlockSpec(memory_space=pl.ANY)] * len(operands),
        out_specs=[pl.BlockSpec(memory_space=pl.ANY)] * 5,
        out_shape=results,
        scratch_shapes=[pltpu.VMEM(a.shape, a.dtype) for a in (*operands, *results)]
        + [
            pltpu.VMEM((width, 4 * HS), jnp.bfloat16),
            pltpu.SemaphoreType.DMA((6,)),
            pltpu.SemaphoreType.DMA((4,)),
            pltpu.SemaphoreType.DMA((11,)),
        ],
        compiler_params=pltpu.CompilerParams(vmem_limit_bytes=24 * 2**20),
        cost_estimate=pl.CostEstimate(
            flops=2 * (keys * 4 + rows * 2) * width * HS, bytes_accessed=6 * 2**20, transcendentals=0
        ),
    )(seq, *in_hbm(*operands))


def prepare_kernel(*refs):
    sources, (kv_ref, vt_ref, norm_ref) = refs[:-3], refs[-3:]
    each = KEY_BLOCKS // len(sources)
    most = None
    for t in range(KEY_BLOCKS):
        at = t % each
        tile = sources[t // each][at * BLOCK : (at + 1) * BLOCK, :]
        kv_ref[t * BLOCK : (t + 1) * BLOCK, :] = tile
        turned = tile.T
        vt_ref[:HS, t * BLOCK : (t + 1) * BLOCK] = turned[HS:, :]
        k = turned[:HS, :].astype(jnp.float32)
        squares = jnp.sum(k * k, axis=0, keepdims=True)
        most = squares if most is None else jnp.maximum(most, squares)
    vt_ref[HS:, :] = jnp.ones((ACC_ROWS - HS, KEY_BLOCKS * BLOCK), jnp.bfloat16)
    norm_ref[0] = jnp.max(most)


def prepare(*sources):
    keys = sum(source.shape[0] for source in sources)
    return pl.pallas_call(
        prepare_kernel,
        in_specs=[VMEM] * len(sources),
        out_specs=[VMEM, VMEM, SMEM],
        out_shape=[
            jax.ShapeDtypeStruct((keys, 2 * HS), jnp.bfloat16),
            jax.ShapeDtypeStruct((ACC_ROWS, keys), jnp.bfloat16),
            jax.ShapeDtypeStruct((1,), jnp.float32),
        ],
        compiler_params=pltpu.CompilerParams(vmem_limit_bytes=24 * 2**20),
    )(*sources)


def attention_kernel(steps, far, seq_ref, code_ref, norm_ref, pos_ref, kv_ref, vt_ref, *rest):
    chips = len(steps)
    q_refs, rest = rest[:chips], rest[chips:]
    before_refs, rest = (rest[:chips], rest[chips:]) if far else (None, rest)
    o_refs, (q_all, p_a, p_b, s_all, acc) = rest[:chips], rest[chips:]
    table = FAR if far else 0
    blocks = 4 * chips
    me = seq_ref[0]
    keys_of = jnp.bitwise_xor(me, 2) if far else me
    own_base = keys_of * (KEY_BLOCKS // 2 * BLOCK)
    partner_base = jnp.bitwise_xor(keys_of, 1) * (KEY_BLOCKS // 2 * BLOCK)
    sources = [came_from(me, step) for step in steps]
    iota = lax.broadcasted_iota(jnp.int32, (BLOCK, ROWS), 0)
    in_first = lax.broadcasted_iota(jnp.int32, (1, ROWS), 1) < BLOCK
    iota_half = iota.astype(jnp.float32).astype(jnp.bfloat16)

    most = None
    for i, ref in enumerate(q_refs):
        for j in range(ref.shape[0]):
            q = ref[j]
            q_all[i * ref.shape[0] + j] = q
            q = q.astype(jnp.float32)
            squares = jnp.sum(q * q, axis=0, keepdims=True)
            most = squares if most is None else jnp.maximum(most, squares)
    safe = jnp.max(most) * norm_ref[0] <= SAFE_SCORE * SAFE_SCORE

    def clamp(r):
        return jnp.minimum(r, blocks - 1)

    def whole_block(r):
        shard = sources[-1]
        for i in range(chips - 1):
            shard = jnp.where(lax.div(r, 4) == i, sources[i], shard)
        return jnp.bitwise_xor(shard, jnp.bitwise_and(lax.div(r, 2), 1)) * 2 + lax.rem(r, 2)

    def offset(i):
        return pl.multiple_of(i * BLOCK, BLOCK)

    def row_offset(i):
        return pl.multiple_of(i * ROWS, ROWS)

    def query(r):
        q = q_all[lax.div(r, 2), :, pl.ds(row_offset(lax.rem(r, 2)), ROWS)]
        return jnp.concatenate([q, jnp.zeros_like(q)], 0)

    def key_blocks(row, c):
        return [jnp.bitwise_and(code_ref[row, table + c * TILES + t], KEY_BLOCKS - 1) for t in range(TILES)]

    def products(row, r, c):
        keys = jnp.concatenate([kv_ref[pl.ds(offset(k), BLOCK), :] for k in key_blocks(row, c)], 0)
        return jnp.dot(keys, query(r), preferred_element_type=jnp.float32)

    def values(row, c):
        return jnp.concatenate([vt_ref[:, pl.ds(offset(k), BLOCK)] for k in key_blocks(row, c)], 1)

    def last_key(row, c, t, pos, real):
        code = code_ref[row, table + c * TILES + t]
        k = jnp.bitwise_and(code, KEY_BLOCKS - 1)
        half = KEY_BLOCKS // 2
        base = jnp.where(k < half, own_base, partner_base - half * BLOCK) + k * BLOCK
        real = jnp.logical_and(real, code >= 4 * KEY_BLOCKS)
        reach = [jnp.where(jnp.bitwise_and(code, n * KEY_BLOCKS) > 0, 1 << 30, BLOCK) for n in (1, 2)]
        reach = jnp.where(in_first, *[jnp.where(real, n, -(1 << 30)) for n in reach])
        ahead = pos - base
        return jnp.where(ahead < reach, jnp.minimum(ahead, BLOCK - 1), -1)

    def put(i, rr, a, top):
        at = (lax.div(rr, 2), slice(None), pl.ds(row_offset(lax.rem(rr, 2)), ROWS))
        if far:
            before = before_refs[i][at].astype(jnp.float32)
            top_before, top_now = before[HS + 1 : HS + 2], top
            top = jnp.maximum(top_before, top_now)
            shrink, shrink_before = jnp.exp(top_now - top), jnp.exp(top_before - top)
            total = a[HS : HS + 1] * shrink + (before[HS : HS + 1] + before[HS + 2 : HS + 3]) * shrink_before
            a = a * shrink + before * shrink_before
        else:
            total = a[HS : HS + 1]
        low = total - total.astype(jnp.bfloat16).astype(jnp.float32)
        out = jnp.concatenate([a[:HS], total, top, low, a[HS + 3 :]], 0)
        o_refs[i][at] = out.astype(jnp.bfloat16)

    def advance(r, c):
        last = c + 1 >= code_ref[whole_block(clamp(r)), table + KEY_BLOCKS]
        return jnp.where(last, jnp.minimum(r + 1, blocks), r), jnp.where(last, 0, c + 1)

    def step_slots(r, c):
        slots = []
        for _ in range(SLOTS):
            slots.append((r, c))
            r, c = advance(r, c)
        return slots, r, c

    @pl.when(safe)
    def _():
        acc[...] = jnp.zeros_like(acc)

        def weigh(p_ref, slots):
            for g, (r, c) in enumerate(slots):
                rr = clamp(r)
                row = whole_block(rr)
                s = products(row, rr, c)
                pos = pos_ref[pl.ds(row, 1), :]
                for t in range(TILES):
                    p = jnp.exp2(s[t * BLOCK : (t + 1) * BLOCK] * LOG2E).astype(jnp.bfloat16)
                    last = last_key(row, c, t, pos, r < blocks).astype(jnp.float32).astype(jnp.bfloat16)
                    at = (g * TILES + t) * BLOCK
                    p_ref[at : at + BLOCK, :] = jnp.where(iota_half <= last, p, jnp.zeros_like(p))

        def add(p_ref, slots):
            for g, (r, c) in enumerate(slots):
                v = values(whole_block(clamp(r)), c)
                at = g * TILES * BLOCK
                acc[r] += jnp.dot(v, p_ref[at : at + TILES * BLOCK, :], preferred_element_type=jnp.float32)

        slots_0, r0, c0 = step_slots(jnp.int32(0), jnp.int32(0))
        weigh(p_a, slots_0)

        def two_steps(_, state):
            r, c, r1, c1 = state
            slots, _, _ = step_slots(r, c)
            slots_1, r2, c2 = step_slots(r1, c1)
            weigh(p_b, slots_1)
            add(p_a, slots)
            slots_2, r3, c3 = step_slots(r2, c2)
            weigh(p_a, slots_2)
            add(p_b, slots_1)
            return r2, c2, r3, c3

        items = lax.fori_loop(0, blocks, lambda r, n: n + code_ref[whole_block(r), table + KEY_BLOCKS], jnp.int32(0))
        turns = lax.div(items + (2 * SLOTS - 1), 2 * SLOTS)
        lax.fori_loop(0, turns, two_steps, (jnp.int32(0), jnp.int32(0), r0, c0))

        for i in range(chips):
            def finish(rr, _, i=i):
                a = acc[i * 4 + rr]
                put(i, rr, a, jnp.where(a[HS : HS + 1] > 0, 0.0, lowest_max))
                return 0

            lax.fori_loop(0, 4, finish, 0)

    @pl.when(jnp.logical_not(safe))
    def _():
        for i in range(chips):
            def one_block(rr, _, i=i):
                r = i * 4 + rr
                row = whole_block(r)
                pos = pos_ref[pl.ds(row, 1), :]
                acc[0] = jnp.zeros((ACC_ROWS, ROWS), jnp.float32)

                def one_slot(c, top):
                    s = products(row, r, c)
                    best = top
                    for t in range(TILES):
                        tile = s[t * BLOCK : (t + 1) * BLOCK]
                        tile = jnp.where(iota <= last_key(row, c, t, pos, True), tile, masked_score)
                        s_all[t * BLOCK : (t + 1) * BLOCK, :] = tile
                        best = jnp.maximum(best, jnp.max(tile, 0, keepdims=True))
                    best = best.astype(jnp.bfloat16).astype(jnp.float32)
                    p = jnp.exp2((s_all[...] - best) * LOG2E).astype(jnp.bfloat16)
                    shrink = jnp.exp2((top - best) * LOG2E)
                    acc[0] = acc[0] * shrink + jnp.dot(values(row, c), p, preferred_element_type=jnp.float32)
                    return best

                start = jnp.full((1, ROWS), lowest_max, jnp.bfloat16).astype(jnp.float32)
                top = lax.fori_loop(0, code_ref[row, table + KEY_BLOCKS], one_slot, start)
                put(i, rr, acc[0], top)
                return 0

            lax.fori_loop(0, 4, one_block, 0)


def attend(steps, seq, codes, spots, held, queries, before=()):
    kv, vt, norm = held
    chips = len(steps)
    out = jax.ShapeDtypeStruct((2, ACC_ROWS, queries[0].shape[2]), jnp.bfloat16)
    return pl.pallas_call(
        functools.partial(attention_kernel, steps, bool(before)),
        in_specs=[SMEM] * 3 + [VMEM] * (3 + len(queries) + len(before)),
        out_specs=[VMEM] * chips,
        out_shape=[out] * chips,
        scratch_shapes=[
            pltpu.VMEM((2 * chips, HS, queries[0].shape[2]), jnp.bfloat16),
            pltpu.VMEM((SLOTS * TILES * BLOCK, ROWS), jnp.bfloat16),
            pltpu.VMEM((SLOTS * TILES * BLOCK, ROWS), jnp.bfloat16),
            pltpu.VMEM((TILES * BLOCK, ROWS), jnp.float32),
            pltpu.VMEM((4 * chips + 1, ACC_ROWS, ROWS), jnp.float32),
        ],
        compiler_params=pltpu.CompilerParams(vmem_limit_bytes=32 * 2**20),
        cost_estimate=pl.CostEstimate(
            flops=chips * 6 * 10**9, bytes_accessed=4 * 2**20, transcendentals=chips * 2**20
        ),
    )(seq, codes, norm, spots, kv, vt, *queries, *before)


def combine_kernel(core_ref, *refs):
    parts, out_ref = refs[:-1], refs[-1]
    groups = out_ref.shape[0] // 2
    half = out_ref.shape[1]
    for j in range(2):
        tops = [p[j, HS + 1 : HS + 2, :].astype(jnp.float32) for p in parts]
        top = functools.reduce(jnp.maximum, tops)
        scales = [jnp.exp(t - top) for t in tops]
        total = sum(
            (p[j, HS : HS + 1, :].astype(jnp.float32) + p[j, HS + 2 : HS + 3, :].astype(jnp.float32)) * scale
            for p, scale in zip(parts, scales)
        )
        summed = sum(p[j, :HS, :].astype(jnp.float32) * scale for p, scale in zip(parts, scales))
        rows = (summed / total).T.astype(jnp.bfloat16)
        first = jnp.bitwise_xor(core_ref[0], j) * groups
        for g in range(groups):
            upper = rows[2 * g * half : (2 * g + 1) * half]
            lower = rows[(2 * g + 1) * half : (2 * g + 2) * half]
            out_ref[first + g] = jnp.concatenate([upper, lower], 1)


def combine(core, parts):
    half = parts[0].shape[2] // 16
    return pl.pallas_call(
        combine_kernel,
        in_specs=[SMEM] + [VMEM] * len(parts),
        out_specs=VMEM,
        out_shape=jax.ShapeDtypeStruct((16, half, 2 * HS), jnp.bfloat16),
        compiler_params=pltpu.CompilerParams(vmem_limit_bytes=32 * 2**20),
    )(core, *parts)


def finish_kernel(grp_ref, pieces_ref, *refs):
    w_refs, out_ref = refs[:-1], refs[-1]
    groups = pieces_ref.shape[0] // 2
    me = grp_ref[0]
    result = None
    for k, w_ref in enumerate(w_refs):
        near = jnp.bitwise_xor(me, k)
        order = [c * groups + g for g in (near, jnp.bitwise_xor(near, 4)) for c in range(2)]
        blocks = [pieces_ref[i] for i in order]
        upper = jnp.concatenate([p[:, :HS] for p in blocks], 1)
        lower = jnp.concatenate([p[:, HS:] for p in blocks], 1)
        attention = jnp.concatenate([upper, lower], 0)
        term = jnp.dot(attention, w_ref[...], preferred_element_type=jnp.float32)
        result = term if result is None else result + term
    out_ref[...] = result.astype(jnp.bfloat16)


def finish(grp, pieces, w_turns):
    return pl.pallas_call(
        finish_kernel,
        in_specs=[SMEM] + [VMEM] * (1 + len(w_turns)),
        out_specs=VMEM,
        out_shape=jax.ShapeDtypeStruct((2 * pieces.shape[1], w_turns[0].shape[1]), jnp.bfloat16),
        compiler_params=pltpu.CompilerParams(vmem_limit_bytes=24 * 2**20),
    )(grp, pieces, *w_turns)


def along_x(by):
    return [(s, s ^ (4 * by)) for s in range(16)]


def came_from(s, by):
    return jnp.bitwise_xor(s, 4 * by)


NEAR_CALLS = ((0,), (1, 3, 2))
FAR_CALLS = ((2, 1, 3), (0,))
CORE_SWAP = [(s, s ^ 1) for s in range(16)]
Y_SWAP = [(s, s ^ 2) for s in range(16)]


def body(inputs, latents, w_query, w_key, w_value, w_out, positions, block_mask):
    seq = lax.axis_index("seq")[None]
    grp = lax.axis_index("grp")[None]
    core = jnp.bitwise_and(seq, 1)

    w_other = lax.ppermute(w_out, "grp", [(g, g ^ 4) for g in range(8)])
    q_chip, theirs, kv_own, kv_other, codes = front(
        seq, latents, inputs, w_query, w_key, w_value, positions, block_mask
    )
    theirs, kv_other, kv_own, w_other = lax.optimization_barrier((theirs, kv_other, kv_own, w_other))
    q_chip = q_chip.at[1].set(lax.ppermute(theirs, "seq", CORE_SWAP))
    queries = {by: q_chip if by == 0 else lax.ppermute(q_chip, "seq", along_x(by)) for by in (0, 1, 3, 2)}
    kv_partner = lax.ppermute(kv_other, "seq", CORE_SWAP)
    near = prepare(kv_own, kv_partner)
    kv_far = [lax.ppermute(kv, "seq", Y_SWAP) for kv in (kv_own, kv_partner)]

    spots = positions.reshape(-1, ROWS)
    near_parts = dict(zip(NEAR_CALLS[0], attend(NEAR_CALLS[0], seq, codes, spots, near, [q_chip])))
    w_other, near_parts[0] = lax.optimization_barrier((w_other, near_parts[0]))
    w_pair = jnp.concatenate([w_out, w_other], 0)
    w_turns = [w_pair] + [
        lax.ppermute(w_pair, "grp", [(g, g ^ k) for g in range(8)]) for k in (1, 2, 3)
    ]

    parts = {}
    last = 0
    for call in NEAR_CALLS[1:]:
        queries[call[0]], near_parts[last], kv_far[0] = lax.optimization_barrier(
            (queries[call[0]], near_parts[last], kv_far[0])
        )
        near_parts.update(zip(call, attend(call, seq, codes, spots, near, [queries[by] for by in call])))
        last = call[-1]
    kv_far, near_parts[last] = lax.optimization_barrier((kv_far, near_parts[last]))
    far = prepare(*kv_far)
    last = None
    for call in FAR_CALLS:
        if last is not None:
            queries[call[0]], parts[last] = lax.optimization_barrier((queries[call[0]], parts[last]))
        done = attend(
            call, seq, codes, spots, far, [queries[by] for by in call], [near_parts[by] for by in call]
        )
        parts.update(zip(call, done))
        last = call[-1]

    parts = [part if by == 0 else lax.ppermute(part, "seq", along_x(by)) for by, part in parts.items()]
    parts, w_turns = lax.optimization_barrier((parts, w_turns))
    pieces = combine(core, parts)
    owners = [[(4 * x + 2 * y + c) * 8 + g for c in range(2) for g in range(8)] for x in range(4) for y in range(2)]
    pieces = lax.all_to_all(pieces, ("seq", "grp"), 0, 0, axis_index_groups=owners)
    return finish(grp, pieces, w_turns)


def solution(mesh):
    return jax.shard_map(
        body,
        mesh=mesh,
        in_specs=(
            P("seq", None),
            P("seq", None),
            P(None, "grp"),
            P(None, "grp"),
            P(None, "grp"),
            P("grp", None),
            P(),
            P(),
        ),
        out_specs=P(("seq", "grp"), None),
        check_vma=False,
    )
```

```python
import functools

import jax
import jax.numpy as jnp
from jax import lax
from jax.experimental import pallas as pl
from jax.experimental.pallas import tpu as pltpu
from jax.sharding import PartitionSpec as P

HS = 64
BLOCK = 128
TILES = 4
SLOTS = 2
ROWS = 2 * BLOCK
FAR = 64
KEY_BLOCKS = 32
ACC_ROWS = 72
LOG2E = 1.4426950408889634
SAFE_SCORE = 60.0
masked_score = -1e30
lowest_max = -1e29
SMEM = pl.BlockSpec(memory_space=pltpu.SMEM)
VMEM = pl.BlockSpec(memory_space=pltpu.VMEM)


def in_hbm(*arrays):
    return [pltpu.with_memory_space_constraint(a, pltpu.HBM) for a in arrays]


def list_work(me, pos_ref, mask_ref, code_ref):
    half = KEY_BLOCKS // 2
    both = 2 * KEY_BLOCKS
    blocks = pos_ref.shape[0]

    def held(t):
        source = jnp.bitwise_xor(me, lax.shift_right_logical(t, 4))
        return source * half + jnp.bitwise_and(t, half - 1)

    spots = pos_ref[...].T
    own_block = lax.shift_right_logical(spots, 7)
    furthest = jnp.max(own_block, axis=0, keepdims=True)
    t_rows = lax.broadcasted_iota(jnp.int32, (both, blocks), 0)
    own = jnp.zeros((both, blocks), jnp.int32)
    for t in range(both):
        found = jnp.max((own_block == held(jnp.int32(t))).astype(jnp.int32), axis=0, keepdims=True)
        own = jnp.where(t_rows == t, found, own)

    def exact(condition):
        return condition.astype(jnp.float32).astype(jnp.bfloat16)

    columns = mask_ref.shape[1]
    pick = exact(
        lax.broadcasted_iota(jnp.int32, (both, columns), 1)
        == held(lax.broadcasted_iota(jnp.int32, (both, columns), 0))
    )
    listed = lax.dot_general(
        pick, exact(mask_ref[...] == 1), (((1,), (1,)), ((), ())), preferred_element_type=jnp.float32
    )
    active = exact((own > 0) | ((listed > 0.5) & (held(t_rows) <= furthest)))
    listed = exact(listed > 0.5)

    row = lax.broadcasted_iota(jnp.int32, (blocks, BLOCK), 0)
    col = lax.broadcasted_iota(jnp.int32, (blocks, BLOCK), 1)
    first, second = exact(row == 2 * col), exact(row == 2 * col + 1)
    active = jnp.dot(active, first + second, preferred_element_type=jnp.float32) > 0.5
    listed = [jnp.dot(listed, pairs, preferred_element_type=jnp.float32).astype(jnp.int32) for pairs in (first, second)]
    row = lax.broadcasted_iota(jnp.int32, (both, both), 0)
    col = lax.broadcasted_iota(jnp.int32, (both, both), 1)
    earlier = exact((col < row) & (lax.shift_right_logical(row, 5) == lax.shift_right_logical(col, 5)))
    place = jnp.dot(earlier, exact(active), preferred_element_type=jnp.float32).astype(jnp.int32)
    t_rows = lax.broadcasted_iota(jnp.int32, (both, BLOCK), 0)
    value = jnp.bitwise_and(t_rows, KEY_BLOCKS - 1) + KEY_BLOCKS * (listed[0] + 2 * listed[1] + 4)
    packed = jnp.where(active, place * 512 + value, -1)
    ones = active.astype(jnp.int32)
    slot_rows = lax.broadcasted_iota(jnp.int32, (KEY_BLOCKS, BLOCK), 0)
    tables = []
    for n in range(2):
        codes = jnp.zeros((KEY_BLOCKS, BLOCK), jnp.int32)
        for t in range(n * KEY_BLOCKS, (n + 1) * KEY_BLOCKS):
            one = packed[t : t + 1, :]
            codes = jnp.where(lax.shift_right_arithmetic(one, 9) == slot_rows, jnp.bitwise_and(one, 511), codes)
        count = jnp.sum(ones[n * KEY_BLOCKS : (n + 1) * KEY_BLOCKS], axis=0, keepdims=True)
        slots = jnp.maximum(lax.shift_right_logical(count + (TILES - 1), 2), 1)
        tables += [codes, jnp.broadcast_to(slots, (FAR - KEY_BLOCKS, BLOCK))]
    code_ref[...] = jnp.concatenate(tables, 0).T[: code_ref.shape[0]]


def front_kernel(seq_ref, lat_hbm, x_hbm, wq_hbm, wk_hbm, wv_hbm, pos_hbm, mask_hbm, *rest):
    pair_hbm, theirs_hbm, own_hbm, other_hbm, code_hbm = rest[:5]
    lat, x, wq, wk, wv, pos, mask, pair_ref, theirs_ref, own_ref, other_ref, code_ref = rest[5:17]
    w_all, sems, x_sems, out_sems = rest[17:]
    sent = []

    def send(source, target):
        sent.append(pltpu.make_async_copy(source, target, out_sems.at[len(sent)]))
        sent[-1].start()

    small = [
        pltpu.make_async_copy(source, target, sems.at[i])
        for i, (source, target) in enumerate(
            [(pos_hbm, pos), (mask_hbm, mask), (wq_hbm, wq), (lat_hbm, lat), (wk_hbm, wk), (wv_hbm, wv)]
        )
    ]
    rows = x.shape[0] // x_sems.shape[0]
    parts = [pl.ds(i * rows, rows) for i in range(x_sems.shape[0])]
    large = [pltpu.make_async_copy(x_hbm.at[p], x.at[p], x_sems.at[i]) for i, p in enumerate(parts)]
    for copy in small + large:
        copy.start()
    got_pos, got_mask, got_wq, got_lat, got_wk, got_wv = small
    first = jnp.bitwise_and(seq_ref[0], 1) == 0

    got_pos.wait()
    got_mask.wait()
    list_work(seq_ref[0], pos, mask, code_ref)
    send(code_ref, code_hbm)

    got_wq.wait()
    got_lat.wait()
    q = jnp.dot(lat[...], wq[...], preferred_element_type=jnp.float32).T
    q = q.astype(jnp.bfloat16) * jnp.bfloat16(HS ** -0.5)
    mine = jnp.where(first, q[:HS], q[HS:])
    pair_ref[0] = mine
    pair_ref[1] = mine
    theirs_ref[...] = jnp.where(first, q[HS:], q[:HS])
    send(pair_ref, pair_hbm)
    send(theirs_ref, theirs_hbm)

    got_wk.wait()
    got_wv.wait()
    k, v = wk[...], wv[...]
    head_0 = jnp.concatenate([k[:, :HS], v[:, :HS]], 1)
    head_1 = jnp.concatenate([k[:, HS:], v[:, HS:]], 1)
    w_all[:, : 2 * HS] = jnp.where(first, head_0, head_1)
    w_all[:, 2 * HS :] = jnp.where(first, head_1, head_0)
    for copy, part in zip(large, parts):
        copy.wait()
        both = jnp.dot(x[part, :], w_all[...], preferred_element_type=jnp.float32).astype(jnp.bfloat16)
        own_ref[part, :] = both[:, : 2 * HS]
        other_ref[part, :] = both[:, 2 * HS :]
        send(own_ref.at[part], own_hbm.at[part])
        send(other_ref.at[part], other_hbm.at[part])
    for copy in sent:
        copy.wait()


def front(seq, latents, inputs, w_query, w_key, w_value, positions, block_mask):
    rows, width = latents.shape
    keys = inputs.shape[0]
    spots = positions.reshape(-1, BLOCK)
    operands = (latents, inputs, w_query, w_key, w_value, spots, block_mask)
    q = jax.ShapeDtypeStruct((HS, rows), jnp.bfloat16)
    kv = jax.ShapeDtypeStruct((keys, 2 * HS), jnp.bfloat16)
    results = [jax.ShapeDtypeStruct((2, HS, rows), jnp.bfloat16), q, kv, kv, jax.ShapeDtypeStruct((spots.shape[0] // 2, BLOCK), jnp.int32)]
    return pl.pallas_call(
        front_kernel,
        in_specs=[SMEM] + [pl.BlockSpec(memory_space=pl.ANY)] * len(operands),
        out_specs=[pl.BlockSpec(memory_space=pl.ANY)] * 5,
        out_shape=results,
        scratch_shapes=[pltpu.VMEM(a.shape, a.dtype) for a in (*operands, *results)]
        + [
            pltpu.VMEM((width, 4 * HS), jnp.bfloat16),
            pltpu.SemaphoreType.DMA((6,)),
            pltpu.SemaphoreType.DMA((1,)),
            pltpu.SemaphoreType.DMA((5,)),
        ],
        compiler_params=pltpu.CompilerParams(vmem_limit_bytes=24 * 2**20),
        cost_estimate=pl.CostEstimate(
            flops=2 * (keys * 4 + rows * 2) * width * HS, bytes_accessed=6 * 2**20, transcendentals=0
        ),
    )(seq, *in_hbm(*operands))


def prepare_kernel(*refs):
    sources, (kv_ref, vt_ref, norm_ref) = refs[:-3], refs[-3:]
    each = KEY_BLOCKS // len(sources)
    most = None
    for t in range(KEY_BLOCKS):
        at = t % each
        tile = sources[t // each][at * BLOCK : (at + 1) * BLOCK, :]
        kv_ref[t * BLOCK : (t + 1) * BLOCK, :] = tile
        turned = tile.T
        vt_ref[:HS, t * BLOCK : (t + 1) * BLOCK] = turned[HS:, :]
        k = turned[:HS, :].astype(jnp.float32)
        squares = jnp.sum(k * k, axis=0, keepdims=True)
        most = squares if most is None else jnp.maximum(most, squares)
    vt_ref[HS:, :] = jnp.ones((ACC_ROWS - HS, KEY_BLOCKS * BLOCK), jnp.bfloat16)
    norm_ref[0] = jnp.max(most)


def prepare(*sources):
    keys = sum(source.shape[0] for source in sources)
    return pl.pallas_call(
        prepare_kernel,
        in_specs=[VMEM] * len(sources),
        out_specs=[VMEM, VMEM, SMEM],
        out_shape=[
            jax.ShapeDtypeStruct((keys, 2 * HS), jnp.bfloat16),
            jax.ShapeDtypeStruct((ACC_ROWS, keys), jnp.bfloat16),
            jax.ShapeDtypeStruct((1,), jnp.float32),
        ],
        compiler_params=pltpu.CompilerParams(vmem_limit_bytes=24 * 2**20),
    )(*sources)


def attention_kernel(steps, far, seq_ref, code_ref, norm_ref, pos_ref, kv_ref, vt_ref, *rest):
    chips = len(steps)
    q_refs, rest = rest[:chips], rest[chips:]
    before_refs, rest = (rest[:chips], rest[chips:]) if far else (None, rest)
    o_refs, (q_all, p_a, p_b, s_all, acc) = rest[:chips], rest[chips:]
    table = FAR if far else 0
    blocks = 4 * chips
    me = seq_ref[0]
    keys_of = jnp.bitwise_xor(me, 2) if far else me
    own_base = keys_of * (KEY_BLOCKS // 2 * BLOCK)
    partner_base = jnp.bitwise_xor(keys_of, 1) * (KEY_BLOCKS // 2 * BLOCK)
    sources = [came_from(me, step) for step in steps]
    iota = lax.broadcasted_iota(jnp.int32, (BLOCK, ROWS), 0)
    in_first = lax.broadcasted_iota(jnp.int32, (1, ROWS), 1) < BLOCK
    iota_half = iota.astype(jnp.float32).astype(jnp.bfloat16)

    most = None
    for i, ref in enumerate(q_refs):
        for j in range(ref.shape[0]):
            q = ref[j]
            q_all[i * ref.shape[0] + j] = q
            q = q.astype(jnp.float32)
            squares = jnp.sum(q * q, axis=0, keepdims=True)
            most = squares if most is None else jnp.maximum(most, squares)
    safe = jnp.max(most) * norm_ref[0] <= SAFE_SCORE * SAFE_SCORE

    def clamp(r):
        return jnp.minimum(r, blocks - 1)

    def whole_block(r):
        shard = sources[-1]
        for i in range(chips - 1):
            shard = jnp.where(lax.div(r, 4) == i, sources[i], shard)
        return jnp.bitwise_xor(shard, jnp.bitwise_and(lax.div(r, 2), 1)) * 2 + lax.rem(r, 2)

    def offset(i):
        return pl.multiple_of(i * BLOCK, BLOCK)

    def row_offset(i):
        return pl.multiple_of(i * ROWS, ROWS)

    def query(r):
        q = q_all[lax.div(r, 2), :, pl.ds(row_offset(lax.rem(r, 2)), ROWS)]
        return jnp.concatenate([q, jnp.zeros_like(q)], 0)

    def key_blocks(row, c):
        return [jnp.bitwise_and(code_ref[row, table + c * TILES + t], KEY_BLOCKS - 1) for t in range(TILES)]

    def products(row, r, c):
        keys = jnp.concatenate([kv_ref[pl.ds(offset(k), BLOCK), :] for k in key_blocks(row, c)], 0)
        return jnp.dot(keys, query(r), preferred_element_type=jnp.float32)

    def values(row, c):
        return jnp.concatenate([vt_ref[:, pl.ds(offset(k), BLOCK)] for k in key_blocks(row, c)], 1)

    def last_key(row, c, t, pos, real):
        code = code_ref[row, table + c * TILES + t]
        k = jnp.bitwise_and(code, KEY_BLOCKS - 1)
        half = KEY_BLOCKS // 2
        base = jnp.where(k < half, own_base, partner_base - half * BLOCK) + k * BLOCK
        real = jnp.logical_and(real, code >= 4 * KEY_BLOCKS)
        reach = [jnp.where(jnp.bitwise_and(code, n * KEY_BLOCKS) > 0, 1 << 30, BLOCK) for n in (1, 2)]
        reach = jnp.where(in_first, *[jnp.where(real, n, -(1 << 30)) for n in reach])
        ahead = pos - base
        return jnp.where(ahead < reach, jnp.minimum(ahead, BLOCK - 1), -1)

    def put(i, rr, a, top):
        at = (lax.div(rr, 2), slice(None), pl.ds(row_offset(lax.rem(rr, 2)), ROWS))
        if far:
            before = before_refs[i][at].astype(jnp.float32)
            top_before, top_now = before[HS + 1 : HS + 2], top
            top = jnp.maximum(top_before, top_now)
            shrink, shrink_before = jnp.exp(top_now - top), jnp.exp(top_before - top)
            total = a[HS : HS + 1] * shrink + (before[HS : HS + 1] + before[HS + 2 : HS + 3]) * shrink_before
            a = a * shrink + before * shrink_before
        else:
            total = a[HS : HS + 1]
        low = total - total.astype(jnp.bfloat16).astype(jnp.float32)
        out = jnp.concatenate([a[:HS], total, top, low, a[HS + 3 :]], 0)
        o_refs[i][at] = out.astype(jnp.bfloat16)

    def advance(r, c):
        last = c + 1 >= code_ref[whole_block(clamp(r)), table + KEY_BLOCKS]
        return jnp.where(last, jnp.minimum(r + 1, blocks), r), jnp.where(last, 0, c + 1)

    def step_slots(r, c):
        slots = []
        for _ in range(SLOTS):
            slots.append((r, c))
            r, c = advance(r, c)
        return slots, r, c

    @pl.when(safe)
    def _():
        acc[...] = jnp.zeros_like(acc)

        def weigh(p_ref, slots):
            for g, (r, c) in enumerate(slots):
                rr = clamp(r)
                row = whole_block(rr)
                s = products(row, rr, c)
                pos = pos_ref[pl.ds(row, 1), :]
                for t in range(TILES):
                    p = jnp.exp2(s[t * BLOCK : (t + 1) * BLOCK] * LOG2E).astype(jnp.bfloat16)
                    last = last_key(row, c, t, pos, r < blocks).astype(jnp.float32).astype(jnp.bfloat16)
                    at = (g * TILES + t) * BLOCK
                    p_ref[at : at + BLOCK, :] = jnp.where(iota_half <= last, p, jnp.zeros_like(p))

        def add(p_ref, slots):
            for g, (r, c) in enumerate(slots):
                v = values(whole_block(clamp(r)), c)
                at = g * TILES * BLOCK
                acc[r] += jnp.dot(v, p_ref[at : at + TILES * BLOCK, :], preferred_element_type=jnp.float32)

        slots_0, r0, c0 = step_slots(jnp.int32(0), jnp.int32(0))
        weigh(p_a, slots_0)

        def two_steps(_, state):
            r, c, r1, c1 = state
            slots, _, _ = step_slots(r, c)
            slots_1, r2, c2 = step_slots(r1, c1)
            weigh(p_b, slots_1)
            add(p_a, slots)
            slots_2, r3, c3 = step_slots(r2, c2)
            weigh(p_a, slots_2)
            add(p_b, slots_1)
            return r2, c2, r3, c3

        items = lax.fori_loop(0, blocks, lambda r, n: n + code_ref[whole_block(r), table + KEY_BLOCKS], jnp.int32(0))
        turns = lax.div(items + (2 * SLOTS - 1), 2 * SLOTS)
        lax.fori_loop(0, turns, two_steps, (jnp.int32(0), jnp.int32(0), r0, c0))

        for i in range(chips):
            def finish(rr, _, i=i):
                a = acc[i * 4 + rr]
                put(i, rr, a, jnp.where(a[HS : HS + 1] > 0, 0.0, lowest_max))
                return 0

            lax.fori_loop(0, 4, finish, 0)

    @pl.when(jnp.logical_not(safe))
    def _():
        for i in range(chips):
            def one_block(rr, _, i=i):
                r = i * 4 + rr
                row = whole_block(r)
                pos = pos_ref[pl.ds(row, 1), :]
                acc[0] = jnp.zeros((ACC_ROWS, ROWS), jnp.float32)

                def one_slot(c, top):
                    s = products(row, r, c)
                    best = top
                    for t in range(TILES):
                        tile = s[t * BLOCK : (t + 1) * BLOCK]
                        tile = jnp.where(iota <= last_key(row, c, t, pos, True), tile, masked_score)
                        s_all[t * BLOCK : (t + 1) * BLOCK, :] = tile
                        best = jnp.maximum(best, jnp.max(tile, 0, keepdims=True))
                    best = best.astype(jnp.bfloat16).astype(jnp.float32)
                    p = jnp.exp2((s_all[...] - best) * LOG2E).astype(jnp.bfloat16)
                    shrink = jnp.exp2((top - best) * LOG2E)
                    acc[0] = acc[0] * shrink + jnp.dot(values(row, c), p, preferred_element_type=jnp.float32)
                    return best

                start = jnp.full((1, ROWS), lowest_max, jnp.bfloat16).astype(jnp.float32)
                top = lax.fori_loop(0, code_ref[row, table + KEY_BLOCKS], one_slot, start)
                put(i, rr, acc[0], top)
                return 0

            lax.fori_loop(0, 4, one_block, 0)


def attend(steps, seq, codes, spots, held, queries, before=()):
    kv, vt, norm = held
    chips = len(steps)
    out = jax.ShapeDtypeStruct((2, ACC_ROWS, queries[0].shape[2]), jnp.bfloat16)
    return pl.pallas_call(
        functools.partial(attention_kernel, steps, bool(before)),
        in_specs=[SMEM] * 3 + [VMEM] * (3 + len(queries) + len(before)),
        out_specs=[VMEM] * chips,
        out_shape=[out] * chips,
        scratch_shapes=[
            pltpu.VMEM((2 * chips, HS, queries[0].shape[2]), jnp.bfloat16),
            pltpu.VMEM((SLOTS * TILES * BLOCK, ROWS), jnp.bfloat16),
            pltpu.VMEM((SLOTS * TILES * BLOCK, ROWS), jnp.bfloat16),
            pltpu.VMEM((TILES * BLOCK, ROWS), jnp.float32),
            pltpu.VMEM((4 * chips + 1, ACC_ROWS, ROWS), jnp.float32),
        ],
        compiler_params=pltpu.CompilerParams(vmem_limit_bytes=32 * 2**20),
        cost_estimate=pl.CostEstimate(
            flops=chips * 6 * 10**9, bytes_accessed=4 * 2**20, transcendentals=chips * 2**20
        ),
    )(seq, codes, norm, spots, kv, vt, *queries, *before)


def combine_kernel(core_ref, *refs):
    parts, out_ref = refs[:-1], refs[-1]
    groups = out_ref.shape[0] // 2
    half = out_ref.shape[1]
    for j in range(2):
        tops = [p[j, HS + 1 : HS + 2, :].astype(jnp.float32) for p in parts]
        top = functools.reduce(jnp.maximum, tops)
        scales = [jnp.exp(t - top) for t in tops]
        total = sum(
            (p[j, HS : HS + 1, :].astype(jnp.float32) + p[j, HS + 2 : HS + 3, :].astype(jnp.float32)) * scale
            for p, scale in zip(parts, scales)
        )
        summed = sum(p[j, :HS, :].astype(jnp.float32) * scale for p, scale in zip(parts, scales))
        rows = (summed / total).T.astype(jnp.bfloat16)
        first = jnp.bitwise_xor(core_ref[0], j) * groups
        for g in range(groups):
            upper = rows[2 * g * half : (2 * g + 1) * half]
            lower = rows[(2 * g + 1) * half : (2 * g + 2) * half]
            out_ref[first + g] = jnp.concatenate([upper, lower], 1)


def combine(core, parts):
    half = parts[0].shape[2] // 16
    return pl.pallas_call(
        combine_kernel,
        in_specs=[SMEM] + [VMEM] * len(parts),
        out_specs=VMEM,
        out_shape=jax.ShapeDtypeStruct((16, half, 2 * HS), jnp.bfloat16),
        compiler_params=pltpu.CompilerParams(vmem_limit_bytes=32 * 2**20),
    )(core, *parts)


def finish_kernel(grp_ref, pieces_ref, *refs):
    w_refs, out_ref = refs[:-1], refs[-1]
    groups = pieces_ref.shape[0] // 2
    me = grp_ref[0]
    result = None
    for k, w_ref in enumerate(w_refs):
        near = jnp.bitwise_xor(me, k)
        order = [c * groups + g for g in (near, jnp.bitwise_xor(near, 4)) for c in range(2)]
        blocks = [pieces_ref[i] for i in order]
        upper = jnp.concatenate([p[:, :HS] for p in blocks], 1)
        lower = jnp.concatenate([p[:, HS:] for p in blocks], 1)
        attention = jnp.concatenate([upper, lower], 0)
        term = jnp.dot(attention, w_ref[...], preferred_element_type=jnp.float32)
        result = term if result is None else result + term
    out_ref[...] = result.astype(jnp.bfloat16)


def finish(grp, pieces, w_turns):
    return pl.pallas_call(
        finish_kernel,
        in_specs=[SMEM] + [VMEM] * (1 + len(w_turns)),
        out_specs=VMEM,
        out_shape=jax.ShapeDtypeStruct((2 * pieces.shape[1], w_turns[0].shape[1]), jnp.bfloat16),
        compiler_params=pltpu.CompilerParams(vmem_limit_bytes=24 * 2**20),
    )(grp, pieces, *w_turns)


def along_x(by):
    return [(s, s ^ (4 * by)) for s in range(16)]


def came_from(s, by):
    return jnp.bitwise_xor(s, 4 * by)


NEAR_CALLS = ((0,), (1, 3, 2))
FAR_CALLS = ((2, 1, 3), (0,))
CORE_SWAP = [(s, s ^ 1) for s in range(16)]
Y_SWAP = [(s, s ^ 2) for s in range(16)]


def body(inputs, latents, w_query, w_key, w_value, w_out, positions, block_mask):
    seq = lax.axis_index("seq")[None]
    grp = lax.axis_index("grp")[None]
    core = jnp.bitwise_and(seq, 1)

    w_other = lax.ppermute(w_out, "grp", [(g, g ^ 4) for g in range(8)])
    q_chip, theirs, kv_own, kv_other, codes = front(
        seq, latents, inputs, w_query, w_key, w_value, positions, block_mask
    )
    theirs, kv_other, kv_own, w_other = lax.optimization_barrier((theirs, kv_other, kv_own, w_other))
    q_chip = q_chip.at[1].set(lax.ppermute(theirs, "seq", CORE_SWAP))
    queries = {by: q_chip if by == 0 else lax.ppermute(q_chip, "seq", along_x(by)) for by in (0, 1, 3, 2)}
    kv_partner = lax.ppermute(kv_other, "seq", CORE_SWAP)
    near = prepare(kv_own, kv_partner)
    kv_far = [lax.ppermute(kv, "seq", Y_SWAP) for kv in (kv_own, kv_partner)]

    spots = positions.reshape(-1, ROWS)
    near_parts = dict(zip(NEAR_CALLS[0], attend(NEAR_CALLS[0], seq, codes, spots, near, [q_chip])))
    w_other, near_parts[0] = lax.optimization_barrier((w_other, near_parts[0]))
    w_pair = jnp.concatenate([w_out, w_other], 0)
    w_turns = [w_pair] + [
        lax.ppermute(w_pair, "grp", [(g, g ^ k) for g in range(8)]) for k in (1, 2, 3)
    ]

    parts = {}
    last = 0
    for call in NEAR_CALLS[1:]:
        queries[call[0]], near_parts[last], kv_far[0] = lax.optimization_barrier(
            (queries[call[0]], near_parts[last], kv_far[0])
        )
        near_parts.update(zip(call, attend(call, seq, codes, spots, near, [queries[by] for by in call])))
        last = call[-1]
    kv_far, near_parts[last] = lax.optimization_barrier((kv_far, near_parts[last]))
    far = prepare(*kv_far)
    last = None
    for call in FAR_CALLS:
        if last is not None:
            queries[call[0]], parts[last] = lax.optimization_barrier((queries[call[0]], parts[last]))
        done = attend(
            call, seq, codes, spots, far, [queries[by] for by in call], [near_parts[by] for by in call]
        )
        parts.update(zip(call, done))
        last = call[-1]

    parts = [part if by == 0 else lax.ppermute(part, "seq", along_x(by)) for by, part in parts.items()]
    parts, w_turns = lax.optimization_barrier((parts, w_turns))
    pieces = combine(core, parts)
    owners = [[(4 * x + 2 * y + c) * 8 + g for c in range(2) for g in range(8)] for x in range(4) for y in range(2)]
    pieces = lax.all_to_all(pieces, ("seq", "grp"), 0, 0, axis_index_groups=owners)
    return finish(grp, pieces, w_turns)


def solution(mesh):
    return jax.shard_map(
        body,
        mesh=mesh,
        in_specs=(
            P("seq", None),
            P("seq", None),
            P(None, "grp"),
            P(None, "grp"),
            P(None, "grp"),
            P("grp", None),
            P(),
            P(),
        ),
        out_specs=P(("seq", "grp"), None),
        check_vma=False,
    )
```

```python
import functools

import jax
import jax.numpy as jnp
from jax import lax
from jax.experimental import pallas as pl
from jax.experimental.pallas import tpu as pltpu
from jax.sharding import PartitionSpec as P

HS = 64
BLOCK = 128
TILES = 4
SLOTS = 2
ROWS = 2 * BLOCK
DEVICE = 40
FAR = 64
KEY_BLOCKS = 32
ACC_ROWS = 72
LOG2E = 1.4426950408889634
SAFE_SCORE = 60.0
masked_score = -1e30
lowest_max = -1e29
SMEM = pl.BlockSpec(memory_space=pltpu.SMEM)
VMEM = pl.BlockSpec(memory_space=pltpu.VMEM)


def in_hbm(*arrays):
    return [pltpu.with_memory_space_constraint(a, pltpu.HBM) for a in arrays]


def list_work(me, pos_ref, mask_ref, code_ref):
    half = KEY_BLOCKS // 2
    both = 2 * KEY_BLOCKS
    blocks = pos_ref.shape[0]

    def held(t):
        source = jnp.bitwise_xor(me, lax.shift_right_logical(t, 4))
        return source * half + jnp.bitwise_and(t, half - 1)

    spots = pos_ref[...].T
    own_block = lax.shift_right_logical(spots, 7)
    furthest = jnp.max(own_block, axis=0, keepdims=True)
    t_rows = lax.broadcasted_iota(jnp.int32, (both, blocks), 0)
    own = jnp.zeros((both, blocks), jnp.int32)
    for t in range(both):
        found = jnp.max((own_block == held(jnp.int32(t))).astype(jnp.int32), axis=0, keepdims=True)
        own = jnp.where(t_rows == t, found, own)

    def exact(condition):
        return condition.astype(jnp.float32).astype(jnp.bfloat16)

    columns = mask_ref.shape[1]
    pick = exact(
        lax.broadcasted_iota(jnp.int32, (both, columns), 1)
        == held(lax.broadcasted_iota(jnp.int32, (both, columns), 0))
    )
    listed = lax.dot_general(
        pick, exact(mask_ref[...] == 1), (((1,), (1,)), ((), ())), preferred_element_type=jnp.float32
    )
    active = exact((own > 0) | ((listed > 0.5) & (held(t_rows) <= furthest)))
    listed = exact(listed > 0.5)

    row = lax.broadcasted_iota(jnp.int32, (blocks, BLOCK), 0)
    col = lax.broadcasted_iota(jnp.int32, (blocks, BLOCK), 1)
    first, second = exact(row == 2 * col), exact(row == 2 * col + 1)
    active = jnp.dot(active, first + second, preferred_element_type=jnp.float32) > 0.5
    listed = [jnp.dot(listed, pairs, preferred_element_type=jnp.float32).astype(jnp.int32) for pairs in (first, second)]
    row = lax.broadcasted_iota(jnp.int32, (both, both), 0)
    col = lax.broadcasted_iota(jnp.int32, (both, both), 1)
    earlier = exact((col < row) & (lax.shift_right_logical(row, 5) == lax.shift_right_logical(col, 5)))
    place = jnp.dot(earlier, exact(active), preferred_element_type=jnp.float32).astype(jnp.int32)
    t_rows = lax.broadcasted_iota(jnp.int32, (both, BLOCK), 0)
    value = jnp.bitwise_and(t_rows, KEY_BLOCKS - 1) + KEY_BLOCKS * (listed[0] + 2 * listed[1] + 4)
    packed = jnp.where(active, place * 512 + value, -1)
    ones = active.astype(jnp.int32)
    slot_rows = lax.broadcasted_iota(jnp.int32, (KEY_BLOCKS, BLOCK), 0)
    tables = []
    for n in range(2):
        codes = jnp.zeros((KEY_BLOCKS, BLOCK), jnp.int32)
        for t in range(n * KEY_BLOCKS, (n + 1) * KEY_BLOCKS):
            one = packed[t : t + 1, :]
            codes = jnp.where(lax.shift_right_arithmetic(one, 9) == slot_rows, jnp.bitwise_and(one, 511), codes)
        count = jnp.sum(ones[n * KEY_BLOCKS : (n + 1) * KEY_BLOCKS], axis=0, keepdims=True)
        slots = jnp.maximum(lax.shift_right_logical(count + (TILES - 1), 2), 1)
        tables += [codes, jnp.broadcast_to(slots, (FAR - KEY_BLOCKS, BLOCK))]
    table = jnp.concatenate(tables, 0).T[: code_ref.shape[0]]
    code_ref[...] = jnp.where(lax.broadcasted_iota(jnp.int32, table.shape, 1) == DEVICE, me, table)


def front_kernel(seq_ref, lat_hbm, x_hbm, wq_hbm, wk_hbm, wv_hbm, pos_hbm, mask_hbm, *rest):
    pair_hbm, theirs_hbm, own_hbm, other_hbm, code_hbm = rest[:5]
    lat, x, wq, wk, wv, pos, mask, pair_ref, theirs_ref, own_ref, other_ref, code_ref = rest[5:17]
    w_all, sems, x_sems, out_sems = rest[17:]
    sent = []

    def send(source, target):
        sent.append(pltpu.make_async_copy(source, target, out_sems.at[len(sent)]))
        sent[-1].start()

    small = [
        pltpu.make_async_copy(source, target, sems.at[i])
        for i, (source, target) in enumerate(
            [(pos_hbm, pos), (mask_hbm, mask), (wq_hbm, wq), (lat_hbm, lat), (wk_hbm, wk), (wv_hbm, wv)]
        )
    ]
    rows = x.shape[0] // x_sems.shape[0]
    parts = [pl.ds(i * rows, rows) for i in range(x_sems.shape[0])]
    large = [pltpu.make_async_copy(x_hbm.at[p], x.at[p], x_sems.at[i]) for i, p in enumerate(parts)]
    for copy in small + large:
        copy.start()
    got_pos, got_mask, got_wq, got_lat, got_wk, got_wv = small
    first = jnp.bitwise_and(seq_ref[0], 1) == 0

    got_pos.wait()
    got_mask.wait()
    list_work(seq_ref[0], pos, mask, code_ref)
    send(code_ref, code_hbm)

    got_wq.wait()
    got_lat.wait()
    q = jnp.dot(lat[...], wq[...], preferred_element_type=jnp.float32).T
    q = q.astype(jnp.bfloat16) * jnp.bfloat16(HS ** -0.5)
    mine = jnp.where(first, q[:HS], q[HS:])
    pair_ref[0] = mine
    pair_ref[1] = mine
    theirs_ref[...] = jnp.where(first, q[HS:], q[:HS])
    send(pair_ref, pair_hbm)
    send(theirs_ref, theirs_hbm)

    got_wk.wait()
    got_wv.wait()
    k, v = wk[...], wv[...]
    head_0 = jnp.concatenate([k[:, :HS], v[:, :HS]], 1)
    head_1 = jnp.concatenate([k[:, HS:], v[:, HS:]], 1)
    w_all[:, : 2 * HS] = jnp.where(first, head_0, head_1)
    w_all[:, 2 * HS :] = jnp.where(first, head_1, head_0)
    for copy, part in zip(large, parts):
        copy.wait()
        both = jnp.dot(x[part, :], w_all[...], preferred_element_type=jnp.float32).astype(jnp.bfloat16)
        own_ref[part, :] = both[:, : 2 * HS]
        other_ref[part, :] = both[:, 2 * HS :]
        send(own_ref.at[part], own_hbm.at[part])
        send(other_ref.at[part], other_hbm.at[part])
    for copy in sent:
        copy.wait()


def front(seq, latents, inputs, w_query, w_key, w_value, positions, block_mask):
    rows, width = latents.shape
    keys = inputs.shape[0]
    spots = positions.reshape(-1, BLOCK)
    operands = (latents, inputs, w_query, w_key, w_value, spots, block_mask)
    q = jax.ShapeDtypeStruct((HS, rows), jnp.bfloat16)
    kv = jax.ShapeDtypeStruct((keys, 2 * HS), jnp.bfloat16)
    results = [jax.ShapeDtypeStruct((2, HS, rows), jnp.bfloat16), q, kv, kv, jax.ShapeDtypeStruct((spots.shape[0] // 2, BLOCK), jnp.int32)]
    return pl.pallas_call(
        front_kernel,
        in_specs=[SMEM] + [pl.BlockSpec(memory_space=pl.ANY)] * len(operands),
        out_specs=[pl.BlockSpec(memory_space=pl.ANY)] * 5,
        out_shape=results,
        scratch_shapes=[pltpu.VMEM(a.shape, a.dtype) for a in (*operands, *results)]
        + [
            pltpu.VMEM((width, 4 * HS), jnp.bfloat16),
            pltpu.SemaphoreType.DMA((6,)),
            pltpu.SemaphoreType.DMA((1,)),
            pltpu.SemaphoreType.DMA((5,)),
        ],
        compiler_params=pltpu.CompilerParams(vmem_limit_bytes=24 * 2**20),
        cost_estimate=pl.CostEstimate(
            flops=2 * (keys * 4 + rows * 2) * width * HS, bytes_accessed=6 * 2**20, transcendentals=0
        ),
    )(seq, *in_hbm(*operands))


def prepare_kernel(*refs):
    sources, (kv_ref, vt_ref, norm_ref) = refs[:-3], refs[-3:]
    each = KEY_BLOCKS // len(sources)
    most = None
    for t in range(KEY_BLOCKS):
        at = t % each
        tile = sources[t // each][at * BLOCK : (at + 1) * BLOCK, :]
        kv_ref[t * BLOCK : (t + 1) * BLOCK, :] = tile
        turned = tile.T
        vt_ref[:HS, t * BLOCK : (t + 1) * BLOCK] = turned[HS:, :]
        k = turned[:HS, :].astype(jnp.float32)
        squares = jnp.sum(k * k, axis=0, keepdims=True)
        most = squares if most is None else jnp.maximum(most, squares)
    vt_ref[HS:, :] = jnp.ones((ACC_ROWS - HS, KEY_BLOCKS * BLOCK), jnp.bfloat16)
    norm_ref[...] = most


def prepare(*sources):
    keys = sum(source.shape[0] for source in sources)
    return pl.pallas_call(
        prepare_kernel,
        in_specs=[VMEM] * len(sources),
        out_specs=[VMEM] * 3,
        out_shape=[
            jax.ShapeDtypeStruct((keys, 2 * HS), jnp.bfloat16),
            jax.ShapeDtypeStruct((ACC_ROWS, keys), jnp.bfloat16),
            jax.ShapeDtypeStruct((1, BLOCK), jnp.float32),
        ],
        compiler_params=pltpu.CompilerParams(vmem_limit_bytes=24 * 2**20),
    )(*sources)


def attention_kernel(steps, far, code_any, norm_ref, pos_ref, kv_ref, vt_ref, *rest):
    chips = len(steps)
    q_refs, rest = rest[:chips], rest[chips:]
    before_refs, rest = (rest[:chips], rest[chips:]) if far else (None, rest)
    o_refs, (q_all, p_a, p_b, s_all, acc, code_ref, sem) = rest[:chips], rest[chips:]
    table = FAR if far else 0
    got_codes = pltpu.make_async_copy(code_any, code_ref, sem)
    got_codes.start()
    blocks = 4 * chips
    iota = lax.broadcasted_iota(jnp.int32, (BLOCK, ROWS), 0)
    in_first = lax.broadcasted_iota(jnp.int32, (1, ROWS), 1) < BLOCK
    iota_half = iota.astype(jnp.float32).astype(jnp.bfloat16)

    most = None
    for i, ref in enumerate(q_refs):
        for j in range(ref.shape[0]):
            q = ref[j]
            q_all[i * ref.shape[0] + j] = q
            q = q.astype(jnp.float32)
            squares = jnp.sum(q * q, axis=0, keepdims=True)
            most = squares if most is None else jnp.maximum(most, squares)
    safe = jnp.max(most) * jnp.max(norm_ref[...]) <= SAFE_SCORE * SAFE_SCORE
    got_codes.wait()
    me = code_ref[0, DEVICE]
    keys_of = jnp.bitwise_xor(me, 2) if far else me
    own_base = keys_of * (KEY_BLOCKS // 2 * BLOCK)
    partner_base = jnp.bitwise_xor(keys_of, 1) * (KEY_BLOCKS // 2 * BLOCK)
    sources = [came_from(me, step) for step in steps]

    def clamp(r):
        return jnp.minimum(r, blocks - 1)

    def whole_block(r):
        shard = sources[-1]
        for i in range(chips - 1):
            shard = jnp.where(lax.div(r, 4) == i, sources[i], shard)
        return jnp.bitwise_xor(shard, jnp.bitwise_and(lax.div(r, 2), 1)) * 2 + lax.rem(r, 2)

    def offset(i):
        return pl.multiple_of(i * BLOCK, BLOCK)

    def row_offset(i):
        return pl.multiple_of(i * ROWS, ROWS)

    def query(r):
        q = q_all[lax.div(r, 2), :, pl.ds(row_offset(lax.rem(r, 2)), ROWS)]
        return jnp.concatenate([q, jnp.zeros_like(q)], 0)

    def key_blocks(row, c):
        return [jnp.bitwise_and(code_ref[row, table + c * TILES + t], KEY_BLOCKS - 1) for t in range(TILES)]

    def products(row, r, c):
        keys = jnp.concatenate([kv_ref[pl.ds(offset(k), BLOCK), :] for k in key_blocks(row, c)], 0)
        return jnp.dot(keys, query(r), preferred_element_type=jnp.float32)

    def values(row, c):
        return jnp.concatenate([vt_ref[:, pl.ds(offset(k), BLOCK)] for k in key_blocks(row, c)], 1)

    def last_key(row, c, t, pos, real):
        code = code_ref[row, table + c * TILES + t]
        k = jnp.bitwise_and(code, KEY_BLOCKS - 1)
        half = KEY_BLOCKS // 2
        base = jnp.where(k < half, own_base, partner_base - half * BLOCK) + k * BLOCK
        real = jnp.logical_and(real, code >= 4 * KEY_BLOCKS)
        reach = [jnp.where(jnp.bitwise_and(code, n * KEY_BLOCKS) > 0, 1 << 30, BLOCK) for n in (1, 2)]
        reach = jnp.where(in_first, *[jnp.where(real, n, -(1 << 30)) for n in reach])
        ahead = pos - base
        return jnp.where(ahead < reach, jnp.minimum(ahead, BLOCK - 1), -1)

    def put(i, rr, a, top):
        at = (lax.div(rr, 2), slice(None), pl.ds(row_offset(lax.rem(rr, 2)), ROWS))
        if far:
            before = before_refs[i][at].astype(jnp.float32)
            top_before, top_now = before[HS + 1 : HS + 2], top
            top = jnp.maximum(top_before, top_now)
            shrink, shrink_before = jnp.exp(top_now - top), jnp.exp(top_before - top)
            total = a[HS : HS + 1] * shrink + (before[HS : HS + 1] + before[HS + 2 : HS + 3]) * shrink_before
            a = a * shrink + before * shrink_before
        else:
            total = a[HS : HS + 1]
        low = total - total.astype(jnp.bfloat16).astype(jnp.float32)
        out = jnp.concatenate([a[:HS], total, top, low, a[HS + 3 :]], 0)
        o_refs[i][at] = out.astype(jnp.bfloat16)

    def advance(r, c):
        last = c + 1 >= code_ref[whole_block(clamp(r)), table + KEY_BLOCKS]
        return jnp.where(last, jnp.minimum(r + 1, blocks), r), jnp.where(last, 0, c + 1)

    def step_slots(r, c):
        slots = []
        for _ in range(SLOTS):
            slots.append((r, c))
            r, c = advance(r, c)
        return slots, r, c

    @pl.when(safe)
    def _():
        acc[...] = jnp.zeros_like(acc)

        def weigh(p_ref, slots):
            for g, (r, c) in enumerate(slots):
                rr = clamp(r)
                row = whole_block(rr)
                s = products(row, rr, c)
                pos = pos_ref[pl.ds(row, 1), :]
                for t in range(TILES):
                    p = jnp.exp2(s[t * BLOCK : (t + 1) * BLOCK] * LOG2E).astype(jnp.bfloat16)
                    last = last_key(row, c, t, pos, r < blocks).astype(jnp.float32).astype(jnp.bfloat16)
                    at = (g * TILES + t) * BLOCK
                    p_ref[at : at + BLOCK, :] = jnp.where(iota_half <= last, p, jnp.zeros_like(p))

        def add(p_ref, slots):
            for g, (r, c) in enumerate(slots):
                v = values(whole_block(clamp(r)), c)
                at = g * TILES * BLOCK
                acc[r] += jnp.dot(v, p_ref[at : at + TILES * BLOCK, :], preferred_element_type=jnp.float32)

        slots_0, r0, c0 = step_slots(jnp.int32(0), jnp.int32(0))
        weigh(p_a, slots_0)

        def two_steps(_, state):
            r, c, r1, c1 = state
            slots, _, _ = step_slots(r, c)
            slots_1, r2, c2 = step_slots(r1, c1)
            weigh(p_b, slots_1)
            add(p_a, slots)
            slots_2, r3, c3 = step_slots(r2, c2)
            weigh(p_a, slots_2)
            add(p_b, slots_1)
            return r2, c2, r3, c3

        items = lax.fori_loop(0, blocks, lambda r, n: n + code_ref[whole_block(r), table + KEY_BLOCKS], jnp.int32(0))
        turns = lax.div(items + (2 * SLOTS - 1), 2 * SLOTS)
        lax.fori_loop(0, turns, two_steps, (jnp.int32(0), jnp.int32(0), r0, c0))

        for i in range(chips):
            def finish(rr, _, i=i):
                a = acc[i * 4 + rr]
                put(i, rr, a, jnp.where(a[HS : HS + 1] > 0, 0.0, lowest_max))
                return 0

            lax.fori_loop(0, 4, finish, 0)

    @pl.when(jnp.logical_not(safe))
    def _():
        for i in range(chips):
            def one_block(rr, _, i=i):
                r = i * 4 + rr
                row = whole_block(r)
                pos = pos_ref[pl.ds(row, 1), :]
                acc[0] = jnp.zeros((ACC_ROWS, ROWS), jnp.float32)

                def one_slot(c, top):
                    s = products(row, r, c)
                    best = top
                    for t in range(TILES):
                        tile = s[t * BLOCK : (t + 1) * BLOCK]
                        tile = jnp.where(iota <= last_key(row, c, t, pos, True), tile, masked_score)
                        s_all[t * BLOCK : (t + 1) * BLOCK, :] = tile
                        best = jnp.maximum(best, jnp.max(tile, 0, keepdims=True))
                    best = best.astype(jnp.bfloat16).astype(jnp.float32)
                    p = jnp.exp2((s_all[...] - best) * LOG2E).astype(jnp.bfloat16)
                    shrink = jnp.exp2((top - best) * LOG2E)
                    acc[0] = acc[0] * shrink + jnp.dot(values(row, c), p, preferred_element_type=jnp.float32)
                    return best

                start = jnp.full((1, ROWS), lowest_max, jnp.bfloat16).astype(jnp.float32)
                top = lax.fori_loop(0, code_ref[row, table + KEY_BLOCKS], one_slot, start)
                put(i, rr, acc[0], top)
                return 0

            lax.fori_loop(0, 4, one_block, 0)


def attend(steps, codes, spots, held, queries, before=()):
    kv, vt, norm = held
    chips = len(steps)
    out = jax.ShapeDtypeStruct((2, ACC_ROWS, queries[0].shape[2]), jnp.bfloat16)
    return pl.pallas_call(
        functools.partial(attention_kernel, steps, bool(before)),
        in_specs=[pl.BlockSpec(memory_space=pl.ANY)] + [VMEM] * (4 + len(queries) + len(before)),
        out_specs=[VMEM] * chips,
        out_shape=[out] * chips,
        scratch_shapes=[
            pltpu.VMEM((2 * chips, HS, queries[0].shape[2]), jnp.bfloat16),
            pltpu.VMEM((SLOTS * TILES * BLOCK, ROWS), jnp.bfloat16),
            pltpu.VMEM((SLOTS * TILES * BLOCK, ROWS), jnp.bfloat16),
            pltpu.VMEM((TILES * BLOCK, ROWS), jnp.float32),
            pltpu.VMEM((4 * chips + 1, ACC_ROWS, ROWS), jnp.float32),
            pltpu.SMEM(codes.shape, jnp.int32),
            pltpu.SemaphoreType.DMA,
        ],
        compiler_params=pltpu.CompilerParams(vmem_limit_bytes=32 * 2**20),
        cost_estimate=pl.CostEstimate(
            flops=chips * 6 * 10**9, bytes_accessed=4 * 2**20, transcendentals=chips * 2**20
        ),
    )(codes, norm, spots, kv, vt, *queries, *before)


def combine_kernel(core_ref, *refs):
    parts, out_ref = refs[:-1], refs[-1]
    groups = out_ref.shape[0] // 2
    half = out_ref.shape[1]
    for j in range(2):
        tops = [p[j, HS + 1 : HS + 2, :].astype(jnp.float32) for p in parts]
        top = functools.reduce(jnp.maximum, tops)
        scales = [jnp.exp(t - top) for t in tops]
        total = sum(
            (p[j, HS : HS + 1, :].astype(jnp.float32) + p[j, HS + 2 : HS + 3, :].astype(jnp.float32)) * scale
            for p, scale in zip(parts, scales)
        )
        summed = sum(p[j, :HS, :].astype(jnp.float32) * scale for p, scale in zip(parts, scales))
        rows = (summed / total).T.astype(jnp.bfloat16)
        first = jnp.bitwise_xor(core_ref[0], j) * groups
        for g in range(groups):
            upper = rows[2 * g * half : (2 * g + 1) * half]
            lower = rows[(2 * g + 1) * half : (2 * g + 2) * half]
            out_ref[first + g] = jnp.concatenate([upper, lower], 1)


def combine(core, parts):
    half = parts[0].shape[2] // 16
    return pl.pallas_call(
        combine_kernel,
        in_specs=[SMEM] + [VMEM] * len(parts),
        out_specs=VMEM,
        out_shape=jax.ShapeDtypeStruct((16, half, 2 * HS), jnp.bfloat16),
        compiler_params=pltpu.CompilerParams(vmem_limit_bytes=32 * 2**20),
    )(core, *parts)


def finish_kernel(grp_ref, pieces_ref, *refs):
    w_refs, out_ref = refs[:-1], refs[-1]
    groups = pieces_ref.shape[0] // 2
    me = grp_ref[0]
    result = None
    for k, w_ref in enumerate(w_refs):
        near = jnp.bitwise_xor(me, k)
        order = [c * groups + g for g in (near, jnp.bitwise_xor(near, 4)) for c in range(2)]
        blocks = [pieces_ref[i] for i in order]
        upper = jnp.concatenate([p[:, :HS] for p in blocks], 1)
        lower = jnp.concatenate([p[:, HS:] for p in blocks], 1)
        attention = jnp.concatenate([upper, lower], 0)
        term = jnp.dot(attention, w_ref[...], preferred_element_type=jnp.float32)
        result = term if result is None else result + term
    out_ref[...] = result.astype(jnp.bfloat16)


def finish(grp, pieces, w_turns):
    return pl.pallas_call(
        finish_kernel,
        in_specs=[SMEM] + [VMEM] * (1 + len(w_turns)),
        out_specs=VMEM,
        out_shape=jax.ShapeDtypeStruct((2 * pieces.shape[1], w_turns[0].shape[1]), jnp.bfloat16),
        compiler_params=pltpu.CompilerParams(vmem_limit_bytes=24 * 2**20),
    )(grp, pieces, *w_turns)


def along_x(by):
    return [(s, s ^ (4 * by)) for s in range(16)]


def came_from(s, by):
    return jnp.bitwise_xor(s, 4 * by)


NEAR_CALLS = ((0,), (1, 3, 2))
FAR_CALLS = ((2, 1, 3), (0,))
CORE_SWAP = [(s, s ^ 1) for s in range(16)]
Y_SWAP = [(s, s ^ 2) for s in range(16)]


def body(inputs, latents, w_query, w_key, w_value, w_out, positions, block_mask):
    seq = lax.axis_index("seq")[None]
    grp = lax.axis_index("grp")[None]
    core = jnp.bitwise_and(seq, 1)

    w_other = lax.ppermute(w_out, "grp", [(g, g ^ 4) for g in range(8)])
    q_chip, theirs, kv_own, kv_other, codes = front(
        seq, latents, inputs, w_query, w_key, w_value, positions, block_mask
    )
    kv_other, kv_own, w_other = lax.optimization_barrier((kv_other, kv_own, w_other))
    q_chip = q_chip.at[1].set(lax.ppermute(theirs, "seq", CORE_SWAP))
    queries = {by: q_chip if by == 0 else lax.ppermute(q_chip, "seq", along_x(by)) for by in (0, 1, 3, 2)}
    kv_partner = lax.ppermute(kv_other, "seq", CORE_SWAP)
    near = prepare(kv_own, kv_partner)
    kv_far = [lax.ppermute(kv, "seq", Y_SWAP) for kv in (kv_own, kv_partner)]

    spots = positions.reshape(-1, ROWS)
    near_parts = dict(zip(NEAR_CALLS[0], attend(NEAR_CALLS[0], codes, spots, near, [q_chip])))
    w_other, near_parts[0] = lax.optimization_barrier((w_other, near_parts[0]))
    w_pair = jnp.concatenate([w_out, w_other], 0)
    w_turns = [w_pair] + [
        lax.ppermute(w_pair, "grp", [(g, g ^ k) for g in range(8)]) for k in (1, 2, 3)
    ]

    parts = {}
    last = 0
    for call in NEAR_CALLS[1:]:
        queries[call[0]], near_parts[last], kv_far[0] = lax.optimization_barrier(
            (queries[call[0]], near_parts[last], kv_far[0])
        )
        near_parts.update(zip(call, attend(call, codes, spots, near, [queries[by] for by in call])))
        last = call[-1]
    kv_far, near_parts[last] = lax.optimization_barrier((kv_far, near_parts[last]))
    far = prepare(*kv_far)
    last = None
    for call in FAR_CALLS:
        if last is not None:
            queries[call[0]], parts[last] = lax.optimization_barrier((queries[call[0]], parts[last]))
        done = attend(
            call, codes, spots, far, [queries[by] for by in call], [near_parts[by] for by in call]
        )
        parts.update(zip(call, done))
        last = call[-1]

    parts = [part if by == 0 else lax.ppermute(part, "seq", along_x(by)) for by, part in parts.items()]
    parts, w_turns = lax.optimization_barrier((parts, w_turns))
    pieces = combine(core, parts)
    owners = [[(4 * x + 2 * y + c) * 8 + g for c in range(2) for g in range(8)] for x in range(4) for y in range(2)]
    pieces = lax.all_to_all(pieces, ("seq", "grp"), 0, 0, axis_index_groups=owners)
    return finish(grp, pieces, w_turns)


def solution(mesh):
    return jax.shard_map(
        body,
        mesh=mesh,
        in_specs=(
            P("seq", None),
            P("seq", None),
            P(None, "grp"),
            P(None, "grp"),
            P(None, "grp"),
            P("grp", None),
            P(),
            P(),
        ),
        out_specs=P(("seq", "grp"), None),
        check_vma=False,
    )
```

```python
import functools

import jax
import jax.numpy as jnp
from jax import lax
from jax.experimental import pallas as pl
from jax.experimental.pallas import tpu as pltpu
from jax.sharding import PartitionSpec as P

HS = 64
BLOCK = 128
TILES = 4
SLOTS = 2
ROWS = 2 * BLOCK
DEVICE = 40
FAR = 64
KEY_BLOCKS = 32
ACC_ROWS = 72
LOG2E = 1.4426950408889634
SAFE_SCORE = 60.0
masked_score = -1e30
lowest_max = -1e29
SMEM = pl.BlockSpec(memory_space=pltpu.SMEM)
VMEM = pl.BlockSpec(memory_space=pltpu.VMEM)


def in_hbm(*arrays):
    return [pltpu.with_memory_space_constraint(a, pltpu.HBM) for a in arrays]


def list_work(me, pos_ref, mask_ref, code_ref):
    half = KEY_BLOCKS // 2
    both = 2 * KEY_BLOCKS
    blocks = pos_ref.shape[0]

    def held(t):
        source = jnp.bitwise_xor(me, lax.shift_right_logical(t, 4))
        return source * half + jnp.bitwise_and(t, half - 1)

    spots = pos_ref[...].T
    own_block = lax.shift_right_logical(spots, 7)
    furthest = jnp.max(own_block, axis=0, keepdims=True)
    t_rows = lax.broadcasted_iota(jnp.int32, (both, blocks), 0)
    own = jnp.zeros((both, blocks), jnp.int32)
    for t in range(both):
        found = jnp.max((own_block == held(jnp.int32(t))).astype(jnp.int32), axis=0, keepdims=True)
        own = jnp.where(t_rows == t, found, own)

    def exact(condition):
        return condition.astype(jnp.float32).astype(jnp.bfloat16)

    columns = mask_ref.shape[1]
    pick = exact(
        lax.broadcasted_iota(jnp.int32, (both, columns), 1)
        == held(lax.broadcasted_iota(jnp.int32, (both, columns), 0))
    )
    listed = lax.dot_general(
        pick, exact(mask_ref[...] == 1), (((1,), (1,)), ((), ())), preferred_element_type=jnp.float32
    )
    active = exact((own > 0) | ((listed > 0.5) & (held(t_rows) <= furthest)))
    listed = exact(listed > 0.5)

    row = lax.broadcasted_iota(jnp.int32, (blocks, BLOCK), 0)
    col = lax.broadcasted_iota(jnp.int32, (blocks, BLOCK), 1)
    first, second = exact(row == 2 * col), exact(row == 2 * col + 1)
    active = jnp.dot(active, first + second, preferred_element_type=jnp.float32) > 0.5
    listed = [jnp.dot(listed, pairs, preferred_element_type=jnp.float32).astype(jnp.int32) for pairs in (first, second)]
    row = lax.broadcasted_iota(jnp.int32, (both, both), 0)
    col = lax.broadcasted_iota(jnp.int32, (both, both), 1)
    earlier = exact((col < row) & (lax.shift_right_logical(row, 5) == lax.shift_right_logical(col, 5)))
    place = jnp.dot(earlier, exact(active), preferred_element_type=jnp.float32).astype(jnp.int32)
    t_rows = lax.broadcasted_iota(jnp.int32, (both, BLOCK), 0)
    value = jnp.bitwise_and(t_rows, KEY_BLOCKS - 1) + KEY_BLOCKS * (listed[0] + 2 * listed[1] + 4)
    packed = jnp.where(active, place * 512 + value, -1)
    ones = active.astype(jnp.int32)
    slot_rows = lax.broadcasted_iota(jnp.int32, (KEY_BLOCKS, BLOCK), 0)
    tables = []
    for n in range(2):
        codes = jnp.zeros((KEY_BLOCKS, BLOCK), jnp.int32)
        for t in range(n * KEY_BLOCKS, (n + 1) * KEY_BLOCKS):
            one = packed[t : t + 1, :]
            codes = jnp.where(lax.shift_right_arithmetic(one, 9) == slot_rows, jnp.bitwise_and(one, 511), codes)
        count = jnp.sum(ones[n * KEY_BLOCKS : (n + 1) * KEY_BLOCKS], axis=0, keepdims=True)
        slots = jnp.maximum(lax.shift_right_logical(count + (TILES - 1), 2), 1)
        tables += [codes, jnp.broadcast_to(slots, (FAR - KEY_BLOCKS, BLOCK))]
    table = jnp.concatenate(tables, 0).T[: code_ref.shape[0]]
    code_ref[...] = jnp.where(lax.broadcasted_iota(jnp.int32, table.shape, 1) == DEVICE, me, table)


def front_kernel(seq_ref, lat_hbm, x_hbm, wq_hbm, wk_hbm, wv_hbm, pos_hbm, mask_hbm, *rest):
    pair_hbm, theirs_hbm, own_hbm, other_hbm, code_hbm = rest[:5]
    lat, x, wq, wk, wv, pos, mask, pair_ref, theirs_ref, own_ref, other_ref, code_ref = rest[5:17]
    w_all, sems, x_sems, out_sems = rest[17:]
    sent = []

    def send(source, target):
        sent.append(pltpu.make_async_copy(source, target, out_sems.at[len(sent)]))
        sent[-1].start()

    small = [
        pltpu.make_async_copy(source, target, sems.at[i])
        for i, (source, target) in enumerate(
            [(pos_hbm, pos), (mask_hbm, mask), (wq_hbm, wq), (lat_hbm, lat), (wk_hbm, wk), (wv_hbm, wv)]
        )
    ]
    rows = x.shape[0] // x_sems.shape[0]
    parts = [pl.ds(i * rows, rows) for i in range(x_sems.shape[0])]
    large = [pltpu.make_async_copy(x_hbm.at[p], x.at[p], x_sems.at[i]) for i, p in enumerate(parts)]
    for copy in small + large:
        copy.start()
    got_pos, got_mask, got_wq, got_lat, got_wk, got_wv = small
    first = jnp.bitwise_and(seq_ref[0], 1) == 0

    got_pos.wait()
    got_mask.wait()
    list_work(seq_ref[0], pos, mask, code_ref)
    send(code_ref, code_hbm)

    got_wq.wait()
    got_lat.wait()
    q = jnp.dot(lat[...], wq[...], preferred_element_type=jnp.float32).T
    q = q.astype(jnp.bfloat16) * jnp.bfloat16(HS ** -0.5)
    mine = jnp.where(first, q[:HS], q[HS:])
    pair_ref[0] = mine
    pair_ref[1] = mine
    theirs_ref[...] = jnp.where(first, q[HS:], q[:HS])
    send(pair_ref, pair_hbm)
    send(theirs_ref, theirs_hbm)

    got_wk.wait()
    got_wv.wait()
    k, v = wk[...], wv[...]
    head_0 = jnp.concatenate([k[:, :HS], v[:, :HS]], 1)
    head_1 = jnp.concatenate([k[:, HS:], v[:, HS:]], 1)
    w_all[:, : 2 * HS] = jnp.where(first, head_0, head_1)
    w_all[:, 2 * HS :] = jnp.where(first, head_1, head_0)
    for copy, part in zip(large, parts):
        copy.wait()
        both = jnp.dot(x[part, :], w_all[...], preferred_element_type=jnp.float32).astype(jnp.bfloat16)
        own_ref[part, :] = both[:, : 2 * HS]
        other_ref[part, :] = both[:, 2 * HS :]
        send(own_ref.at[part], own_hbm.at[part])
        send(other_ref.at[part], other_hbm.at[part])
    for copy in sent:
        copy.wait()


def front(seq, latents, inputs, w_query, w_key, w_value, positions, block_mask):
    rows, width = latents.shape
    keys = inputs.shape[0]
    spots = positions.reshape(-1, BLOCK)
    operands = (latents, inputs, w_query, w_key, w_value, spots, block_mask)
    q = jax.ShapeDtypeStruct((HS, rows), jnp.bfloat16)
    kv = jax.ShapeDtypeStruct((keys, 2 * HS), jnp.bfloat16)
    results = [jax.ShapeDtypeStruct((2, HS, rows), jnp.bfloat16), q, kv, kv, jax.ShapeDtypeStruct((spots.shape[0] // 2, BLOCK), jnp.int32)]
    return pl.pallas_call(
        front_kernel,
        in_specs=[SMEM] + [pl.BlockSpec(memory_space=pl.ANY)] * len(operands),
        out_specs=[pl.BlockSpec(memory_space=pl.ANY)] * 5,
        out_shape=results,
        scratch_shapes=[pltpu.VMEM(a.shape, a.dtype) for a in (*operands, *results)]
        + [
            pltpu.VMEM((width, 4 * HS), jnp.bfloat16),
            pltpu.SemaphoreType.DMA((6,)),
            pltpu.SemaphoreType.DMA((1,)),
            pltpu.SemaphoreType.DMA((5,)),
        ],
        compiler_params=pltpu.CompilerParams(vmem_limit_bytes=24 * 2**20),
        cost_estimate=pl.CostEstimate(
            flops=2 * (keys * 4 + rows * 2) * width * HS, bytes_accessed=6 * 2**20, transcendentals=0
        ),
    )(seq, *in_hbm(*operands))


def prepare_kernel(*refs):
    sources, (kv_ref, vt_ref, norm_ref) = refs[:-3], refs[-3:]
    each = KEY_BLOCKS // len(sources)
    most = None
    for t in range(KEY_BLOCKS):
        at = t % each
        tile = sources[t // each][at * BLOCK : (at + 1) * BLOCK, :]
        kv_ref[t * BLOCK : (t + 1) * BLOCK, :] = tile
        turned = tile.T
        vt_ref[:HS, t * BLOCK : (t + 1) * BLOCK] = turned[HS:, :]
        k = turned[:HS, :].astype(jnp.float32)
        squares = jnp.sum(k * k, axis=0, keepdims=True)
        most = squares if most is None else jnp.maximum(most, squares)
    vt_ref[HS:, :] = jnp.ones((ACC_ROWS - HS, KEY_BLOCKS * BLOCK), jnp.bfloat16)
    norm_ref[...] = most


def prepare(*sources):
    keys = sum(source.shape[0] for source in sources)
    return pl.pallas_call(
        prepare_kernel,
        in_specs=[VMEM] * len(sources),
        out_specs=[VMEM] * 3,
        out_shape=[
            jax.ShapeDtypeStruct((keys, 2 * HS), jnp.bfloat16),
            jax.ShapeDtypeStruct((ACC_ROWS, keys), jnp.bfloat16),
            jax.ShapeDtypeStruct((1, BLOCK), jnp.float32),
        ],
        compiler_params=pltpu.CompilerParams(vmem_limit_bytes=24 * 2**20),
    )(*sources)


def attention_kernel(steps, far, code_any, norm_ref, pos_ref, kv_ref, vt_ref, *rest):
    chips = len(steps)
    q_refs, rest = rest[:chips], rest[chips:]
    before_refs, rest = (rest[:chips], rest[chips:]) if far else (None, rest)
    o_refs, (q_all, p_a, p_b, s_all, acc, code_ref, sem) = rest[:chips], rest[chips:]
    table = FAR if far else 0
    got_codes = pltpu.make_async_copy(code_any, code_ref, sem)
    got_codes.start()
    blocks = 4 * chips
    iota = lax.broadcasted_iota(jnp.int32, (BLOCK, ROWS), 0)
    in_first = lax.broadcasted_iota(jnp.int32, (1, ROWS), 1) < BLOCK
    iota_half = iota.astype(jnp.float32).astype(jnp.bfloat16)

    most = None
    for i, ref in enumerate(q_refs):
        for j in range(ref.shape[0]):
            q = ref[j]
            q_all[i * ref.shape[0] + j] = q
            q = q.astype(jnp.float32)
            squares = jnp.sum(q * q, axis=0, keepdims=True)
            most = squares if most is None else jnp.maximum(most, squares)
    safe = jnp.max(most) * jnp.max(norm_ref[...]) <= SAFE_SCORE * SAFE_SCORE
    got_codes.wait()
    me = code_ref[0, DEVICE]
    keys_of = jnp.bitwise_xor(me, 2) if far else me
    own_base = keys_of * (KEY_BLOCKS // 2 * BLOCK)
    partner_base = jnp.bitwise_xor(keys_of, 1) * (KEY_BLOCKS // 2 * BLOCK)
    sources = [came_from(me, step) for step in steps]

    def clamp(r):
        return jnp.minimum(r, blocks - 1)

    def whole_block(r):
        shard = sources[-1]
        for i in range(chips - 1):
            shard = jnp.where(lax.div(r, 4) == i, sources[i], shard)
        return jnp.bitwise_xor(shard, jnp.bitwise_and(lax.div(r, 2), 1)) * 2 + lax.rem(r, 2)

    def offset(i):
        return pl.multiple_of(i * BLOCK, BLOCK)

    def row_offset(i):
        return pl.multiple_of(i * ROWS, ROWS)

    def query(r):
        q = q_all[lax.div(r, 2), :, pl.ds(row_offset(lax.rem(r, 2)), ROWS)]
        return jnp.concatenate([q, jnp.zeros_like(q)], 0)

    def key_blocks(row, c):
        return [jnp.bitwise_and(code_ref[row, table + c * TILES + t], KEY_BLOCKS - 1) for t in range(TILES)]

    def products(row, r, c):
        keys = jnp.concatenate([kv_ref[pl.ds(offset(k), BLOCK), :] for k in key_blocks(row, c)], 0)
        return jnp.dot(keys, query(r), preferred_element_type=jnp.float32)

    def values(row, c):
        return jnp.concatenate([vt_ref[:, pl.ds(offset(k), BLOCK)] for k in key_blocks(row, c)], 1)

    def last_key(row, c, t, pos, real):
        code = code_ref[row, table + c * TILES + t]
        k = jnp.bitwise_and(code, KEY_BLOCKS - 1)
        half = KEY_BLOCKS // 2
        base = jnp.where(k < half, own_base, partner_base - half * BLOCK) + k * BLOCK
        real = jnp.logical_and(real, code >= 4 * KEY_BLOCKS)
        reach = [jnp.where(jnp.bitwise_and(code, n * KEY_BLOCKS) > 0, 1 << 30, BLOCK) for n in (1, 2)]
        reach = jnp.where(in_first, *[jnp.where(real, n, -(1 << 30)) for n in reach])
        ahead = pos - base
        return jnp.where(ahead < reach, jnp.minimum(ahead, BLOCK - 1), -1)

    def put(i, rr, a, top):
        at = (lax.div(rr, 2), slice(None), pl.ds(row_offset(lax.rem(rr, 2)), ROWS))
        if far:
            before = before_refs[i][at].astype(jnp.float32)
            top_before, top_now = before[HS + 1 : HS + 2], top
            top = jnp.maximum(top_before, top_now)
            shrink, shrink_before = jnp.exp(top_now - top), jnp.exp(top_before - top)
            total = a[HS : HS + 1] * shrink + (before[HS : HS + 1] + before[HS + 2 : HS + 3]) * shrink_before
            a = a * shrink + before * shrink_before
        else:
            total = a[HS : HS + 1]
        low = total - total.astype(jnp.bfloat16).astype(jnp.float32)
        out = jnp.concatenate([a[:HS], total, top, low, a[HS + 3 :]], 0)
        o_refs[i][at] = out.astype(jnp.bfloat16)

    def advance(r, c):
        last = c + 1 >= code_ref[whole_block(clamp(r)), table + KEY_BLOCKS]
        return jnp.where(last, jnp.minimum(r + 1, blocks), r), jnp.where(last, 0, c + 1)

    def step_slots(r, c):
        slots = []
        for _ in range(SLOTS):
            slots.append((r, c))
            r, c = advance(r, c)
        return slots, r, c

    @pl.when(safe)
    def _():
        acc[...] = jnp.zeros_like(acc)

        def weigh(p_ref, slots):
            for g, (r, c) in enumerate(slots):
                rr = clamp(r)
                row = whole_block(rr)
                s = products(row, rr, c)
                pos = pos_ref[pl.ds(row, 1), :]
                for t in range(TILES):
                    p = jnp.exp2(s[t * BLOCK : (t + 1) * BLOCK] * LOG2E).astype(jnp.bfloat16)
                    last = last_key(row, c, t, pos, r < blocks).astype(jnp.float32).astype(jnp.bfloat16)
                    at = (g * TILES + t) * BLOCK
                    p_ref[at : at + BLOCK, :] = jnp.where(iota_half <= last, p, jnp.zeros_like(p))

        def add(p_ref, slots):
            for g, (r, c) in enumerate(slots):
                v = values(whole_block(clamp(r)), c)
                at = g * TILES * BLOCK
                acc[r] += jnp.dot(v, p_ref[at : at + TILES * BLOCK, :], preferred_element_type=jnp.float32)

        slots_0, r0, c0 = step_slots(jnp.int32(0), jnp.int32(0))
        weigh(p_a, slots_0)

        def two_steps(_, state):
            r, c, r1, c1 = state
            slots, _, _ = step_slots(r, c)
            slots_1, r2, c2 = step_slots(r1, c1)
            weigh(p_b, slots_1)
            add(p_a, slots)
            slots_2, r3, c3 = step_slots(r2, c2)
            weigh(p_a, slots_2)
            add(p_b, slots_1)
            return r2, c2, r3, c3

        items = lax.fori_loop(0, blocks, lambda r, n: n + code_ref[whole_block(r), table + KEY_BLOCKS], jnp.int32(0))
        turns = lax.div(items + (2 * SLOTS - 1), 2 * SLOTS)
        lax.fori_loop(0, turns, two_steps, (jnp.int32(0), jnp.int32(0), r0, c0))

        for i in range(chips):
            def finish(rr, _, i=i):
                a = acc[i * 4 + rr]
                put(i, rr, a, jnp.where(a[HS : HS + 1] > 0, 0.0, lowest_max))
                return 0

            lax.fori_loop(0, 4, finish, 0)

    @pl.when(jnp.logical_not(safe))
    def _():
        for i in range(chips):
            def one_block(rr, _, i=i):
                r = i * 4 + rr
                row = whole_block(r)
                pos = pos_ref[pl.ds(row, 1), :]
                acc[0] = jnp.zeros((ACC_ROWS, ROWS), jnp.float32)

                def one_slot(c, top):
                    s = products(row, r, c)
                    best = top
                    for t in range(TILES):
                        tile = s[t * BLOCK : (t + 1) * BLOCK]
                        tile = jnp.where(iota <= last_key(row, c, t, pos, True), tile, masked_score)
                        s_all[t * BLOCK : (t + 1) * BLOCK, :] = tile
                        best = jnp.maximum(best, jnp.max(tile, 0, keepdims=True))
                    best = best.astype(jnp.bfloat16).astype(jnp.float32)
                    p = jnp.exp2((s_all[...] - best) * LOG2E).astype(jnp.bfloat16)
                    shrink = jnp.exp2((top - best) * LOG2E)
                    acc[0] = acc[0] * shrink + jnp.dot(values(row, c), p, preferred_element_type=jnp.float32)
                    return best

                start = jnp.full((1, ROWS), lowest_max, jnp.bfloat16).astype(jnp.float32)
                top = lax.fori_loop(0, code_ref[row, table + KEY_BLOCKS], one_slot, start)
                put(i, rr, acc[0], top)
                return 0

            lax.fori_loop(0, 4, one_block, 0)


def attend(steps, codes, spots, held, queries, before=()):
    kv, vt, norm = held
    chips = len(steps)
    out = jax.ShapeDtypeStruct((2, ACC_ROWS, queries[0].shape[2]), jnp.bfloat16)
    return pl.pallas_call(
        functools.partial(attention_kernel, steps, bool(before)),
        in_specs=[pl.BlockSpec(memory_space=pl.ANY)] + [VMEM] * (4 + len(queries) + len(before)),
        out_specs=[VMEM] * chips,
        out_shape=[out] * chips,
        scratch_shapes=[
            pltpu.VMEM((2 * chips, HS, queries[0].shape[2]), jnp.bfloat16),
            pltpu.VMEM((SLOTS * TILES * BLOCK, ROWS), jnp.bfloat16),
            pltpu.VMEM((SLOTS * TILES * BLOCK, ROWS), jnp.bfloat16),
            pltpu.VMEM((TILES * BLOCK, ROWS), jnp.float32),
            pltpu.VMEM((4 * chips + 1, ACC_ROWS, ROWS), jnp.float32),
            pltpu.SMEM(codes.shape, jnp.int32),
            pltpu.SemaphoreType.DMA,
        ],
        compiler_params=pltpu.CompilerParams(vmem_limit_bytes=32 * 2**20),
        cost_estimate=pl.CostEstimate(
            flops=chips * 6 * 10**9, bytes_accessed=4 * 2**20, transcendentals=chips * 2**20
        ),
    )(codes, norm, spots, kv, vt, *queries, *before)


def combine_kernel(core_ref, *refs):
    parts, out_ref = refs[:-1], refs[-1]
    groups = out_ref.shape[0] // 2
    half = out_ref.shape[1]
    for j in range(2):
        tops = [p[j, HS + 1 : HS + 2, :].astype(jnp.float32) for p in parts]
        top = functools.reduce(jnp.maximum, tops)
        scales = [jnp.exp(t - top) for t in tops]
        total = sum(
            (p[j, HS : HS + 1, :].astype(jnp.float32) + p[j, HS + 2 : HS + 3, :].astype(jnp.float32)) * scale
            for p, scale in zip(parts, scales)
        )
        summed = sum(p[j, :HS, :].astype(jnp.float32) * scale for p, scale in zip(parts, scales))
        rows = (summed / total).T.astype(jnp.bfloat16)
        first = jnp.bitwise_xor(core_ref[0], j) * groups
        for g in range(groups):
            upper = rows[2 * g * half : (2 * g + 1) * half]
            lower = rows[(2 * g + 1) * half : (2 * g + 2) * half]
            out_ref[first + g] = jnp.concatenate([upper, lower], 1)


def combine(core, parts):
    half = parts[0].shape[2] // 16
    return pl.pallas_call(
        combine_kernel,
        in_specs=[SMEM] + [VMEM] * len(parts),
        out_specs=VMEM,
        out_shape=jax.ShapeDtypeStruct((16, half, 2 * HS), jnp.bfloat16),
        compiler_params=pltpu.CompilerParams(vmem_limit_bytes=32 * 2**20),
    )(core, *parts)


def finish_kernel(grp_ref, pieces_ref, *refs):
    w_refs, out_ref = refs[:-1], refs[-1]
    groups = pieces_ref.shape[0] // 2
    me = grp_ref[0]
    result = None
    for k, w_ref in enumerate(w_refs):
        near = jnp.bitwise_xor(me, k)
        order = [c * groups + g for g in (near, jnp.bitwise_xor(near, 4)) for c in range(2)]
        blocks = [pieces_ref[i] for i in order]
        upper = jnp.concatenate([p[:, :HS] for p in blocks], 1)
        lower = jnp.concatenate([p[:, HS:] for p in blocks], 1)
        attention = jnp.concatenate([upper, lower], 0)
        term = jnp.dot(attention, w_ref[...], preferred_element_type=jnp.float32)
        result = term if result is None else result + term
    out_ref[...] = result.astype(jnp.bfloat16)


def finish(grp, pieces, w_turns):
    return pl.pallas_call(
        finish_kernel,
        in_specs=[SMEM] + [VMEM] * (1 + len(w_turns)),
        out_specs=VMEM,
        out_shape=jax.ShapeDtypeStruct((2 * pieces.shape[1], w_turns[0].shape[1]), jnp.bfloat16),
        compiler_params=pltpu.CompilerParams(vmem_limit_bytes=24 * 2**20),
    )(grp, pieces, *w_turns)


def along_x(by):
    return [(s, s ^ (4 * by)) for s in range(16)]


def came_from(s, by):
    return jnp.bitwise_xor(s, 4 * by)


NEAR_CALLS = ((0,), (1, 3, 2))
FAR_CALLS = ((2, 1, 3), (0,))
CORE_SWAP = [(s, s ^ 1) for s in range(16)]
Y_SWAP = [(s, s ^ 2) for s in range(16)]


def body(inputs, latents, w_query, w_key, w_value, w_out, positions, block_mask):
    seq = lax.axis_index("seq")[None]
    grp = lax.axis_index("grp")[None]
    core = jnp.bitwise_and(seq, 1)

    w_other = lax.ppermute(w_out, "grp", [(g, g ^ 4) for g in range(8)])
    q_chip, theirs, kv_own, kv_other, codes = front(
        seq, latents, inputs, w_query, w_key, w_value, positions, block_mask
    )
    theirs, kv_other, kv_own, w_other = lax.optimization_barrier((theirs, kv_other, kv_own, w_other))
    q_chip = q_chip.at[1].set(lax.ppermute(theirs, "seq", CORE_SWAP))
    queries = {by: q_chip if by == 0 else lax.ppermute(q_chip, "seq", along_x(by)) for by in (0, 1, 3, 2)}
    kv_partner = lax.ppermute(kv_other, "seq", CORE_SWAP)
    near = prepare(kv_own, kv_partner)
    kv_far = [lax.ppermute(kv, "seq", Y_SWAP) for kv in (kv_own, kv_partner)]

    spots = positions.reshape(-1, ROWS)
    near_parts = dict(zip(NEAR_CALLS[0], attend(NEAR_CALLS[0], codes, spots, near, [q_chip])))
    w_other, near_parts[0] = lax.optimization_barrier((w_other, near_parts[0]))
    w_pair = jnp.concatenate([w_out, w_other], 0)
    w_turns = [w_pair] + [
        lax.ppermute(w_pair, "grp", [(g, g ^ k) for g in range(8)]) for k in (1, 2, 3)
    ]

    parts = {}
    last = 0
    for call in NEAR_CALLS[1:]:
        queries[call[0]], near_parts[last], kv_far[0] = lax.optimization_barrier(
            (queries[call[0]], near_parts[last], kv_far[0])
        )
        near_parts.update(zip(call, attend(call, codes, spots, near, [queries[by] for by in call])))
        last = call[-1]
    kv_far, near_parts[last] = lax.optimization_barrier((kv_far, near_parts[last]))
    far = prepare(*kv_far)
    last = None
    for call in FAR_CALLS:
        if last is not None:
            queries[call[0]], parts[last] = lax.optimization_barrier((queries[call[0]], parts[last]))
        done = attend(
            call, codes, spots, far, [queries[by] for by in call], [near_parts[by] for by in call]
        )
        parts.update(zip(call, done))
        last = call[-1]

    parts = [part if by == 0 else lax.ppermute(part, "seq", along_x(by)) for by, part in parts.items()]
    parts, w_turns = lax.optimization_barrier((parts, w_turns))
    pieces = combine(core, parts)
    owners = [[(4 * x + 2 * y + c) * 8 + g for c in range(2) for g in range(8)] for x in range(4) for y in range(2)]
    pieces = lax.all_to_all(pieces, ("seq", "grp"), 0, 0, axis_index_groups=owners)
    return finish(grp, pieces, w_turns)


def solution(mesh):
    return jax.shard_map(
        body,
        mesh=mesh,
        in_specs=(
            P("seq", None),
            P("seq", None),
            P(None, "grp"),
            P(None, "grp"),
            P(None, "grp"),
            P("grp", None),
            P(),
            P(),
        ),
        out_specs=P(("seq", "grp"), None),
        check_vma=False,
    )
```

```python
import functools

import jax
import jax.numpy as jnp
from jax import lax
from jax.experimental import pallas as pl
from jax.experimental.pallas import tpu as pltpu
from jax.sharding import PartitionSpec as P

HS = 64
BLOCK = 128
TILES = 4
SLOTS = 2
ROWS = 2 * BLOCK
DEVICE = 40
FAR = 64
KEY_BLOCKS = 32
ACC_ROWS = 72
LOG2E = 1.4426950408889634
SAFE_SCORE = 60.0
masked_score = -1e30
lowest_max = -1e29
VMEM = pl.BlockSpec(memory_space=pltpu.VMEM)


def in_hbm(*arrays):
    return [pltpu.with_memory_space_constraint(a, pltpu.HBM) for a in arrays]


def list_work(me, pos_ref, mask_ref, code_ref):
    half = KEY_BLOCKS // 2
    both = 2 * KEY_BLOCKS
    blocks = pos_ref.shape[0]

    def held(t):
        source = jnp.bitwise_xor(me, lax.shift_right_logical(t, 4))
        return source * half + jnp.bitwise_and(t, half - 1)

    spots = pos_ref[...].T
    own_block = lax.shift_right_logical(spots, 7)
    furthest = jnp.max(own_block, axis=0, keepdims=True)
    t_rows = lax.broadcasted_iota(jnp.int32, (both, blocks), 0)
    own = jnp.zeros((both, blocks), jnp.int32)
    for t in range(both):
        found = jnp.max((own_block == held(jnp.int32(t))).astype(jnp.int32), axis=0, keepdims=True)
        own = jnp.where(t_rows == t, found, own)

    def exact(condition):
        return condition.astype(jnp.float32).astype(jnp.bfloat16)

    columns = mask_ref.shape[1]
    pick = exact(
        lax.broadcasted_iota(jnp.int32, (both, columns), 1)
        == held(lax.broadcasted_iota(jnp.int32, (both, columns), 0))
    )
    listed = lax.dot_general(
        pick, exact(mask_ref[...] == 1), (((1,), (1,)), ((), ())), preferred_element_type=jnp.float32
    )
    active = exact((own > 0) | ((listed > 0.5) & (held(t_rows) <= furthest)))
    listed = exact(listed > 0.5)

    row = lax.broadcasted_iota(jnp.int32, (blocks, BLOCK), 0)
    col = lax.broadcasted_iota(jnp.int32, (blocks, BLOCK), 1)
    first, second = exact(row == 2 * col), exact(row == 2 * col + 1)
    active = jnp.dot(active, first + second, preferred_element_type=jnp.float32) > 0.5
    listed = [jnp.dot(listed, pairs, preferred_element_type=jnp.float32).astype(jnp.int32) for pairs in (first, second)]
    row = lax.broadcasted_iota(jnp.int32, (both, both), 0)
    col = lax.broadcasted_iota(jnp.int32, (both, both), 1)
    earlier = exact((col < row) & (lax.shift_right_logical(row, 5) == lax.shift_right_logical(col, 5)))
    place = jnp.dot(earlier, exact(active), preferred_element_type=jnp.float32).astype(jnp.int32)
    t_rows = lax.broadcasted_iota(jnp.int32, (both, BLOCK), 0)
    value = jnp.bitwise_and(t_rows, KEY_BLOCKS - 1) + KEY_BLOCKS * (listed[0] + 2 * listed[1] + 4)
    packed = jnp.where(active, place * 512 + value, -1)
    ones = active.astype(jnp.int32)
    slot_rows = lax.broadcasted_iota(jnp.int32, (KEY_BLOCKS, BLOCK), 0)
    tables = []
    for n in range(2):
        codes = jnp.zeros((KEY_BLOCKS, BLOCK), jnp.int32)
        for t in range(n * KEY_BLOCKS, (n + 1) * KEY_BLOCKS):
            one = packed[t : t + 1, :]
            codes = jnp.where(lax.shift_right_arithmetic(one, 9) == slot_rows, jnp.bitwise_and(one, 511), codes)
        count = jnp.sum(ones[n * KEY_BLOCKS : (n + 1) * KEY_BLOCKS], axis=0, keepdims=True)
        slots = jnp.maximum(lax.shift_right_logical(count + (TILES - 1), 2), 1)
        tables += [codes, jnp.broadcast_to(slots, (FAR - KEY_BLOCKS, BLOCK))]
    table = jnp.concatenate(tables, 0).T[: code_ref.shape[0]]
    code_ref[...] = jnp.where(lax.broadcasted_iota(jnp.int32, table.shape, 1) == DEVICE, me, table)


def front_kernel(lat_hbm, x_hbm, wq_hbm, wk_hbm, wv_hbm, pos_hbm, mask_hbm, *rest):
    pair_hbm, theirs_hbm, own_hbm, other_hbm, code_hbm = rest[:5]
    lat, x, wq, wk, wv, pos, mask, pair_ref, theirs_ref, own_ref, other_ref, code_ref = rest[5:17]
    w_all, sems, x_sems, out_sems = rest[17:]
    sent = []

    def send(source, target):
        sent.append(pltpu.make_async_copy(source, target, out_sems.at[len(sent)]))
        sent[-1].start()

    small = [
        pltpu.make_async_copy(source, target, sems.at[i])
        for i, (source, target) in enumerate(
            [(pos_hbm, pos), (mask_hbm, mask), (wq_hbm, wq), (lat_hbm, lat), (wk_hbm, wk), (wv_hbm, wv)]
        )
    ]
    rows = x.shape[0] // x_sems.shape[0]
    parts = [pl.ds(i * rows, rows) for i in range(x_sems.shape[0])]
    large = [pltpu.make_async_copy(x_hbm.at[p], x.at[p], x_sems.at[i]) for i, p in enumerate(parts)]
    for copy in small + large:
        copy.start()
    got_pos, got_mask, got_wq, got_lat, got_wk, got_wv = small
    me = lax.axis_index("seq")
    first = jnp.bitwise_and(me, 1) == 0

    got_pos.wait()
    got_mask.wait()
    list_work(me, pos, mask, code_ref)
    send(code_ref, code_hbm)

    got_wq.wait()
    got_lat.wait()
    q = jnp.dot(lat[...], wq[...], preferred_element_type=jnp.float32).T
    q = q.astype(jnp.bfloat16) * jnp.bfloat16(HS ** -0.5)
    mine = jnp.where(first, q[:HS], q[HS:])
    pair_ref[0] = mine
    pair_ref[1] = mine
    theirs_ref[...] = jnp.where(first, q[HS:], q[:HS])
    send(pair_ref, pair_hbm)
    send(theirs_ref, theirs_hbm)

    got_wk.wait()
    got_wv.wait()
    k, v = wk[...], wv[...]
    head_0 = jnp.concatenate([k[:, :HS], v[:, :HS]], 1)
    head_1 = jnp.concatenate([k[:, HS:], v[:, HS:]], 1)
    w_all[:, : 2 * HS] = jnp.where(first, head_0, head_1)
    w_all[:, 2 * HS :] = jnp.where(first, head_1, head_0)
    for copy, part in zip(large, parts):
        copy.wait()
        both = jnp.dot(x[part, :], w_all[...], preferred_element_type=jnp.float32).astype(jnp.bfloat16)
        own_ref[part, :] = both[:, : 2 * HS]
        other_ref[part, :] = both[:, 2 * HS :]
        send(own_ref.at[part], own_hbm.at[part])
        send(other_ref.at[part], other_hbm.at[part])
    for copy in sent:
        copy.wait()


def front(latents, inputs, w_query, w_key, w_value, positions, block_mask):
    rows, width = latents.shape
    keys = inputs.shape[0]
    spots = positions.reshape(-1, BLOCK)
    operands = (latents, inputs, w_query, w_key, w_value, spots, block_mask)
    q = jax.ShapeDtypeStruct((HS, rows), jnp.bfloat16)
    kv = jax.ShapeDtypeStruct((keys, 2 * HS), jnp.bfloat16)
    results = [jax.ShapeDtypeStruct((2, HS, rows), jnp.bfloat16), q, kv, kv, jax.ShapeDtypeStruct((spots.shape[0] // 2, BLOCK), jnp.int32)]
    return pl.pallas_call(
        front_kernel,
        in_specs=[pl.BlockSpec(memory_space=pl.ANY)] * len(operands),
        out_specs=[pl.BlockSpec(memory_space=pl.ANY)] * 5,
        out_shape=results,
        scratch_shapes=[pltpu.VMEM(a.shape, a.dtype) for a in (*operands, *results)]
        + [
            pltpu.VMEM((width, 4 * HS), jnp.bfloat16),
            pltpu.SemaphoreType.DMA((6,)),
            pltpu.SemaphoreType.DMA((1,)),
            pltpu.SemaphoreType.DMA((5,)),
        ],
        compiler_params=pltpu.CompilerParams(vmem_limit_bytes=24 * 2**20),
        cost_estimate=pl.CostEstimate(
            flops=2 * (keys * 4 + rows * 2) * width * HS, bytes_accessed=6 * 2**20, transcendentals=0
        ),
    )(*in_hbm(*operands))


def prepare_kernel(*refs):
    sources, (kv_ref, vt_ref, norm_ref) = refs[:-3], refs[-3:]
    each = KEY_BLOCKS // len(sources)
    most = None
    for t in range(KEY_BLOCKS):
        at = t % each
        tile = sources[t // each][at * BLOCK : (at + 1) * BLOCK, :]
        kv_ref[t * BLOCK : (t + 1) * BLOCK, :] = tile
        turned = tile.T
        vt_ref[:HS, t * BLOCK : (t + 1) * BLOCK] = turned[HS:, :]
        k = turned[:HS, :].astype(jnp.float32)
        squares = jnp.sum(k * k, axis=0, keepdims=True)
        most = squares if most is None else jnp.maximum(most, squares)
    vt_ref[HS:, :] = jnp.ones((ACC_ROWS - HS, KEY_BLOCKS * BLOCK), jnp.bfloat16)
    norm_ref[...] = most


def prepare(*sources):
    keys = sum(source.shape[0] for source in sources)
    return pl.pallas_call(
        prepare_kernel,
        in_specs=[VMEM] * len(sources),
        out_specs=[VMEM] * 3,
        out_shape=[
            jax.ShapeDtypeStruct((keys, 2 * HS), jnp.bfloat16),
            jax.ShapeDtypeStruct((ACC_ROWS, keys), jnp.bfloat16),
            jax.ShapeDtypeStruct((1, BLOCK), jnp.float32),
        ],
        compiler_params=pltpu.CompilerParams(vmem_limit_bytes=24 * 2**20),
    )(*sources)


def attention_kernel(steps, far, code_any, norm_ref, pos_ref, kv_ref, vt_ref, *rest):
    chips = len(steps)
    q_refs, rest = rest[:chips], rest[chips:]
    before_refs, rest = (rest[:chips], rest[chips:]) if far else (None, rest)
    o_refs, (q_all, p_a, p_b, s_all, acc, code_ref, sem) = rest[:chips], rest[chips:]
    table = FAR if far else 0
    got_codes = pltpu.make_async_copy(code_any, code_ref, sem)
    got_codes.start()
    blocks = 4 * chips
    iota = lax.broadcasted_iota(jnp.int32, (BLOCK, ROWS), 0)
    in_first = lax.broadcasted_iota(jnp.int32, (1, ROWS), 1) < BLOCK
    iota_half = iota.astype(jnp.float32).astype(jnp.bfloat16)

    most = None
    for i, ref in enumerate(q_refs):
        for j in range(ref.shape[0]):
            q = ref[j]
            q_all[i * ref.shape[0] + j] = q
            q = q.astype(jnp.float32)
            squares = jnp.sum(q * q, axis=0, keepdims=True)
            most = squares if most is None else jnp.maximum(most, squares)
    safe = jnp.max(most) * jnp.max(norm_ref[...]) <= SAFE_SCORE * SAFE_SCORE
    got_codes.wait()
    me = code_ref[0, DEVICE]
    keys_of = jnp.bitwise_xor(me, 2) if far else me
    own_base = keys_of * (KEY_BLOCKS // 2 * BLOCK)
    partner_base = jnp.bitwise_xor(keys_of, 1) * (KEY_BLOCKS // 2 * BLOCK)
    sources = [came_from(me, step) for step in steps]

    def clamp(r):
        return jnp.minimum(r, blocks - 1)

    def whole_block(r):
        shard = sources[-1]
        for i in range(chips - 1):
            shard = jnp.where(lax.div(r, 4) == i, sources[i], shard)
        return jnp.bitwise_xor(shard, jnp.bitwise_and(lax.div(r, 2), 1)) * 2 + lax.rem(r, 2)

    def offset(i):
        return pl.multiple_of(i * BLOCK, BLOCK)

    def row_offset(i):
        return pl.multiple_of(i * ROWS, ROWS)

    def query(r):
        q = q_all[lax.div(r, 2), :, pl.ds(row_offset(lax.rem(r, 2)), ROWS)]
        return jnp.concatenate([q, jnp.zeros_like(q)], 0)

    def key_blocks(row, c):
        return [jnp.bitwise_and(code_ref[row, table + c * TILES + t], KEY_BLOCKS - 1) for t in range(TILES)]

    def products(row, r, c):
        keys = jnp.concatenate([kv_ref[pl.ds(offset(k), BLOCK), :] for k in key_blocks(row, c)], 0)
        return jnp.dot(keys, query(r), preferred_element_type=jnp.float32)

    def values(row, c):
        return jnp.concatenate([vt_ref[:, pl.ds(offset(k), BLOCK)] for k in key_blocks(row, c)], 1)

    def last_key(row, c, t, pos, real):
        code = code_ref[row, table + c * TILES + t]
        k = jnp.bitwise_and(code, KEY_BLOCKS - 1)
        half = KEY_BLOCKS // 2
        base = jnp.where(k < half, own_base, partner_base - half * BLOCK) + k * BLOCK
        real = jnp.logical_and(real, code >= 4 * KEY_BLOCKS)
        reach = [jnp.where(jnp.bitwise_and(code, n * KEY_BLOCKS) > 0, 1 << 30, BLOCK) for n in (1, 2)]
        reach = jnp.where(in_first, *[jnp.where(real, n, -(1 << 30)) for n in reach])
        ahead = pos - base
        return jnp.where(ahead < reach, jnp.minimum(ahead, BLOCK - 1), -1)

    def put(i, rr, a, top):
        at = (lax.div(rr, 2), slice(None), pl.ds(row_offset(lax.rem(rr, 2)), ROWS))
        if far:
            before = before_refs[i][at].astype(jnp.float32)
            top_before, top_now = before[HS + 1 : HS + 2], top
            top = jnp.maximum(top_before, top_now)
            shrink, shrink_before = jnp.exp(top_now - top), jnp.exp(top_before - top)
            total = a[HS : HS + 1] * shrink + (before[HS : HS + 1] + before[HS + 2 : HS + 3]) * shrink_before
            a = a * shrink + before * shrink_before
        else:
            total = a[HS : HS + 1]
        low = total - total.astype(jnp.bfloat16).astype(jnp.float32)
        out = jnp.concatenate([a[:HS], total, top, low, a[HS + 3 :]], 0)
        o_refs[i][at] = out.astype(jnp.bfloat16)

    def advance(r, c):
        last = c + 1 >= code_ref[whole_block(clamp(r)), table + KEY_BLOCKS]
        return jnp.where(last, jnp.minimum(r + 1, blocks), r), jnp.where(last, 0, c + 1)

    def step_slots(r, c):
        slots = []
        for _ in range(SLOTS):
            slots.append((r, c))
            r, c = advance(r, c)
        return slots, r, c

    @pl.when(safe)
    def _():
        acc[...] = jnp.zeros_like(acc)

        def weigh(p_ref, slots):
            for g, (r, c) in enumerate(slots):
                rr = clamp(r)
                row = whole_block(rr)
                s = products(row, rr, c)
                pos = pos_ref[pl.ds(row, 1), :]
                for t in range(TILES):
                    p = jnp.exp2(s[t * BLOCK : (t + 1) * BLOCK] * LOG2E).astype(jnp.bfloat16)
                    last = last_key(row, c, t, pos, r < blocks).astype(jnp.float32).astype(jnp.bfloat16)
                    at = (g * TILES + t) * BLOCK
                    p_ref[at : at + BLOCK, :] = jnp.where(iota_half <= last, p, jnp.zeros_like(p))

        def add(p_ref, slots):
            for g, (r, c) in enumerate(slots):
                v = values(whole_block(clamp(r)), c)
                at = g * TILES * BLOCK
                acc[r] += jnp.dot(v, p_ref[at : at + TILES * BLOCK, :], preferred_element_type=jnp.float32)

        slots_0, r0, c0 = step_slots(jnp.int32(0), jnp.int32(0))
        weigh(p_a, slots_0)

        def two_steps(_, state):
            r, c, r1, c1 = state
            slots, _, _ = step_slots(r, c)
            slots_1, r2, c2 = step_slots(r1, c1)
            weigh(p_b, slots_1)
            add(p_a, slots)
            slots_2, r3, c3 = step_slots(r2, c2)
            weigh(p_a, slots_2)
            add(p_b, slots_1)
            return r2, c2, r3, c3

        items = lax.fori_loop(0, blocks, lambda r, n: n + code_ref[whole_block(r), table + KEY_BLOCKS], jnp.int32(0))
        turns = lax.div(items + (2 * SLOTS - 1), 2 * SLOTS)
        lax.fori_loop(0, turns, two_steps, (jnp.int32(0), jnp.int32(0), r0, c0))

        for i in range(chips):
            def finish(rr, _, i=i):
                a = acc[i * 4 + rr]
                put(i, rr, a, jnp.where(a[HS : HS + 1] > 0, 0.0, lowest_max))
                return 0

            lax.fori_loop(0, 4, finish, 0)

    @pl.when(jnp.logical_not(safe))
    def _():
        for i in range(chips):
            def one_block(rr, _, i=i):
                r = i * 4 + rr
                row = whole_block(r)
                pos = pos_ref[pl.ds(row, 1), :]
                acc[0] = jnp.zeros((ACC_ROWS, ROWS), jnp.float32)

                def one_slot(c, top):
                    s = products(row, r, c)
                    best = top
                    for t in range(TILES):
                        tile = s[t * BLOCK : (t + 1) * BLOCK]
                        tile = jnp.where(iota <= last_key(row, c, t, pos, True), tile, masked_score)
                        s_all[t * BLOCK : (t + 1) * BLOCK, :] = tile
                        best = jnp.maximum(best, jnp.max(tile, 0, keepdims=True))
                    best = best.astype(jnp.bfloat16).astype(jnp.float32)
                    p = jnp.exp2((s_all[...] - best) * LOG2E).astype(jnp.bfloat16)
                    shrink = jnp.exp2((top - best) * LOG2E)
                    acc[0] = acc[0] * shrink + jnp.dot(values(row, c), p, preferred_element_type=jnp.float32)
                    return best

                start = jnp.full((1, ROWS), lowest_max, jnp.bfloat16).astype(jnp.float32)
                top = lax.fori_loop(0, code_ref[row, table + KEY_BLOCKS], one_slot, start)
                put(i, rr, acc[0], top)
                return 0

            lax.fori_loop(0, 4, one_block, 0)


def attend(steps, codes, spots, held, queries, before=()):
    kv, vt, norm = held
    chips = len(steps)
    out = jax.ShapeDtypeStruct((2, ACC_ROWS, queries[0].shape[2]), jnp.bfloat16)
    return pl.pallas_call(
        functools.partial(attention_kernel, steps, bool(before)),
        in_specs=[pl.BlockSpec(memory_space=pl.ANY)] + [VMEM] * (4 + len(queries) + len(before)),
        out_specs=[VMEM] * chips,
        out_shape=[out] * chips,
        scratch_shapes=[
            pltpu.VMEM((2 * chips, HS, queries[0].shape[2]), jnp.bfloat16),
            pltpu.VMEM((SLOTS * TILES * BLOCK, ROWS), jnp.bfloat16),
            pltpu.VMEM((SLOTS * TILES * BLOCK, ROWS), jnp.bfloat16),
            pltpu.VMEM((TILES * BLOCK, ROWS), jnp.float32),
            pltpu.VMEM((4 * chips + 1, ACC_ROWS, ROWS), jnp.float32),
            pltpu.SMEM(codes.shape, jnp.int32),
            pltpu.SemaphoreType.DMA,
        ],
        compiler_params=pltpu.CompilerParams(vmem_limit_bytes=32 * 2**20),
        cost_estimate=pl.CostEstimate(
            flops=chips * 6 * 10**9, bytes_accessed=4 * 2**20, transcendentals=chips * 2**20
        ),
    )(codes, norm, spots, kv, vt, *queries, *before)


def combine_kernel(*refs):
    core = jnp.bitwise_and(lax.axis_index("seq"), 1)
    parts, out_ref = refs[:-1], refs[-1]
    groups = out_ref.shape[0] // 2
    half = out_ref.shape[1]
    for j in range(2):
        tops = [p[j, HS + 1 : HS + 2, :].astype(jnp.float32) for p in parts]
        top = functools.reduce(jnp.maximum, tops)
        scales = [jnp.exp(t - top) for t in tops]
        total = sum(
            (p[j, HS : HS + 1, :].astype(jnp.float32) + p[j, HS + 2 : HS + 3, :].astype(jnp.float32)) * scale
            for p, scale in zip(parts, scales)
        )
        summed = sum(p[j, :HS, :].astype(jnp.float32) * scale for p, scale in zip(parts, scales))
        rows = (summed / total).T.astype(jnp.bfloat16)
        first = jnp.bitwise_xor(core, j) * groups
        for g in range(groups):
            upper = rows[2 * g * half : (2 * g + 1) * half]
            lower = rows[(2 * g + 1) * half : (2 * g + 2) * half]
            out_ref[first + g] = jnp.concatenate([upper, lower], 1)


def combine(parts):
    half = parts[0].shape[2] // 16
    return pl.pallas_call(
        combine_kernel,
        in_specs=[VMEM] * len(parts),
        out_specs=VMEM,
        out_shape=jax.ShapeDtypeStruct((16, half, 2 * HS), jnp.bfloat16),
        compiler_params=pltpu.CompilerParams(vmem_limit_bytes=32 * 2**20),
    )(*parts)


def finish_kernel(pieces_ref, *refs):
    w_refs, out_ref = refs[:-1], refs[-1]
    groups = pieces_ref.shape[0] // 2
    me = lax.axis_index("grp")
    result = None
    for k, w_ref in enumerate(w_refs):
        near = jnp.bitwise_xor(me, k)
        order = [c * groups + g for g in (near, jnp.bitwise_xor(near, 4)) for c in range(2)]
        blocks = [pieces_ref[i] for i in order]
        upper = jnp.concatenate([p[:, :HS] for p in blocks], 1)
        lower = jnp.concatenate([p[:, HS:] for p in blocks], 1)
        attention = jnp.concatenate([upper, lower], 0)
        term = jnp.dot(attention, w_ref[...], preferred_element_type=jnp.float32)
        result = term if result is None else result + term
    out_ref[...] = result.astype(jnp.bfloat16)


def finish(pieces, w_turns):
    return pl.pallas_call(
        finish_kernel,
        in_specs=[VMEM] * (1 + len(w_turns)),
        out_specs=VMEM,
        out_shape=jax.ShapeDtypeStruct((2 * pieces.shape[1], w_turns[0].shape[1]), jnp.bfloat16),
        compiler_params=pltpu.CompilerParams(vmem_limit_bytes=24 * 2**20),
    )(pieces, *w_turns)


def along_x(by):
    return [(s, s ^ (4 * by)) for s in range(16)]


def came_from(s, by):
    return jnp.bitwise_xor(s, 4 * by)


NEAR_CALLS = ((0,), (1, 3, 2))
FAR_CALLS = ((2, 1, 3), (0,))
CORE_SWAP = [(s, s ^ 1) for s in range(16)]
Y_SWAP = [(s, s ^ 2) for s in range(16)]


def body(inputs, latents, w_query, w_key, w_value, w_out, positions, block_mask):
    w_other = lax.ppermute(w_out, "grp", [(g, g ^ 4) for g in range(8)])
    q_chip, theirs, kv_own, kv_other, codes = front(
        latents, inputs, w_query, w_key, w_value, positions, block_mask
    )
    theirs, kv_other, kv_own, w_other = lax.optimization_barrier((theirs, kv_other, kv_own, w_other))
    q_chip = q_chip.at[1].set(lax.ppermute(theirs, "seq", CORE_SWAP))
    queries = {by: q_chip if by == 0 else lax.ppermute(q_chip, "seq", along_x(by)) for by in (0, 1, 3, 2)}
    kv_partner = lax.ppermute(kv_other, "seq", CORE_SWAP)
    near = prepare(kv_own, kv_partner)
    kv_far = [lax.ppermute(kv, "seq", Y_SWAP) for kv in (kv_own, kv_partner)]

    spots = positions.reshape(-1, ROWS)
    near_parts = dict(zip(NEAR_CALLS[0], attend(NEAR_CALLS[0], codes, spots, near, [q_chip])))
    w_other, near_parts[0] = lax.optimization_barrier((w_other, near_parts[0]))
    w_pair = jnp.concatenate([w_out, w_other], 0)
    w_turns = [w_pair] + [
        lax.ppermute(w_pair, "grp", [(g, g ^ k) for g in range(8)]) for k in (1, 2, 3)
    ]

    parts = {}
    last = 0
    for call in NEAR_CALLS[1:]:
        queries[call[0]], near_parts[last], kv_far[0] = lax.optimization_barrier(
            (queries[call[0]], near_parts[last], kv_far[0])
        )
        near_parts.update(zip(call, attend(call, codes, spots, near, [queries[by] for by in call])))
        last = call[-1]
    kv_far, near_parts[last] = lax.optimization_barrier((kv_far, near_parts[last]))
    far = prepare(*kv_far)
    last = None
    for call in FAR_CALLS:
        if last is not None:
            queries[call[0]], parts[last] = lax.optimization_barrier((queries[call[0]], parts[last]))
        done = attend(
            call, codes, spots, far, [queries[by] for by in call], [near_parts[by] for by in call]
        )
        parts.update(zip(call, done))
        last = call[-1]

    parts = [part if by == 0 else lax.ppermute(part, "seq", along_x(by)) for by, part in parts.items()]
    parts, w_turns = lax.optimization_barrier((parts, w_turns))
    pieces = combine(parts)
    owners = [[(4 * x + 2 * y + c) * 8 + g for c in range(2) for g in range(8)] for x in range(4) for y in range(2)]
    pieces = lax.all_to_all(pieces, ("seq", "grp"), 0, 0, axis_index_groups=owners)
    return finish(pieces, w_turns)


def solution(mesh):
    return jax.shard_map(
        body,
        mesh=mesh,
        in_specs=(
            P("seq", None),
            P("seq", None),
            P(None, "grp"),
            P(None, "grp"),
            P(None, "grp"),
            P("grp", None),
            P(),
            P(),
        ),
        out_specs=P(("seq", "grp"), None),
        check_vma=False,
    )
```

```python
import functools

import jax
import jax.numpy as jnp
from jax import lax
from jax.experimental import pallas as pl
from jax.experimental.pallas import tpu as pltpu
from jax.sharding import PartitionSpec as P

HS = 64
BLOCK = 128
TILES = 4
SLOTS = 2
ROWS = 2 * BLOCK
DEVICE = 40
FAR = 64
KEY_BLOCKS = 32
ACC_ROWS = 72
LOG2E = 1.4426950408889634
SAFE_SCORE = 60.0
masked_score = -1e30
lowest_max = -1e29
VMEM = pl.BlockSpec(memory_space=pltpu.VMEM)


def in_hbm(*arrays):
    return [pltpu.with_memory_space_constraint(a, pltpu.HBM) for a in arrays]


def list_work(me, pos_ref, mask_ref, code_ref):
    half = KEY_BLOCKS // 2
    both = 2 * KEY_BLOCKS
    blocks = pos_ref.shape[0]

    def held(t):
        source = jnp.bitwise_xor(me, lax.shift_right_logical(t, 4))
        return source * half + jnp.bitwise_and(t, half - 1)

    spots = pos_ref[...].T
    own_block = lax.shift_right_logical(spots, 7)
    furthest = jnp.max(own_block, axis=0, keepdims=True)
    t_rows = lax.broadcasted_iota(jnp.int32, (both, blocks), 0)
    own = jnp.zeros((both, blocks), jnp.int32)
    for t in range(both):
        found = jnp.max((own_block == held(jnp.int32(t))).astype(jnp.int32), axis=0, keepdims=True)
        own = jnp.where(t_rows == t, found, own)

    def exact(condition):
        return condition.astype(jnp.float32).astype(jnp.bfloat16)

    columns = mask_ref.shape[1]
    pick = exact(
        lax.broadcasted_iota(jnp.int32, (both, columns), 1)
        == held(lax.broadcasted_iota(jnp.int32, (both, columns), 0))
    )
    listed = lax.dot_general(
        pick, exact(mask_ref[...] == 1), (((1,), (1,)), ((), ())), preferred_element_type=jnp.float32
    )
    active = exact((own > 0) | ((listed > 0.5) & (held(t_rows) <= furthest)))
    listed = exact(listed > 0.5)

    row = lax.broadcasted_iota(jnp.int32, (blocks, BLOCK), 0)
    col = lax.broadcasted_iota(jnp.int32, (blocks, BLOCK), 1)
    first, second = exact(row == 2 * col), exact(row == 2 * col + 1)
    active = jnp.dot(active, first + second, preferred_element_type=jnp.float32) > 0.5
    listed = [jnp.dot(listed, pairs, preferred_element_type=jnp.float32).astype(jnp.int32) for pairs in (first, second)]
    row = lax.broadcasted_iota(jnp.int32, (both, both), 0)
    col = lax.broadcasted_iota(jnp.int32, (both, both), 1)
    earlier = exact((col < row) & (lax.shift_right_logical(row, 5) == lax.shift_right_logical(col, 5)))
    place = jnp.dot(earlier, exact(active), preferred_element_type=jnp.float32).astype(jnp.int32)
    t_rows = lax.broadcasted_iota(jnp.int32, (both, BLOCK), 0)
    value = jnp.bitwise_and(t_rows, KEY_BLOCKS - 1) + KEY_BLOCKS * (listed[0] + 2 * listed[1] + 4)
    packed = jnp.where(active, place * 512 + value, -1)
    ones = active.astype(jnp.int32)
    slot_rows = lax.broadcasted_iota(jnp.int32, (KEY_BLOCKS, BLOCK), 0)
    tables = []
    for n in range(2):
        codes = jnp.zeros((KEY_BLOCKS, BLOCK), jnp.int32)
        for t in range(n * KEY_BLOCKS, (n + 1) * KEY_BLOCKS):
            one = packed[t : t + 1, :]
            codes = jnp.where(lax.shift_right_arithmetic(one, 9) == slot_rows, jnp.bitwise_and(one, 511), codes)
        count = jnp.sum(ones[n * KEY_BLOCKS : (n + 1) * KEY_BLOCKS], axis=0, keepdims=True)
        slots = jnp.maximum(lax.shift_right_logical(count + (TILES - 1), 2), 1)
        tables += [codes, jnp.broadcast_to(slots, (FAR - KEY_BLOCKS, BLOCK))]
    table = jnp.concatenate(tables, 0).T[: code_ref.shape[0]]
    code_ref[...] = jnp.where(lax.broadcasted_iota(jnp.int32, table.shape, 1) == DEVICE, me, table)


def front_kernel(lat_hbm, x_hbm, wq_hbm, wk_hbm, wv_hbm, pos_hbm, mask_hbm, *rest):
    pair_hbm, theirs_hbm, own_hbm, other_hbm, code_hbm = rest[:5]
    lat, x, wq, wk, wv, pos, mask, pair_ref, theirs_ref, own_ref, other_ref, code_ref = rest[5:17]
    w_all, sems, x_sems, out_sems = rest[17:]
    sent = []

    def send(source, target):
        sent.append(pltpu.make_async_copy(source, target, out_sems.at[len(sent)]))
        sent[-1].start()

    small = [
        pltpu.make_async_copy(source, target, sems.at[i])
        for i, (source, target) in enumerate(
            [(pos_hbm, pos), (mask_hbm, mask), (wq_hbm, wq), (lat_hbm, lat), (wk_hbm, wk), (wv_hbm, wv)]
        )
    ]
    rows = x.shape[0] // x_sems.shape[0]
    parts = [pl.ds(i * rows, rows) for i in range(x_sems.shape[0])]
    large = [pltpu.make_async_copy(x_hbm.at[p], x.at[p], x_sems.at[i]) for i, p in enumerate(parts)]
    for copy in small + large:
        copy.start()
    got_pos, got_mask, got_wq, got_lat, got_wk, got_wv = small
    me = lax.axis_index("seq")
    first = jnp.bitwise_and(me, 1) == 0

    got_pos.wait()
    got_mask.wait()
    list_work(me, pos, mask, code_ref)
    send(code_ref, code_hbm)

    got_wq.wait()
    got_lat.wait()
    q = jnp.dot(lat[...], wq[...], preferred_element_type=jnp.float32).T
    q = q.astype(jnp.bfloat16) * jnp.bfloat16(HS ** -0.5)
    mine = jnp.where(first, q[:HS], q[HS:])
    pair_ref[0] = mine
    pair_ref[1] = mine
    theirs_ref[...] = jnp.where(first, q[HS:], q[:HS])
    send(pair_ref, pair_hbm)
    send(theirs_ref, theirs_hbm)

    got_wk.wait()
    got_wv.wait()
    k, v = wk[...], wv[...]
    head_0 = jnp.concatenate([k[:, :HS], v[:, :HS]], 1)
    head_1 = jnp.concatenate([k[:, HS:], v[:, HS:]], 1)
    w_all[:, : 2 * HS] = jnp.where(first, head_0, head_1)
    w_all[:, 2 * HS :] = jnp.where(first, head_1, head_0)
    for copy, part in zip(large, parts):
        copy.wait()
        both = jnp.dot(x[part, :], w_all[...], preferred_element_type=jnp.float32).astype(jnp.bfloat16)
        own_ref[part, :] = both[:, : 2 * HS]
        other_ref[part, :] = both[:, 2 * HS :]
        send(own_ref.at[part], own_hbm.at[part])
        send(other_ref.at[part], other_hbm.at[part])
    for copy in sent:
        copy.wait()


def front(latents, inputs, w_query, w_key, w_value, positions, block_mask):
    rows, width = latents.shape
    keys = inputs.shape[0]
    spots = positions.reshape(-1, BLOCK)
    operands = (latents, inputs, w_query, w_key, w_value, spots, block_mask)
    q = jax.ShapeDtypeStruct((HS, rows), jnp.bfloat16)
    kv = jax.ShapeDtypeStruct((keys, 2 * HS), jnp.bfloat16)
    results = [jax.ShapeDtypeStruct((2, HS, rows), jnp.bfloat16), q, kv, kv, jax.ShapeDtypeStruct((spots.shape[0] // 2, BLOCK), jnp.int32)]
    return pl.pallas_call(
        front_kernel,
        in_specs=[pl.BlockSpec(memory_space=pl.ANY)] * len(operands),
        out_specs=[pl.BlockSpec(memory_space=pl.ANY)] * 5,
        out_shape=results,
        scratch_shapes=[pltpu.VMEM(a.shape, a.dtype) for a in (*operands, *results)]
        + [
            pltpu.VMEM((width, 4 * HS), jnp.bfloat16),
            pltpu.SemaphoreType.DMA((6,)),
            pltpu.SemaphoreType.DMA((1,)),
            pltpu.SemaphoreType.DMA((5,)),
        ],
        compiler_params=pltpu.CompilerParams(vmem_limit_bytes=24 * 2**20),
        cost_estimate=pl.CostEstimate(
            flops=2 * (keys * 4 + rows * 2) * width * HS, bytes_accessed=6 * 2**20, transcendentals=0
        ),
    )(*in_hbm(*operands))


def prepare_kernel(*refs):
    sources, (kv_ref, vt_ref, norm_ref) = refs[:-3], refs[-3:]
    each = KEY_BLOCKS // len(sources)
    most = None
    for t in range(KEY_BLOCKS):
        at = t % each
        tile = sources[t // each][at * BLOCK : (at + 1) * BLOCK, :]
        kv_ref[t * BLOCK : (t + 1) * BLOCK, :] = tile
        turned = tile.T
        vt_ref[:HS, t * BLOCK : (t + 1) * BLOCK] = turned[HS:, :]
        k = turned[:HS, :].astype(jnp.float32)
        squares = jnp.sum(k * k, axis=0, keepdims=True)
        most = squares if most is None else jnp.maximum(most, squares)
    vt_ref[HS:, :] = jnp.ones((ACC_ROWS - HS, KEY_BLOCKS * BLOCK), jnp.bfloat16)
    norm_ref[...] = most


def prepare(*sources):
    keys = sum(source.shape[0] for source in sources)
    return pl.pallas_call(
        prepare_kernel,
        in_specs=[VMEM] * len(sources),
        out_specs=[VMEM] * 3,
        out_shape=[
            jax.ShapeDtypeStruct((keys, 2 * HS), jnp.bfloat16),
            jax.ShapeDtypeStruct((ACC_ROWS, keys), jnp.bfloat16),
            jax.ShapeDtypeStruct((1, BLOCK), jnp.float32),
        ],
        compiler_params=pltpu.CompilerParams(vmem_limit_bytes=24 * 2**20),
    )(*sources)


def attention_kernel(steps, far, code_any, norm_ref, pos_ref, kv_ref, vt_ref, *rest):
    chips = len(steps)
    q_refs, rest = rest[:chips], rest[chips:]
    before_refs, rest = (rest[:chips], rest[chips:]) if far else (None, rest)
    o_refs, (q_all, p_a, p_b, s_all, acc, code_ref, sem) = rest[:chips], rest[chips:]
    table = FAR if far else 0
    got_codes = pltpu.make_async_copy(code_any, code_ref, sem)
    got_codes.start()
    blocks = 4 * chips
    iota = lax.broadcasted_iota(jnp.int32, (BLOCK, ROWS), 0)
    in_first = lax.broadcasted_iota(jnp.int32, (1, ROWS), 1) < BLOCK
    iota_half = iota.astype(jnp.float32).astype(jnp.bfloat16)

    most = None
    for i, ref in enumerate(q_refs):
        for j in range(ref.shape[0]):
            q = ref[j]
            q_all[i * ref.shape[0] + j] = q
            q = q.astype(jnp.float32)
            squares = jnp.sum(q * q, axis=0, keepdims=True)
            most = squares if most is None else jnp.maximum(most, squares)
    safe = jnp.max(most) * jnp.max(norm_ref[...]) <= SAFE_SCORE * SAFE_SCORE
    got_codes.wait()
    me = code_ref[0, DEVICE]
    keys_of = jnp.bitwise_xor(me, 2) if far else me
    own_base = keys_of * (KEY_BLOCKS // 2 * BLOCK)
    partner_base = jnp.bitwise_xor(keys_of, 1) * (KEY_BLOCKS // 2 * BLOCK)
    sources = [came_from(me, step) for step in steps]

    def clamp(r):
        return jnp.minimum(r, blocks - 1)

    def whole_block(r):
        shard = sources[-1]
        for i in range(chips - 1):
            shard = jnp.where(lax.div(r, 4) == i, sources[i], shard)
        return jnp.bitwise_xor(shard, jnp.bitwise_and(lax.div(r, 2), 1)) * 2 + lax.rem(r, 2)

    def offset(i):
        return pl.multiple_of(i * BLOCK, BLOCK)

    def row_offset(i):
        return pl.multiple_of(i * ROWS, ROWS)

    def query(r):
        q = q_all[lax.div(r, 2), :, pl.ds(row_offset(lax.rem(r, 2)), ROWS)]
        return jnp.concatenate([q, jnp.zeros_like(q)], 0)

    def key_blocks(row, c):
        return [jnp.bitwise_and(code_ref[row, table + c * TILES + t], KEY_BLOCKS - 1) for t in range(TILES)]

    def products(row, r, c):
        keys = jnp.concatenate([kv_ref[pl.ds(offset(k), BLOCK), :] for k in key_blocks(row, c)], 0)
        return jnp.dot(keys, query(r), preferred_element_type=jnp.float32)

    def values(row, c):
        return jnp.concatenate([vt_ref[:, pl.ds(offset(k), BLOCK)] for k in key_blocks(row, c)], 1)

    def last_key(row, c, t, pos, real):
        code = code_ref[row, table + c * TILES + t]
        k = jnp.bitwise_and(code, KEY_BLOCKS - 1)
        half = KEY_BLOCKS // 2
        base = jnp.where(k < half, own_base, partner_base - half * BLOCK) + k * BLOCK
        real = jnp.logical_and(real, code >= 4 * KEY_BLOCKS)
        reach = [jnp.where(jnp.bitwise_and(code, n * KEY_BLOCKS) > 0, 1 << 30, BLOCK) for n in (1, 2)]
        reach = jnp.where(in_first, *[jnp.where(real, n, -(1 << 30)) for n in reach])
        ahead = pos - base
        return jnp.where(ahead < reach, ahead, -1)

    def put(i, rr, a, top):
        at = (lax.div(rr, 2), slice(None), pl.ds(row_offset(lax.rem(rr, 2)), ROWS))
        if far:
            before = before_refs[i][at].astype(jnp.float32)
            top_before, top_now = before[HS + 1 : HS + 2], top
            top = jnp.maximum(top_before, top_now)
            shrink, shrink_before = jnp.exp(top_now - top), jnp.exp(top_before - top)
            total = a[HS : HS + 1] * shrink + (before[HS : HS + 1] + before[HS + 2 : HS + 3]) * shrink_before
            a = a * shrink + before * shrink_before
        else:
            total = a[HS : HS + 1]
        low = total - total.astype(jnp.bfloat16).astype(jnp.float32)
        out = jnp.concatenate([a[:HS], total, top, low, a[HS + 3 :]], 0)
        o_refs[i][at] = out.astype(jnp.bfloat16)

    def advance(r, c):
        last = c + 1 >= code_ref[whole_block(clamp(r)), table + KEY_BLOCKS]
        return jnp.where(last, jnp.minimum(r + 1, blocks), r), jnp.where(last, 0, c + 1)

    def step_slots(r, c):
        slots = []
        for _ in range(SLOTS):
            slots.append((r, c))
            r, c = advance(r, c)
        return slots, r, c

    @pl.when(safe)
    def _():
        acc[...] = jnp.zeros_like(acc)

        def weigh(p_ref, slots):
            for g, (r, c) in enumerate(slots):
                rr = clamp(r)
                row = whole_block(rr)
                s = products(row, rr, c)
                pos = pos_ref[pl.ds(row, 1), :]
                for t in range(TILES):
                    p = jnp.exp2(s[t * BLOCK : (t + 1) * BLOCK] * LOG2E).astype(jnp.bfloat16)
                    last = last_key(row, c, t, pos, r < blocks).astype(jnp.float32).astype(jnp.bfloat16)
                    at = (g * TILES + t) * BLOCK
                    p_ref[at : at + BLOCK, :] = jnp.where(iota_half <= last, p, jnp.zeros_like(p))

        def add(p_ref, slots):
            for g, (r, c) in enumerate(slots):
                v = values(whole_block(clamp(r)), c)
                at = g * TILES * BLOCK
                acc[r] += jnp.dot(v, p_ref[at : at + TILES * BLOCK, :], preferred_element_type=jnp.float32)

        slots_0, r0, c0 = step_slots(jnp.int32(0), jnp.int32(0))
        weigh(p_a, slots_0)

        def two_steps(_, state):
            r, c, r1, c1 = state
            slots, _, _ = step_slots(r, c)
            slots_1, r2, c2 = step_slots(r1, c1)
            weigh(p_b, slots_1)
            add(p_a, slots)
            slots_2, r3, c3 = step_slots(r2, c2)
            weigh(p_a, slots_2)
            add(p_b, slots_1)
            return r2, c2, r3, c3

        items = lax.fori_loop(0, blocks, lambda r, n: n + code_ref[whole_block(r), table + KEY_BLOCKS], jnp.int32(0))
        turns = lax.div(items + (2 * SLOTS - 1), 2 * SLOTS)
        lax.fori_loop(0, turns, two_steps, (jnp.int32(0), jnp.int32(0), r0, c0))

        for i in range(chips):
            def finish(rr, _, i=i):
                a = acc[i * 4 + rr]
                put(i, rr, a, jnp.where(a[HS : HS + 1] > 0, 0.0, lowest_max))
                return 0

            lax.fori_loop(0, 4, finish, 0)

    @pl.when(jnp.logical_not(safe))
    def _():
        for i in range(chips):
            def one_block(rr, _, i=i):
                r = i * 4 + rr
                row = whole_block(r)
                pos = pos_ref[pl.ds(row, 1), :]
                acc[0] = jnp.zeros((ACC_ROWS, ROWS), jnp.float32)

                def one_slot(c, top):
                    s = products(row, r, c)
                    best = top
                    for t in range(TILES):
                        tile = s[t * BLOCK : (t + 1) * BLOCK]
                        tile = jnp.where(iota <= last_key(row, c, t, pos, True), tile, masked_score)
                        s_all[t * BLOCK : (t + 1) * BLOCK, :] = tile
                        best = jnp.maximum(best, jnp.max(tile, 0, keepdims=True))
                    best = best.astype(jnp.bfloat16).astype(jnp.float32)
                    p = jnp.exp2((s_all[...] - best) * LOG2E).astype(jnp.bfloat16)
                    shrink = jnp.exp2((top - best) * LOG2E)
                    acc[0] = acc[0] * shrink + jnp.dot(values(row, c), p, preferred_element_type=jnp.float32)
                    return best

                start = jnp.full((1, ROWS), lowest_max, jnp.bfloat16).astype(jnp.float32)
                top = lax.fori_loop(0, code_ref[row, table + KEY_BLOCKS], one_slot, start)
                put(i, rr, acc[0], top)
                return 0

            lax.fori_loop(0, 4, one_block, 0)


def attend(steps, codes, spots, held, queries, before=()):
    kv, vt, norm = held
    chips = len(steps)
    out = jax.ShapeDtypeStruct((2, ACC_ROWS, queries[0].shape[2]), jnp.bfloat16)
    return pl.pallas_call(
        functools.partial(attention_kernel, steps, bool(before)),
        in_specs=[pl.BlockSpec(memory_space=pl.ANY)] + [VMEM] * (4 + len(queries) + len(before)),
        out_specs=[VMEM] * chips,
        out_shape=[out] * chips,
        scratch_shapes=[
            pltpu.VMEM((2 * chips, HS, queries[0].shape[2]), jnp.bfloat16),
            pltpu.VMEM((SLOTS * TILES * BLOCK, ROWS), jnp.bfloat16),
            pltpu.VMEM((SLOTS * TILES * BLOCK, ROWS), jnp.bfloat16),
            pltpu.VMEM((TILES * BLOCK, ROWS), jnp.float32),
            pltpu.VMEM((4 * chips + 1, ACC_ROWS, ROWS), jnp.float32),
            pltpu.SMEM(codes.shape, jnp.int32),
            pltpu.SemaphoreType.DMA,
        ],
        compiler_params=pltpu.CompilerParams(vmem_limit_bytes=32 * 2**20),
        cost_estimate=pl.CostEstimate(
            flops=chips * 6 * 10**9, bytes_accessed=4 * 2**20, transcendentals=chips * 2**20
        ),
    )(codes, norm, spots, kv, vt, *queries, *before)


def combine_kernel(*refs):
    core = jnp.bitwise_and(lax.axis_index("seq"), 1)
    parts, out_ref = refs[:-1], refs[-1]
    groups = out_ref.shape[0] // 2
    half = out_ref.shape[1]
    for j in range(2):
        tops = [p[j, HS + 1 : HS + 2, :].astype(jnp.float32) for p in parts]
        top = functools.reduce(jnp.maximum, tops)
        scales = [jnp.exp(t - top) for t in tops]
        total = sum(
            (p[j, HS : HS + 1, :].astype(jnp.float32) + p[j, HS + 2 : HS + 3, :].astype(jnp.float32)) * scale
            for p, scale in zip(parts, scales)
        )
        summed = sum(p[j, :HS, :].astype(jnp.float32) * scale for p, scale in zip(parts, scales))
        rows = (summed / total).T.astype(jnp.bfloat16)
        first = jnp.bitwise_xor(core, j) * groups
        for g in range(groups):
            upper = rows[2 * g * half : (2 * g + 1) * half]
            lower = rows[(2 * g + 1) * half : (2 * g + 2) * half]
            out_ref[first + g] = jnp.concatenate([upper, lower], 1)


def combine(parts):
    half = parts[0].shape[2] // 16
    return pl.pallas_call(
        combine_kernel,
        in_specs=[VMEM] * len(parts),
        out_specs=VMEM,
        out_shape=jax.ShapeDtypeStruct((16, half, 2 * HS), jnp.bfloat16),
        compiler_params=pltpu.CompilerParams(vmem_limit_bytes=32 * 2**20),
    )(*parts)


def finish_kernel(pieces_ref, *refs):
    w_refs, out_ref = refs[:-1], refs[-1]
    groups = pieces_ref.shape[0] // 2
    me = lax.axis_index("grp")
    result = None
    for k, w_ref in enumerate(w_refs):
        near = jnp.bitwise_xor(me, k)
        order = [c * groups + g for g in (near, jnp.bitwise_xor(near, 4)) for c in range(2)]
        blocks = [pieces_ref[i] for i in order]
        upper = jnp.concatenate([p[:, :HS] for p in blocks], 1)
        lower = jnp.concatenate([p[:, HS:] for p in blocks], 1)
        attention = jnp.concatenate([upper, lower], 0)
        term = jnp.dot(attention, w_ref[...], preferred_element_type=jnp.float32)
        result = term if result is None else result + term
    out_ref[...] = result.astype(jnp.bfloat16)


def finish(pieces, w_turns):
    return pl.pallas_call(
        finish_kernel,
        in_specs=[VMEM] * (1 + len(w_turns)),
        out_specs=VMEM,
        out_shape=jax.ShapeDtypeStruct((2 * pieces.shape[1], w_turns[0].shape[1]), jnp.bfloat16),
        compiler_params=pltpu.CompilerParams(vmem_limit_bytes=24 * 2**20),
    )(pieces, *w_turns)


def along_x(by):
    return [(s, s ^ (4 * by)) for s in range(16)]


def came_from(s, by):
    return jnp.bitwise_xor(s, 4 * by)


NEAR_CALLS = ((0,), (1, 3, 2))
FAR_CALLS = ((2, 1, 3), (0,))
CORE_SWAP = [(s, s ^ 1) for s in range(16)]
Y_SWAP = [(s, s ^ 2) for s in range(16)]


def body(inputs, latents, w_query, w_key, w_value, w_out, positions, block_mask):
    w_other = lax.ppermute(w_out, "grp", [(g, g ^ 4) for g in range(8)])
    q_chip, theirs, kv_own, kv_other, codes = front(
        latents, inputs, w_query, w_key, w_value, positions, block_mask
    )
    theirs, kv_other, kv_own, w_other = lax.optimization_barrier((theirs, kv_other, kv_own, w_other))
    q_chip = q_chip.at[1].set(lax.ppermute(theirs, "seq", CORE_SWAP))
    queries = {by: q_chip if by == 0 else lax.ppermute(q_chip, "seq", along_x(by)) for by in (0, 1, 3, 2)}
    kv_partner = lax.ppermute(kv_other, "seq", CORE_SWAP)
    near = prepare(kv_own, kv_partner)
    kv_far = [lax.ppermute(kv, "seq", Y_SWAP) for kv in (kv_own, kv_partner)]

    spots = positions.reshape(-1, ROWS)
    near_parts = dict(zip(NEAR_CALLS[0], attend(NEAR_CALLS[0], codes, spots, near, [q_chip])))
    w_other, near_parts[0] = lax.optimization_barrier((w_other, near_parts[0]))
    w_pair = jnp.concatenate([w_out, w_other], 0)
    w_turns = [w_pair] + [
        lax.ppermute(w_pair, "grp", [(g, g ^ k) for g in range(8)]) for k in (1, 2, 3)
    ]

    parts = {}
    last = 0
    for call in NEAR_CALLS[1:]:
        queries[call[0]], near_parts[last], kv_far[0] = lax.optimization_barrier(
            (queries[call[0]], near_parts[last], kv_far[0])
        )
        near_parts.update(zip(call, attend(call, codes, spots, near, [queries[by] for by in call])))
        last = call[-1]
    kv_far, near_parts[last] = lax.optimization_barrier((kv_far, near_parts[last]))
    far = prepare(*kv_far)
    last = None
    for call in FAR_CALLS:
        if last is not None:
            queries[call[0]], parts[last] = lax.optimization_barrier((queries[call[0]], parts[last]))
        done = attend(
            call, codes, spots, far, [queries[by] for by in call], [near_parts[by] for by in call]
        )
        parts.update(zip(call, done))
        last = call[-1]

    parts = [part if by == 0 else lax.ppermute(part, "seq", along_x(by)) for by, part in parts.items()]
    parts, w_turns = lax.optimization_barrier((parts, w_turns))
    pieces = combine(parts)
    owners = [[(4 * x + 2 * y + c) * 8 + g for c in range(2) for g in range(8)] for x in range(4) for y in range(2)]
    pieces = lax.all_to_all(pieces, ("seq", "grp"), 0, 0, axis_index_groups=owners)
    return finish(pieces, w_turns)


def solution(mesh):
    return jax.shard_map(
        body,
        mesh=mesh,
        in_specs=(
            P("seq", None),
            P("seq", None),
            P(None, "grp"),
            P(None, "grp"),
            P(None, "grp"),
            P("grp", None),
            P(),
            P(),
        ),
        out_specs=P(("seq", "grp"), None),
        check_vma=False,
    )
```
